32 devices in a mesh: dp: 8 (over z, y), pipe: 4 (over x, core).
Axes of the slice: x: 2, y: 2, z: 4, core: 2. Of those that a mesh axis runs over, the one named last changes fastest.
Arguments:
- tokens: bfloat16 [32, 512, 768], P('dp'), may hold values from -18 to 18
- lengths: int32 [32], P('dp'), may hold values from 8 to 512, as said below
- ema_scales: float32 [4, 4], P('pipe'), may hold values from 2 to 6
- w_qkv: bfloat16 [4, 768, 2304], P('pipe'), may hold values from -0.21875 to 0.21875
- bias_qv: float32 [4, 1536], P('pipe'), may hold values from -4 to 4
- w_out: bfloat16 [4, 768, 768], P('pipe'), may hold values from -0.875 to 0.875
- bias_out: float32 [4, 768], P('pipe'), may hold values from -4 to 4
- w_up: bfloat16 [4, 768, 3072], P('pipe'), may hold values from -0.21875 to 0.21875
- bias_up: float32 [4, 3072], P('pipe'), may hold values from -4 to 4
- w_down: bfloat16 [4, 3072, 768], P('pipe'), may hold values from -0.109375 to 0.109375
- bias_down: float32 [4, 768], P('pipe'), may hold values from -4 to 4
- ln_gain: float32 [4, 2, 768], P('pipe'), may hold values from 0.5 to 1.5
- ln_bias: float32 [4, 2, 768], P('pipe'), may hold values from -4 to 4
- cotangent: bfloat16 [32, 512, 768], P('dp'), may hold values from -6 to 6
Outputs:
- mixed: bfloat16 [32, 512, 768], P('dp', 'pipe')
- grad_tokens: bfloat16 [32, 512, 768], P('dp', 'pipe')
- grad_w_qkv: float32 [4, 768, 2304], P('pipe', 'dp')
- grad_bias_qv: float32 [4, 1536], P('pipe', 'dp')
- grad_w_out: float32 [4, 768, 768], P('pipe', 'dp')
- grad_bias_out: float32 [4, 768], P('pipe', 'dp')
- grad_w_up: float32 [4, 768, 3072], P('pipe', 'dp')
- grad_bias_up: float32 [4, 3072], P('pipe', 'dp')
- grad_w_down: float32 [4, 3072, 768], P('pipe', 'dp')
- grad_bias_down: float32 [4, 768], P('pipe', 'dp')
- grad_ln_gain: float32 [4, 2, 768], P('pipe', None, 'dp')
- grad_ln_bias: float32 [4, 2, 768], P('pipe', None, 'dp')
- batch_max: float32 [4, 4], P('pipe')
The draws below stay inside these ranges and needn't reach their ends.
Inputs may be any that keep to these rules, and one draw needn't show every extreme that they name: `lengths`: each row holds one sequence from position 0: either of 8 to 128 tokens or of more than 128; the rest of its 512 positions is padding. Some row holds 512 tokens.
All inputs are finite; a program needn't handle non-finite values.
Results may differ from the reference program's by a relative error of at most 0.02.
The reference program's roundings to bfloat16 on the way count: a program that leaves them out, or rounds other values in their place, can miss the bound.
Values may be sent and summed in bfloat16 or wider, within the bound.
A program may use at most 576 MiB of HBM per device.

```python
import math
import jax
import jax.numpy as jnp
from jax import lax

D = 768
HEAD_DIM = 64
FF = 3072
SEQ = 512
SHORT = 128
LAYERS = 4
BATCH = 32


def draw_tokens(key, part):
    key = jax.random.fold_in(key, 11)
    row_index = jnp.arange(BATCH, dtype=jnp.float32)
    row_scale = 1.0 + 2.0 * row_index / max(BATCH - 1, 1)
    normal_part = jnp.clip(jax.random.normal(key, (BATCH, SEQ, D), jnp.float32), -6.0, 6.0)
    return (normal_part * row_scale[:, None, None]).astype(jnp.bfloat16)


def draw_lengths(key, part):
    key = jax.random.fold_in(key, 23)
    chooser_key, short_key, lengthy_key, full_key = jax.random.split(key, 4)
    longer = jax.random.randint(chooser_key, (BATCH,), 0, 2)
    short_len = jax.random.randint(short_key, (BATCH,), 8, SHORT + 1)
    lengthy = jax.random.randint(lengthy_key, (BATCH,), SHORT + 1, SEQ + 1)
    full_row = jax.random.randint(full_key, (), 0, BATCH)
    picked = jnp.where(longer == 1, lengthy, short_len)
    return jnp.where(jnp.arange(BATCH) == full_row, SEQ, picked).astype(jnp.int32)


def shard_levels(stream_key, shape, cuts, least, largest):
    factor_of, own = 1.0, jax.random.fold_in(stream_key, 6)
    for dim, parts in cuts:
        heights = jnp.exp(jax.random.uniform(jax.random.fold_in(own, dim), (parts,), jnp.float32, least / len(cuts), largest / len(cuts)))
        factor_of = factor_of * jnp.repeat(heights, shape[dim] // parts).reshape([-1 if axis == dim else 1 for axis in range(len(shape))])
    return factor_of


def scatter_about(rng, shape, scale, limit, shards=(), kind=jnp.bfloat16):
    result = jax.random.normal(rng, shape, jnp.float32) * scale
    if len(shards) > 0:
        result = shard_levels(rng, shape, shards, -0.22, 0.18) * result
    return jnp.clip(result, min=-limit, max=limit).astype(kind)


def setup_inputs(seed: int = 0) -> dict:
    splits = jax.random.split(jax.random.key(seed), 15)
    return {
        "tokens": draw_tokens(jax.random.fold_in(splits[14], 71), 0),
        "lengths": draw_lengths(jax.random.fold_in(splits[14], 71), 0),
        "ema_scales": jnp.clip(jnp.exp(math.log(6.0) - 1.0986123 * jax.random.uniform(splits[2], (LAYERS, 4), jnp.float32) ** shard_levels(splits[2], (LAYERS, 4), ((0, 4),), -0.2, 0.2)), 2.0, 6.0),
        "w_qkv": scatter_about(splits[3], (LAYERS, D, 3 * D), D ** -0.5, 0.21875, ((0, 4),)),
        "bias_qv": scatter_about(splits[4], (LAYERS, 2 * D), 0.3, 4.0, ((0, 4),), jnp.float32),
        "w_out": scatter_about(splits[5], (LAYERS, D, D), (D // 16) ** -0.5, 0.875, ((0, 4),)),
        "bias_out": scatter_about(splits[6], (LAYERS, D), 0.3, 4.0, ((0, 4),), jnp.float32),
        "w_up": scatter_about(splits[7], (LAYERS, D, FF), D ** -0.5, 0.21875, ((0, 4),)),
        "bias_up": scatter_about(splits[8], (LAYERS, FF), 0.3, 4.0, ((0, 4),), jnp.float32),
        "w_down": scatter_about(splits[9], (LAYERS, FF, D), FF ** -0.5, 0.109375, ((0, 4),)),
        "bias_down": scatter_about(splits[10], (LAYERS, D), 0.3, 4.0, ((0, 4),), jnp.float32),
        "ln_gain": jnp.clip(1.0 + 0.1 * jax.random.normal(splits[11], (LAYERS, 2, D), jnp.float32), 0.5, 1.5),
        "ln_bias": scatter_about(splits[12], (LAYERS, 2, D), 0.3, 4.0, ((0, 4),), jnp.float32),
        "cotangent": scatter_about(splits[13], (BATCH, SEQ, D), 1.0, 6.0, ((0, 8),)),
    }


@jax.custom_vjp
def low(v):
    return lax.optimization_barrier(v.astype(jnp.bfloat16)).astype(jnp.float32)

@jax.custom_vjp
def low_back(v):
    return v

def low_keep(v):
    return (low(v), None)

def low_pass(kept, grad):
    return (grad,)

def back_keep(v):
    return (v, None)

def back_low(kept, grad):
    return (low(grad),)
low.defvjp(low_keep, low_pass)
low_back.defvjp(back_keep, back_low)
norm_eps = 1e-06
mask_fill = -1000000000.0
highest = lax.Precision.HIGHEST

def squash(signal, ceiling):
    return ceiling * jnp.tanh(signal / ceiling)

def layer_norm(signal, gain_vec, shift_vec):
    center = signal - lax.optimization_barrier(jnp.mean(signal, -1, keepdims=True))
    spread = lax.optimization_barrier(jnp.mean(center * center, -1, keepdims=True))
    return center * lax.rsqrt(spread + norm_eps) * gain_vec + shift_vec

def product(left_op, right_op):
    return jnp.einsum('gsd,de->gse', left_op, right_op, precision=highest)

def split_heads(signal):
    return signal.reshape(signal.shape[0], signal.shape[1] // HEAD_DIM, HEAD_DIM)

def attend_row(operands):
    queries, keys_low, values_low, length = operands
    seq_len = queries.shape[0]
    scores = jnp.einsum('qhd,khd->hqk', split_heads(queries), split_heads(keys_low), precision=highest) * HEAD_DIM ** (-0.5)
    key_mask = jnp.arange(seq_len) < length
    scores = low_back(jnp.where(key_mask[None, None, :], scores, mask_fill))
    row_top = lax.optimization_barrier(jnp.max(scores, -1, keepdims=True))
    weights = jnp.exp(scores - row_top)
    probabilities = weights / lax.optimization_barrier(jnp.sum(weights, -1, keepdims=True))
    context = jnp.einsum('hqk,khd->qhd', low(probabilities), split_heads(values_low), precision=highest)
    return low_back(context.reshape(queries.shape))

def masked_peak(signal, valid_mask):
    return jnp.max(jnp.where(valid_mask[..., None], jnp.abs(signal), 0.0))

def one_layer(layer_in, lengths, valid_mask, weights, ceilings):
    model_width = layer_in.shape[-1]
    x_low = low(squash(layer_in, ceilings[0]))
    projected = product(x_low, weights['w_qkv'])
    queries = low(low_back(projected[..., :model_width] + weights['bias_qv'][:model_width]))
    keys_low = low(low_back(projected[..., model_width:2 * model_width]))
    values_low = low(low_back(projected[..., 2 * model_width:] + weights['bias_qv'][model_width:]))
    context = lax.map(jax.checkpoint(attend_row), (queries, keys_low, values_low, lengths))
    ctx_low = low(squash(context, ceilings[1]))
    branch = low_back(product(ctx_low, weights['w_out']) + weights['bias_out'])
    hidden = layer_norm(layer_in + branch, weights['ln_gain'][0], weights['ln_bias'][0])
    hid_low = low(squash(hidden, ceilings[2]))
    up_pre = low_back(product(hid_low, weights['w_up']) + weights['bias_up'])
    active = jax.nn.gelu(up_pre, approximate=False)
    act_low = low(squash(active, ceilings[3]))
    down_out = low_back(product(act_low, weights['w_down']) + weights['bias_down'])
    layer_out = low(layer_norm(hidden + down_out, weights['ln_gain'][1], weights['ln_bias'][1]))
    peaks = jnp.stack([masked_peak(layer_in, valid_mask), masked_peak(context, valid_mask), masked_peak(hidden, valid_mask), masked_peak(active, valid_mask)])
    return (layer_out, peaks)

def run_stack(tokens_in, params, lengths, valid_mask, ceilings):
    hidden_state = tokens_in
    maxima = []
    for layer_id in range(LAYERS):
        hidden_state = low_back(hidden_state)
        layer_params = jax.tree.map(lambda tensor: tensor[layer_id], params)
        hidden_state, peaks = one_layer(hidden_state, lengths, valid_mask, layer_params, ceilings[layer_id])
        maxima.append(peaks)
    return (hidden_state, jnp.stack(maxima))

def reference(tokens, lengths, ema_scales, w_qkv, bias_qv, w_out, bias_out, w_up, bias_up, w_down, bias_down, ln_gain, ln_bias, cotangent):
    params = {'w_qkv': w_qkv.astype(jnp.float32), 'bias_qv': bias_qv, 'w_out': w_out.astype(jnp.float32), 'bias_out': bias_out, 'w_up': w_up.astype(jnp.float32), 'bias_up': bias_up, 'w_down': w_down.astype(jnp.float32), 'bias_down': bias_down, 'ln_gain': ln_gain, 'ln_bias': ln_bias}
    group_rows = math.gcd(BATCH, max(1, 4096 // SEQ))
    group_count = BATCH // group_rows
    model_width = tokens.shape[-1]
    blocks = (tokens.reshape(group_count, group_rows, SEQ, model_width), lengths.reshape(group_count, group_rows), cotangent.reshape(group_count, group_rows, SEQ, model_width))

    def scan_step(running, block_in):
        totals, peaks = running
        tokens_in, row_lengths, seed_grad = block_in
        valid_mask = jnp.arange(SEQ)[None, :] < row_lengths[:, None]

        def forward(hidden_state, weights):
            return run_stack(hidden_state, weights, row_lengths, valid_mask, ema_scales)
        layer_out, pull_back, maxima = jax.vjp(forward, tokens_in.astype(jnp.float32), params, has_aux=True)
        grad_in, grad_params = pull_back(seed_grad.astype(jnp.float32) * valid_mask[..., None].astype(jnp.float32))
        totals = jax.tree.map(jnp.add, totals, grad_params)
        return ((totals, jnp.maximum(peaks, maxima)), (layer_out.astype(jnp.bfloat16), grad_in.astype(jnp.bfloat16)))
    start_grads = jax.tree.map(jnp.zeros_like, params)
    start_peaks = jnp.zeros((LAYERS, 4), jnp.float32)
    (totals, peaks), (mixed, grad_tokens) = lax.scan(scan_step, (start_grads, start_peaks), blocks)
    mixed = mixed.reshape(BATCH, SEQ, model_width)
    grad_tokens = grad_tokens.reshape(BATCH, SEQ, model_width)
    return (mixed, grad_tokens, totals['w_qkv'], totals['bias_qv'], totals['w_out'], totals['bias_out'], totals['w_up'], totals['bias_up'], totals['w_down'], totals['bias_down'], totals['ln_gain'], totals['ln_bias'], peaks)
```

```python
import jax
import jax.numpy as jnp
from jax import lax
from jax.experimental import pallas as pl
from jax.experimental.pallas import tpu as pltpu
from jax.sharding import PartitionSpec as P

HEAD_DIM = 64
PAIR = 2 * HEAD_DIM
EPS = 1e-06
MASKED = -1000000000.0
CHUNK = 512
ROWS = 64
LOGICAL = pl.DeviceIdType.MESH
F32 = jnp.float32
BF16 = jnp.bfloat16

ERF_POLY = (
    0.7978846780398201,
    0.03633450830808018,
    -3.432973817348946e-05,
    -5.463434792182573e-05,
    3.860434711489827e-06,
    -1.254735264100511e-07,
    1.6084598007909267e-09,
)
ERF_CLAMP = 5.3 * 5.3
INV_SQRT_2PI = 0.3989422804014327


def dot_nn(a, b):
    return jnp.dot(a, b, preferred_element_type=F32)


def dot_nt(a, b):
    return lax.dot_general(a, b, (((1,), (1,)), ((), ())), preferred_element_type=F32)


def fold_rows(v):
    return jnp.sum(v.reshape(v.shape[0] // 8, 8, v.shape[1]), 0)


def peak_rows(v):
    tiles = [v[:, i : i + 128] for i in range(0, v.shape[1], 128)]
    top = tiles[0]
    for tile in tiles[1:]:
        top = jnp.maximum(top, tile)
    return jnp.max(top.reshape(v.shape[0] // 8, 8, 128), 0)


def split3(v):
    hi = v.astype(BF16)
    rest = v - hi.astype(F32)
    mid = rest.astype(BF16)
    low = (rest - mid.astype(F32)).astype(BF16)
    return hi, mid, low


def greet(stage, count):
    barrier = pltpu.get_barrier_semaphore()
    for step in range(1, count):
        peer = lax.rem(stage + step, count)
        pl.semaphore_signal(barrier, inc=1, device_id={"pipe": peer}, device_id_type=LOGICAL)
    pl.semaphore_wait(barrier, count - 1)


def activation(u, ceiling, inv_ceiling):
    w = jnp.minimum(u * u, ERF_CLAMP)
    poly = w * ERF_POLY[-1] + ERF_POLY[-2]
    for coef in ERF_POLY[-3::-1]:
        poly = poly * w + coef
    phi_cdf = 0.5 + 0.5 * jnp.tanh(u * poly)
    act = u * phi_cdf
    ratio = jnp.tanh(act * inv_ceiling)
    slope = (1.0 - ratio * ratio) * (
        phi_cdf + (u * INV_SQRT_2PI) * jnp.exp(u * u * -0.5)
    )
    return act, ceiling * ratio, slope


def fwd_kernel(count, *refs):
    (
        lens, scales, tokens, w_qkv, b_qkv, w_out, b_out, w_up, b_up, w_down, b_down, gain, shift,
        x_o, xq_o, qkv_o, lse_o, ctx_o, cq_o, n1_o, rs1_o, hq_o, aq_o, sl_o, n2_o, rs2_o,
        mixed_o, peaks_o,
        xin, xout, xq_s, qkv_s, lse_s, ctx_s, cq_s, n1_s, rs1_s, hq_s, aq_s, sl_s, n2_s, rs2_s,
        acc, hid, up_s, save_sem, in_sem, send_sem, recv_sem, mix_send, mix_recv,
    ) = refs
    r = pl.program_id(0)
    rows = pl.num_programs(0)
    row_count = tokens.shape[0]
    seq, width = tokens.shape[1], tokens.shape[2]
    ff = w_up.shape[1]
    piece = seq // count
    stage = lax.axis_index("pipe")
    first = stage == 0
    last = stage == count - 1

    staged = {
        "x": (xin.at[r], x_o), "xq": (xq_s, xq_o), "qkv": (qkv_s, qkv_o), "lse": (lse_s, lse_o),
        "ctx": (ctx_s, ctx_o), "cq": (cq_s, cq_o), "n1": (n1_s, n1_o), "rs1": (rs1_s, rs1_o),
        "hq": (hq_s, hq_o), "aq": (aq_s, aq_o), "sl": (sl_s, sl_o), "n2": (n2_s, n2_o),
        "rs2": (rs2_s, rs2_o),
    }
    order = list(staged)

    def save_copy(name):
        src, dst = staged[name]
        return pltpu.make_async_copy(src, dst.at[r], save_sem.at[order.index(name)])

    def save(name):
        save_copy(name).start()

    def reuse(*names):
        @pl.when(r > 0)
        def _():
            for name in names:
                save_copy(name).wait()

    def token_copy(i):
        return pltpu.make_async_copy(tokens.at[i], xin.at[i], in_sem.at[i])

    def hop(i):
        return pltpu.make_async_remote_copy(
            src_ref=xout.at[i], dst_ref=xin.at[i], send_sem=send_sem.at[i], recv_sem=recv_sem.at[i],
            device_id={"pipe": lax.rem(stage + 1, count)}, device_id_type=LOGICAL,
        )

    def mix_part(i, p):
        return pltpu.make_async_remote_copy(
            src_ref=xout.at[i, pl.ds(p * piece, piece)], dst_ref=mixed_o.at[i],
            send_sem=mix_send.at[i, p], recv_sem=mix_recv.at[i],
            device_id={"pipe": jnp.int32(p)}, device_id_type=LOGICAL,
        )

    def mix_own(i):
        return pltpu.make_async_copy(
            xout.at[i, pl.ds((count - 1) * piece, piece)], mixed_o.at[i], mix_send.at[i, count - 1]
        )

    @pl.when(r == 0)
    def _():
        greet(stage, count)
        peaks_o[...] = jnp.zeros_like(peaks_o)

        @pl.when(first)
        def _():
            for i in range(row_count):
                token_copy(i).start()

    @pl.when(first)
    def _():
        token_copy(r).wait()

    @pl.when(jnp.logical_not(first))
    def _():
        hop(r).wait_recv()

    length = lens[r]
    m0, m1, m2, m3 = scales[0, 0], scales[0, 1], scales[0, 2], scales[0, 3]
    i0, i1, i2, i3 = 1.0 / m0, 1.0 / m1, 1.0 / m2, 1.0 / m3
    steps = seq // ROWS

    def row_mask(start, size):
        return (start + lax.broadcasted_iota(jnp.int32, (size, 1), 0)) < length

    def note_peak(k, v, start):
        top = jnp.where(row_mask(start, v.shape[0]), jnp.abs(v), 0.0)
        peaks_o[k] = jnp.maximum(peaks_o[k], peak_rows(top))

    @pl.when(r > 0)
    def _():
        save_copy("x").wait()

    save("x")
    reuse("xq", "qkv", "lse", "ctx", "cq")

    def quant_in(i, _):
        at = pl.ds(pl.multiple_of(i * ROWS, ROWS), ROWS)
        x = xin[r, at, :].astype(F32)
        note_peak(0, x, i * ROWS)
        xq_s[at, :] = (m0 * jnp.tanh(x * i0)).astype(BF16)
        return 0

    lax.fori_loop(0, steps, quant_in, 0)
    save("xq")

    for j in range(3):
        cols = pl.ds(j * width, width)
        proj = dot_nn(xq_s[...], w_qkv[:, cols]) + b_qkv[:, cols]
        qkv_s[:, cols] = proj.astype(BF16)
    save("qkv")

    lane = lax.broadcasted_iota(jnp.int32, (seq, PAIR), 1)
    lo = lane < HEAD_DIM
    key_bias = jnp.where(lax.broadcasted_iota(jnp.int32, (seq, PAIR), 0) < length, 0.0, MASKED).astype(BF16)
    one = jnp.ones((), BF16)
    zero = jnp.zeros((), BF16)

    def attend(p, _):
        at = pl.multiple_of(p * PAIR, PAIR)
        q2 = qkv_s[:, pl.ds(at, PAIR)] * jnp.asarray(HEAD_DIM ** -0.5, BF16)
        k2 = qkv_s[:, pl.ds(pl.multiple_of(width + at, PAIR), PAIR)]
        v2 = qkv_s[:, pl.ds(pl.multiple_of(2 * width + at, PAIR), PAIR)]
        q_a, q_b = jnp.where(lo, q2, one), jnp.where(lo, one, q2)
        k_a = jnp.where(lo, k2, jnp.where(lane == HEAD_DIM, key_bias, zero))
        k_b = jnp.where(lo, jnp.where(lane == 0, key_bias, zero), k2)
        s_a = dot_nt(q_a, k_a)
        s_b = dot_nt(q_b, k_b)
        top_a = jnp.max(s_a, -1, keepdims=True)
        e_a = jnp.exp(s_a - top_a).astype(BF16)
        top_b = jnp.max(s_b, -1, keepdims=True)
        o_a = dot_nn(e_a, jnp.where(lo, v2, one))
        e_b = jnp.exp(s_b - top_b).astype(BF16)
        o_b = dot_nn(e_b, jnp.where(lo, one, v2))
        total = pltpu.roll(jnp.where(lo, o_b, o_a), HEAD_DIM, 1)
        ctx_s[:, pl.ds(at, PAIR)] = jnp.where(lo, o_a, o_b) / total
        lse_s[:, pl.ds(at, PAIR)] = jnp.where(lo, top_a, top_b) + jnp.log(total)
        return 0

    lax.fori_loop(0, width // PAIR, attend, 0)
    save("lse")
    save("ctx")

    def quant_ctx(i, _):
        at = pl.ds(pl.multiple_of(i * ROWS, ROWS), ROWS)
        c = ctx_s[at, :]
        note_peak(1, c, i * ROWS)
        cq_s[at, :] = (m1 * jnp.tanh(c * i1)).astype(BF16)
        return 0

    lax.fori_loop(0, steps, quant_ctx, 0)
    save("cq")
    acc[...] = dot_nn(cq_s[...], w_out[...])
    reuse("n1", "rs1", "hq")

    def norm_one(i, _):
        at = pl.ds(pl.multiple_of(i * ROWS, ROWS), ROWS)
        s = xin[r, at, :].astype(F32) + (acc[at, :] + b_out[...])
        center = s - jnp.mean(s, -1, keepdims=True)
        rs = lax.rsqrt(jnp.mean(center * center, -1, keepdims=True) + EPS)
        n = center * rs
        h = n * gain[0:1, :] + shift[0:1, :]
        n1_s[at, :] = n.astype(BF16)
        rs1_s[at, :] = jnp.broadcast_to(rs, (ROWS, 128))
        hid[at, :] = h
        hq_s[at, :] = (m2 * jnp.tanh(h * i2)).astype(BF16)
        note_peak(2, h, i * ROWS)
        return 0

    lax.fori_loop(0, steps, norm_one, 0)
    save("n1")
    save("rs1")
    save("hq")
    reuse("aq", "sl")

    chunks = ff // CHUNK
    mask_all = row_mask(0, seq)

    def up_chunk(c):
        cols = pl.ds(c * CHUNK, CHUNK)
        up_s[c % 2] = dot_nn(hq_s[...], w_up[:, cols]) + b_up[:, cols]

    def act_chunk(c):
        cols = pl.ds(c * CHUNK, CHUNK)
        act, low, slope = activation(up_s[c % 2], m3, i3)
        aq_s[:, cols] = low.astype(BF16)
        sl_s[:, cols] = slope.astype(BF16)
        top = jnp.where(mask_all, jnp.abs(act), 0.0)
        peaks_o[3] = jnp.maximum(peaks_o[3], peak_rows(top))

    def down_chunk(c):
        cols = pl.ds(c * CHUNK, CHUNK)
        part = dot_nn(aq_s[:, cols], w_down[cols, :])
        if c == 0:
            acc[...] = part
        else:
            acc[...] += part

    up_chunk(0)
    for c in range(chunks):
        if c + 1 < chunks:
            up_chunk(c + 1)
        act_chunk(c)
        if c > 0:
            down_chunk(c - 1)
    down_chunk(chunks - 1)
    save("aq")
    save("sl")
    reuse("n2", "rs2")

    def norm_two(i, _):
        at = pl.ds(pl.multiple_of(i * ROWS, ROWS), ROWS)
        s = hid[at, :] + (acc[at, :] + b_down[...])
        center = s - jnp.mean(s, -1, keepdims=True)
        rs = lax.rsqrt(jnp.mean(center * center, -1, keepdims=True) + EPS)
        n = center * rs
        n2_s[at, :] = n.astype(BF16)
        rs2_s[at, :] = jnp.broadcast_to(rs, (ROWS, 128))
        xout[r, at, :] = (n * gain[1:2, :] + shift[1:2, :]).astype(BF16)
        return 0

    lax.fori_loop(0, steps, norm_two, 0)
    save("n2")
    save("rs2")

    @pl.when(jnp.logical_not(last))
    def _():
        hop(r).start()

    @pl.when(last)
    def _():
        for p in range(count - 1):
            mix_part(r, p).start()
        mix_own(r).start()

    @pl.when(r == rows - 1)
    def _():
        for name in order:
            save_copy(name).wait()

        @pl.when(jnp.logical_not(last))
        def _():
            for i in range(row_count):
                hop(i).wait_send()
            for i in range(row_count):
                mix_part(i, 0).wait_recv()

        @pl.when(last)
        def _():
            for i in range(row_count):
                for p in range(count - 1):
                    mix_part(i, p).wait_send()
                mix_own(i).wait()


def bwd_kernel(count, *refs):
    (
        lens, scales, seeds, w_qkv, w_out, w_up, w_down, gain, shift,
        x_i, qkv_i, lse_i, ctx_i, n1_i, rs1_i, sl_i, n2_i, rs2_i,
        dproj_o, dbr_o, dup_o, ddn_o, gtok_o, small_o,
        gin, gout, x_s, qkv_s, lse_s, ctx_s, n1_s, rs1_s, sl_s, n2_s, rs2_s,
        dproj_s, dbr_s, dup_s, ddn_s, dctx_s, acc, dr,
        load_sem, save_sem, in_sem, send_sem, recv_sem, tok_send, tok_recv,
    ) = refs
    r = pl.program_id(0)
    rows = pl.num_programs(0)
    row_count = seeds.shape[0]
    seq, width = seeds.shape[1], seeds.shape[2]
    ff = w_up.shape[1]
    piece = seq // count
    stage = lax.axis_index("pipe")
    first = stage == 0
    last = stage == count - 1
    steps = seq // ROWS

    loaded = {
        "n2": (n2_i, n2_s), "rs2": (rs2_i, rs2_s), "sl": (sl_i, sl_s), "n1": (n1_i, n1_s),
        "rs1": (rs1_i, rs1_s), "ctx": (ctx_i, ctx_s), "qkv": (qkv_i, qkv_s), "lse": (lse_i, lse_s),
        "x": (x_i, x_s),
    }
    load_order = list(loaded)
    staged = {
        "ddn": (ddn_s, ddn_o), "dup": (dup_s, dup_o), "dbr": (dbr_s, dbr_o), "dproj": (dproj_s, dproj_o),
    }
    save_order = list(staged)

    def load_copy(name, i):
        src, dst = loaded[name]
        return pltpu.make_async_copy(src.at[i], dst, load_sem.at[load_order.index(name)])

    def fetch_next(*names):
        @pl.when(r + 1 < rows)
        def _():
            for name in names:
                load_copy(name, r + 1).start()

    def ready(*names):
        for name in names:
            load_copy(name, r).wait()

    def save_copy(name):
        src, dst = staged[name]
        return pltpu.make_async_copy(src, dst.at[r], save_sem.at[save_order.index(name)])

    def save(name):
        save_copy(name).start()

    def reuse(*names):
        @pl.when(r > 0)
        def _():
            for name in names:
                save_copy(name).wait()

    def seed_copy(i):
        return pltpu.make_async_copy(seeds.at[i], gin.at[i], in_sem.at[i])

    def hop(i):
        return pltpu.make_async_remote_copy(
            src_ref=gout.at[i], dst_ref=gin.at[i], send_sem=send_sem.at[i], recv_sem=recv_sem.at[i],
            device_id={"pipe": lax.rem(stage + count - 1, count)}, device_id_type=LOGICAL,
        )

    def tok_part(i, p):
        return pltpu.make_async_remote_copy(
            src_ref=gout.at[i, pl.ds(p * piece, piece)], dst_ref=gtok_o.at[i],
            send_sem=tok_send.at[i, p], recv_sem=tok_recv.at[i],
            device_id={"pipe": jnp.int32(p)}, device_id_type=LOGICAL,
        )

    def tok_own(i):
        return pltpu.make_async_copy(gout.at[i, pl.ds(0, piece)], gtok_o.at[i], tok_send.at[i, 0])

    @pl.when(r == 0)
    def _():
        greet(stage, count)
        small_o[...] = jnp.zeros_like(small_o)
        for name in load_order:
            load_copy(name, 0).start()

        @pl.when(last)
        def _():
            for i in range(row_count):
                seed_copy(i).start()

    @pl.when(last)
    def _():
        seed_copy(r).wait()

    @pl.when(jnp.logical_not(last))
    def _():
        hop(r).wait_recv()

    length = lens[r]
    m0, m1, m2 = scales[0, 0], scales[0, 1], scales[0, 2]
    i0, i1, i2 = 1.0 / m0, 1.0 / m1, 1.0 / m2

    offsets = {}
    at_col = 0
    for name, size in (
        ("gain0", width), ("gain1", width), ("shift0", width), ("shift1", width),
        ("out", width), ("down", width), ("up", ff), ("qkv", 3 * width),
    ):
        offsets[name] = at_col
        at_col += size

    def add_small(name, v, col=0):
        at = pl.ds(offsets[name] + col, v.shape[1])
        small_o[:, at] += fold_rows(v)

    ready("n2", "rs2")
    reuse("ddn")

    def norm_two(i, _):
        start = pl.multiple_of(i * ROWS, ROWS)
        at = pl.ds(start, ROWS)
        valid = (start + lax.broadcasted_iota(jnp.int32, (ROWS, 1), 0)) < length
        dy = jnp.where(valid, gin[r, at, :].astype(F32), 0.0)
        n = n2_s[at, :].astype(F32)
        rs = rs2_s[at, 0:1]
        dyn = dy * n
        e = dy * gain[1:2, :]
        mean_e = jnp.mean(e, -1, keepdims=True)
        mean_en = jnp.mean(e * n, -1, keepdims=True)
        d = (e - mean_e - n * mean_en) * rs
        dr[at, :] = d
        ddn_s[at, :] = d.astype(BF16)
        add_small("gain1", dyn)
        add_small("shift1", dy)
        add_small("down", d)
        return 0

    lax.fori_loop(0, steps, norm_two, 0)
    save("ddn")
    fetch_next("n2", "rs2")
    ready("sl")
    reuse("dup")

    chunks = ff // CHUNK

    def dact_chunk(c):
        cols = pl.ds(c * CHUNK, CHUNK)
        d = dot_nt(ddn_s[...], w_down[cols, :]) * sl_s[:, cols].astype(F32)
        dup_s[:, cols] = d.astype(BF16)
        add_small("up", d, c * CHUNK)

    def dhid_chunk(c):
        cols = pl.ds(c * CHUNK, CHUNK)
        part = dot_nt(dup_s[:, cols], w_up[:, cols])
        if c == 0:
            acc[...] = part
        else:
            acc[...] += part

    dact_chunk(0)
    for c in range(1, chunks):
        dact_chunk(c)
        dhid_chunk(c - 1)
    dhid_chunk(chunks - 1)
    save("dup")
    fetch_next("sl")
    ready("n1", "rs1")
    reuse("dbr")

    def norm_one(i, _):
        start = pl.multiple_of(i * ROWS, ROWS)
        at = pl.ds(start, ROWS)
        n = n1_s[at, :].astype(F32)
        rs = rs1_s[at, 0:1]
        t = jnp.tanh((n * gain[0:1, :] + shift[0:1, :]) * i2)
        dy = dr[at, :] + acc[at, :] * (1.0 - t * t)
        dyn = dy * n
        e = dy * gain[0:1, :]
        mean_e = jnp.mean(e, -1, keepdims=True)
        mean_en = jnp.mean(e * n, -1, keepdims=True)
        d = (e - mean_e - n * mean_en) * rs
        dr[at, :] = d
        dbr_s[at, :] = d.astype(BF16)
        add_small("gain0", dyn)
        add_small("shift0", dy)
        add_small("out", d)
        return 0

    lax.fori_loop(0, steps, norm_one, 0)
    save("dbr")
    fetch_next("n1", "rs1")
    ready("ctx")
    acc[...] = dot_nt(dbr_s[...], w_out[...])

    def quant_ctx(i, _):
        at = pl.ds(pl.multiple_of(i * ROWS, ROWS), ROWS)
        t = jnp.tanh(ctx_s[at, :] * i1)
        dctx_s[at, :] = (acc[at, :] * (1.0 - t * t)).astype(BF16)
        return 0

    lax.fori_loop(0, steps, quant_ctx, 0)
    ready("qkv", "lse")
    reuse("dproj")

    lane = lax.broadcasted_iota(jnp.int32, (seq, PAIR), 1)
    lo = lane < HEAD_DIM
    spot = jnp.where(lo, lane, lane - HEAD_DIM)
    key_bias = jnp.where(lax.broadcasted_iota(jnp.int32, (seq, PAIR), 0) < length, 0.0, MASKED).astype(BF16)
    one = jnp.ones((), BF16)
    zero = jnp.zeros((), BF16)
    scale = jnp.asarray(HEAD_DIM ** -0.5, BF16)
    src = lax.broadcasted_iota(jnp.int32, (PAIR, PAIR), 0) < HEAD_DIM
    dst = lax.broadcasted_iota(jnp.int32, (PAIR, PAIR), 1) < HEAD_DIM
    swap_sum = jnp.where(src == dst, 0.0, 1.0).astype(BF16)

    def attend(p, _):
        at = pl.multiple_of(p * PAIR, PAIR)
        here = pl.ds(at, PAIR)
        q2 = qkv_s[:, here] * scale
        k2 = qkv_s[:, pl.ds(pl.multiple_of(width + at, PAIR), PAIR)]
        v2 = qkv_s[:, pl.ds(pl.multiple_of(2 * width + at, PAIR), PAIR)]
        do2 = dctx_s[:, here]
        l_hi, l_mid, l_low = split3(pltpu.roll(lse_s[:, here], HEAD_DIM, 1))
        extra_q = jnp.where(
            spot == 0, one, jnp.where(spot == 1, -l_hi, jnp.where(spot == 2, -l_mid, -l_low))
        )
        extra_k = jnp.where(spot == 0, key_bias, jnp.where(spot <= 3, one, zero))
        e_hi, e_mid, e_low = split3(do2.astype(F32) * ctx_s[:, here])
        inner = dot_nn(e_hi, swap_sum) + dot_nn(e_mid, swap_sum)
        d_hi, d_mid, d_low = split3(inner)
        extra_do = jnp.where(spot == 0, -d_hi, jnp.where(spot == 1, -d_mid, -d_low))
        extra_v = jnp.where(spot <= 2, one, zero)
        k_t = k2.T

        def head(is_a):
            mine = lo if is_a else jnp.logical_not(lo)
            s = dot_nt(jnp.where(mine, k2, extra_k), jnp.where(mine, q2, extra_q))
            prob = jnp.exp(s)
            grad_p = dot_nt(jnp.where(mine, v2, extra_v), jnp.where(mine, do2, extra_do))
            grad_v = dot_nn(prob.astype(BF16), do2)
            grad_s = (prob * grad_p).astype(BF16)
            grad_k = dot_nn(grad_s, q2)
            half = k_t[0:HEAD_DIM] if is_a else k_t[HEAD_DIM:PAIR]
            return dot_nn(half, grad_s), grad_k, grad_v

        qa, ka, va = head(True)
        qb, kb, vb = head(False)
        grad_q = jnp.concatenate([qa, qb], 0).T * (HEAD_DIM ** -0.5)
        dproj_s[:, here] = grad_q.astype(BF16)
        dproj_s[:, pl.ds(pl.multiple_of(width + at, PAIR), PAIR)] = jnp.where(lo, ka, kb).astype(BF16)
        dproj_s[:, pl.ds(pl.multiple_of(2 * width + at, PAIR), PAIR)] = jnp.where(lo, va, vb).astype(BF16)
        return 0

    lax.fori_loop(0, width // PAIR, attend, 0)
    save("dproj")
    fetch_next("ctx", "qkv", "lse")
    for j in range(3):
        cols = pl.ds(j * width, width)
        part = dot_nt(dproj_s[:, cols], w_qkv[:, cols])
        if j == 0:
            acc[...] = part
        else:
            acc[...] += part
        if j != 1:
            add_small("qkv", dproj_s[:, cols].astype(F32), j * width)
    ready("x")

    def quant_in(i, _):
        at = pl.ds(pl.multiple_of(i * ROWS, ROWS), ROWS)
        t = jnp.tanh(x_s[at, :].astype(F32) * i0)
        gout[r, at, :] = (dr[at, :] + acc[at, :] * (1.0 - t * t)).astype(BF16)
        return 0

    lax.fori_loop(0, steps, quant_in, 0)
    fetch_next("x")

    @pl.when(jnp.logical_not(first))
    def _():
        hop(r).start()

    @pl.when(first)
    def _():
        for p in range(1, count):
            tok_part(r, p).start()
        tok_own(r).start()

    @pl.when(r == rows - 1)
    def _():
        for name in save_order:
            save_copy(name).wait()

        @pl.when(jnp.logical_not(first))
        def _():
            for i in range(row_count):
                hop(i).wait_send()
            for i in range(row_count):
                tok_part(i, 0).wait_recv()

        @pl.when(first)
        def _():
            for i in range(row_count):
                for p in range(1, count):
                    tok_part(i, p).wait_send()
                tok_own(i).wait()


def whole(a):
    return pl.BlockSpec(a.shape, lambda r, n=a.ndim: (0,) * n, pipeline_mode=pl.Buffered(1))


ANYWHERE = pl.BlockSpec(memory_space=pl.ANY)
SCALAR = pl.BlockSpec(memory_space=pltpu.SMEM)
VMEM_LIMIT = 60 * 1024 * 1024


def run_forward(count, tokens, lengths, scales, weights):
    w_qkv, b_qkv, w_out, b_out, w_up, b_up, w_down, b_down, gain, shift = weights
    rows, seq, width = tokens.shape
    ff = w_up.shape[1]
    big = lambda n, t: jax.ShapeDtypeStruct((rows, seq, n), t)
    saves = [
        (width, BF16), (width, BF16), (3 * width, BF16), (width, F32), (width, F32), (width, BF16),
        (width, BF16), (128, F32), (width, BF16), (ff, BF16), (ff, BF16), (width, BF16), (128, F32),
    ]
    dense = (w_qkv, b_qkv, w_out, b_out, w_up, b_up, w_down, b_down, gain, shift)
    tok = rows * seq
    return pl.pallas_call(
        lambda *refs: fwd_kernel(count, *refs),
        grid=(rows,),
        in_specs=[SCALAR, SCALAR, ANYWHERE] + [whole(a) for a in dense],
        out_specs=[ANYWHERE] * 14 + [pl.BlockSpec((4, 8, 128), lambda r: (0, 0, 0))],
        out_shape=[big(n, t) for n, t in saves]
        + [
            jax.ShapeDtypeStruct((rows, seq // count, width), BF16),
            jax.ShapeDtypeStruct((4, 8, 128), F32),
        ],
        scratch_shapes=[pltpu.VMEM((rows, seq, width), BF16), pltpu.VMEM((rows, seq, width), BF16)]
        + [pltpu.VMEM((seq, n), t) for n, t in saves[1:]]
        + [
            pltpu.VMEM((seq, width), F32),
            pltpu.VMEM((seq, width), F32),
            pltpu.VMEM((2, seq, CHUNK), F32),
            pltpu.SemaphoreType.DMA((13,)),
            pltpu.SemaphoreType.DMA((rows,)),
            pltpu.SemaphoreType.DMA((rows,)),
            pltpu.SemaphoreType.DMA((rows,)),
            pltpu.SemaphoreType.DMA((rows, count)),
            pltpu.SemaphoreType.DMA((rows,)),
        ],
        compiler_params=pltpu.CompilerParams(
            collective_id=0, has_side_effects=True, vmem_limit_bytes=VMEM_LIMIT,
            dimension_semantics=("arbitrary",),
        ),
        cost_estimate=pl.CostEstimate(
            flops=2 * tok * (4 * width * width + 2 * width * ff + 2 * seq * width),
            bytes_accessed=tok * 28000, transcendentals=tok * 3 * ff,
        ),
    )(lengths, scales, tokens, *dense)


def run_backward(count, seeds, lengths, scales, weights, kept):
    w_qkv, b_qkv, w_out, b_out, w_up, b_up, w_down, b_down, gain, shift = weights
    x, xq, qkv, lse, ctx, cq, n1, rs1, hq, aq, sl, n2, rs2 = kept
    rows, seq, width = seeds.shape
    ff = w_up.shape[1]
    big = lambda n, t: jax.ShapeDtypeStruct((rows, seq, n), t)
    saves = [(3 * width, BF16), (width, BF16), (ff, BF16), (width, BF16)]
    loads = (x, qkv, lse, ctx, n1, rs1, sl, n2, rs2)
    dense = (w_qkv, w_out, w_up, w_down, gain, shift)
    tok = rows * seq
    small = 6 * width + ff + 3 * width
    return pl.pallas_call(
        lambda *refs: bwd_kernel(count, *refs),
        grid=(rows,),
        in_specs=[SCALAR, SCALAR, ANYWHERE] + [whole(a) for a in dense] + [ANYWHERE] * 9,
        out_specs=[ANYWHERE] * 5 + [pl.BlockSpec((8, small), lambda r: (0, 0))],
        out_shape=[big(n, t) for n, t in saves]
        + [
            jax.ShapeDtypeStruct((rows, seq // count, width), BF16),
            jax.ShapeDtypeStruct((8, small), F32),
        ],
        scratch_shapes=[pltpu.VMEM((rows, seq, width), BF16), pltpu.VMEM((rows, seq, width), BF16)]
        + [pltpu.VMEM(a.shape[1:], a.dtype) for a in loads]
        + [pltpu.VMEM((seq, n), t) for n, t in saves]
        + [
            pltpu.VMEM((seq, width), BF16),
            pltpu.VMEM((seq, width), F32),
            pltpu.VMEM((seq, width), F32),
            pltpu.SemaphoreType.DMA((9,)),
            pltpu.SemaphoreType.DMA((4,)),
            pltpu.SemaphoreType.DMA((rows,)),
            pltpu.SemaphoreType.DMA((rows,)),
            pltpu.SemaphoreType.DMA((rows,)),
            pltpu.SemaphoreType.DMA((rows, count)),
            pltpu.SemaphoreType.DMA((rows,)),
        ],
        compiler_params=pltpu.CompilerParams(
            collective_id=1, has_side_effects=True, vmem_limit_bytes=VMEM_LIMIT,
            dimension_semantics=("arbitrary",),
        ),
        cost_estimate=pl.CostEstimate(
            flops=2 * tok * (4 * width * width + 2 * width * ff + 5 * seq * width),
            bytes_accessed=tok * 28000, transcendentals=tok * ff,
        ),
    )(lengths, scales, seeds, *dense, *loads)


def weight_grad(left, right):
    g = jnp.einsum("rsd,rse->de", left, right, preferred_element_type=F32).astype(BF16)
    return lax.psum_scatter(g, "dp", scatter_dimension=0, tiled=True).astype(F32)


def max_over(v, axis):
    size = lax.axis_size(axis)
    shift = 1
    while shift < size:
        v = jnp.maximum(v, lax.ppermute(v, axis, [(i, (i + shift) % size) for i in range(size)]))
        shift *= 2
    return v


def shards(
    tokens, lengths, ema_scales, w_qkv, bias_qv, w_out, bias_out, w_up, bias_up, w_down, bias_down,
    ln_gain, ln_bias, cotangent,
):
    count = lax.axis_size("pipe")
    width = tokens.shape[2]
    ff = w_up.shape[2]
    b_qkv = jnp.concatenate([bias_qv[:, :width], jnp.zeros_like(bias_qv[:, :width]), bias_qv[:, width:]], 1)
    weights = (
        w_qkv[0], b_qkv, w_out[0], bias_out, w_up[0], bias_up, w_down[0], bias_down, ln_gain[0], ln_bias[0],
    )
    *kept, mixed, peaks = run_forward(count, tokens, lengths, ema_scales, weights)
    x, xq, qkv, lse, ctx, cq, n1, rs1, hq, aq, sl, n2, rs2 = kept
    dproj, dbr, dup, ddn, grad_tokens, small = run_backward(
        count, cotangent, lengths, ema_scales, weights, kept
    )
    batch_max = max_over(jnp.max(peaks, (1, 2))[None], "dp")
    g_down = weight_grad(aq, ddn)
    g_up = weight_grad(hq, dup)
    g_out = weight_grad(cq, dbr)
    g_qkv = weight_grad(xq, dproj)
    n = lax.axis_size("dp")
    sums = jnp.sum(small, 0)
    parts, at = [], 0
    for size in (width, width, width, width, width, width, ff, 3 * width):
        parts.append(sums[at : at + size])
        at += size
    gain0, gain1, shift0, shift1, s_out, s_down, s_up, s_qkv = parts
    s_qv = jnp.concatenate([s_qkv[:width], s_qkv[2 * width :]])
    packed = jnp.concatenate(
        [v.reshape(n, -1) for v in (gain0, gain1, shift0, shift1, s_out, s_down, s_up, s_qv)], 1
    )
    mine = lax.psum_scatter(packed, "dp", scatter_dimension=0, tiled=True)
    outs, at = [], 0
    for size in (width, width, width, width, width, width, ff, 2 * width):
        outs.append(mine[:, at : at + size // n])
        at += size // n
    gain0, gain1, shift0, shift1, s_out, s_down, s_up, s_qv = outs
    g_gain = jnp.stack([gain0, gain1], 1)
    g_shift = jnp.stack([shift0, shift1], 1)
    return (
        mixed, grad_tokens, g_qkv[None], s_qv, g_out[None], s_out, g_up[None], s_up, g_down[None], s_down,
        g_gain, g_shift, batch_max,
    )


def solution(mesh):
    return jax.shard_map(
        shards,
        mesh=mesh,
        in_specs=(
            P("dp", None, None), P("dp"), P("pipe", None), P("pipe", None, None), P("pipe", None),
            P("pipe", None, None), P("pipe", None), P("pipe", None, None), P("pipe", None),
            P("pipe", None, None), P("pipe", None), P("pipe", None, None), P("pipe", None, None),
            P("dp", None, None),
        ),
        out_specs=(
            P("dp", "pipe", None), P("dp", "pipe", None), P("pipe", "dp", None), P("pipe", "dp"),
            P("pipe", "dp", None), P("pipe", "dp"), P("pipe", "dp", None), P("pipe", "dp"),
            P("pipe", "dp", None), P("pipe", "dp"), P("pipe", None, "dp"), P("pipe", None, "dp"),
            P("pipe", None),
        ),
        check_vma=False,
    )
```

```python
import jax
import jax.numpy as jnp
from jax import lax
from jax.experimental import pallas as pl
from jax.experimental.pallas import tpu as pltpu
from jax.sharding import PartitionSpec as P

HEAD_DIM = 64
PAIR = 2 * HEAD_DIM
EPS = 1e-06
MASKED = -1000000000.0
CHUNK = 512
ROWS = 64
LOGICAL = pl.DeviceIdType.MESH
F32 = jnp.float32
BF16 = jnp.bfloat16

ERF_POLY = (
    0.7978846780398201,
    0.03633450830808018,
    -3.432973817348946e-05,
    -5.463434792182573e-05,
    3.860434711489827e-06,
    -1.254735264100511e-07,
    1.6084598007909267e-09,
)
ERF_CLAMP = 5.3 * 5.3
INV_SQRT_2PI = 0.3989422804014327


def dot_nn(a, b):
    return jnp.dot(a, b, preferred_element_type=F32)


def dot_nt(a, b):
    return lax.dot_general(a, b, (((1,), (1,)), ((), ())), preferred_element_type=F32)


def dot_tn(a, b):
    return lax.dot_general(a, b, (((0,), (0,)), ((), ())), preferred_element_type=F32)


def fold_rows(v):
    return jnp.sum(v.reshape(v.shape[0] // 8, 8, v.shape[1]), 0)


def peak_rows(v):
    tiles = [v[:, i : i + 128] for i in range(0, v.shape[1], 128)]
    top = tiles[0]
    for tile in tiles[1:]:
        top = jnp.maximum(top, tile)
    return jnp.max(top.reshape(v.shape[0] // 8, 8, 128), 0)


def split3(v):
    hi = v.astype(BF16)
    rest = v - hi.astype(F32)
    mid = rest.astype(BF16)
    low = (rest - mid.astype(F32)).astype(BF16)
    return hi, mid, low


def greet(stage, count):
    barrier = pltpu.get_barrier_semaphore()
    for step in range(1, count):
        peer = lax.rem(stage + step, count)
        pl.semaphore_signal(barrier, inc=1, device_id={"pipe": peer}, device_id_type=LOGICAL)
    pl.semaphore_wait(barrier, count - 1)


def activation(u, ceiling, inv_ceiling):
    w = jnp.minimum(u * u, ERF_CLAMP)
    poly = w * ERF_POLY[-1] + ERF_POLY[-2]
    for coef in ERF_POLY[-3::-1]:
        poly = poly * w + coef
    phi_cdf = 0.5 + 0.5 * jnp.tanh(u * poly)
    act = u * phi_cdf
    ratio = jnp.tanh(act * inv_ceiling)
    slope = (1.0 - ratio * ratio) * (
        phi_cdf + (u * INV_SQRT_2PI) * jnp.exp(u * u * -0.5)
    )
    return act, ceiling * ratio, slope


def fwd_kernel(count, *refs):
    (
        lens, scales, tokens, w_qkv, b_qkv, w_out, b_out, w_up, b_up, w_down, b_down, gain, shift,
        x_o, xq_o, qkv_o, lse_o, ctx_o, cq_o, n1_o, rs1_o, hq_o, aq_o, sl_o, n2_o, rs2_o,
        mixed_o, peaks_o,
        xin, xout, xq_s, qkv_s, lse_s, ctx_s, cq_s, n1_s, rs1_s, hq_s, aq_s, sl_s, n2_s, rs2_s,
        acc, hid, up_s, save_sem, in_sem, send_sem, recv_sem, mix_send, mix_recv,
    ) = refs
    r = pl.program_id(0)
    rows = pl.num_programs(0)
    row_count = tokens.shape[0]
    seq, width = tokens.shape[1], tokens.shape[2]
    ff = w_up.shape[1]
    piece = seq // count
    stage = lax.axis_index("pipe")
    first = stage == 0
    last = stage == count - 1

    staged = {
        "x": (xin.at[r], x_o), "xq": (xq_s, xq_o), "qkv": (qkv_s, qkv_o), "lse": (lse_s, lse_o),
        "ctx": (ctx_s, ctx_o), "cq": (cq_s, cq_o), "n1": (n1_s, n1_o), "rs1": (rs1_s, rs1_o),
        "hq": (hq_s, hq_o), "aq": (aq_s, aq_o), "sl": (sl_s, sl_o), "n2": (n2_s, n2_o),
        "rs2": (rs2_s, rs2_o),
    }
    order = list(staged)

    def save_copy(name):
        src, dst = staged[name]
        return pltpu.make_async_copy(src, dst.at[r], save_sem.at[order.index(name)])

    def save(name):
        save_copy(name).start()

    def reuse(*names):
        @pl.when(r > 0)
        def _():
            for name in names:
                save_copy(name).wait()

    def token_copy(i):
        return pltpu.make_async_copy(tokens.at[i], xin.at[i], in_sem.at[i])

    def hop(i):
        return pltpu.make_async_remote_copy(
            src_ref=xout.at[i], dst_ref=xin.at[i], send_sem=send_sem.at[i], recv_sem=recv_sem.at[i],
            device_id={"pipe": lax.rem(stage + 1, count)}, device_id_type=LOGICAL,
        )

    def mix_part(i, p):
        return pltpu.make_async_remote_copy(
            src_ref=xout.at[i, pl.ds(p * piece, piece)], dst_ref=mixed_o.at[i],
            send_sem=mix_send.at[i, p], recv_sem=mix_recv.at[i],
            device_id={"pipe": jnp.int32(p)}, device_id_type=LOGICAL,
        )

    def mix_own(i):
        return pltpu.make_async_copy(
            xout.at[i, pl.ds((count - 1) * piece, piece)], mixed_o.at[i], mix_send.at[i, count - 1]
        )

    @pl.when(r == 0)
    def _():
        greet(stage, count)
        peaks_o[...] = jnp.zeros_like(peaks_o)

        @pl.when(first)
        def _():
            for i in range(row_count):
                token_copy(i).start()

    @pl.when(first)
    def _():
        token_copy(r).wait()

    @pl.when(jnp.logical_not(first))
    def _():
        hop(r).wait_recv()

    length = lens[r]
    m0, m1, m2, m3 = scales[0, 0], scales[0, 1], scales[0, 2], scales[0, 3]
    i0, i1, i2, i3 = 1.0 / m0, 1.0 / m1, 1.0 / m2, 1.0 / m3
    steps = seq // ROWS

    def row_mask(start, size):
        return (start + lax.broadcasted_iota(jnp.int32, (size, 1), 0)) < length

    def note_peak(k, v, start):
        top = jnp.where(row_mask(start, v.shape[0]), jnp.abs(v), 0.0)
        peaks_o[k] = jnp.maximum(peaks_o[k], peak_rows(top))

    @pl.when(r > 0)
    def _():
        save_copy("x").wait()

    save("x")
    reuse("xq", "qkv", "lse", "ctx", "cq")

    def quant_in(i, _):
        at = pl.ds(pl.multiple_of(i * ROWS, ROWS), ROWS)
        x = xin[r, at, :].astype(F32)
        note_peak(0, x, i * ROWS)
        xq_s[at, :] = (m0 * jnp.tanh(x * i0)).astype(BF16)
        return 0

    lax.fori_loop(0, steps, quant_in, 0)
    save("xq")

    for j in range(3):
        cols = pl.ds(j * width, width)
        proj = dot_nn(xq_s[...], w_qkv[:, cols]) + b_qkv[:, cols]
        qkv_s[:, cols] = proj.astype(BF16)
    save("qkv")

    lane = lax.broadcasted_iota(jnp.int32, (seq, PAIR), 1)
    lo = lane < HEAD_DIM
    key_bias = jnp.where(lax.broadcasted_iota(jnp.int32, (seq, PAIR), 0) < length, 0.0, MASKED).astype(BF16)
    one = jnp.ones((), BF16)
    zero = jnp.zeros((), BF16)

    def attend(p, _):
        at = pl.multiple_of(p * PAIR, PAIR)
        q2 = qkv_s[:, pl.ds(at, PAIR)] * jnp.asarray(HEAD_DIM ** -0.5, BF16)
        k2 = qkv_s[:, pl.ds(pl.multiple_of(width + at, PAIR), PAIR)]
        v2 = qkv_s[:, pl.ds(pl.multiple_of(2 * width + at, PAIR), PAIR)]
        q_a, q_b = jnp.where(lo, q2, one), jnp.where(lo, one, q2)
        k_a = jnp.where(lo, k2, jnp.where(lane == HEAD_DIM, key_bias, zero))
        k_b = jnp.where(lo, jnp.where(lane == 0, key_bias, zero), k2)
        s_a = dot_nt(q_a, k_a)
        s_b = dot_nt(q_b, k_b)
        top_a = jnp.max(s_a, -1, keepdims=True)
        e_a = jnp.exp(s_a - top_a).astype(BF16)
        top_b = jnp.max(s_b, -1, keepdims=True)
        o_a = dot_nn(e_a, jnp.where(lo, v2, one))
        e_b = jnp.exp(s_b - top_b).astype(BF16)
        o_b = dot_nn(e_b, jnp.where(lo, one, v2))
        total = pltpu.roll(jnp.where(lo, o_b, o_a), HEAD_DIM, 1)
        ctx_s[:, pl.ds(at, PAIR)] = jnp.where(lo, o_a, o_b) / total
        lse_s[:, pl.ds(at, PAIR)] = jnp.where(lo, top_a, top_b) + jnp.log(total)
        return 0

    lax.fori_loop(0, width // PAIR, attend, 0)
    save("lse")
    save("ctx")

    def quant_ctx(i, _):
        at = pl.ds(pl.multiple_of(i * ROWS, ROWS), ROWS)
        c = ctx_s[at, :]
        note_peak(1, c, i * ROWS)
        cq_s[at, :] = (m1 * jnp.tanh(c * i1)).astype(BF16)
        return 0

    lax.fori_loop(0, steps, quant_ctx, 0)
    save("cq")
    acc[...] = dot_nn(cq_s[...], w_out[...])
    reuse("n1", "rs1", "hq")

    def norm_one(i, _):
        at = pl.ds(pl.multiple_of(i * ROWS, ROWS), ROWS)
        s = xin[r, at, :].astype(F32) + (acc[at, :] + b_out[...])
        center = s - jnp.mean(s, -1, keepdims=True)
        rs = lax.rsqrt(jnp.mean(center * center, -1, keepdims=True) + EPS)
        n = center * rs
        h = n * gain[0:1, :] + shift[0:1, :]
        n1_s[at, :] = n.astype(BF16)
        rs1_s[at, :] = jnp.broadcast_to(rs, (ROWS, 128))
        hid[at, :] = h
        hq_s[at, :] = (m2 * jnp.tanh(h * i2)).astype(BF16)
        note_peak(2, h, i * ROWS)
        return 0

    lax.fori_loop(0, steps, norm_one, 0)
    save("n1")
    save("rs1")
    save("hq")
    reuse("aq", "sl")

    chunks = ff // CHUNK
    mask_all = row_mask(0, seq)

    def up_chunk(c):
        cols = pl.ds(c * CHUNK, CHUNK)
        up_s[c % 2] = dot_nn(hq_s[...], w_up[:, cols]) + b_up[:, cols]

    def act_chunk(c):
        cols = pl.ds(c * CHUNK, CHUNK)
        act, low, slope = activation(up_s[c % 2], m3, i3)
        aq_s[:, cols] = low.astype(BF16)
        sl_s[:, cols] = slope.astype(BF16)
        top = jnp.where(mask_all, jnp.abs(act), 0.0)
        peaks_o[3] = jnp.maximum(peaks_o[3], peak_rows(top))

    def down_chunk(c):
        cols = pl.ds(c * CHUNK, CHUNK)
        part = dot_nn(aq_s[:, cols], w_down[cols, :])
        if c == 0:
            acc[...] = part
        else:
            acc[...] += part

    up_chunk(0)
    for c in range(chunks):
        if c + 1 < chunks:
            up_chunk(c + 1)
        act_chunk(c)
        if c > 0:
            down_chunk(c - 1)
    down_chunk(chunks - 1)
    save("aq")
    save("sl")
    reuse("n2", "rs2")

    def norm_two(i, _):
        at = pl.ds(pl.multiple_of(i * ROWS, ROWS), ROWS)
        s = hid[at, :] + (acc[at, :] + b_down[...])
        center = s - jnp.mean(s, -1, keepdims=True)
        rs = lax.rsqrt(jnp.mean(center * center, -1, keepdims=True) + EPS)
        n = center * rs
        n2_s[at, :] = n.astype(BF16)
        rs2_s[at, :] = jnp.broadcast_to(rs, (ROWS, 128))
        xout[r, at, :] = (n * gain[1:2, :] + shift[1:2, :]).astype(BF16)
        return 0

    lax.fori_loop(0, steps, norm_two, 0)
    save("n2")
    save("rs2")

    @pl.when(jnp.logical_not(last))
    def _():
        hop(r).start()

    @pl.when(last)
    def _():
        for p in range(count - 1):
            mix_part(r, p).start()
        mix_own(r).start()

    @pl.when(r == rows - 1)
    def _():
        for name in order:
            save_copy(name).wait()

        @pl.when(jnp.logical_not(last))
        def _():
            for i in range(row_count):
                hop(i).wait_send()
            for i in range(row_count):
                mix_part(i, 0).wait_recv()

        @pl.when(last)
        def _():
            for i in range(row_count):
                for p in range(count - 1):
                    mix_part(i, p).wait_send()
                mix_own(i).wait()


def bwd_kernel(count, *refs):
    (
        lens, scales, seeds, w_qkv, w_out, w_up, w_down, gain, shift,
        x_i, qkv_i, lse_i, ctx_i, n1_i, rs1_i, sl_i, n2_i, rs2_i,
        dproj_o, dbr_o, dup_o, ddn_o, gtok_o, small_o,
        gin, gout, x_s, qkv_s, lse_s, ctx_s, n1_s, rs1_s, sl_s, n2_s, rs2_s,
        dproj_s, dbr_s, dup_s, ddn_s, dctx_s, acc, dr,
        load_sem, save_sem, in_sem, send_sem, recv_sem, tok_send,
    ) = refs
    r = pl.program_id(0)
    rows = pl.num_programs(0)
    row_count = seeds.shape[0]
    seq, width = seeds.shape[1], seeds.shape[2]
    ff = w_up.shape[1]
    piece = seq // count
    stage = lax.axis_index("pipe")
    first = stage == 0
    last = stage == count - 1
    steps = seq // ROWS

    loaded = {
        "n2": (n2_i, n2_s), "rs2": (rs2_i, rs2_s), "sl": (sl_i, sl_s), "n1": (n1_i, n1_s),
        "rs1": (rs1_i, rs1_s), "ctx": (ctx_i, ctx_s), "qkv": (qkv_i, qkv_s), "lse": (lse_i, lse_s),
        "x": (x_i, x_s),
    }
    load_order = list(loaded)
    staged = {
        "ddn": (ddn_s, ddn_o), "dup": (dup_s, dup_o), "dbr": (dbr_s, dbr_o), "dproj": (dproj_s, dproj_o),
    }
    save_order = list(staged)

    def load_copy(name, i):
        src, dst = loaded[name]
        return pltpu.make_async_copy(src.at[i], dst, load_sem.at[load_order.index(name)])

    def fetch_next(*names):
        @pl.when(r + 1 < rows)
        def _():
            for name in names:
                load_copy(name, r + 1).start()

    def ready(*names):
        for name in names:
            load_copy(name, r).wait()

    def save_copy(name):
        src, dst = staged[name]
        return pltpu.make_async_copy(src, dst.at[r], save_sem.at[save_order.index(name)])

    def save(name):
        save_copy(name).start()

    def reuse(*names):
        @pl.when(r > 0)
        def _():
            for name in names:
                save_copy(name).wait()

    def seed_copy(i):
        return pltpu.make_async_copy(seeds.at[i], gin.at[i], in_sem.at[i])

    def hop(i):
        return pltpu.make_async_remote_copy(
            src_ref=gout.at[i], dst_ref=gin.at[i], send_sem=send_sem.at[i], recv_sem=recv_sem.at[i],
            device_id={"pipe": lax.rem(stage + count - 1, count)}, device_id_type=LOGICAL,
        )

    def tok_copy(i):
        return pltpu.make_async_copy(gout.at[i], gtok_o.at[i], tok_send.at[i])

    @pl.when(r == 0)
    def _():
        greet(stage, count)
        small_o[...] = jnp.zeros_like(small_o)
        for name in load_order:
            load_copy(name, 0).start()

        @pl.when(last)
        def _():
            for i in range(row_count):
                seed_copy(i).start()

    @pl.when(last)
    def _():
        seed_copy(r).wait()

    @pl.when(jnp.logical_not(last))
    def _():
        hop(r).wait_recv()

    length = lens[r]
    m0, m1, m2 = scales[0, 0], scales[0, 1], scales[0, 2]
    i0, i1, i2 = 1.0 / m0, 1.0 / m1, 1.0 / m2

    offsets = {}
    at_col = 0
    for name, size in (
        ("gain0", width), ("gain1", width), ("shift0", width), ("shift1", width),
        ("out", width), ("down", width), ("up", ff), ("qkv", 3 * width),
    ):
        offsets[name] = at_col
        at_col += size

    def add_small(name, v, col=0):
        at = pl.ds(offsets[name] + col, v.shape[1])
        small_o[:, at] += fold_rows(v)

    ready("n2", "rs2")
    reuse("ddn")

    def norm_two(i, _):
        start = pl.multiple_of(i * ROWS, ROWS)
        at = pl.ds(start, ROWS)
        valid = (start + lax.broadcasted_iota(jnp.int32, (ROWS, 1), 0)) < length
        dy = jnp.where(valid, gin[r, at, :].astype(F32), 0.0)
        n = n2_s[at, :].astype(F32)
        rs = rs2_s[at, 0:1]
        dyn = dy * n
        e = dy * gain[1:2, :]
        mean_e = jnp.mean(e, -1, keepdims=True)
        mean_en = jnp.mean(e * n, -1, keepdims=True)
        d = (e - mean_e - n * mean_en) * rs
        dr[at, :] = d
        ddn_s[at, :] = d.astype(BF16)
        add_small("gain1", dyn)
        add_small("shift1", dy)
        add_small("down", d)
        return 0

    lax.fori_loop(0, steps, norm_two, 0)
    save("ddn")
    fetch_next("n2", "rs2")
    ready("sl")
    reuse("dup")

    chunks = ff // CHUNK

    def dact_chunk(c):
        cols = pl.ds(c * CHUNK, CHUNK)
        d = dot_nt(ddn_s[...], w_down[cols, :]) * sl_s[:, cols].astype(F32)
        dup_s[:, cols] = d.astype(BF16)
        add_small("up", d, c * CHUNK)

    def dhid_chunk(c):
        cols = pl.ds(c * CHUNK, CHUNK)
        part = dot_nt(dup_s[:, cols], w_up[:, cols])
        if c == 0:
            acc[...] = part
        else:
            acc[...] += part

    dact_chunk(0)
    for c in range(1, chunks):
        dact_chunk(c)
        dhid_chunk(c - 1)
    dhid_chunk(chunks - 1)
    save("dup")
    fetch_next("sl")
    ready("n1", "rs1")
    reuse("dbr")

    def norm_one(i, _):
        start = pl.multiple_of(i * ROWS, ROWS)
        at = pl.ds(start, ROWS)
        n = n1_s[at, :].astype(F32)
        rs = rs1_s[at, 0:1]
        t = jnp.tanh((n * gain[0:1, :] + shift[0:1, :]) * i2)
        dy = dr[at, :] + acc[at, :] * (1.0 - t * t)
        dyn = dy * n
        e = dy * gain[0:1, :]
        mean_e = jnp.mean(e, -1, keepdims=True)
        mean_en = jnp.mean(e * n, -1, keepdims=True)
        d = (e - mean_e - n * mean_en) * rs
        dr[at, :] = d
        dbr_s[at, :] = d.astype(BF16)
        add_small("gain0", dyn)
        add_small("shift0", dy)
        add_small("out", d)
        return 0

    lax.fori_loop(0, steps, norm_one, 0)
    save("dbr")
    fetch_next("n1", "rs1")
    ready("ctx")
    acc[...] = dot_nt(dbr_s[...], w_out[...])

    def quant_ctx(i, _):
        at = pl.ds(pl.multiple_of(i * ROWS, ROWS), ROWS)
        t = jnp.tanh(ctx_s[at, :] * i1)
        dctx_s[at, :] = (acc[at, :] * (1.0 - t * t)).astype(BF16)
        return 0

    lax.fori_loop(0, steps, quant_ctx, 0)
    ready("qkv", "lse")
    reuse("dproj")

    lane = lax.broadcasted_iota(jnp.int32, (seq, PAIR), 1)
    lo = lane < HEAD_DIM
    spot = jnp.where(lo, lane, lane - HEAD_DIM)
    key_bias = jnp.where(lax.broadcasted_iota(jnp.int32, (seq, PAIR), 0) < length, 0.0, MASKED).astype(BF16)
    one = jnp.ones((), BF16)
    zero = jnp.zeros((), BF16)
    scale = jnp.asarray(HEAD_DIM ** -0.5, BF16)
    src = lax.broadcasted_iota(jnp.int32, (PAIR, PAIR), 0) < HEAD_DIM
    dst = lax.broadcasted_iota(jnp.int32, (PAIR, PAIR), 1) < HEAD_DIM
    swap_sum = jnp.where(src == dst, 0.0, 1.0).astype(BF16)

    def attend(p, _):
        at = pl.multiple_of(p * PAIR, PAIR)
        here = pl.ds(at, PAIR)
        q2 = qkv_s[:, here] * scale
        k2 = qkv_s[:, pl.ds(pl.multiple_of(width + at, PAIR), PAIR)]
        v2 = qkv_s[:, pl.ds(pl.multiple_of(2 * width + at, PAIR), PAIR)]
        do2 = dctx_s[:, here]
        l_hi, l_mid, l_low = split3(pltpu.roll(lse_s[:, here], HEAD_DIM, 1))
        extra_q = jnp.where(
            spot == 0, one, jnp.where(spot == 1, -l_hi, jnp.where(spot == 2, -l_mid, -l_low))
        )
        extra_k = jnp.where(spot == 0, key_bias, jnp.where(spot <= 3, one, zero))
        e_hi, e_mid, e_low = split3(do2.astype(F32) * ctx_s[:, here])
        inner = dot_nn(e_hi, swap_sum) + dot_nn(e_mid, swap_sum)
        d_hi, d_mid, d_low = split3(inner)
        extra_do = jnp.where(spot == 0, -d_hi, jnp.where(spot == 1, -d_mid, -d_low))
        extra_v = jnp.where(spot <= 2, one, zero)
        k_t = k2.T

        def head(is_a):
            mine = lo if is_a else jnp.logical_not(lo)
            s = dot_nt(jnp.where(mine, k2, extra_k), jnp.where(mine, q2, extra_q))
            prob = jnp.exp(s)
            grad_p = dot_nt(jnp.where(mine, v2, extra_v), jnp.where(mine, do2, extra_do))
            grad_v = dot_nn(prob.astype(BF16), do2)
            grad_s = (prob * grad_p).astype(BF16)
            grad_k = dot_nn(grad_s, q2)
            half = k_t[0:HEAD_DIM] if is_a else k_t[HEAD_DIM:PAIR]
            return dot_nn(half, grad_s), grad_k, grad_v

        qa, ka, va = head(True)
        qb, kb, vb = head(False)
        grad_q = jnp.concatenate([qa, qb], 0).T * (HEAD_DIM ** -0.5)
        dproj_s[:, here] = grad_q.astype(BF16)
        dproj_s[:, pl.ds(pl.multiple_of(width + at, PAIR), PAIR)] = jnp.where(lo, ka, kb).astype(BF16)
        dproj_s[:, pl.ds(pl.multiple_of(2 * width + at, PAIR), PAIR)] = jnp.where(lo, va, vb).astype(BF16)
        return 0

    lax.fori_loop(0, width // PAIR, attend, 0)
    save("dproj")
    fetch_next("ctx", "qkv", "lse")
    for j in range(3):
        cols = pl.ds(j * width, width)
        part = dot_nt(dproj_s[:, cols], w_qkv[:, cols])
        if j == 0:
            acc[...] = part
        else:
            acc[...] += part
        if j != 1:
            add_small("qkv", dproj_s[:, cols].astype(F32), j * width)
    ready("x")

    def quant_in(i, _):
        at = pl.ds(pl.multiple_of(i * ROWS, ROWS), ROWS)
        t = jnp.tanh(x_s[at, :].astype(F32) * i0)
        gout[r, at, :] = (dr[at, :] + acc[at, :] * (1.0 - t * t)).astype(BF16)
        return 0

    lax.fori_loop(0, steps, quant_in, 0)
    fetch_next("x")

    @pl.when(jnp.logical_not(first))
    def _():
        hop(r).start()

    @pl.when(first)
    def _():
        tok_copy(r).start()

    @pl.when(r == rows - 1)
    def _():
        for name in save_order:
            save_copy(name).wait()

        @pl.when(jnp.logical_not(first))
        def _():
            for i in range(row_count):
                hop(i).wait_send()

        @pl.when(first)
        def _():
            for i in range(row_count):
                tok_copy(i).wait()


def whole(a):
    return pl.BlockSpec(a.shape, lambda r, n=a.ndim: (0,) * n, pipeline_mode=pl.Buffered(1))


ANYWHERE = pl.BlockSpec(memory_space=pl.ANY)
SCALAR = pl.BlockSpec(memory_space=pltpu.SMEM)
VMEM_LIMIT = 60 * 1024 * 1024


def run_forward(count, tokens, lengths, scales, weights):
    w_qkv, b_qkv, w_out, b_out, w_up, b_up, w_down, b_down, gain, shift = weights
    rows, seq, width = tokens.shape
    ff = w_up.shape[1]
    big = lambda n, t: jax.ShapeDtypeStruct((rows, seq, n), t)
    saves = [
        (width, BF16), (width, BF16), (3 * width, BF16), (width, F32), (width, F32), (width, BF16),
        (width, BF16), (128, F32), (width, BF16), (ff, BF16), (ff, BF16), (width, BF16), (128, F32),
    ]
    dense = (w_qkv, b_qkv, w_out, b_out, w_up, b_up, w_down, b_down, gain, shift)
    tok = rows * seq
    return pl.pallas_call(
        lambda *refs: fwd_kernel(count, *refs),
        grid=(rows,),
        in_specs=[SCALAR, SCALAR, ANYWHERE] + [whole(a) for a in dense],
        out_specs=[ANYWHERE] * 14 + [pl.BlockSpec((4, 8, 128), lambda r: (0, 0, 0))],
        out_shape=[big(n, t) for n, t in saves]
        + [
            jax.ShapeDtypeStruct((rows, seq // count, width), BF16),
            jax.ShapeDtypeStruct((4, 8, 128), F32),
        ],
        scratch_shapes=[pltpu.VMEM((rows, seq, width), BF16), pltpu.VMEM((rows, seq, width), BF16)]
        + [pltpu.VMEM((seq, n), t) for n, t in saves[1:]]
        + [
            pltpu.VMEM((seq, width), F32),
            pltpu.VMEM((seq, width), F32),
            pltpu.VMEM((2, seq, CHUNK), F32),
            pltpu.SemaphoreType.DMA((13,)),
            pltpu.SemaphoreType.DMA((rows,)),
            pltpu.SemaphoreType.DMA((rows,)),
            pltpu.SemaphoreType.DMA((rows,)),
            pltpu.SemaphoreType.DMA((rows, count)),
            pltpu.SemaphoreType.DMA((rows,)),
        ],
        compiler_params=pltpu.CompilerParams(
            collective_id=0, has_side_effects=True, vmem_limit_bytes=VMEM_LIMIT,
            dimension_semantics=("arbitrary",),
        ),
        cost_estimate=pl.CostEstimate(
            flops=2 * tok * (4 * width * width + 2 * width * ff + 2 * seq * width),
            bytes_accessed=tok * 28000, transcendentals=tok * 3 * ff,
        ),
    )(lengths, scales, tokens, *dense)


def run_backward(count, seeds, lengths, scales, weights, kept):
    w_qkv, b_qkv, w_out, b_out, w_up, b_up, w_down, b_down, gain, shift = weights
    x, xq, qkv, lse, ctx, cq, n1, rs1, hq, aq, sl, n2, rs2 = kept
    rows, seq, width = seeds.shape
    ff = w_up.shape[1]
    big = lambda n, t: jax.ShapeDtypeStruct((rows, seq, n), t)
    saves = [(3 * width, BF16), (width, BF16), (ff, BF16), (width, BF16)]
    loads = (x, qkv, lse, ctx, n1, rs1, sl, n2, rs2)
    dense = (w_qkv, w_out, w_up, w_down, gain, shift)
    tok = rows * seq
    small = 6 * width + ff + 3 * width
    return pl.pallas_call(
        lambda *refs: bwd_kernel(count, *refs),
        grid=(rows,),
        in_specs=[SCALAR, SCALAR, ANYWHERE] + [whole(a) for a in dense] + [ANYWHERE] * 9,
        out_specs=[ANYWHERE] * 5 + [pl.BlockSpec((8, small), lambda r: (0, 0))],
        out_shape=[big(n, t) for n, t in saves]
        + [big(width, BF16), jax.ShapeDtypeStruct((8, small), F32)],
        scratch_shapes=[pltpu.VMEM((rows, seq, width), BF16), pltpu.VMEM((rows, seq, width), BF16)]
        + [pltpu.VMEM(a.shape[1:], a.dtype) for a in loads]
        + [pltpu.VMEM((seq, n), t) for n, t in saves]
        + [
            pltpu.VMEM((seq, width), BF16),
            pltpu.VMEM((seq, width), F32),
            pltpu.VMEM((seq, width), F32),
            pltpu.SemaphoreType.DMA((9,)),
            pltpu.SemaphoreType.DMA((4,)),
            pltpu.SemaphoreType.DMA((rows,)),
            pltpu.SemaphoreType.DMA((rows,)),
            pltpu.SemaphoreType.DMA((rows,)),
            pltpu.SemaphoreType.DMA((rows,)),
        ],
        compiler_params=pltpu.CompilerParams(
            collective_id=1, has_side_effects=True, vmem_limit_bytes=VMEM_LIMIT,
            dimension_semantics=("arbitrary",),
        ),
        cost_estimate=pl.CostEstimate(
            flops=2 * tok * (4 * width * width + 2 * width * ff + 5 * seq * width),
            bytes_accessed=tok * 28000, transcendentals=tok * ff,
        ),
    )(lengths, scales, seeds, *dense, *loads)


def ring_to_dp(pos, n):
    return jnp.where(pos < n // 2, 2 * pos, 2 * (n - pos) - 1)


def dp_to_ring(j, n):
    return jnp.where(j % 2 == 0, j // 2, n - 1 - j // 2)


def grad_kernel(count, n, *refs):
    (
        aq, hq, cq, xq, ddn, dbr, dup, dproj, small, g0,
        gq_o, go_o, gu_o, gd_o, small_o, gtok_o,
        slots_d, slots_u, slots_q, slots_s, aq_v, ddn_v, left_v, right_v, own_u, own_q,
        aq_sem, ddn_sem, left_sem, right_sem,
        send_d, recv_d, send_u, recv_u, send_q, recv_q, send_s, recv_s, tok_send, tok_recv,
    ) = refs
    width = ddn.shape[1]
    ff = aq.shape[1]
    shard, shard_ff = width // n, ff // n
    row_count, seq = g0.shape[0], g0.shape[1]
    piece = seq // count
    stage = lax.axis_index("pipe")
    me = lax.axis_index("dp")
    pos = dp_to_ring(me, n)
    first = stage == 0
    ahead = ring_to_dp(lax.rem(pos + 1, n), n)
    behind = ring_to_dp(lax.rem(pos + n - 1, n), n)
    target = (ahead, behind)

    barrier = pltpu.get_barrier_semaphore()
    for peer in target:
        pl.semaphore_signal(barrier, inc=1, device_id={"dp": peer}, device_id_type=LOGICAL)

    @pl.when(first)
    def _():
        pl.semaphore_wait(barrier, 1 + count)

    @pl.when(jnp.logical_not(first))
    def _():
        pl.semaphore_signal(barrier, inc=1, device_id={"pipe": jnp.int32(0)}, device_id_type=LOGICAL)
        pl.semaphore_wait(barrier, 2)

    def tok_part(i, p):
        return pltpu.make_async_remote_copy(
            src_ref=g0.at[i, pl.ds(p * piece, piece)], dst_ref=gtok_o.at[i],
            send_sem=tok_send.at[i, p], recv_sem=tok_recv.at[i],
            device_id={"pipe": jnp.int32(p)}, device_id_type=LOGICAL,
        )

    def tok_own(i):
        return pltpu.make_async_copy(g0.at[i, pl.ds(0, piece)], gtok_o.at[i], tok_send.at[i, 0])

    def chunk(d, step):
        at = pos + 2 * n - 1 - step if d == 0 else pos + 1 + step
        return ring_to_dp(lax.rem(at, n), n)

    def aq_copy(d, step, slot):
        cols = pl.ds(pl.multiple_of(chunk(d, step) * shard_ff, 128), shard_ff)
        return pltpu.make_async_copy(aq.at[:, cols], aq_v.at[d, slot], aq_sem.at[d, slot])

    blocks = [(hq, dup, i, own_u, i) for i in range(ff // width)]
    blocks += [(xq, dproj, i, own_q, i) for i in range(3)] + [(cq, dbr, 0, own_q, 3)]
    lefts = [hq, xq, cq]

    def left_copy(k):
        return pltpu.make_async_copy(lefts[k], left_v.at[k % 2], left_sem.at[k])

    def right_copy(b):
        return pltpu.make_async_copy(
            blocks[b][1].at[:, pl.ds(blocks[b][2] * width, width)], right_v.at[b % 2], right_sem.at[b]
        )

    def block_left(b):
        return [k for k in range(3) if lefts[k] is blocks[b][0]][0]

    ddn_copy = pltpu.make_async_copy(ddn, ddn_v, ddn_sem.at[0])
    ddn_copy.start()
    for d in range(2):
        aq_copy(d, 0, 0).start()
    left_copy(0).start()
    right_copy(0).start()
    right_copy(1).start()
    left_copy(1).start()

    @pl.when(first)
    def _():
        for i in range(row_count):
            for p in range(1, count):
                tok_part(i, p).start()
            tok_own(i).start()

    ddn_copy.wait()

    def product(b):
        k = block_left(b)
        if b == 0 or block_left(b - 1) != k:
            left_copy(k).wait()
        right_copy(b).wait()
        part = dot_tn(left_v[k % 2], right_v[b % 2])
        blocks[b][3][:, pl.ds(blocks[b][4] * width, width)] = part.astype(BF16)
        if b + 2 < len(blocks):
            right_copy(b + 2).start()
        if k + 2 < 3 and block_left(b + 1) != k:
            left_copy(k + 2).start()

    def lane(slots, send, recv, d, step, own, finish):
        def message(at):
            return pltpu.make_async_remote_copy(
                src_ref=slots.at[d, at], dst_ref=slots.at[d, jnp.minimum(at + 1, n - 1)],
                send_sem=send.at[d, at], recv_sem=recv.at[d, jnp.minimum(at + 1, n - 1)],
                device_id={"dp": target[d]}, device_id_type=LOGICAL,
            )

        def arrived(at):
            return pltpu.make_async_remote_copy(
                src_ref=slots.at[d, at], dst_ref=slots.at[d, at],
                send_sem=send.at[d, at], recv_sem=recv.at[d, at],
                device_id={"dp": target[d]}, device_id_type=LOGICAL,
            )

        if own is None:
            return message

        @pl.when(step == 0)
        def _():
            slots[d, 0] = own().astype(BF16)

        @pl.when(step > 0)
        def _():
            mine = own()
            arrived(step).wait_recv()
            total = slots[d, step].astype(F32) + mine

            @pl.when(step < n - 1)
            def _():
                slots[d, step] = total.astype(BF16)

            @pl.when(step == n - 1)
            def _():
                finish(total)

        @pl.when(step < n - 1)
        def _():
            message(step).start()

    def small_message(at):
        return pltpu.make_async_remote_copy(
            src_ref=slots_s.at[at], dst_ref=slots_s.at[jnp.minimum(at + 1, n - 1)],
            send_sem=send_s.at[at], recv_sem=recv_s.at[jnp.minimum(at + 1, n - 1)],
            device_id={"dp": target[0]}, device_id_type=LOGICAL,
        )

    def small_arrived(at):
        return pltpu.make_async_remote_copy(
            src_ref=slots_s.at[at], dst_ref=slots_s.at[at], send_sem=send_s.at[at],
            recv_sem=recv_s.at[at], device_id={"dp": target[0]}, device_id_type=LOGICAL,
        )

    half = width // 2
    sum_rows = lax.broadcasted_iota(jnp.int32, (16, 128), 0) < 9

    def small_step(step):
        mine = small[chunk(0, step)]

        @pl.when(step == 0)
        def _():
            slots_s[0] = mine

        @pl.when(step > 0)
        def _():
            small_arrived(step).wait_recv()
            got = slots_s[step]
            slots_s[step] = jnp.where(sum_rows, got + mine, jnp.maximum(got, mine))

        @pl.when(step < n - 1)
        def _():
            small_message(step).start()

        @pl.when(step == n - 1)
        def _():
            small_o[...] = slots_s[step]

    def down_lane(d, step):
        slot = lax.rem(step, 2)

        def own():
            part = dot_tn(aq_v[d, slot], ddn_v[:, d * half : (d + 1) * half])
            return part

        def finish(total):
            gd_o[:, d * half : (d + 1) * half] = total

        aq_copy(d, step, slot).wait()

        @pl.when(step < n - 1)
        def _():
            aq_copy(d, step + 1, 1 - slot).start()

        lane(slots_d, send_d, recv_d, d, step, own, finish)

    def rows_of(own_ref, d, step):
        at = pl.ds(pl.multiple_of(chunk(d, step) * shard, 16), shard)
        span = own_ref.shape[1] // 2
        return own_ref[at, d * span : (d + 1) * span].astype(F32)

    def up_lane(d, step):
        def finish(total):
            gu_o[:, d * (ff // 2) : (d + 1) * (ff // 2)] = total

        lane(slots_u, send_u, recv_u, d, step, lambda: rows_of(own_u, d, step), finish)

    def qkvo_lane(d, step):
        def finish(total):
            if d == 0:
                gq_o[:, 0 : 2 * width] = total
            else:
                gq_o[:, 2 * width : 3 * width] = total[:, 0:width]
                go_o[...] = total[:, width : 2 * width]

        lane(slots_q, send_q, recv_q, d, step, lambda: rows_of(own_q, d, step), finish)

    def turn(t, _):
        @pl.when(t < n)
        def _():
            for d in range(2):
                down_lane(d, t)
            small_step(t)

        @pl.when(jnp.logical_and(t >= 2, t < n + 2))
        def _():
            for d in range(2):
                up_lane(d, t - 2)

        @pl.when(t >= 4)
        def _():
            for d in range(2):
                qkvo_lane(d, t - 4)

        for turn_at in range(4):
            @pl.when(t == turn_at)
            def _():
                for b in range(2 * turn_at, 2 * turn_at + 2):
                    product(b)

        return 0

    lax.fori_loop(0, n + 4, turn, 0)

    def drain(at, _):
        for d in range(2):
            lane(slots_d, send_d, recv_d, d, 0, None, None)(at).wait_send()
            lane(slots_u, send_u, recv_u, d, 0, None, None)(at).wait_send()
            lane(slots_q, send_q, recv_q, d, 0, None, None)(at).wait_send()
        small_message(at).wait_send()
        return 0

    lax.fori_loop(0, n - 1, drain, 0)

    @pl.when(first)
    def _():
        for i in range(row_count):
            for p in range(1, count):
                tok_part(i, p).wait_send()
            tok_own(i).wait()

    @pl.when(jnp.logical_not(first))
    def _():
        for i in range(row_count):
            tok_part(i, 1).wait_recv()


def run_grads(count, n, kept, dproj, dbr, dup, ddn, g0, small):
    x, xq, qkv, lse, ctx, cq, n1, rs1, hq, aq, sl, n2, rs2 = kept
    rows, seq, width = g0.shape
    ff = aq.shape[2]
    flat = lambda a: a.reshape(rows * seq, a.shape[2])
    tok = rows * seq
    shard, shard_ff = width // n, ff // n
    ops = [flat(a) for a in (aq, hq, cq, xq, ddn, dbr, dup, dproj)]
    vmem = pl.BlockSpec(memory_space=pltpu.VMEM)
    sem = pltpu.SemaphoreType.DMA
    return pl.pallas_call(
        lambda *refs: grad_kernel(count, n, *refs),
        in_specs=[ANYWHERE] * 8 + [vmem, ANYWHERE],
        out_specs=[vmem] * 5 + [ANYWHERE],
        out_shape=[
            jax.ShapeDtypeStruct((shard, 3 * width), F32),
            jax.ShapeDtypeStruct((shard, width), F32),
            jax.ShapeDtypeStruct((shard, ff), F32),
            jax.ShapeDtypeStruct((shard_ff, width), F32),
            jax.ShapeDtypeStruct((16, 128), F32),
            jax.ShapeDtypeStruct((rows, seq // count, width), BF16),
        ],
        scratch_shapes=[
            pltpu.VMEM((2, n, shard_ff, width // 2), BF16),
            pltpu.VMEM((2, n, shard, ff // 2), BF16),
            pltpu.VMEM((2, n, shard, 2 * width), BF16),
            pltpu.VMEM((n, 16, 128), F32),
            pltpu.VMEM((2, 2, tok, shard_ff), BF16),
            pltpu.VMEM((tok, width), BF16),
            pltpu.VMEM((2, tok, width), BF16),
            pltpu.VMEM((2, tok, width), BF16),
            pltpu.VMEM((width, ff), BF16),
            pltpu.VMEM((width, 4 * width), BF16),
            sem((2, 2)), sem((1,)), sem((3,)), sem((8,)),
            sem((2, n)), sem((2, n)), sem((2, n)), sem((2, n)), sem((2, n)), sem((2, n)),
            sem((n,)), sem((n,)), sem((rows, count)), sem((rows,)),
        ],
        compiler_params=pltpu.CompilerParams(
            collective_id=2, has_side_effects=True, vmem_limit_bytes=VMEM_LIMIT,
        ),
        cost_estimate=pl.CostEstimate(
            flops=2 * tok * (4 * width * width + 2 * width * ff), bytes_accessed=tok * 25000, transcendentals=0,
        ),
    )(*ops, small, g0)


def weight_grad(left, right):
    g = jnp.einsum("rsd,rse->de", left, right, preferred_element_type=F32).astype(BF16)
    return lax.psum_scatter(g, "dp", scatter_dimension=0, tiled=True).astype(F32)


def share_pieces(whole_rows, count, stage):
    piece = whole_rows.shape[1] // count
    mine = whole_rows[:, :piece]
    for p in range(1, count):
        got = lax.ppermute(whole_rows[:, p * piece : (p + 1) * piece], "pipe", [(0, p)])
        mine = jnp.where(stage == p, got, mine)
    return mine


def shards(
    tokens, lengths, ema_scales, w_qkv, bias_qv, w_out, bias_out, w_up, bias_up, w_down, bias_down,
    ln_gain, ln_bias, cotangent,
):
    count = lax.axis_size("pipe")
    n = lax.axis_size("dp")
    width = tokens.shape[2]
    ff = w_up.shape[2]
    b_qkv = jnp.concatenate([bias_qv[:, :width], jnp.zeros_like(bias_qv[:, :width]), bias_qv[:, width:]], 1)
    weights = (
        w_qkv[0], b_qkv, w_out[0], bias_out, w_up[0], bias_up, w_down[0], bias_down, ln_gain[0], ln_bias[0],
    )
    *kept, mixed, peaks = run_forward(count, tokens, lengths, ema_scales, weights)
    x, xq, qkv, lse, ctx, cq, n1, rs1, hq, aq, sl, n2, rs2 = kept
    dproj, dbr, dup, ddn, g0, small = run_backward(
        count, cotangent, lengths, ema_scales, weights, kept
    )
    sums = jnp.sum(small, 0)
    parts, at = [], 0
    for size in (width, width, width, width, width, width, ff, width, width, width):
        parts.append(sums[at : at + size])
        at += size
    parts[7:] = [jnp.concatenate([parts[7], parts[9]])]
    packed = jnp.concatenate([v.reshape(n, -1) for v in parts], 1)
    peak = jnp.max(peaks, (1, 2))
    sums_width = packed.shape[1]
    if n >= 4 and n % 2 == 0 and width // n % 16 == 0 and ff // n % 128 == 0 and sums_width == 9 * 128:
        top = jnp.broadcast_to(jnp.pad(peak, (0, 124))[None, None], (n, 7, 128))
        with_peak = jnp.concatenate([packed.reshape(n, 9, 128), top], 1)
        g_qkv, g_out, g_up, g_down, small_sum, grad_tokens = run_grads(
            count, n, kept, dproj, dbr, dup, ddn, g0, with_peak
        )
        mine = small_sum[:9].reshape(1, sums_width)
        batch_max = small_sum[9:10, :4]
    else:
        g_down = weight_grad(aq, ddn)
        g_up = weight_grad(hq, dup)
        g_out = weight_grad(cq, dbr)
        g_qkv = weight_grad(xq, dproj)
        mine = lax.psum_scatter(packed, "dp", scatter_dimension=0, tiled=True)
        batch_max = lax.pmax(peak, "dp")[None]
        grad_tokens = share_pieces(g0, count, lax.axis_index("pipe"))
    outs, at = [], 0
    for size in (width, width, width, width, width, width, ff, 2 * width):
        outs.append(mine[:, at : at + size // n])
        at += size // n
    gain0, gain1, shift0, shift1, s_out, s_down, s_up, s_qv = outs
    g_gain = jnp.stack([gain0, gain1], 1)
    g_shift = jnp.stack([shift0, shift1], 1)
    return (
        mixed, grad_tokens, g_qkv[None], s_qv, g_out[None], s_out, g_up[None], s_up, g_down[None], s_down,
        g_gain, g_shift, batch_max,
    )


def solution(mesh):
    return jax.shard_map(
        shards,
        mesh=mesh,
        in_specs=(
            P("dp", None, None), P("dp"), P("pipe", None), P("pipe", None, None), P("pipe", None),
            P("pipe", None, None), P("pipe", None), P("pipe", None, None), P("pipe", None),
            P("pipe", None, None), P("pipe", None), P("pipe", None, None), P("pipe", None, None),
            P("dp", None, None),
        ),
        out_specs=(
            P("dp", "pipe", None), P("dp", "pipe", None), P("pipe", "dp", None), P("pipe", "dp"),
            P("pipe", "dp", None), P("pipe", "dp"), P("pipe", "dp", None), P("pipe", "dp"),
            P("pipe", "dp", None), P("pipe", "dp"), P("pipe", None, "dp"), P("pipe", None, "dp"),
            P("pipe", None),
        ),
        check_vma=False,
    )
```

```python
import jax
import jax.numpy as jnp
from jax import lax
from jax.experimental import pallas as pl
from jax.experimental.pallas import tpu as pltpu
from jax.sharding import PartitionSpec as P

HEAD_DIM = 64
PAIR = 2 * HEAD_DIM
EPS = 1e-06
MASKED = -1000000000.0
CHUNK = 512
BLOCK = 16
OPS = 64
LOGICAL = pl.DeviceIdType.MESH
F32 = jnp.float32
BF16 = jnp.bfloat16

ERF_POLY = (
    0.7978846780398201,
    0.03633450830808018,
    -3.432973817348946e-05,
    -5.463434792182573e-05,
    3.860434711489827e-06,
    -1.254735264100511e-07,
    1.6084598007909267e-09,
)
ERF_CLAMP = 5.3 * 5.3
HALF_LOG2E = -0.7213475204444817
LOG2_DENSITY = -1.3257480647361593


def dot_nn(a, b):
    return jnp.dot(a, b, preferred_element_type=F32)


def dot_nt(a, b):
    return lax.dot_general(a, b, (((1,), (1,)), ((), ())), preferred_element_type=F32)


def dot_tn(a, b):
    return lax.dot_general(a, b, (((0,), (0,)), ((), ())), preferred_element_type=F32)


def fold_rows(v):
    return jnp.sum(v.reshape(v.shape[0] // 8, 8, v.shape[1]), 0)


def peak_rows(v):
    tiles = [v[:, i : i + 128] for i in range(0, v.shape[1], 128)]
    top = tiles[0]
    for tile in tiles[1:]:
        top = jnp.maximum(top, tile)
    return jnp.max(top.reshape(v.shape[0] // 8, 8, 128), 0)


def split3(v):
    hi = v.astype(BF16)
    rest = v - hi.astype(F32)
    mid = rest.astype(BF16)
    low = (rest - mid.astype(F32)).astype(BF16)
    return hi, mid, low


def greet(stage, count):
    barrier = pltpu.get_barrier_semaphore()
    for step in range(1, count):
        peer = lax.rem(stage + step, count)
        pl.semaphore_signal(barrier, inc=1, device_id={"pipe": peer}, device_id_type=LOGICAL)
    pl.semaphore_wait(barrier, count - 1)


def activation(u, ceiling, inv_ceiling):
    square = u * u
    w = jnp.minimum(square, ERF_CLAMP)
    poly = w * ERF_POLY[-1] + ERF_POLY[-2]
    for coef in ERF_POLY[-3::-1]:
        poly = poly * w + coef
    t = jnp.tanh(u * poly)
    half = 0.5 * u
    act = half + half * t
    ratio = jnp.tanh(act * inv_ceiling)
    density = jnp.exp2(square * HALF_LOG2E + LOG2_DENSITY)
    slope = (1.0 - ratio * ratio) * ((0.5 + 0.5 * t) + u * density)
    return act, ceiling * ratio, slope


def fwd_kernel(count, *refs):
    (
        lens, scales, tokens, w_qkv, b_qkv, w_out, b_out, w_up, b_up, w_down, b_down, gain, shift,
        x_o, xq_o, qkv_o, lse_o, ctx_o, cq_o, n1_o, rs1_o, hq_o, aq_o, sl_o, n2_o, rs2_o,
        mixed_o, peaks_o,
        xin, xout, xq_s, qkv_s, lse_s, ctx_s, cq_s, n1_s, rs1_s, hq_s, aq_s, sl_s, n2_s, rs2_s,
        acc, hid, up_s, ops_s, s_s, e_s, o_s, top_s, amax_s,
        save_sem, in_sem, send_sem, recv_sem, mix_send, mix_recv,
    ) = refs
    r = pl.program_id(0)
    rows = pl.num_programs(0)
    row_count = tokens.shape[0]
    seq, width = tokens.shape[1], tokens.shape[2]
    ff = w_up.shape[1]
    piece = seq // count
    stage = lax.axis_index("pipe")
    first = stage == 0
    last = stage == count - 1

    staged = {
        "x": (xin.at[r], x_o), "xq": (xq_s, xq_o), "qkv": (qkv_s, qkv_o), "lse": (lse_s, lse_o),
        "ctx": (ctx_s, ctx_o), "cq": (cq_s, cq_o), "n1": (n1_s, n1_o), "rs1": (rs1_s, rs1_o),
        "hq": (hq_s, hq_o), "aq": (aq_s, aq_o), "sl": (sl_s, sl_o), "n2": (n2_s, n2_o),
        "rs2": (rs2_s, rs2_o),
    }
    order = list(staged)

    def save_copy(name):
        src, dst = staged[name]
        return pltpu.make_async_copy(src, dst.at[r], save_sem.at[order.index(name)])

    def save(name):
        save_copy(name).start()

    def reuse(*names):
        @pl.when(r > 0)
        def _():
            for name in names:
                save_copy(name).wait()

    def token_copy(i):
        return pltpu.make_async_copy(tokens.at[i], xin.at[i], in_sem.at[i])

    def hop(i):
        return pltpu.make_async_remote_copy(
            src_ref=xout.at[i], dst_ref=xin.at[i], send_sem=send_sem.at[i], recv_sem=recv_sem.at[i],
            device_id={"pipe": lax.rem(stage + 1, count)}, device_id_type=LOGICAL,
        )

    def mix_part(i, p):
        return pltpu.make_async_remote_copy(
            src_ref=xout.at[i, pl.ds(p * piece, piece)], dst_ref=mixed_o.at[i],
            send_sem=mix_send.at[i, p], recv_sem=mix_recv.at[i],
            device_id={"pipe": jnp.int32(p)}, device_id_type=LOGICAL,
        )

    def mix_own(i):
        return pltpu.make_async_copy(
            xout.at[i, pl.ds((count - 1) * piece, piece)], mixed_o.at[i], mix_send.at[i, count - 1]
        )

    @pl.when(r == 0)
    def _():
        greet(stage, count)
        peaks_o[...] = jnp.zeros_like(peaks_o)

        @pl.when(first)
        def _():
            for i in range(row_count):
                token_copy(i).start()

    @pl.when(first)
    def _():
        token_copy(r).wait()

    @pl.when(jnp.logical_not(first))
    def _():
        hop(r).wait_recv()

    length = lens[r]
    m0, m1, m2, m3 = scales[0, 0], scales[0, 1], scales[0, 2], scales[0, 3]
    i0, i1, i2, i3 = 1.0 / m0, 1.0 / m1, 1.0 / m2, 1.0 / m3

    def row_mask(start, size):
        return (start + lax.broadcasted_iota(jnp.int32, (size, 1), 0)) < length

    def blocks(size, body, init=0):
        return lax.fori_loop(0, seq // size, lambda i, c: body(i * size, pl.ds(i * size, size), c), init, unroll=True)

    no_peak = jnp.zeros((8, 128), F32)

    @pl.when(r > 0)
    def _():
        save_copy("x").wait()

    save("x")
    reuse("xq", "qkv", "lse", "ctx", "cq")

    def quant_in(start, at, top):
        x = xin[r, at, :].astype(F32)
        xq_s[at, :] = (m0 * jnp.tanh(x * i0)).astype(BF16)
        return jnp.maximum(top, masked_peak(x, start))

    def masked_peak(v, start):
        return peak_rows(jnp.where(row_mask(start, v.shape[0]), jnp.abs(v), 0.0))

    peaks_o[0] = jnp.maximum(peaks_o[0], blocks(BLOCK, quant_in, no_peak))
    save("xq")

    for j in range(3):
        cols = pl.ds(j * width, width)
        proj = dot_nn(xq_s[...], w_qkv[:, cols]) + b_qkv[:, cols]
        qkv_s[:, cols] = proj.astype(BF16)
    save("qkv")

    one = jnp.ones((), BF16)
    zero = jnp.zeros((), BF16)
    head_scale = jnp.asarray(HEAD_DIM ** -0.5, BF16)

    def prepare(p):
        slot = p % 2

        def body(start, at, c):
            lane = lax.broadcasted_iota(jnp.int32, (OPS, PAIR), 1)
            lo = lane < HEAD_DIM
            spot = jnp.where(lo, lane, lane - HEAD_DIM)
            bias = jnp.where(row_mask(start, OPS), 0.0, MASKED)
            extra = jnp.where(spot == 0, jnp.broadcast_to(bias, (OPS, PAIR)), 0.0).astype(BF16)
            q2 = qkv_s[at, p * PAIR : (p + 1) * PAIR] * head_scale
            k2 = qkv_s[at, width + p * PAIR : width + (p + 1) * PAIR]
            v2 = qkv_s[at, 2 * width + p * PAIR : 2 * width + (p + 1) * PAIR]
            ops_s[slot, 0, at, :] = jnp.where(lo, q2, one)
            ops_s[slot, 1, at, :] = jnp.where(lo, one, q2)
            ops_s[slot, 2, at, :] = jnp.where(lo, k2, extra)
            ops_s[slot, 3, at, :] = jnp.where(lo, extra, k2)
            ops_s[slot, 4, at, :] = jnp.where(lo, v2, one)
            ops_s[slot, 5, at, :] = jnp.where(lo, one, v2)
            return c

        blocks(OPS, body)

    def scores(h):
        p, side = h // 2, h % 2
        s_s[side] = dot_nt(ops_s[p % 2, side], ops_s[p % 2, 2 + side])

    def soften(h):
        side = h % 2

        def body(start, at, c):
            s = s_s[side, at, :]
            top = jnp.max(s, -1, keepdims=True)
            e_s[side, at, :] = jnp.exp(s - top).astype(BF16)
            top_s[side, at, :] = jnp.broadcast_to(top, (BLOCK, PAIR))
            return c

        blocks(BLOCK, body)

    def collect(h):
        p, side = h // 2, h % 2
        o_s[side] = dot_nn(e_s[side], ops_s[p % 2, 4 + side])

    def settle(p, peak):
        cols = slice(p * PAIR, (p + 1) * PAIR)

        def body(start, at, top):
            lo = lax.broadcasted_iota(jnp.int32, (OPS, PAIR), 1) < HEAD_DIM
            o_a, o_b = o_s[0, at, :], o_s[1, at, :]
            total = pltpu.roll(jnp.where(lo, o_b, o_a), HEAD_DIM, 1)
            c = jnp.where(lo, o_a, o_b) / total
            ctx_s[at, cols] = c
            lse_s[at, cols] = jnp.where(lo, top_s[0, at, :], top_s[1, at, :]) + jnp.log(total)
            cq_s[at, cols] = (m1 * jnp.tanh(c * i1)).astype(BF16)
            return jnp.maximum(top, masked_peak(c, start))

        return blocks(OPS, body, peak)

    heads = 2 * (width // PAIR)
    peak = no_peak
    prepare(0)
    scores(0)
    for h in range(heads):
        if h + 1 < heads:
            if (h + 1) % 2 == 0:
                prepare((h + 1) // 2)
            scores(h + 1)
        soften(h)
        collect(h)
        if h % 2 == 1:
            peak = settle(h // 2, peak)
    peaks_o[1] = jnp.maximum(peaks_o[1], peak)
    save("lse")
    save("ctx")
    save("cq")
    acc[...] = dot_nn(cq_s[...], w_out[...])
    reuse("n1", "rs1", "hq")

    def norm_one(start, at, top):
        s = xin[r, at, :].astype(F32) + (acc[at, :] + b_out[...])
        center = s - jnp.mean(s, -1, keepdims=True)
        rs = lax.rsqrt(jnp.mean(center * center, -1, keepdims=True) + EPS)
        n = center * rs
        h = n * gain[0:1, :] + shift[0:1, :]
        n1_s[at, :] = n.astype(BF16)
        rs1_s[at, :] = jnp.broadcast_to(rs, (BLOCK, 128))
        hid[at, :] = h
        hq_s[at, :] = (m2 * jnp.tanh(h * i2)).astype(BF16)
        return jnp.maximum(top, masked_peak(h, start))

    peaks_o[2] = jnp.maximum(peaks_o[2], blocks(BLOCK, norm_one, no_peak))
    save("n1")
    save("rs1")
    save("hq")
    reuse("aq", "sl")

    chunks = ff // CHUNK

    def up_chunk(c):
        cols = pl.ds(c * CHUNK, CHUNK)
        up_s[c % 2] = dot_nn(hq_s[...], w_up[:, cols])

    def act_chunk(c):
        cols = pl.ds(c * CHUNK, CHUNK)

        def body(start, at, carry):
            act, low, slope = activation(up_s[c % 2, at, :] + b_up[:, cols], m3, i3)
            aq_s[at, cols] = low.astype(BF16)
            sl_s[at, cols] = slope.astype(BF16)
            size = jnp.abs(act)
            top = size[:, 0:128]
            for i in range(128, CHUNK, 128):
                top = jnp.maximum(top, size[:, i : i + 128])
            amax_s[at, :] = top if c == 0 else jnp.maximum(amax_s[at, :], top)
            return carry

        blocks(BLOCK, body)

    def down_chunk(c):
        cols = pl.ds(c * CHUNK, CHUNK)
        part = dot_nn(aq_s[:, cols], w_down[cols, :])
        if c == 0:
            acc[...] = part
        else:
            acc[...] += part

    up_chunk(0)
    for c in range(chunks):
        if c + 1 < chunks:
            up_chunk(c + 1)
        act_chunk(c)
        if c > 0:
            down_chunk(c - 1)
    down_chunk(chunks - 1)
    peaks_o[3] = jnp.maximum(peaks_o[3], masked_peak(amax_s[...], 0))
    save("aq")
    save("sl")
    reuse("n2", "rs2")

    def norm_two(start, at, c):
        s = hid[at, :] + (acc[at, :] + b_down[...])
        center = s - jnp.mean(s, -1, keepdims=True)
        rs = lax.rsqrt(jnp.mean(center * center, -1, keepdims=True) + EPS)
        n = center * rs
        n2_s[at, :] = n.astype(BF16)
        rs2_s[at, :] = jnp.broadcast_to(rs, (BLOCK, 128))
        xout[r, at, :] = (n * gain[1:2, :] + shift[1:2, :]).astype(BF16)
        return c

    blocks(BLOCK, norm_two)
    save("n2")
    save("rs2")

    @pl.when(jnp.logical_not(last))
    def _():
        hop(r).start()

    @pl.when(last)
    def _():
        for p in range(count - 1):
            mix_part(r, p).start()
        mix_own(r).start()

    @pl.when(r == rows - 1)
    def _():
        for name in order:
            save_copy(name).wait()

        @pl.when(jnp.logical_not(last))
        def _():
            for i in range(row_count):
                hop(i).wait_send()
            for i in range(row_count):
                mix_part(i, 0).wait_recv()

        @pl.when(last)
        def _():
            for i in range(row_count):
                for p in range(count - 1):
                    mix_part(i, p).wait_send()
                mix_own(i).wait()


def bwd_kernel(count, *refs):
    (
        lens, scales, seeds, w_qkv, w_out, w_up, w_down, gain, shift,
        x_i, qkv_i, lse_i, ctx_i, n1_i, rs1_i, sl_i, n2_i, rs2_i,
        dproj_o, dbr_o, dup_o, ddn_o, gtok_o, small_o,
        gin, gout, x_s, qkv_s, lse_s, ctx_s, n1_s, rs1_s, sl_s, n2_s, rs2_s,
        dproj_s, dbr_s, dup_s, ddn_s, dctx_s, acc, dr,
        up_s, ops_s, s_s, g_s, p_s, ds_s, gv_s, gk_s, gq_s, k_t, in_s, inner_s,
        load_sem, save_sem, in_sem, send_sem, recv_sem, tok_send,
    ) = refs
    r = pl.program_id(0)
    rows = pl.num_programs(0)
    row_count = seeds.shape[0]
    seq, width = seeds.shape[1], seeds.shape[2]
    ff = w_up.shape[1]
    piece = seq // count
    stage = lax.axis_index("pipe")
    first = stage == 0
    last = stage == count - 1

    loaded = {
        "n2": (n2_i, n2_s), "rs2": (rs2_i, rs2_s), "sl": (sl_i, sl_s), "n1": (n1_i, n1_s),
        "rs1": (rs1_i, rs1_s), "ctx": (ctx_i, ctx_s), "qkv": (qkv_i, qkv_s), "lse": (lse_i, lse_s),
        "x": (x_i, x_s),
    }
    load_order = list(loaded)
    staged = {
        "ddn": (ddn_s, ddn_o), "dup": (dup_s, dup_o), "dbr": (dbr_s, dbr_o), "dproj": (dproj_s, dproj_o),
    }
    save_order = list(staged)

    def load_copy(name, i):
        src, dst = loaded[name]
        return pltpu.make_async_copy(src.at[i], dst, load_sem.at[load_order.index(name)])

    def fetch_next(*names):
        @pl.when(r + 1 < rows)
        def _():
            for name in names:
                load_copy(name, r + 1).start()

    def ready(*names):
        for name in names:
            load_copy(name, r).wait()

    def save_copy(name):
        src, dst = staged[name]
        return pltpu.make_async_copy(src, dst.at[r], save_sem.at[save_order.index(name)])

    def save(name):
        save_copy(name).start()

    def reuse(*names):
        @pl.when(r > 0)
        def _():
            for name in names:
                save_copy(name).wait()

    def seed_copy(i):
        return pltpu.make_async_copy(seeds.at[i], gin.at[i], in_sem.at[i])

    def hop(i):
        return pltpu.make_async_remote_copy(
            src_ref=gout.at[i], dst_ref=gin.at[i], send_sem=send_sem.at[i], recv_sem=recv_sem.at[i],
            device_id={"pipe": lax.rem(stage + count - 1, count)}, device_id_type=LOGICAL,
        )

    def tok_copy(i):
        return pltpu.make_async_copy(gout.at[i], gtok_o.at[i], tok_send.at[i])

    @pl.when(r == 0)
    def _():
        greet(stage, count)
        small_o[...] = jnp.zeros_like(small_o)
        for name in load_order:
            load_copy(name, 0).start()

        @pl.when(last)
        def _():
            for i in range(row_count):
                seed_copy(i).start()

    @pl.when(last)
    def _():
        seed_copy(r).wait()

    @pl.when(jnp.logical_not(last))
    def _():
        hop(r).wait_recv()

    length = lens[r]
    m0, m1, m2 = scales[0, 0], scales[0, 1], scales[0, 2]
    i0, i1, i2 = 1.0 / m0, 1.0 / m1, 1.0 / m2

    offsets = {}
    at_col = 0
    for name, size in (
        ("gain0", width), ("gain1", width), ("shift0", width), ("shift1", width),
        ("out", width), ("down", width), ("up", ff), ("qkv", 3 * width),
    ):
        offsets[name] = at_col
        at_col += size

    def blocks(size, body, init=0):
        return lax.fori_loop(0, seq // size, lambda i, c: body(i * size, pl.ds(i * size, size), c), init, unroll=True)

    def row_mask(start, size):
        return (start + lax.broadcasted_iota(jnp.int32, (size, 1), 0)) < length

    def put_small(name, v, col=0):
        small_o[:, pl.ds(offsets[name] + col, v.shape[1])] += v

    no_sum = jnp.zeros((8, width), F32)

    ready("n2", "rs2")
    reuse("ddn")

    def norm_two(start, at, sums):
        dy = jnp.where(row_mask(start, BLOCK), gin[r, at, :].astype(F32), 0.0)
        n = n2_s[at, :].astype(F32)
        e = dy * gain[1:2, :]
        mean_e = jnp.mean(e, -1, keepdims=True)
        mean_en = jnp.mean(e * n, -1, keepdims=True)
        d = (e - mean_e - n * mean_en) * rs2_s[at, 0:1]
        dr[at, :] = d
        ddn_s[at, :] = d.astype(BF16)
        return sums[0] + fold_rows(dy * n), sums[1] + fold_rows(dy), sums[2] + fold_rows(d)

    for name, v in zip(("gain1", "shift1", "down"), blocks(BLOCK, norm_two, (no_sum,) * 3)):
        put_small(name, v)
    save("ddn")
    fetch_next("n2", "rs2")
    ready("sl")
    reuse("dup")

    chunks = ff // CHUNK

    def dact_chunk(c):
        up_s[c % 2] = dot_nt(ddn_s[...], w_down[pl.ds(c * CHUNK, CHUNK), :])

    def slope_chunk(c):
        cols = pl.ds(c * CHUNK, CHUNK)

        def body(start, at, total):
            d = up_s[c % 2, at, :] * sl_s[at, cols].astype(F32)
            dup_s[at, cols] = d.astype(BF16)
            return total + fold_rows(d)

        put_small("up", blocks(BLOCK, body, jnp.zeros((8, CHUNK), F32)), c * CHUNK)

    def dhid_chunk(c):
        cols = pl.ds(c * CHUNK, CHUNK)
        part = dot_nt(dup_s[:, cols], w_up[:, cols])
        if c == 0:
            acc[...] = part
        else:
            acc[...] += part

    dact_chunk(0)
    for c in range(chunks):
        if c + 1 < chunks:
            dact_chunk(c + 1)
        slope_chunk(c)
        if c > 0:
            dhid_chunk(c - 1)
    dhid_chunk(chunks - 1)
    save("dup")
    fetch_next("sl")
    ready("n1", "rs1")
    reuse("dbr")

    def norm_one(start, at, sums):
        n = n1_s[at, :].astype(F32)
        t = jnp.tanh((n * gain[0:1, :] + shift[0:1, :]) * i2)
        dy = dr[at, :] + acc[at, :] * (1.0 - t * t)
        e = dy * gain[0:1, :]
        mean_e = jnp.mean(e, -1, keepdims=True)
        mean_en = jnp.mean(e * n, -1, keepdims=True)
        d = (e - mean_e - n * mean_en) * rs1_s[at, 0:1]
        dr[at, :] = d
        dbr_s[at, :] = d.astype(BF16)
        return sums[0] + fold_rows(dy * n), sums[1] + fold_rows(dy), sums[2] + fold_rows(d)

    for name, v in zip(("gain0", "shift0", "out"), blocks(BLOCK, norm_one, (no_sum,) * 3)):
        put_small(name, v)
    save("dbr")
    fetch_next("n1", "rs1")
    ready("ctx")
    acc[...] = dot_nt(dbr_s[...], w_out[...])
    ready("qkv", "lse")
    reuse("dproj")

    one = jnp.ones((), BF16)
    zero = jnp.zeros((), BF16)
    head_scale = jnp.asarray(HEAD_DIM ** -0.5, BF16)
    src = lax.broadcasted_iota(jnp.int32, (PAIR, PAIR), 0) < HEAD_DIM
    dst = lax.broadcasted_iota(jnp.int32, (PAIR, PAIR), 1) < HEAD_DIM
    swap_sum = jnp.where(src == dst, 0.0, 1.0).astype(BF16)

    def prepare(p):
        slot = p % 2
        cols = slice(p * PAIR, (p + 1) * PAIR)

        def first_half(start, at, c):
            ctx = ctx_s[at, cols]
            t = jnp.tanh(ctx * i1)
            low = (acc[at, cols] * (1.0 - t * t)).astype(BF16)
            dctx_s[slot, at, :] = low
            hi, mid, _ = split3(low.astype(F32) * ctx)
            in_s[0, at, :] = hi
            in_s[1, at, :] = mid
            return c

        blocks(OPS, first_half)
        inner_s[...] = dot_nn(in_s[0], swap_sum) + dot_nn(in_s[1], swap_sum)

        def second_half(start, at, c):
            lane = lax.broadcasted_iota(jnp.int32, (OPS, PAIR), 1)
            lo = lane < HEAD_DIM
            spot = jnp.where(lo, lane, lane - HEAD_DIM)
            bias = jnp.broadcast_to(jnp.where(row_mask(start, OPS), 0.0, MASKED), (OPS, PAIR))
            q2 = qkv_s[at, p * PAIR : (p + 1) * PAIR] * head_scale
            k2 = qkv_s[at, width + p * PAIR : width + (p + 1) * PAIR]
            v2 = qkv_s[at, 2 * width + p * PAIR : 2 * width + (p + 1) * PAIR]
            do2 = dctx_s[slot, at, :]
            l_hi, l_mid, l_low = split3(pltpu.roll(lse_s[at, cols], HEAD_DIM, 1))
            extra_q = jnp.where(
                spot == 0, one, jnp.where(spot == 1, -l_hi, jnp.where(spot == 2, -l_mid, -l_low))
            )
            extra_k = jnp.where(spot == 0, bias, jnp.where(spot <= 3, 1.0, 0.0)).astype(BF16)
            d_hi, d_mid, d_low = split3(inner_s[at, :])
            extra_do = jnp.where(spot == 0, -d_hi, jnp.where(spot == 1, -d_mid, -d_low))
            extra_v = jnp.where(spot <= 2, 1.0, 0.0).astype(BF16)
            ops_s[slot, 0, at, :] = jnp.where(lo, q2, extra_q)
            ops_s[slot, 1, at, :] = jnp.where(lo, extra_q, q2)
            ops_s[slot, 2, at, :] = jnp.where(lo, k2, extra_k)
            ops_s[slot, 3, at, :] = jnp.where(lo, extra_k, k2)
            ops_s[slot, 4, at, :] = jnp.where(lo, v2, extra_v)
            ops_s[slot, 5, at, :] = jnp.where(lo, extra_v, v2)
            ops_s[slot, 6, at, :] = jnp.where(lo, do2, extra_do)
            ops_s[slot, 7, at, :] = jnp.where(lo, extra_do, do2)
            ops_s[slot, 8, at, :] = q2
            return c

        blocks(OPS, second_half)
        k_t[slot] = qkv_s[:, width + p * PAIR : width + (p + 1) * PAIR].T

    def scores(h):
        slot, side = h // 2 % 2, h % 2
        s_s[side] = dot_nt(ops_s[slot, 2 + side], ops_s[slot, side])
        g_s[side] = dot_nt(ops_s[slot, 4 + side], ops_s[slot, 6 + side])

    def soften(h):
        side = h % 2

        def body(start, at, c):
            prob = jnp.exp(s_s[side, at, :])
            p_s[side, at, :] = prob.astype(BF16)
            ds_s[side, at, :] = (prob * g_s[side, at, :]).astype(BF16)
            return c

        blocks(BLOCK, body)

    def collect(h):
        slot, side = h // 2 % 2, h % 2
        rows = slice(side * HEAD_DIM, (side + 1) * HEAD_DIM)
        gv_s[side] = dot_nn(p_s[side], dctx_s[slot])
        gk_s[side] = dot_nn(ds_s[side], ops_s[slot, 8])
        gq_s[rows, :] = dot_nn(k_t[slot, rows, :], ds_s[side])

    def settle(p):
        dproj_s[:, p * PAIR : (p + 1) * PAIR] = (gq_s[...].T * (HEAD_DIM ** -0.5)).astype(BF16)

        def body(start, at, c):
            lo = lax.broadcasted_iota(jnp.int32, (OPS, PAIR), 1) < HEAD_DIM
            k = jnp.where(lo, gk_s[0, at, :], gk_s[1, at, :])
            v = jnp.where(lo, gv_s[0, at, :], gv_s[1, at, :])
            dproj_s[at, width + p * PAIR : width + (p + 1) * PAIR] = k.astype(BF16)
            dproj_s[at, 2 * width + p * PAIR : 2 * width + (p + 1) * PAIR] = v.astype(BF16)
            return c

        blocks(OPS, body)

    heads = 2 * (width // PAIR)
    prepare(0)
    scores(0)
    for h in range(heads):
        if h + 1 < heads:
            if (h + 1) % 2 == 0:
                prepare((h + 1) // 2)
            scores(h + 1)
        soften(h)
        collect(h)
        if h % 2 == 1:
            settle(h // 2)
    save("dproj")
    fetch_next("ctx", "qkv", "lse")
    for j in range(3):
        cols = pl.ds(j * width, width)
        part = dot_nt(dproj_s[:, cols], w_qkv[:, cols])
        if j == 0:
            acc[...] = part
        else:
            acc[...] += part
    ready("x")

    def quant_in(start, at, sums):
        t = jnp.tanh(x_s[at, :].astype(F32) * i0)
        gout[r, at, :] = (dr[at, :] + acc[at, :] * (1.0 - t * t)).astype(BF16)
        return (
            sums[0] + fold_rows(dproj_s[at, 0:width].astype(F32)),
            sums[1] + fold_rows(dproj_s[at, 2 * width : 3 * width].astype(F32)),
        )

    sums = blocks(BLOCK, quant_in, (no_sum,) * 2)
    put_small("qkv", sums[0])
    put_small("qkv", sums[1], 2 * width)
    fetch_next("x")

    @pl.when(jnp.logical_not(first))
    def _():
        hop(r).start()

    @pl.when(first)
    def _():
        tok_copy(r).start()

    @pl.when(r == rows - 1)
    def _():
        for name in save_order:
            save_copy(name).wait()

        @pl.when(jnp.logical_not(first))
        def _():
            for i in range(row_count):
                hop(i).wait_send()

        @pl.when(first)
        def _():
            for i in range(row_count):
                tok_copy(i).wait()


def whole(a):
    return pl.BlockSpec(a.shape, lambda r, n=a.ndim: (0,) * n, pipeline_mode=pl.Buffered(1))


ANYWHERE = pl.BlockSpec(memory_space=pl.ANY)
SCALAR = pl.BlockSpec(memory_space=pltpu.SMEM)
VMEM_LIMIT = 60 * 1024 * 1024


def run_forward(count, tokens, lengths, scales, weights):
    w_qkv, b_qkv, w_out, b_out, w_up, b_up, w_down, b_down, gain, shift = weights
    rows, seq, width = tokens.shape
    ff = w_up.shape[1]
    big = lambda n, t: jax.ShapeDtypeStruct((rows, seq, n), t)
    saves = [
        (width, BF16), (width, BF16), (3 * width, BF16), (width, F32), (width, F32), (width, BF16),
        (width, BF16), (128, F32), (width, BF16), (ff, BF16), (ff, BF16), (width, BF16), (128, F32),
    ]
    dense = (w_qkv, b_qkv, w_out, b_out, w_up, b_up, w_down, b_down, gain, shift)
    tok = rows * seq
    return pl.pallas_call(
        lambda *refs: fwd_kernel(count, *refs),
        grid=(rows,),
        in_specs=[SCALAR, SCALAR, ANYWHERE] + [whole(a) for a in dense],
        out_specs=[ANYWHERE] * 14 + [pl.BlockSpec((4, 8, 128), lambda r: (0, 0, 0))],
        out_shape=[big(n, t) for n, t in saves]
        + [
            jax.ShapeDtypeStruct((rows, seq // count, width), BF16),
            jax.ShapeDtypeStruct((4, 8, 128), F32),
        ],
        scratch_shapes=[pltpu.VMEM((rows, seq, width), BF16), pltpu.VMEM((rows, seq, width), BF16)]
        + [pltpu.VMEM((seq, n), t) for n, t in saves[1:]]
        + [
            pltpu.VMEM((seq, width), F32),
            pltpu.VMEM((seq, width), F32),
            pltpu.VMEM((2, seq, CHUNK), F32),
            pltpu.VMEM((2, 6, seq, PAIR), BF16),
            pltpu.VMEM((2, seq, seq), F32),
            pltpu.VMEM((2, seq, seq), BF16),
            pltpu.VMEM((2, seq, PAIR), F32),
            pltpu.VMEM((2, seq, PAIR), F32),
            pltpu.VMEM((seq, 128), F32),
            pltpu.SemaphoreType.DMA((13,)),
            pltpu.SemaphoreType.DMA((rows,)),
            pltpu.SemaphoreType.DMA((rows,)),
            pltpu.SemaphoreType.DMA((rows,)),
            pltpu.SemaphoreType.DMA((rows, count)),
            pltpu.SemaphoreType.DMA((rows,)),
        ],
        compiler_params=pltpu.CompilerParams(
            collective_id=0, has_side_effects=True, vmem_limit_bytes=VMEM_LIMIT,
            dimension_semantics=("arbitrary",),
        ),
        cost_estimate=pl.CostEstimate(
            flops=2 * tok * (4 * width * width + 2 * width * ff + 2 * seq * width),
            bytes_accessed=tok * 28000, transcendentals=tok * 3 * ff,
        ),
    )(lengths, scales, tokens, *dense)


def run_backward(count, seeds, lengths, scales, weights, kept):
    w_qkv, b_qkv, w_out, b_out, w_up, b_up, w_down, b_down, gain, shift = weights
    x, xq, qkv, lse, ctx, cq, n1, rs1, hq, aq, sl, n2, rs2 = kept
    rows, seq, width = seeds.shape
    ff = w_up.shape[1]
    big = lambda n, t: jax.ShapeDtypeStruct((rows, seq, n), t)
    saves = [(3 * width, BF16), (width, BF16), (ff, BF16), (width, BF16)]
    loads = (x, qkv, lse, ctx, n1, rs1, sl, n2, rs2)
    dense = (w_qkv, w_out, w_up, w_down, gain, shift)
    tok = rows * seq
    small = 6 * width + ff + 3 * width
    return pl.pallas_call(
        lambda *refs: bwd_kernel(count, *refs),
        grid=(rows,),
        in_specs=[SCALAR, SCALAR, ANYWHERE] + [whole(a) for a in dense] + [ANYWHERE] * 9,
        out_specs=[ANYWHERE] * 5 + [pl.BlockSpec((8, small), lambda r: (0, 0))],
        out_shape=[big(n, t) for n, t in saves]
        + [big(width, BF16), jax.ShapeDtypeStruct((8, small), F32)],
        scratch_shapes=[pltpu.VMEM((rows, seq, width), BF16), pltpu.VMEM((rows, seq, width), BF16)]
        + [pltpu.VMEM(a.shape[1:], a.dtype) for a in loads]
        + [pltpu.VMEM((seq, n), t) for n, t in saves]
        + [
            pltpu.VMEM((2, seq, PAIR), BF16),
            pltpu.VMEM((seq, width), F32),
            pltpu.VMEM((seq, width), F32),
            pltpu.VMEM((2, seq, CHUNK), F32),
            pltpu.VMEM((2, 9, seq, PAIR), BF16),
            pltpu.VMEM((2, seq, seq), F32),
            pltpu.VMEM((2, seq, seq), F32),
            pltpu.VMEM((2, seq, seq), BF16),
            pltpu.VMEM((2, seq, seq), BF16),
            pltpu.VMEM((2, seq, PAIR), F32),
            pltpu.VMEM((2, seq, PAIR), F32),
            pltpu.VMEM((PAIR, seq), F32),
            pltpu.VMEM((2, PAIR, seq), BF16),
            pltpu.VMEM((2, seq, PAIR), BF16),
            pltpu.VMEM((seq, PAIR), F32),
            pltpu.SemaphoreType.DMA((9,)),
            pltpu.SemaphoreType.DMA((4,)),
            pltpu.SemaphoreType.DMA((rows,)),
            pltpu.SemaphoreType.DMA((rows,)),
            pltpu.SemaphoreType.DMA((rows,)),
            pltpu.SemaphoreType.DMA((rows,)),
        ],
        compiler_params=pltpu.CompilerParams(
            collective_id=1, has_side_effects=True, vmem_limit_bytes=VMEM_LIMIT,
            dimension_semantics=("arbitrary",),
        ),
        cost_estimate=pl.CostEstimate(
            flops=2 * tok * (4 * width * width + 2 * width * ff + 5 * seq * width),
            bytes_accessed=tok * 28000, transcendentals=tok * ff,
        ),
    )(lengths, scales, seeds, *dense, *loads)


def ring_to_dp(pos, n):
    return jnp.where(pos < n // 2, 2 * pos, 2 * (n - pos) - 1)


def dp_to_ring(j, n):
    return jnp.where(j % 2 == 0, j // 2, n - 1 - j // 2)


def grad_kernel(count, n, *refs):
    (
        aq, hq, cq, xq, ddn, dbr, dup, dproj, small, g0,
        gq_o, go_o, gu_o, gd_o, small_o, gtok_o,
        slots_d, slots_u, slots_q, slots_s, aq_v, ddn_v, left_v, right_v, own_u, own_q,
        aq_sem, ddn_sem, left_sem, right_sem,
        send_d, recv_d, send_u, recv_u, send_q, recv_q, send_s, recv_s, tok_send, tok_recv,
    ) = refs
    width = ddn.shape[1]
    ff = aq.shape[1]
    shard, shard_ff = width // n, ff // n
    row_count, seq = g0.shape[0], g0.shape[1]
    piece = seq // count
    stage = lax.axis_index("pipe")
    me = lax.axis_index("dp")
    pos = dp_to_ring(me, n)
    first = stage == 0
    ahead = ring_to_dp(lax.rem(pos + 1, n), n)
    behind = ring_to_dp(lax.rem(pos + n - 1, n), n)
    target = (ahead, behind)

    barrier = pltpu.get_barrier_semaphore()
    for peer in target:
        pl.semaphore_signal(barrier, inc=1, device_id={"dp": peer}, device_id_type=LOGICAL)

    @pl.when(first)
    def _():
        pl.semaphore_wait(barrier, 1 + count)

    @pl.when(jnp.logical_not(first))
    def _():
        pl.semaphore_signal(barrier, inc=1, device_id={"pipe": jnp.int32(0)}, device_id_type=LOGICAL)
        pl.semaphore_wait(barrier, 2)

    def tok_part(i, p):
        return pltpu.make_async_remote_copy(
            src_ref=g0.at[i, pl.ds(p * piece, piece)], dst_ref=gtok_o.at[i],
            send_sem=tok_send.at[i, p], recv_sem=tok_recv.at[i],
            device_id={"pipe": jnp.int32(p)}, device_id_type=LOGICAL,
        )

    def tok_own(i):
        return pltpu.make_async_copy(g0.at[i, pl.ds(0, piece)], gtok_o.at[i], tok_send.at[i, 0])

    def chunk(d, step):
        at = pos + 2 * n - 1 - step if d == 0 else pos + 1 + step
        return ring_to_dp(lax.rem(at, n), n)

    def aq_copy(d, step, slot):
        cols = pl.ds(pl.multiple_of(chunk(d, step) * shard_ff, 128), shard_ff)
        return pltpu.make_async_copy(aq.at[:, cols], aq_v.at[d, slot], aq_sem.at[d, slot])

    blocks = [(hq, dup, i, own_u, i) for i in range(ff // width)]
    blocks += [(xq, dproj, i, own_q, i) for i in range(3)] + [(cq, dbr, 0, own_q, 3)]
    lefts = [hq, xq, cq]

    def left_copy(k):
        return pltpu.make_async_copy(lefts[k], left_v.at[k % 2], left_sem.at[k])

    def right_copy(b):
        return pltpu.make_async_copy(
            blocks[b][1].at[:, pl.ds(blocks[b][2] * width, width)], right_v.at[b % 2], right_sem.at[b]
        )

    def block_left(b):
        return [k for k in range(3) if lefts[k] is blocks[b][0]][0]

    ddn_copy = pltpu.make_async_copy(ddn, ddn_v, ddn_sem.at[0])
    ddn_copy.start()
    for d in range(2):
        aq_copy(d, 0, 0).start()
    left_copy(0).start()
    right_copy(0).start()
    right_copy(1).start()
    left_copy(1).start()

    @pl.when(first)
    def _():
        for i in range(row_count):
            for p in range(1, count):
                tok_part(i, p).start()
            tok_own(i).start()

    ddn_copy.wait()

    def product(b):
        k = block_left(b)
        if b == 0 or block_left(b - 1) != k:
            left_copy(k).wait()
        right_copy(b).wait()
        part = dot_tn(left_v[k % 2], right_v[b % 2])
        blocks[b][3][:, pl.ds(blocks[b][4] * width, width)] = part.astype(BF16)
        if b + 2 < len(blocks):
            right_copy(b + 2).start()
        if k + 2 < 3 and block_left(b + 1) != k:
            left_copy(k + 2).start()

    def lane(slots, send, recv, d, step, own, finish):
        def message(at):
            return pltpu.make_async_remote_copy(
                src_ref=slots.at[d, at], dst_ref=slots.at[d, jnp.minimum(at + 1, n - 1)],
                send_sem=send.at[d, at], recv_sem=recv.at[d, jnp.minimum(at + 1, n - 1)],
                device_id={"dp": target[d]}, device_id_type=LOGICAL,
            )

        def arrived(at):
            return pltpu.make_async_remote_copy(
                src_ref=slots.at[d, at], dst_ref=slots.at[d, at],
                send_sem=send.at[d, at], recv_sem=recv.at[d, at],
                device_id={"dp": target[d]}, device_id_type=LOGICAL,
            )

        if own is None:
            return message

        @pl.when(step == 0)
        def _():
            slots[d, 0] = own().astype(BF16)

        @pl.when(step > 0)
        def _():
            mine = own()
            arrived(step).wait_recv()
            total = slots[d, step].astype(F32) + mine

            @pl.when(step < n - 1)
            def _():
                slots[d, step] = total.astype(BF16)

            @pl.when(step == n - 1)
            def _():
                finish(total)

        @pl.when(step < n - 1)
        def _():
            message(step).start()

    def small_message(at):
        return pltpu.make_async_remote_copy(
            src_ref=slots_s.at[at], dst_ref=slots_s.at[jnp.minimum(at + 1, n - 1)],
            send_sem=send_s.at[at], recv_sem=recv_s.at[jnp.minimum(at + 1, n - 1)],
            device_id={"dp": target[0]}, device_id_type=LOGICAL,
        )

    def small_arrived(at):
        return pltpu.make_async_remote_copy(
            src_ref=slots_s.at[at], dst_ref=slots_s.at[at], send_sem=send_s.at[at],
            recv_sem=recv_s.at[at], device_id={"dp": target[0]}, device_id_type=LOGICAL,
        )

    half = width // 2
    sum_rows = lax.broadcasted_iota(jnp.int32, (16, 128), 0) < 9

    def small_step(step):
        mine = small[chunk(0, step)]

        @pl.when(step == 0)
        def _():
            slots_s[0] = mine

        @pl.when(step > 0)
        def _():
            small_arrived(step).wait_recv()
            got = slots_s[step]
            slots_s[step] = jnp.where(sum_rows, got + mine, jnp.maximum(got, mine))

        @pl.when(step < n - 1)
        def _():
            small_message(step).start()

        @pl.when(step == n - 1)
        def _():
            small_o[...] = slots_s[step]

    def down_lane(d, step):
        slot = lax.rem(step, 2)

        def own():
            part = dot_tn(aq_v[d, slot], ddn_v[:, d * half : (d + 1) * half])
            return part

        def finish(total):
            gd_o[:, d * half : (d + 1) * half] = total

        aq_copy(d, step, slot).wait()

        @pl.when(step < n - 1)
        def _():
            aq_copy(d, step + 1, 1 - slot).start()

        lane(slots_d, send_d, recv_d, d, step, own, finish)

    def rows_of(own_ref, d, step):
        at = pl.ds(pl.multiple_of(chunk(d, step) * shard, 16), shard)
        span = own_ref.shape[1] // 2
        return own_ref[at, d * span : (d + 1) * span].astype(F32)

    def up_lane(d, step):
        def finish(total):
            gu_o[:, d * (ff // 2) : (d + 1) * (ff // 2)] = total

        lane(slots_u, send_u, recv_u, d, step, lambda: rows_of(own_u, d, step), finish)

    def qkvo_lane(d, step):
        def finish(total):
            if d == 0:
                gq_o[:, 0 : 2 * width] = total
            else:
                gq_o[:, 2 * width : 3 * width] = total[:, 0:width]
                go_o[...] = total[:, width : 2 * width]

        lane(slots_q, send_q, recv_q, d, step, lambda: rows_of(own_q, d, step), finish)

    def turn(t, _):
        @pl.when(t < n)
        def _():
            for d in range(2):
                down_lane(d, t)
            small_step(t)

        @pl.when(jnp.logical_and(t >= 2, t < n + 2))
        def _():
            for d in range(2):
                up_lane(d, t - 2)

        @pl.when(t >= 4)
        def _():
            for d in range(2):
                qkvo_lane(d, t - 4)

        for turn_at in range(4):
            @pl.when(t == turn_at)
            def _():
                for b in range(2 * turn_at, 2 * turn_at + 2):
                    product(b)

        return 0

    lax.fori_loop(0, n + 4, turn, 0)

    def drain(at, _):
        for d in range(2):
            lane(slots_d, send_d, recv_d, d, 0, None, None)(at).wait_send()
            lane(slots_u, send_u, recv_u, d, 0, None, None)(at).wait_send()
            lane(slots_q, send_q, recv_q, d, 0, None, None)(at).wait_send()
        small_message(at).wait_send()
        return 0

    lax.fori_loop(0, n - 1, drain, 0)

    @pl.when(first)
    def _():
        for i in range(row_count):
            for p in range(1, count):
                tok_part(i, p).wait_send()
            tok_own(i).wait()

    @pl.when(jnp.logical_not(first))
    def _():
        for i in range(row_count):
            tok_part(i, 1).wait_recv()


def run_grads(count, n, kept, dproj, dbr, dup, ddn, g0, small):
    x, xq, qkv, lse, ctx, cq, n1, rs1, hq, aq, sl, n2, rs2 = kept
    rows, seq, width = g0.shape
    ff = aq.shape[2]
    flat = lambda a: a.reshape(rows * seq, a.shape[2])
    tok = rows * seq
    shard, shard_ff = width // n, ff // n
    ops = [flat(a) for a in (aq, hq, cq, xq, ddn, dbr, dup, dproj)]
    vmem = pl.BlockSpec(memory_space=pltpu.VMEM)
    sem = pltpu.SemaphoreType.DMA
    return pl.pallas_call(
        lambda *refs: grad_kernel(count, n, *refs),
        in_specs=[ANYWHERE] * 8 + [vmem, ANYWHERE],
        out_specs=[vmem] * 5 + [ANYWHERE],
        out_shape=[
            jax.ShapeDtypeStruct((shard, 3 * width), F32),
            jax.ShapeDtypeStruct((shard, width), F32),
            jax.ShapeDtypeStruct((shard, ff), F32),
            jax.ShapeDtypeStruct((shard_ff, width), F32),
            jax.ShapeDtypeStruct((16, 128), F32),
            jax.ShapeDtypeStruct((rows, seq // count, width), BF16),
        ],
        scratch_shapes=[
            pltpu.VMEM((2, n, shard_ff, width // 2), BF16),
            pltpu.VMEM((2, n, shard, ff // 2), BF16),
            pltpu.VMEM((2, n, shard, 2 * width), BF16),
            pltpu.VMEM((n, 16, 128), F32),
            pltpu.VMEM((2, 2, tok, shard_ff), BF16),
            pltpu.VMEM((tok, width), BF16),
            pltpu.VMEM((2, tok, width), BF16),
            pltpu.VMEM((2, tok, width), BF16),
            pltpu.VMEM((width, ff), BF16),
            pltpu.VMEM((width, 4 * width), BF16),
            sem((2, 2)), sem((1,)), sem((3,)), sem((8,)),
            sem((2, n)), sem((2, n)), sem((2, n)), sem((2, n)), sem((2, n)), sem((2, n)),
            sem((n,)), sem((n,)), sem((rows, count)), sem((rows,)),
        ],
        compiler_params=pltpu.CompilerParams(
            collective_id=2, has_side_effects=True, vmem_limit_bytes=VMEM_LIMIT,
        ),
        cost_estimate=pl.CostEstimate(
            flops=2 * tok * (4 * width * width + 2 * width * ff), bytes_accessed=tok * 25000, transcendentals=0,
        ),
    )(*ops, small, g0)


def weight_grad(left, right):
    g = jnp.einsum("rsd,rse->de", left, right, preferred_element_type=F32).astype(BF16)
    return lax.psum_scatter(g, "dp", scatter_dimension=0, tiled=True).astype(F32)


def share_pieces(whole_rows, count, stage):
    piece = whole_rows.shape[1] // count
    mine = whole_rows[:, :piece]
    for p in range(1, count):
        got = lax.ppermute(whole_rows[:, p * piece : (p + 1) * piece], "pipe", [(0, p)])
        mine = jnp.where(stage == p, got, mine)
    return mine


def shards(
    tokens, lengths, ema_scales, w_qkv, bias_qv, w_out, bias_out, w_up, bias_up, w_down, bias_down,
    ln_gain, ln_bias, cotangent,
):
    count = lax.axis_size("pipe")
    n = lax.axis_size("dp")
    width = tokens.shape[2]
    ff = w_up.shape[2]
    b_qkv = jnp.concatenate([bias_qv[:, :width], jnp.zeros_like(bias_qv[:, :width]), bias_qv[:, width:]], 1)
    weights = (
        w_qkv[0], b_qkv, w_out[0], bias_out, w_up[0], bias_up, w_down[0], bias_down, ln_gain[0], ln_bias[0],
    )
    *kept, mixed, peaks = run_forward(count, tokens, lengths, ema_scales, weights)
    x, xq, qkv, lse, ctx, cq, n1, rs1, hq, aq, sl, n2, rs2 = kept
    dproj, dbr, dup, ddn, g0, small = run_backward(
        count, cotangent, lengths, ema_scales, weights, kept
    )
    sums = jnp.sum(small, 0)
    parts, at = [], 0
    for size in (width, width, width, width, width, width, ff, width, width, width):
        parts.append(sums[at : at + size])
        at += size
    parts[7:] = [jnp.concatenate([parts[7], parts[9]])]
    packed = jnp.concatenate([v.reshape(n, -1) for v in parts], 1)
    peak = jnp.max(peaks, (1, 2))
    sums_width = packed.shape[1]
    if n >= 4 and n % 2 == 0 and width // n % 16 == 0 and ff // n % 128 == 0 and sums_width == 9 * 128:
        top = jnp.broadcast_to(jnp.pad(peak, (0, 124))[None, None], (n, 7, 128))
        with_peak = jnp.concatenate([packed.reshape(n, 9, 128), top], 1)
        g_qkv, g_out, g_up, g_down, small_sum, grad_tokens = run_grads(
            count, n, kept, dproj, dbr, dup, ddn, g0, with_peak
        )
        mine = small_sum[:9].reshape(1, sums_width)
        batch_max = small_sum[9:10, :4]
    else:
        g_down = weight_grad(aq, ddn)
        g_up = weight_grad(hq, dup)
        g_out = weight_grad(cq, dbr)
        g_qkv = weight_grad(xq, dproj)
        mine = lax.psum_scatter(packed, "dp", scatter_dimension=0, tiled=True)
        batch_max = lax.pmax(peak, "dp")[None]
        grad_tokens = share_pieces(g0, count, lax.axis_index("pipe"))
    outs, at = [], 0
    for size in (width, width, width, width, width, width, ff, 2 * width):
        outs.append(mine[:, at : at + size // n])
        at += size // n
    gain0, gain1, shift0, shift1, s_out, s_down, s_up, s_qv = outs
    g_gain = jnp.stack([gain0, gain1], 1)
    g_shift = jnp.stack([shift0, shift1], 1)
    return (
        mixed, grad_tokens, g_qkv[None], s_qv, g_out[None], s_out, g_up[None], s_up, g_down[None], s_down,
        g_gain, g_shift, batch_max,
    )


def solution(mesh):
    return jax.shard_map(
        shards,
        mesh=mesh,
        in_specs=(
            P("dp", None, None), P("dp"), P("pipe", None), P("pipe", None, None), P("pipe", None),
            P("pipe", None, None), P("pipe", None), P("pipe", None, None), P("pipe", None),
            P("pipe", None, None), P("pipe", None), P("pipe", None, None), P("pipe", None, None),
            P("dp", None, None),
        ),
        out_specs=(
            P("dp", "pipe", None), P("dp", "pipe", None), P("pipe", "dp", None), P("pipe", "dp"),
            P("pipe", "dp", None), P("pipe", "dp"), P("pipe", "dp", None), P("pipe", "dp"),
            P("pipe", "dp", None), P("pipe", "dp"), P("pipe", None, "dp"), P("pipe", None, "dp"),
            P("pipe", None),
        ),
        check_vma=False,
    )
```

```python
import jax
import jax.numpy as jnp
from jax import lax
from jax.experimental import pallas as pl
from jax.experimental.pallas import tpu as pltpu
from jax.sharding import PartitionSpec as P

HEAD_DIM = 64
PAIR = 2 * HEAD_DIM
EPS = 1e-06
MASKED = -1000000000.0
CHUNK = 512
BLOCK = 16
OPS = 64
LOGICAL = pl.DeviceIdType.MESH
F32 = jnp.float32
BF16 = jnp.bfloat16

ERF_POLY = (
    0.7978823511659165,
    0.03634481045269742,
    -4.5110171354091134e-05,
    -5.02654469142584e-05,
    3.0867937984305273e-06,
    -6.60140005994544e-08,
)
ERF_CLAMP = 5.2 * 5.2
HALF_LOG2E = -0.7213475204444817
LOG2_DENSITY = -1.3257480647361593


def dot_nn(a, b):
    return jnp.dot(a, b, preferred_element_type=F32)


def dot_nt(a, b):
    return lax.dot_general(a, b, (((1,), (1,)), ((), ())), preferred_element_type=F32)


def dot_tn(a, b):
    return lax.dot_general(a, b, (((0,), (0,)), ((), ())), preferred_element_type=F32)


def fold_rows(v):
    return jnp.sum(v.reshape(v.shape[0] // 8, 8, v.shape[1]), 0)


def peak_rows(v):
    tiles = [v[:, i : i + 128] for i in range(0, v.shape[1], 128)]
    top = tiles[0]
    for tile in tiles[1:]:
        top = jnp.maximum(top, tile)
    return jnp.max(top.reshape(v.shape[0] // 8, 8, 128), 0)


def split3(v):
    hi = v.astype(BF16)
    rest = v - hi.astype(F32)
    mid = rest.astype(BF16)
    low = (rest - mid.astype(F32)).astype(BF16)
    return hi, mid, low


def greet(stage, count):
    barrier = pltpu.get_barrier_semaphore()
    for step in range(1, count):
        peer = lax.rem(stage + step, count)
        pl.semaphore_signal(barrier, inc=1, device_id={"pipe": peer}, device_id_type=LOGICAL)
    pl.semaphore_wait(barrier, count - 1)


def activation(u, ceiling, inv_ceiling):
    square = u * u
    w = jnp.minimum(square, ERF_CLAMP)
    poly = w * ERF_POLY[-1] + ERF_POLY[-2]
    for coef in ERF_POLY[-3::-1]:
        poly = poly * w + coef
    t = jnp.tanh(u * poly)
    half = 0.5 * u
    act = half + half * t
    ratio = jnp.tanh(act * inv_ceiling)
    density = jnp.exp2(square * HALF_LOG2E + LOG2_DENSITY)
    slope = (1.0 - ratio * ratio) * ((0.5 + 0.5 * t) + u * density)
    return act, ceiling * ratio, slope


def fwd_kernel(count, *refs):
    (
        lens, scales, tokens, h_qkv, h_out, h_up, h_down, b_qkv, b_out, b_up, b_down, gain, shift,
        x_o, qkv_o, lse_o, ctx_o, n1_o, rs1_o, sl_o, n2_o, rs2_o, left_o,
        mixed_o, peaks_o,
        w_qkv, w_out, w_up, w_down, w_sem,
        xin, xout, qkv_s, lse_s, ctx_s, n1_s, rs1_s, sl_s, n2_s, rs2_s, aq_s, hq_s, xq_s, cq_s,
        acc, hid, up_s, ops_s, s_s, e_s, o_s, top_s, amax_s,
        save_sem, in_sem, send_sem, recv_sem, mix_send, mix_recv,
    ) = refs
    r = pl.program_id(0)
    rows = pl.num_programs(0)
    row_count = tokens.shape[0]
    seq, width = tokens.shape[1], tokens.shape[2]
    ff = w_up.shape[1]
    piece = seq // count
    stage = lax.axis_index("pipe")
    first = stage == 0
    last = stage == count - 1

    left = {"aq": (0, ff), "hq": (ff, width), "xq": (ff + width, width), "cq": (ff + 2 * width, width)}
    staged = {
        "x": (xin.at[r], x_o), "qkv": (qkv_s, qkv_o), "lse": (lse_s, lse_o), "ctx": (ctx_s, ctx_o),
        "n1": (n1_s, n1_o), "rs1": (rs1_s, rs1_o), "sl": (sl_s, sl_o), "n2": (n2_s, n2_o),
        "rs2": (rs2_s, rs2_o), "aq": (aq_s, left_o), "hq": (hq_s, left_o), "xq": (xq_s, left_o),
        "cq": (cq_s, left_o),
    }
    order = list(staged)
    fetches = [(h_qkv, w_qkv), (h_out, w_out), (h_up, w_up), (h_down, w_down)]

    def weight_copy(k):
        return pltpu.make_async_copy(fetches[k][0], fetches[k][1], w_sem.at[k])

    def weight_ready(k):
        @pl.when(r == 0)
        def _():
            weight_copy(k).wait()

    def save_copy(name):
        src, dst = staged[name]
        dst = dst.at[r]
        if name in left:
            dst = dst.at[:, pl.ds(*left[name])]
        return pltpu.make_async_copy(src, dst, save_sem.at[order.index(name)])

    def save(name):
        save_copy(name).start()

    def reuse(*names):
        @pl.when(r > 0)
        def _():
            for name in names:
                save_copy(name).wait()

    def token_copy(i):
        return pltpu.make_async_copy(tokens.at[i], xin.at[i], in_sem.at[i])

    def hop(i):
        return pltpu.make_async_remote_copy(
            src_ref=xout.at[i], dst_ref=xin.at[i], send_sem=send_sem.at[i], recv_sem=recv_sem.at[i],
            device_id={"pipe": lax.rem(stage + 1, count)}, device_id_type=LOGICAL,
        )

    def mix_part(i, p):
        return pltpu.make_async_remote_copy(
            src_ref=xout.at[i, pl.ds(p * piece, piece)], dst_ref=mixed_o.at[i],
            send_sem=mix_send.at[i, p], recv_sem=mix_recv.at[i],
            device_id={"pipe": jnp.int32(p)}, device_id_type=LOGICAL,
        )

    def mix_own(i):
        return pltpu.make_async_copy(
            xout.at[i, pl.ds((count - 1) * piece, piece)], mixed_o.at[i], mix_send.at[i, count - 1]
        )

    @pl.when(r == 0)
    def _():
        greet(stage, count)
        peaks_o[...] = jnp.zeros_like(peaks_o)
        for k in range(4):
            weight_copy(k).start()

        @pl.when(first)
        def _():
            for i in range(row_count):
                token_copy(i).start()

    @pl.when(first)
    def _():
        token_copy(r).wait()

    @pl.when(jnp.logical_not(first))
    def _():
        hop(r).wait_recv()

    length = lens[r]
    m0, m1, m2, m3 = scales[0, 0], scales[0, 1], scales[0, 2], scales[0, 3]
    i0, i1, i2, i3 = 1.0 / m0, 1.0 / m1, 1.0 / m2, 1.0 / m3

    def row_mask(start, size):
        return (start + lax.broadcasted_iota(jnp.int32, (size, 1), 0)) < length

    def blocks(size, body, init=0):
        return lax.fori_loop(0, seq // size, lambda i, c: body(i * size, pl.ds(i * size, size), c), init, unroll=True)

    no_peak = jnp.zeros((8, 128), F32)

    @pl.when(r > 0)
    def _():
        save_copy("x").wait()

    save("x")
    reuse("xq", "qkv", "lse", "ctx", "cq")

    def quant_in(start, at, top):
        x = xin[r, at, :].astype(F32)
        xq_s[at, :] = (m0 * jnp.tanh(x * i0)).astype(BF16)
        return jnp.maximum(top, masked_peak(x, start))

    def masked_peak(v, start):
        return peak_rows(jnp.where(row_mask(start, v.shape[0]), jnp.abs(v), 0.0))

    peaks_o[0] = jnp.maximum(peaks_o[0], blocks(BLOCK, quant_in, no_peak))
    save("xq")

    weight_ready(0)
    for j in range(3):
        cols = pl.ds(j * width, width)
        proj = dot_nn(xq_s[...], w_qkv[:, cols]) + b_qkv[:, cols]
        qkv_s[:, cols] = proj.astype(BF16)
    save("qkv")

    one = jnp.ones((), BF16)
    zero = jnp.zeros((), BF16)
    head_scale = jnp.asarray(HEAD_DIM ** -0.5, BF16)

    def prepare(p):
        slot = p % 2

        def body(start, at, c):
            lane = lax.broadcasted_iota(jnp.int32, (OPS, PAIR), 1)
            lo = lane < HEAD_DIM
            spot = jnp.where(lo, lane, lane - HEAD_DIM)
            bias = jnp.where(row_mask(start, OPS), 0.0, MASKED)
            extra = jnp.where(spot == 0, jnp.broadcast_to(bias, (OPS, PAIR)), 0.0).astype(BF16)
            q2 = qkv_s[at, p * PAIR : (p + 1) * PAIR] * head_scale
            k2 = qkv_s[at, width + p * PAIR : width + (p + 1) * PAIR]
            v2 = qkv_s[at, 2 * width + p * PAIR : 2 * width + (p + 1) * PAIR]
            ops_s[slot, 0, at, :] = jnp.where(lo, q2, one)
            ops_s[slot, 1, at, :] = jnp.where(lo, one, q2)
            ops_s[slot, 2, at, :] = jnp.where(lo, k2, extra)
            ops_s[slot, 3, at, :] = jnp.where(lo, extra, k2)
            ops_s[slot, 4, at, :] = jnp.where(lo, v2, one)
            ops_s[slot, 5, at, :] = jnp.where(lo, one, v2)
            return c

        blocks(OPS, body)

    def scores(h):
        p, side = h // 2, h % 2
        s_s[side] = dot_nt(ops_s[p % 2, side], ops_s[p % 2, 2 + side])

    def soften(h):
        side = h % 2

        def body(start, at, c):
            s = s_s[side, at, :]
            top = jnp.max(s, -1, keepdims=True)
            e_s[side, at, :] = jnp.exp(s - top).astype(BF16)
            top_s[side, at, :] = jnp.broadcast_to(top, (BLOCK, PAIR))
            return c

        blocks(BLOCK, body)

    def collect(h):
        p, side = h // 2, h % 2
        o_s[side] = dot_nn(e_s[side], ops_s[p % 2, 4 + side])

    def settle(p, peak):
        cols = slice(p * PAIR, (p + 1) * PAIR)

        def body(start, at, top):
            lo = lax.broadcasted_iota(jnp.int32, (OPS, PAIR), 1) < HEAD_DIM
            o_a, o_b = o_s[0, at, :], o_s[1, at, :]
            total = pltpu.roll(jnp.where(lo, o_b, o_a), HEAD_DIM, 1)
            c = jnp.where(lo, o_a, o_b) / total
            ctx_s[at, cols] = c
            lse_s[at, cols] = jnp.where(lo, top_s[0, at, :], top_s[1, at, :]) + jnp.log(total)
            cq_s[at, cols] = (m1 * jnp.tanh(c * i1)).astype(BF16)
            return jnp.maximum(top, masked_peak(c, start))

        return blocks(OPS, body, peak)

    heads = 2 * (width // PAIR)
    peak = no_peak
    prepare(0)
    scores(0)
    for h in range(heads):
        if h + 1 < heads:
            if (h + 1) % 2 == 0:
                prepare((h + 1) // 2)
            scores(h + 1)
        soften(h)
        collect(h)
        if h % 2 == 1:
            peak = settle(h // 2, peak)
    peaks_o[1] = jnp.maximum(peaks_o[1], peak)
    save("lse")
    save("ctx")
    save("cq")
    weight_ready(1)
    acc[...] = dot_nn(cq_s[...], w_out[...])
    reuse("n1", "rs1", "hq")

    def norm_one(start, at, top):
        s = xin[r, at, :].astype(F32) + (acc[at, :] + b_out[...])
        center = s - jnp.mean(s, -1, keepdims=True)
        rs = lax.rsqrt(jnp.mean(center * center, -1, keepdims=True) + EPS)
        n = center * rs
        h = n * gain[0:1, :] + shift[0:1, :]
        n1_s[at, :] = n.astype(BF16)
        rs1_s[at, :] = jnp.broadcast_to(rs, (BLOCK, 128))
        hid[at, :] = h
        hq_s[at, :] = (m2 * jnp.tanh(h * i2)).astype(BF16)
        return jnp.maximum(top, masked_peak(h, start))

    peaks_o[2] = jnp.maximum(peaks_o[2], blocks(BLOCK, norm_one, no_peak))
    save("n1")
    save("rs1")
    save("hq")
    reuse("aq", "sl")

    chunks = ff // CHUNK

    def up_chunk(c):
        cols = pl.ds(c * CHUNK, CHUNK)
        up_s[c % 2] = dot_nn(hq_s[...], w_up[:, cols])

    def act_chunk(c):
        cols = pl.ds(c * CHUNK, CHUNK)

        def body(start, at, carry):
            act, low, slope = activation(up_s[c % 2, at, :] + b_up[:, cols], m3, i3)
            aq_s[at, cols] = low.astype(BF16)
            sl_s[at, cols] = slope.astype(BF16)
            size = jnp.abs(act)
            top = size[:, 0:128]
            for i in range(128, CHUNK, 128):
                top = jnp.maximum(top, size[:, i : i + 128])
            amax_s[at, :] = top if c == 0 else jnp.maximum(amax_s[at, :], top)
            return carry

        blocks(BLOCK, body)

    def down_chunk(c):
        cols = pl.ds(c * CHUNK, CHUNK)
        part = dot_nn(aq_s[:, cols], w_down[cols, :])
        if c == 0:
            acc[...] = part
        else:
            acc[...] += part

    weight_ready(2)
    weight_ready(3)
    up_chunk(0)
    for c in range(chunks):
        if c + 1 < chunks:
            up_chunk(c + 1)
        act_chunk(c)
        if c > 0:
            down_chunk(c - 1)
    down_chunk(chunks - 1)
    peaks_o[3] = jnp.maximum(peaks_o[3], masked_peak(amax_s[...], 0))
    save("aq")
    save("sl")
    reuse("n2", "rs2")

    def norm_two(start, at, c):
        s = hid[at, :] + (acc[at, :] + b_down[...])
        center = s - jnp.mean(s, -1, keepdims=True)
        rs = lax.rsqrt(jnp.mean(center * center, -1, keepdims=True) + EPS)
        n = center * rs
        n2_s[at, :] = n.astype(BF16)
        rs2_s[at, :] = jnp.broadcast_to(rs, (BLOCK, 128))
        xout[r, at, :] = (n * gain[1:2, :] + shift[1:2, :]).astype(BF16)
        return c

    blocks(BLOCK, norm_two)
    save("n2")
    save("rs2")

    @pl.when(jnp.logical_not(last))
    def _():
        hop(r).start()

    @pl.when(last)
    def _():
        for p in range(count - 1):
            mix_part(r, p).start()
        mix_own(r).start()

    @pl.when(r == rows - 1)
    def _():
        for name in order:
            save_copy(name).wait()

        @pl.when(jnp.logical_not(last))
        def _():
            for i in range(row_count):
                hop(i).wait_send()
            for i in range(row_count):
                mix_part(i, 0).wait_recv()

        @pl.when(last)
        def _():
            for i in range(row_count):
                for p in range(count - 1):
                    mix_part(i, p).wait_send()
                mix_own(i).wait()


def bwd_kernel(count, *refs):
    (
        lens, scales, seeds, h_qkv, h_out, h_up, h_down, gain, shift, left_i,
        x_i, qkv_i, lse_i, ctx_i, n1_i, rs1_i, sl_i, n2_i, rs2_i,
        dproj_o, dbr_o, dup_o, ddn_o, gtok_o, left_o, small_o,
        w_qkv, w_out, w_up, w_down, w_sem, turn_in, turn_out, turn_in_sem, turn_out_sem,
        gin, gout, x_s, qkv_s, lse_s, ctx_s, n1_s, rs1_s, sl_s, n2_s, rs2_s,
        dproj_s, dbr_s, dup_s, ddn_s, dctx_s, acc, dr,
        up_s, ops_s, s_s, g_s, p_s, ds_s, gv_s, gk_s, gq_s, k_t, in_s, inner_s,
        load_sem, save_sem, in_sem, send_sem, recv_sem, tok_send,
    ) = refs
    r = pl.program_id(0)
    rows = pl.num_programs(0)
    row_count = seeds.shape[0]
    seq, width = seeds.shape[1], seeds.shape[2]
    ff = w_up.shape[1]
    piece = seq // count
    stage = lax.axis_index("pipe")
    first = stage == 0
    last = stage == count - 1

    loaded = {
        "n2": (n2_i, n2_s), "rs2": (rs2_i, rs2_s), "sl": (sl_i, sl_s), "n1": (n1_i, n1_s),
        "rs1": (rs1_i, rs1_s), "ctx": (ctx_i, ctx_s), "qkv": (qkv_i, qkv_s), "lse": (lse_i, lse_s),
        "x": (x_i, x_s),
    }
    load_order = list(loaded)
    staged = {
        "ddn": (ddn_s, ddn_o), "dup": (dup_s, dup_o), "dbr": (dbr_s, dbr_o), "dproj": (dproj_s, dproj_o),
    }
    save_order = list(staged)

    def load_copy(name, i):
        src, dst = loaded[name]
        return pltpu.make_async_copy(src.at[i], dst, load_sem.at[load_order.index(name)])

    def fetch_next(*names):
        @pl.when(r + 1 < rows)
        def _():
            for name in names:
                load_copy(name, r + 1).start()

    def ready(*names):
        for name in names:
            load_copy(name, r).wait()

    def save_copy(name):
        src, dst = staged[name]
        return pltpu.make_async_copy(src, dst.at[r], save_sem.at[save_order.index(name)])

    def save(name):
        save_copy(name).start()

    def reuse(*names):
        @pl.when(r > 0)
        def _():
            for name in names:
                save_copy(name).wait()

    def seed_copy(i):
        return pltpu.make_async_copy(seeds.at[i], gin.at[i], in_sem.at[i])

    def hop(i):
        return pltpu.make_async_remote_copy(
            src_ref=gout.at[i], dst_ref=gin.at[i], send_sem=send_sem.at[i], recv_sem=recv_sem.at[i],
            device_id={"pipe": lax.rem(stage + count - 1, count)}, device_id_type=LOGICAL,
        )

    def tok_copy(i):
        return pltpu.make_async_copy(gout.at[i], gtok_o.at[i], tok_send.at[i])

    fetches = [(h_down, w_down), (h_up, w_up), (h_out, w_out), (h_qkv, w_qkv)]

    def weight_copy(k):
        return pltpu.make_async_copy(fetches[k][0], fetches[k][1], w_sem.at[k])

    def weight_ready(k):
        @pl.when(r == 0)
        def _():
            weight_copy(k).wait()

    parts = left_i.shape[2] // width
    turns = row_count * parts

    def turn_load(i):
        cols = pl.ds(pl.multiple_of(i % parts * width, 128), width)
        return pltpu.make_async_copy(left_i.at[i // parts, :, cols], turn_in.at[i % 2], turn_in_sem.at[i % 2])

    def turn_store(i):
        rows_at = pl.ds(pl.multiple_of(i % parts * width, 128), width)
        cols = pl.ds(pl.multiple_of(i // parts * seq, 128), seq)
        return pltpu.make_async_copy(turn_out.at[i % 2], left_o.at[rows_at, cols], turn_out_sem.at[i % 2])

    def turn_left():
        turn_load(0).start()

        def body(i, c):
            @pl.when(i + 1 < turns)
            def _():
                turn_load(i + 1).start()

            turn_load(i).wait()

            @pl.when(i >= 2)
            def _():
                turn_store(i - 2).wait()

            turn_out[i % 2] = turn_in[i % 2].T
            turn_store(i).start()
            return c

        lax.fori_loop(0, turns, body, 0)
        turn_store(turns - 2).wait()
        turn_store(turns - 1).wait()

    @pl.when(r == 0)
    def _():
        greet(stage, count)
        small_o[...] = jnp.zeros_like(small_o)

        @pl.when(last)
        def _():
            for i in range(row_count):
                seed_copy(i).start()

        for name in ("n2", "rs2"):
            load_copy(name, 0).start()
        weight_copy(0).start()
        load_copy("sl", 0).start()
        for k in (1, 2, 3):
            weight_copy(k).start()
        for name in load_order[3:]:
            load_copy(name, 0).start()

        @pl.when(jnp.logical_not(last))
        def _():
            turn_left()

    @pl.when(last)
    def _():
        seed_copy(r).wait()

    @pl.when(jnp.logical_not(last))
    def _():
        hop(r).wait_recv()

    length = lens[r]
    m0, m1, m2 = scales[0, 0], scales[0, 1], scales[0, 2]
    i0, i1, i2 = 1.0 / m0, 1.0 / m1, 1.0 / m2

    offsets = {}
    at_col = 0
    for name, size in (
        ("gain0", width), ("gain1", width), ("shift0", width), ("shift1", width),
        ("out", width), ("down", width), ("up", ff), ("qkv", 3 * width),
    ):
        offsets[name] = at_col
        at_col += size

    def blocks(size, body, init=0):
        return lax.fori_loop(0, seq // size, lambda i, c: body(i * size, pl.ds(i * size, size), c), init, unroll=True)

    def row_mask(start, size):
        return (start + lax.broadcasted_iota(jnp.int32, (size, 1), 0)) < length

    def put_small(name, v, col=0):
        small_o[:, pl.ds(offsets[name] + col, v.shape[1])] += v

    no_sum = jnp.zeros((8, width), F32)

    ready("n2", "rs2")
    reuse("ddn")

    def norm_two(start, at, sums):
        dy = jnp.where(row_mask(start, BLOCK), gin[r, at, :].astype(F32), 0.0)
        n = n2_s[at, :].astype(F32)
        e = dy * gain[1:2, :]
        mean_e = jnp.mean(e, -1, keepdims=True)
        mean_en = jnp.mean(e * n, -1, keepdims=True)
        d = (e - mean_e - n * mean_en) * rs2_s[at, 0:1]
        dr[at, :] = d
        ddn_s[at, :] = d.astype(BF16)
        return sums[0] + fold_rows(dy * n), sums[1] + fold_rows(dy), sums[2] + fold_rows(d)

    for name, v in zip(("gain1", "shift1", "down"), blocks(BLOCK, norm_two, (no_sum,) * 3)):
        put_small(name, v)
    save("ddn")
    fetch_next("n2", "rs2")
    ready("sl")
    reuse("dup")

    chunks = ff // CHUNK

    def dact_chunk(c):
        up_s[c % 2] = dot_nt(ddn_s[...], w_down[pl.ds(c * CHUNK, CHUNK), :])

    def slope_chunk(c):
        cols = pl.ds(c * CHUNK, CHUNK)

        def body(start, at, total):
            d = up_s[c % 2, at, :] * sl_s[at, cols].astype(F32)
            dup_s[at, cols] = d.astype(BF16)
            return total + fold_rows(d)

        put_small("up", blocks(BLOCK, body, jnp.zeros((8, CHUNK), F32)), c * CHUNK)

    def dhid_chunk(c):
        cols = pl.ds(c * CHUNK, CHUNK)
        part = dot_nt(dup_s[:, cols], w_up[:, cols])
        if c == 0:
            acc[...] = part
        else:
            acc[...] += part

    weight_ready(0)
    weight_ready(1)
    dact_chunk(0)
    for c in range(chunks):
        if c + 1 < chunks:
            dact_chunk(c + 1)
        slope_chunk(c)
        if c > 0:
            dhid_chunk(c - 1)
    dhid_chunk(chunks - 1)
    save("dup")
    fetch_next("sl")
    ready("n1", "rs1")
    reuse("dbr")

    def norm_one(start, at, sums):
        n = n1_s[at, :].astype(F32)
        t = jnp.tanh((n * gain[0:1, :] + shift[0:1, :]) * i2)
        dy = dr[at, :] + acc[at, :] * (1.0 - t * t)
        e = dy * gain[0:1, :]
        mean_e = jnp.mean(e, -1, keepdims=True)
        mean_en = jnp.mean(e * n, -1, keepdims=True)
        d = (e - mean_e - n * mean_en) * rs1_s[at, 0:1]
        dr[at, :] = d
        dbr_s[at, :] = d.astype(BF16)
        return sums[0] + fold_rows(dy * n), sums[1] + fold_rows(dy), sums[2] + fold_rows(d)

    for name, v in zip(("gain0", "shift0", "out"), blocks(BLOCK, norm_one, (no_sum,) * 3)):
        put_small(name, v)
    save("dbr")
    fetch_next("n1", "rs1")
    ready("ctx")
    weight_ready(2)
    acc[...] = dot_nt(dbr_s[...], w_out[...])
    ready("qkv", "lse")
    reuse("dproj")

    one = jnp.ones((), BF16)
    zero = jnp.zeros((), BF16)
    head_scale = jnp.asarray(HEAD_DIM ** -0.5, BF16)
    src = lax.broadcasted_iota(jnp.int32, (PAIR, PAIR), 0) < HEAD_DIM
    dst = lax.broadcasted_iota(jnp.int32, (PAIR, PAIR), 1) < HEAD_DIM
    swap_sum = jnp.where(src == dst, 0.0, 1.0).astype(BF16)

    def prepare(p):
        slot = p % 2
        cols = slice(p * PAIR, (p + 1) * PAIR)

        def first_half(start, at, c):
            ctx = ctx_s[at, cols]
            t = jnp.tanh(ctx * i1)
            low = (acc[at, cols] * (1.0 - t * t)).astype(BF16)
            dctx_s[slot, at, :] = low
            hi, mid, _ = split3(low.astype(F32) * ctx)
            in_s[0, at, :] = hi
            in_s[1, at, :] = mid
            return c

        blocks(OPS, first_half)
        inner_s[...] = dot_nn(in_s[0], swap_sum) + dot_nn(in_s[1], swap_sum)

        def second_half(start, at, c):
            lane = lax.broadcasted_iota(jnp.int32, (OPS, PAIR), 1)
            lo = lane < HEAD_DIM
            spot = jnp.where(lo, lane, lane - HEAD_DIM)
            bias = jnp.broadcast_to(jnp.where(row_mask(start, OPS), 0.0, MASKED), (OPS, PAIR))
            q2 = qkv_s[at, p * PAIR : (p + 1) * PAIR] * head_scale
            k2 = qkv_s[at, width + p * PAIR : width + (p + 1) * PAIR]
            v2 = qkv_s[at, 2 * width + p * PAIR : 2 * width + (p + 1) * PAIR]
            do2 = dctx_s[slot, at, :]
            l_hi, l_mid, l_low = split3(pltpu.roll(lse_s[at, cols], HEAD_DIM, 1))
            extra_q = jnp.where(
                spot == 0, one, jnp.where(spot == 1, -l_hi, jnp.where(spot == 2, -l_mid, -l_low))
            )
            extra_k = jnp.where(spot == 0, bias, jnp.where(spot <= 3, 1.0, 0.0)).astype(BF16)
            d_hi, d_mid, d_low = split3(inner_s[at, :])
            extra_do = jnp.where(spot == 0, -d_hi, jnp.where(spot == 1, -d_mid, -d_low))
            extra_v = jnp.where(spot <= 2, 1.0, 0.0).astype(BF16)
            ops_s[slot, 0, at, :] = jnp.where(lo, q2, extra_q)
            ops_s[slot, 1, at, :] = jnp.where(lo, extra_q, q2)
            ops_s[slot, 2, at, :] = jnp.where(lo, k2, extra_k)
            ops_s[slot, 3, at, :] = jnp.where(lo, extra_k, k2)
            ops_s[slot, 4, at, :] = jnp.where(lo, v2, extra_v)
            ops_s[slot, 5, at, :] = jnp.where(lo, extra_v, v2)
            ops_s[slot, 6, at, :] = jnp.where(lo, do2, extra_do)
            ops_s[slot, 7, at, :] = jnp.where(lo, extra_do, do2)
            ops_s[slot, 8, at, :] = q2
            return c

        blocks(OPS, second_half)
        k_t[slot] = qkv_s[:, width + p * PAIR : width + (p + 1) * PAIR].T

    def scores(h):
        slot, side = h // 2 % 2, h % 2
        s_s[side] = dot_nt(ops_s[slot, 2 + side], ops_s[slot, side])
        g_s[side] = dot_nt(ops_s[slot, 4 + side], ops_s[slot, 6 + side])

    def soften(h):
        side = h % 2

        def body(start, at, c):
            prob = jnp.exp(s_s[side, at, :])
            p_s[side, at, :] = prob.astype(BF16)
            ds_s[side, at, :] = (prob * g_s[side, at, :]).astype(BF16)
            return c

        blocks(BLOCK, body)

    def collect(h):
        slot, side = h // 2 % 2, h % 2
        rows = slice(side * HEAD_DIM, (side + 1) * HEAD_DIM)
        gv_s[side] = dot_nn(p_s[side], dctx_s[slot])
        gk_s[side] = dot_nn(ds_s[side], ops_s[slot, 8])
        gq_s[rows, :] = dot_nn(k_t[slot, rows, :], ds_s[side])

    def settle(p):
        dproj_s[:, p * PAIR : (p + 1) * PAIR] = (gq_s[...].T * (HEAD_DIM ** -0.5)).astype(BF16)

        def body(start, at, c):
            lo = lax.broadcasted_iota(jnp.int32, (OPS, PAIR), 1) < HEAD_DIM
            k = jnp.where(lo, gk_s[0, at, :], gk_s[1, at, :])
            v = jnp.where(lo, gv_s[0, at, :], gv_s[1, at, :])
            dproj_s[at, width + p * PAIR : width + (p + 1) * PAIR] = k.astype(BF16)
            dproj_s[at, 2 * width + p * PAIR : 2 * width + (p + 1) * PAIR] = v.astype(BF16)
            return c

        blocks(OPS, body)

    heads = 2 * (width // PAIR)
    prepare(0)
    scores(0)
    for h in range(heads):
        if h + 1 < heads:
            if (h + 1) % 2 == 0:
                prepare((h + 1) // 2)
            scores(h + 1)
        soften(h)
        collect(h)
        if h % 2 == 1:
            settle(h // 2)
    save("dproj")
    fetch_next("ctx", "qkv", "lse")
    weight_ready(3)
    for j in range(3):
        cols = pl.ds(j * width, width)
        part = dot_nt(dproj_s[:, cols], w_qkv[:, cols])
        if j == 0:
            acc[...] = part
        else:
            acc[...] += part
    ready("x")

    def quant_in(start, at, sums):
        t = jnp.tanh(x_s[at, :].astype(F32) * i0)
        gout[r, at, :] = (dr[at, :] + acc[at, :] * (1.0 - t * t)).astype(BF16)
        return (
            sums[0] + fold_rows(dproj_s[at, 0:width].astype(F32)),
            sums[1] + fold_rows(dproj_s[at, 2 * width : 3 * width].astype(F32)),
        )

    sums = blocks(BLOCK, quant_in, (no_sum,) * 2)
    put_small("qkv", sums[0])
    put_small("qkv", sums[1], 2 * width)
    fetch_next("x")

    @pl.when(jnp.logical_not(first))
    def _():
        hop(r).start()

    @pl.when(first)
    def _():
        tok_copy(r).start()

    @pl.when(r == rows - 1)
    def _():
        @pl.when(last)
        def _():
            turn_left()

        for name in save_order:
            save_copy(name).wait()

        @pl.when(jnp.logical_not(first))
        def _():
            for i in range(row_count):
                hop(i).wait_send()

        @pl.when(first)
        def _():
            for i in range(row_count):
                tok_copy(i).wait()


def whole(a):
    return pl.BlockSpec(a.shape, lambda r, n=a.ndim: (0,) * n, pipeline_mode=pl.Buffered(1))


ANYWHERE = pl.BlockSpec(memory_space=pl.ANY)
SCALAR = pl.BlockSpec(memory_space=pltpu.SMEM)
VMEM_LIMIT = 60 * 1024 * 1024


def run_forward(count, tokens, lengths, scales, weights):
    w_qkv, b_qkv, w_out, b_out, w_up, b_up, w_down, b_down, gain, shift = weights
    rows, seq, width = tokens.shape
    ff = w_up.shape[1]
    big = lambda n, t: jax.ShapeDtypeStruct((rows, seq, n), t)
    saves = [
        (width, BF16), (3 * width, BF16), (width, F32), (width, F32), (width, BF16), (128, F32),
        (ff, BF16), (width, BF16), (128, F32),
    ]
    lefts = [(ff, BF16), (width, BF16), (width, BF16), (width, BF16)]
    heavy = (w_qkv, w_out, w_up, w_down)
    dense = (b_qkv, b_out, b_up, b_down, gain, shift)
    tok = rows * seq
    return pl.pallas_call(
        lambda *refs: fwd_kernel(count, *refs),
        grid=(rows,),
        in_specs=[SCALAR, SCALAR, ANYWHERE] + [ANYWHERE] * 4 + [whole(a) for a in dense],
        out_specs=[ANYWHERE] * 11 + [pl.BlockSpec((4, 8, 128), lambda r: (0, 0, 0))],
        out_shape=[big(n, t) for n, t in saves]
        + [
            big(ff + 3 * width, BF16),
            jax.ShapeDtypeStruct((rows, seq // count, width), BF16),
            jax.ShapeDtypeStruct((4, 8, 128), F32),
        ],
        scratch_shapes=[pltpu.VMEM(a.shape, a.dtype) for a in heavy]
        + [pltpu.SemaphoreType.DMA((4,))]
        + [pltpu.VMEM((rows, seq, width), BF16), pltpu.VMEM((rows, seq, width), BF16)]
        + [pltpu.VMEM((seq, n), t) for n, t in saves[1:] + lefts]
        + [
            pltpu.VMEM((seq, width), F32),
            pltpu.VMEM((seq, width), F32),
            pltpu.VMEM((2, seq, CHUNK), F32),
            pltpu.VMEM((2, 6, seq, PAIR), BF16),
            pltpu.VMEM((2, seq, seq), F32),
            pltpu.VMEM((2, seq, seq), BF16),
            pltpu.VMEM((2, seq, PAIR), F32),
            pltpu.VMEM((2, seq, PAIR), F32),
            pltpu.VMEM((seq, 128), F32),
            pltpu.SemaphoreType.DMA((13,)),
            pltpu.SemaphoreType.DMA((rows,)),
            pltpu.SemaphoreType.DMA((rows,)),
            pltpu.SemaphoreType.DMA((rows,)),
            pltpu.SemaphoreType.DMA((rows, count)),
            pltpu.SemaphoreType.DMA((rows,)),
        ],
        compiler_params=pltpu.CompilerParams(
            collective_id=0, has_side_effects=True, vmem_limit_bytes=VMEM_LIMIT,
            dimension_semantics=("arbitrary",),
        ),
        cost_estimate=pl.CostEstimate(
            flops=2 * tok * (4 * width * width + 2 * width * ff + 2 * seq * width),
            bytes_accessed=tok * 28000, transcendentals=tok * 3 * ff,
        ),
    )(lengths, scales, tokens, *heavy, *dense)


def run_backward(count, seeds, lengths, scales, weights, kept):
    w_qkv, b_qkv, w_out, b_out, w_up, b_up, w_down, b_down, gain, shift = weights
    *loads, left = kept
    rows, seq, width = seeds.shape
    ff = w_up.shape[1]
    big = lambda n, t: jax.ShapeDtypeStruct((rows, seq, n), t)
    saves = [(3 * width, BF16), (width, BF16), (ff, BF16), (width, BF16)]
    heavy = (w_qkv, w_out, w_up, w_down)
    dense = (gain, shift)
    tok = rows * seq
    small = 6 * width + ff + 3 * width
    return pl.pallas_call(
        lambda *refs: bwd_kernel(count, *refs),
        grid=(rows,),
        in_specs=[SCALAR, SCALAR, ANYWHERE] + [ANYWHERE] * 4 + [whole(a) for a in dense] + [ANYWHERE] * 10,
        out_specs=[ANYWHERE] * 6 + [pl.BlockSpec((8, small), lambda r: (0, 0))],
        out_shape=[big(n, t) for n, t in saves]
        + [
            big(width, BF16), jax.ShapeDtypeStruct((left.shape[2], rows * seq), BF16),
            jax.ShapeDtypeStruct((8, small), F32),
        ],
        scratch_shapes=[pltpu.VMEM(a.shape, a.dtype) for a in heavy]
        + [
            pltpu.SemaphoreType.DMA((4,)),
            pltpu.VMEM((2, seq, width), BF16),
            pltpu.VMEM((2, width, seq), BF16),
            pltpu.SemaphoreType.DMA((2,)),
            pltpu.SemaphoreType.DMA((2,)),
        ]
        + [pltpu.VMEM((rows, seq, width), BF16), pltpu.VMEM((rows, seq, width), BF16)]
        + [pltpu.VMEM(a.shape[1:], a.dtype) for a in loads]
        + [pltpu.VMEM((seq, n), t) for n, t in saves]
        + [
            pltpu.VMEM((2, seq, PAIR), BF16),
            pltpu.VMEM((seq, width), F32),
            pltpu.VMEM((seq, width), F32),
            pltpu.VMEM((2, seq, CHUNK), F32),
            pltpu.VMEM((2, 9, seq, PAIR), BF16),
            pltpu.VMEM((2, seq, seq), F32),
            pltpu.VMEM((2, seq, seq), F32),
            pltpu.VMEM((2, seq, seq), BF16),
            pltpu.VMEM((2, seq, seq), BF16),
            pltpu.VMEM((2, seq, PAIR), F32),
            pltpu.VMEM((2, seq, PAIR), F32),
            pltpu.VMEM((PAIR, seq), F32),
            pltpu.VMEM((2, PAIR, seq), BF16),
            pltpu.VMEM((2, seq, PAIR), BF16),
            pltpu.VMEM((seq, PAIR), F32),
            pltpu.SemaphoreType.DMA((9,)),
            pltpu.SemaphoreType.DMA((4,)),
            pltpu.SemaphoreType.DMA((rows,)),
            pltpu.SemaphoreType.DMA((rows,)),
            pltpu.SemaphoreType.DMA((rows,)),
            pltpu.SemaphoreType.DMA((rows,)),
        ],
        compiler_params=pltpu.CompilerParams(
            collective_id=1, has_side_effects=True, vmem_limit_bytes=VMEM_LIMIT,
            dimension_semantics=("arbitrary",),
        ),
        cost_estimate=pl.CostEstimate(
            flops=2 * tok * (4 * width * width + 2 * width * ff + 5 * seq * width),
            bytes_accessed=tok * 28000, transcendentals=tok * ff,
        ),
    )(lengths, scales, seeds, *heavy, *dense, left, *loads)


def ring_to_dp(pos, n):
    return jnp.where(pos < n // 2, 2 * pos, 2 * (n - pos) - 1)


def dp_to_ring(j, n):
    return jnp.where(j % 2 == 0, j // 2, n - 1 - j // 2)


def grad_kernel(count, n, *refs):
    (
        left, ddn, dup, dproj, dbr, small, g0,
        gq_o, go_o, gu_o, gd_o, small_o, gtok_o,
        slots_d, slots_u, slots_q, slots_s, wide_v, thin_v, ddn_v, dup_v, dpo_v,
        wide_sem, thin_sem, right_sem,
        send_d, recv_d, send_u, recv_u, send_q, recv_q, send_s, recv_s, tok_send, tok_recv,
    ) = refs
    width = ddn.shape[1]
    ff = dup.shape[1]
    shard, shard_ff = width // n, ff // n
    row_count, seq = g0.shape[0], g0.shape[1]
    piece = seq // count
    stage = lax.axis_index("pipe")
    me = lax.axis_index("dp")
    pos = dp_to_ring(me, n)
    first = stage == 0
    ahead = ring_to_dp(lax.rem(pos + 1, n), n)
    behind = ring_to_dp(lax.rem(pos + n - 1, n), n)
    target = (ahead, behind)

    def chunk(d, step):
        at = pos + 2 * n - 1 - step if d == 0 else pos + 1 + step
        return ring_to_dp(lax.rem(at, n), n)

    def wide_copy(d, step):
        rows = pl.ds(pl.multiple_of(chunk(d, step) * shard_ff, 16), shard_ff)
        return pltpu.make_async_copy(left.at[rows, :], wide_v.at[d], wide_sem.at[d])

    def thin_copy(k, d, step):
        rows = pl.ds(pl.multiple_of(ff + k * width + chunk(d, step) * shard, 16), shard)
        return pltpu.make_async_copy(left.at[rows, :], thin_v.at[k, d], thin_sem.at[k, d])

    rights = [
        (ddn, ddn_v), (dup, dup_v), (dproj, dpo_v.at[:, pl.ds(0, 3 * width)]),
        (dbr, dpo_v.at[:, pl.ds(3 * width, width)]),
    ]

    def right_copy(k):
        return pltpu.make_async_copy(rights[k][0], rights[k][1], right_sem.at[k])

    for d in range(2):
        wide_copy(d, 0).start()
    right_copy(0).start()
    right_copy(1).start()
    for d in range(2):
        thin_copy(0, d, 0).start()
    right_copy(2).start()
    right_copy(3).start()
    for d in range(2):
        thin_copy(1, d, 0).start()
        if d == 1:
            thin_copy(2, d, 0).start()

    barrier = pltpu.get_barrier_semaphore()
    for peer in target:
        pl.semaphore_signal(barrier, inc=1, device_id={"dp": peer}, device_id_type=LOGICAL)

    @pl.when(first)
    def _():
        pl.semaphore_wait(barrier, 1 + count)

    @pl.when(jnp.logical_not(first))
    def _():
        pl.semaphore_signal(barrier, inc=1, device_id={"pipe": jnp.int32(0)}, device_id_type=LOGICAL)
        pl.semaphore_wait(barrier, 2)

    def tok_part(i, p):
        return pltpu.make_async_remote_copy(
            src_ref=g0.at[i, pl.ds(p * piece, piece)], dst_ref=gtok_o.at[i],
            send_sem=tok_send.at[i, p], recv_sem=tok_recv.at[i],
            device_id={"pipe": jnp.int32(p)}, device_id_type=LOGICAL,
        )

    def tok_own(i):
        return pltpu.make_async_copy(g0.at[i, pl.ds(0, piece)], gtok_o.at[i], tok_send.at[i, 0])

    @pl.when(first)
    def _():
        for i in range(row_count):
            for p in range(1, count):
                tok_part(i, p).start()
            tok_own(i).start()

    def message(slots, send, recv, d, at):
        return pltpu.make_async_remote_copy(
            src_ref=slots.at[d, at], dst_ref=slots.at[d, jnp.minimum(at + 1, n - 1)],
            send_sem=send.at[d, at], recv_sem=recv.at[d, jnp.minimum(at + 1, n - 1)],
            device_id={"dp": target[d]}, device_id_type=LOGICAL,
        )

    def arrived(slots, send, recv, d, at):
        return pltpu.make_async_remote_copy(
            src_ref=slots.at[d, at], dst_ref=slots.at[d, at],
            send_sem=send.at[d, at], recv_sem=recv.at[d, at],
            device_id={"dp": target[d]}, device_id_type=LOGICAL,
        )

    def lane(slots, send, recv, d, step, mine, finish):
        @pl.when(step == 0)
        def _():
            slots[d, 0] = mine.astype(BF16)

        @pl.when(step > 0)
        def _():
            arrived(slots, send, recv, d, step).wait_recv()

            @pl.when(step < n - 1)
            def _():
                slots[d, step] = (slots[d, step].astype(F32) + mine).astype(BF16)

            @pl.when(step == n - 1)
            def _():
                finish(slots[d, step].astype(F32) + mine)

        @pl.when(step < n - 1)
        def _():
            message(slots, send, recv, d, step).start()

    def small_message(at):
        return pltpu.make_async_remote_copy(
            src_ref=slots_s.at[at], dst_ref=slots_s.at[jnp.minimum(at + 1, n - 1)],
            send_sem=send_s.at[at], recv_sem=recv_s.at[jnp.minimum(at + 1, n - 1)],
            device_id={"dp": target[0]}, device_id_type=LOGICAL,
        )

    def small_arrived(at):
        return pltpu.make_async_remote_copy(
            src_ref=slots_s.at[at], dst_ref=slots_s.at[at], send_sem=send_s.at[at],
            recv_sem=recv_s.at[at], device_id={"dp": target[0]}, device_id_type=LOGICAL,
        )

    sum_rows = lax.broadcasted_iota(jnp.int32, (16, 128), 0) < 9

    def small_step(step):
        mine = small[chunk(0, step)]

        @pl.when(step == 0)
        def _():
            slots_s[0] = mine

        @pl.when(step > 0)
        def _():
            small_arrived(step).wait_recv()
            got = slots_s[step]
            slots_s[step] = jnp.where(sum_rows, got + mine, jnp.maximum(got, mine))

        @pl.when(step < n - 1)
        def _():
            small_message(step).start()

        @pl.when(step == n - 1)
        def _():
            small_o[...] = slots_s[step]

    half, half_ff = width // 2, ff // 2

    def fetched(copy, step, *args):
        copy(*args, step).wait()

    def refill(copy, step, *args):
        @pl.when(step < n - 1)
        def _():
            copy(*args, step + 1).start()

    def right_ready(k, step):
        @pl.when(step == 0)
        def _():
            right_copy(k).wait()

    def turn(step, _):
        right_ready(0, step)
        for d in range(2):
            cols = slice(d * half, (d + 1) * half)
            fetched(wide_copy, step, d)
            mine = dot_nn(wide_v[d], ddn_v[:, cols])
            refill(wide_copy, step, d)

            def finish_down(total):
                gd_o[:, cols] = total

            lane(slots_d, send_d, recv_d, d, step, mine, finish_down)
        small_step(step)
        right_ready(1, step)
        for d in range(2):
            cols = slice(d * half_ff, (d + 1) * half_ff)
            fetched(thin_copy, step, 0, d)
            mine = dot_nn(thin_v[0, d], dup_v[:, cols])
            refill(thin_copy, step, 0, d)

            def finish_up(total):
                gu_o[:, cols] = total

            lane(slots_u, send_u, recv_u, d, step, mine, finish_up)
        right_ready(2, step)
        right_ready(3, step)
        fetched(thin_copy, step, 1, 0)
        mine = dot_nn(thin_v[1, 0], dpo_v[:, 0 : 2 * width])
        refill(thin_copy, step, 1, 0)

        def finish_ahead(total):
            gq_o[:, 0 : 2 * width] = total

        lane(slots_q, send_q, recv_q, 0, step, mine, finish_ahead)
        fetched(thin_copy, step, 1, 1)
        fetched(thin_copy, step, 2, 1)
        mine = jnp.concatenate(
            [
                dot_nn(thin_v[1, 1], dpo_v[:, 2 * width : 3 * width]),
                dot_nn(thin_v[2, 1], dpo_v[:, 3 * width : 4 * width]),
            ],
            1,
        )
        refill(thin_copy, step, 1, 1)
        refill(thin_copy, step, 2, 1)

        def finish_behind(total):
            gq_o[:, 2 * width : 3 * width] = total[:, 0:width]
            go_o[...] = total[:, width : 2 * width]

        lane(slots_q, send_q, recv_q, 1, step, mine, finish_behind)
        return 0

    lax.fori_loop(0, n, turn, 0)

    def drain(at, _):
        for d in range(2):
            message(slots_d, send_d, recv_d, d, at).wait_send()
            message(slots_u, send_u, recv_u, d, at).wait_send()
            message(slots_q, send_q, recv_q, d, at).wait_send()
        small_message(at).wait_send()
        return 0

    lax.fori_loop(0, n - 1, drain, 0)

    @pl.when(first)
    def _():
        for i in range(row_count):
            for p in range(1, count):
                tok_part(i, p).wait_send()
            tok_own(i).wait()

    @pl.when(jnp.logical_not(first))
    def _():
        for i in range(row_count):
            tok_part(i, 1).wait_recv()


def run_grads(count, n, left, dproj, dbr, dup, ddn, g0, small):
    rows, seq, width = g0.shape
    ff = dup.shape[2]
    flat = lambda a: a.reshape(rows * seq, a.shape[2])
    tok = rows * seq
    shard, shard_ff = width // n, ff // n
    ops = [left] + [flat(a) for a in (ddn, dup, dproj, dbr)]
    vmem = pl.BlockSpec(memory_space=pltpu.VMEM)
    sem = pltpu.SemaphoreType.DMA
    return pl.pallas_call(
        lambda *refs: grad_kernel(count, n, *refs),
        in_specs=[ANYWHERE] * 5 + [vmem, ANYWHERE],
        out_specs=[vmem] * 5 + [ANYWHERE],
        out_shape=[
            jax.ShapeDtypeStruct((shard, 3 * width), F32),
            jax.ShapeDtypeStruct((shard, width), F32),
            jax.ShapeDtypeStruct((shard, ff), F32),
            jax.ShapeDtypeStruct((shard_ff, width), F32),
            jax.ShapeDtypeStruct((16, 128), F32),
            jax.ShapeDtypeStruct((rows, seq // count, width), BF16),
        ],
        scratch_shapes=[
            pltpu.VMEM((2, n, shard_ff, width // 2), BF16),
            pltpu.VMEM((2, n, shard, ff // 2), BF16),
            pltpu.VMEM((2, n, shard, 2 * width), BF16),
            pltpu.VMEM((n, 16, 128), F32),
            pltpu.VMEM((2, shard_ff, tok), BF16),
            pltpu.VMEM((3, 2, shard, tok), BF16),
            pltpu.VMEM((tok, width), BF16),
            pltpu.VMEM((tok, ff), BF16),
            pltpu.VMEM((tok, 4 * width), BF16),
            sem((2,)), sem((3, 2)), sem((4,)),
            sem((2, n)), sem((2, n)), sem((2, n)), sem((2, n)), sem((2, n)), sem((2, n)),
            sem((n,)), sem((n,)), sem((rows, count)), sem((rows,)),
        ],
        compiler_params=pltpu.CompilerParams(
            collective_id=2, has_side_effects=True, vmem_limit_bytes=VMEM_LIMIT,
        ),
        cost_estimate=pl.CostEstimate(
            flops=2 * tok * (4 * width * width + 2 * width * ff), bytes_accessed=tok * 25000, transcendentals=0,
        ),
    )(*ops, small, g0)


def weight_grad(left, right):
    g = jnp.einsum("rsd,rse->de", left, right, preferred_element_type=F32).astype(BF16)
    return lax.psum_scatter(g, "dp", scatter_dimension=0, tiled=True).astype(F32)


def share_pieces(whole_rows, count, stage):
    piece = whole_rows.shape[1] // count
    mine = whole_rows[:, :piece]
    for p in range(1, count):
        got = lax.ppermute(whole_rows[:, p * piece : (p + 1) * piece], "pipe", [(0, p)])
        mine = jnp.where(stage == p, got, mine)
    return mine


def shards(
    tokens, lengths, ema_scales, w_qkv, bias_qv, w_out, bias_out, w_up, bias_up, w_down, bias_down,
    ln_gain, ln_bias, cotangent,
):
    count = lax.axis_size("pipe")
    n = lax.axis_size("dp")
    width = tokens.shape[2]
    ff = w_up.shape[2]
    b_qkv = jnp.concatenate([bias_qv[:, :width], jnp.zeros_like(bias_qv[:, :width]), bias_qv[:, width:]], 1)
    weights = (
        w_qkv[0], b_qkv, w_out[0], bias_out, w_up[0], bias_up, w_down[0], bias_down, ln_gain[0], ln_bias[0],
    )
    *kept, mixed, peaks = run_forward(count, tokens, lengths, ema_scales, weights)
    left = kept[-1]
    dproj, dbr, dup, ddn, g0, turned, small = run_backward(
        count, cotangent, lengths, ema_scales, weights, kept
    )
    sums = jnp.sum(small, 0)
    parts, at = [], 0
    for size in (width, width, width, width, width, width, ff, width, width, width):
        parts.append(sums[at : at + size])
        at += size
    parts[7:] = [jnp.concatenate([parts[7], parts[9]])]
    packed = jnp.concatenate([v.reshape(n, -1) for v in parts], 1)
    peak = jnp.max(peaks, (1, 2))
    sums_width = packed.shape[1]
    if n >= 4 and n % 2 == 0 and width // n % 16 == 0 and ff // n % 128 == 0 and sums_width == 9 * 128:
        top = jnp.broadcast_to(jnp.pad(peak, (0, 124))[None, None], (n, 7, 128))
        with_peak = jnp.concatenate([packed.reshape(n, 9, 128), top], 1)
        g_qkv, g_out, g_up, g_down, small_sum, grad_tokens = run_grads(
            count, n, turned, dproj, dbr, dup, ddn, g0, with_peak
        )
        mine = small_sum[:9].reshape(1, sums_width)
        batch_max = small_sum[9:10, :4]
    else:
        g_down = weight_grad(left[:, :, :ff], ddn)
        g_up = weight_grad(left[:, :, ff : ff + width], dup)
        g_qkv = weight_grad(left[:, :, ff + width : ff + 2 * width], dproj)
        g_out = weight_grad(left[:, :, ff + 2 * width :], dbr)
        mine = lax.psum_scatter(packed, "dp", scatter_dimension=0, tiled=True)
        batch_max = lax.pmax(peak, "dp")[None]
        grad_tokens = share_pieces(g0, count, lax.axis_index("pipe"))
    outs, at = [], 0
    for size in (width, width, width, width, width, width, ff, 2 * width):
        outs.append(mine[:, at : at + size // n])
        at += size // n
    gain0, gain1, shift0, shift1, s_out, s_down, s_up, s_qv = outs
    g_gain = jnp.stack([gain0, gain1], 1)
    g_shift = jnp.stack([shift0, shift1], 1)
    return (
        mixed, grad_tokens, g_qkv[None], s_qv, g_out[None], s_out, g_up[None], s_up, g_down[None], s_down,
        g_gain, g_shift, batch_max,
    )


def solution(mesh):
    return jax.shard_map(
        shards,
        mesh=mesh,
        in_specs=(
            P("dp", None, None), P("dp"), P("pipe", None), P("pipe", None, None), P("pipe", None),
            P("pipe", None, None), P("pipe", None), P("pipe", None, None), P("pipe", None),
            P("pipe", None, None), P("pipe", None), P("pipe", None, None), P("pipe", None, None),
            P("dp", None, None),
        ),
        out_specs=(
            P("dp", "pipe", None), P("dp", "pipe", None), P("pipe", "dp", None), P("pipe", "dp"),
            P("pipe", "dp", None), P("pipe", "dp"), P("pipe", "dp", None), P("pipe", "dp"),
            P("pipe", "dp", None), P("pipe", "dp"), P("pipe", None, "dp"), P("pipe", None, "dp"),
            P("pipe", None),
        ),
        check_vma=False,
    )
```

```python
import jax
import jax.numpy as jnp
from jax import lax
from jax.experimental import pallas as pl
from jax.experimental.pallas import tpu as pltpu
from jax.sharding import PartitionSpec as P

HEAD_DIM = 64
PAIR = 2 * HEAD_DIM
EPS = 1e-06
MASKED = -1000000000.0
CHUNK = 512
PIECE = 256
BLOCK = 16
OPS = 64
LOGICAL = pl.DeviceIdType.MESH
F32 = jnp.float32
BF16 = jnp.bfloat16

ERF_POLY = (
    0.7978823511659165,
    0.03634481045269742,
    -4.5110171354091134e-05,
    -5.02654469142584e-05,
    3.0867937984305273e-06,
    -6.60140005994544e-08,
)
ERF_CLAMP = 5.2 * 5.2
HALF_LOG2E = -0.7213475204444817
LOG2_DENSITY = -1.3257480647361593


def dot_nn(a, b):
    return jnp.dot(a, b, preferred_element_type=F32)


def dot_nt(a, b):
    return lax.dot_general(a, b, (((1,), (1,)), ((), ())), preferred_element_type=F32)


def dot_tn(a, b):
    return lax.dot_general(a, b, (((0,), (0,)), ((), ())), preferred_element_type=F32)


def fold_rows(v):
    return jnp.sum(v.reshape(v.shape[0] // 8, 8, v.shape[1]), 0)


def peak_rows(v):
    tiles = [v[:, i : i + 128] for i in range(0, v.shape[1], 128)]
    top = tiles[0]
    for tile in tiles[1:]:
        top = jnp.maximum(top, tile)
    return jnp.max(top.reshape(v.shape[0] // 8, 8, 128), 0)


def greet(stage, count):
    barrier = pltpu.get_barrier_semaphore()
    for step in range(1, count):
        peer = lax.rem(stage + step, count)
        pl.semaphore_signal(barrier, inc=1, device_id={"pipe": peer}, device_id_type=LOGICAL)
    pl.semaphore_wait(barrier, count - 1)


def activation(u, ceiling, inv_ceiling):
    square = u * u
    w = jnp.minimum(square, ERF_CLAMP)
    poly = w * ERF_POLY[-1] + ERF_POLY[-2]
    for coef in ERF_POLY[-3::-1]:
        poly = poly * w + coef
    t = jnp.tanh(u * poly)
    half = 0.5 * u
    act = half + half * t
    ratio = jnp.tanh(act * inv_ceiling)
    density = jnp.exp2(square * HALF_LOG2E + LOG2_DENSITY)
    slope = (1.0 - ratio * ratio) * ((0.5 + 0.5 * t) + u * density)
    return act, ceiling * ratio, slope


def fwd_kernel(count, *refs):
    (
        lens, scales, tokens, h_qkv, h_out, h_up, h_down, b_qkv, b_out, b_up, b_down, gain, shift,
        x_o, qkv_o, lse_o, ctx_o, n1_o, rs1_o, sl_o, n2_o, rs2_o, left_o,
        mixed_o, peaks_o,
        w_qkv, w_out, w_up, w_down, w_sem,
        xin, xout, qkv_s, lse_s, ctx_s, n1_s, rs1_s, sl_s, n2_s, rs2_s, aq_s, hq_s, xq_s, cq_s,
        acc, hid, up_s, ops_s, s_s, e_s, o_s, top_s, amax_s, lcol_s,
        save_sem, in_sem, send_sem, recv_sem, mix_send, mix_recv,
    ) = refs
    r = pl.program_id(0)
    rows = pl.num_programs(0)
    row_count = tokens.shape[0]
    seq, width = tokens.shape[1], tokens.shape[2]
    ff = w_up.shape[1]
    piece = seq // count
    stage = lax.axis_index("pipe")
    first = stage == 0
    last = stage == count - 1

    left = {"aq": (0, ff), "hq": (ff, width), "xq": (ff + width, width), "cq": (ff + 2 * width, width)}
    staged = {
        "x": (xin.at[r], x_o), "qkv": (qkv_s, qkv_o), "lse": (lse_s, lse_o), "ctx": (ctx_s, ctx_o),
        "n1": (n1_s, n1_o), "rs1": (rs1_s, rs1_o), "sl": (sl_s, sl_o), "n2": (n2_s, n2_o),
        "rs2": (rs2_s, rs2_o), "aq": (aq_s, left_o), "hq": (hq_s, left_o), "xq": (xq_s, left_o),
        "cq": (cq_s, left_o),
    }
    order = list(staged)
    fetches = [(h_qkv, w_qkv), (h_out, w_out), (h_up, w_up), (h_down, w_down)]

    def weight_copy(k):
        return pltpu.make_async_copy(fetches[k][0], fetches[k][1], w_sem.at[k])

    def weight_ready(k):
        @pl.when(r == 0)
        def _():
            weight_copy(k).wait()

    def save_copy(name):
        src, dst = staged[name]
        dst = dst.at[r]
        if name in left:
            dst = dst.at[:, pl.ds(*left[name])]
        return pltpu.make_async_copy(src, dst, save_sem.at[order.index(name)])

    def save(name):
        save_copy(name).start()

    def reuse(*names):
        @pl.when(r > 0)
        def _():
            for name in names:
                save_copy(name).wait()

    def token_copy(i):
        return pltpu.make_async_copy(tokens.at[i], xin.at[i], in_sem.at[i])

    def hop(i):
        return pltpu.make_async_remote_copy(
            src_ref=xout.at[i], dst_ref=xin.at[i], send_sem=send_sem.at[i], recv_sem=recv_sem.at[i],
            device_id={"pipe": lax.rem(stage + 1, count)}, device_id_type=LOGICAL,
        )

    def mix_part(i, p):
        return pltpu.make_async_remote_copy(
            src_ref=xout.at[i, pl.ds(p * piece, piece)], dst_ref=mixed_o.at[i],
            send_sem=mix_send.at[i, p], recv_sem=mix_recv.at[i],
            device_id={"pipe": jnp.int32(p)}, device_id_type=LOGICAL,
        )

    def mix_own(i):
        return pltpu.make_async_copy(
            xout.at[i, pl.ds((count - 1) * piece, piece)], mixed_o.at[i], mix_send.at[i, count - 1]
        )

    @pl.when(r == 0)
    def _():
        greet(stage, count)
        peaks_o[...] = jnp.zeros_like(peaks_o)
        for k in range(4):
            weight_copy(k).start()

        @pl.when(first)
        def _():
            for i in range(row_count):
                token_copy(i).start()

    @pl.when(first)
    def _():
        token_copy(r).wait()

    @pl.when(jnp.logical_not(first))
    def _():
        hop(r).wait_recv()

    length = lens[r]
    m0, m1, m2, m3 = scales[0, 0], scales[0, 1], scales[0, 2], scales[0, 3]
    i0, i1, i2, i3 = 1.0 / m0, 1.0 / m1, 1.0 / m2, 1.0 / m3

    def row_mask(start, size):
        return (start + lax.broadcasted_iota(jnp.int32, (size, 1), 0)) < length

    def blocks(size, body, init=0, begin=0, end=seq):
        step = lambda i, c: body(i * size, pl.ds(i * size, size), c)
        return lax.fori_loop(begin // size, end // size, step, init, unroll=True)

    def weave(dots, size, body, init=0):
        total, cut = seq // size, 0
        for k, dot in enumerate(dots):
            dot()
            begin, cut = cut, total * (k + 1) // len(dots)
            init = blocks(size, body, init, begin * size, cut * size)
        return init

    no_peak = jnp.zeros((8, 128), F32)

    @pl.when(r > 0)
    def _():
        save_copy("x").wait()

    save("x")
    reuse("xq", "qkv", "lse", "ctx", "cq")

    def quant_in(start, at, top):
        x = xin[r, at, :].astype(F32)
        xq_s[at, :] = (m0 * jnp.tanh(x * i0)).astype(BF16)
        return jnp.maximum(top, masked_peak(x, start))

    def masked_peak(v, start):
        return peak_rows(jnp.where(row_mask(start, v.shape[0]), jnp.abs(v), 0.0))

    peaks_o[0] = jnp.maximum(peaks_o[0], blocks(BLOCK, quant_in, no_peak))
    save("xq")

    weight_ready(0)
    for j in range(3):
        cols = pl.ds(j * width, width)
        proj = dot_nn(xq_s[...], w_qkv[:, cols]) + b_qkv[:, cols]
        qkv_s[:, cols] = proj.astype(BF16)
    save("qkv")

    one = jnp.ones((), BF16)
    zero = jnp.zeros((), BF16)
    head_scale = jnp.asarray(HEAD_DIM ** -0.5, BF16)

    def prepare(p):
        slot = p % 2

        def body(start, at, c):
            lane = lax.broadcasted_iota(jnp.int32, (OPS, PAIR), 1)
            lo = lane < HEAD_DIM
            spot = jnp.where(lo, lane, lane - HEAD_DIM)
            bias = jnp.where(row_mask(start, OPS), 0.0, MASKED)
            extra = jnp.where(spot == 0, jnp.broadcast_to(bias, (OPS, PAIR)), 0.0).astype(BF16)
            q2 = qkv_s[at, p * PAIR : (p + 1) * PAIR] * head_scale
            k2 = qkv_s[at, width + p * PAIR : width + (p + 1) * PAIR]
            v2 = qkv_s[at, 2 * width + p * PAIR : 2 * width + (p + 1) * PAIR]
            ops_s[slot, 0, at, :] = jnp.where(lo, q2, one)
            ops_s[slot, 1, at, :] = jnp.where(lo, one, q2)
            ops_s[slot, 2, at, :] = jnp.where(lo, k2, extra)
            ops_s[slot, 3, at, :] = jnp.where(lo, extra, k2)
            ops_s[slot, 4, at, :] = jnp.where(lo, v2, one)
            ops_s[slot, 5, at, :] = jnp.where(lo, one, v2)
            return c

        blocks(OPS, body)

    def scores(h):
        p, side = h // 2, h % 2

        def piece_of(k):
            def run():
                keys = pl.ds(k * PIECE, PIECE)
                s_s[side, :, keys] = dot_nt(ops_s[p % 2, side], ops_s[p % 2, 2 + side, keys, :])

            return run

        return [piece_of(k) for k in range(seq // PIECE)]

    def soften(h):
        side = h % 2

        def body(start, at, c):
            s = s_s[side, at, :]
            top = jnp.max(s, -1, keepdims=True)
            e_s[side, at, :] = jnp.exp(s - top).astype(BF16)
            top_s[h % 4, at, :] = jnp.broadcast_to(top, (BLOCK, PAIR))
            return c

        return body

    def collect(h):
        p, side = h // 2, h % 2

        def piece_of(k):
            def run():
                queries = pl.ds(k * PIECE, PIECE)
                o_s[side, queries, :] = dot_nn(e_s[side, queries, :], ops_s[p % 2, 4 + side])

            return run

        return [piece_of(k) for k in range(seq // PIECE)]

    def settle(p, peak):
        cols = slice(p * PAIR, (p + 1) * PAIR)

        def body(start, at, top):
            lo = lax.broadcasted_iota(jnp.int32, (OPS, PAIR), 1) < HEAD_DIM
            o_a, o_b = o_s[0, at, :], o_s[1, at, :]
            total = pltpu.roll(jnp.where(lo, o_b, o_a), HEAD_DIM, 1)
            c = jnp.where(lo, o_a, o_b) / total
            ctx_s[at, cols] = c
            lcol_s[at, :] = jnp.where(lo, top_s[2 * p % 4, at, :], top_s[(2 * p + 1) % 4, at, :]) + jnp.log(total)
            cq_s[at, cols] = (m1 * jnp.tanh(c * i1)).astype(BF16)
            return jnp.maximum(top, masked_peak(c, start))

        peak = blocks(OPS, body, peak)
        flipped = lcol_s[...].T
        lse_s[2 * p : 2 * p + 1, :] = flipped[0:1, :]
        lse_s[2 * p + 1 : 2 * p + 2, :] = flipped[HEAD_DIM : HEAD_DIM + 1, :]
        return peak

    heads = 2 * (width // PAIR)
    peak = no_peak
    prepare(0)
    for dot in scores(0):
        dot()
    for h in range(heads):
        dots = []
        if h + 1 < heads:
            if (h + 1) % 2 == 0:
                prepare((h + 1) // 2)
            dots += scores(h + 1)
        if h > 0:
            dots += collect(h - 1)
        weave(dots, BLOCK, soften(h))
        if h > 0 and h % 2 == 0:
            peak = settle(h // 2 - 1, peak)
    for dot in collect(heads - 1):
        dot()
    peak = settle(heads // 2 - 1, peak)
    peaks_o[1] = jnp.maximum(peaks_o[1], peak)
    save("lse")
    save("ctx")
    save("cq")
    weight_ready(1)
    reuse("n1", "rs1", "hq")

    def out_piece(k):
        def run():
            at = pl.ds(k * PIECE, PIECE)
            acc[at, :] = dot_nn(cq_s[at, :], w_out[...])

        return run

    def norm_one(start, at, top):
        s = xin[r, at, :].astype(F32) + (acc[at, :] + b_out[...])
        center = s - jnp.mean(s, -1, keepdims=True)
        rs = lax.rsqrt(jnp.mean(center * center, -1, keepdims=True) + EPS)
        n = center * rs
        h = n * gain[0:1, :] + shift[0:1, :]
        n1_s[at, :] = n.astype(BF16)
        rs1_s[at, :] = jnp.broadcast_to(rs, (BLOCK, 128))
        hid[at, :] = h
        hq_s[at, :] = (m2 * jnp.tanh(h * i2)).astype(BF16)
        return jnp.maximum(top, masked_peak(h, start))

    out_piece(0)()
    top = weave([out_piece(k) for k in range(1, seq // PIECE)] + [lambda: None], BLOCK, norm_one, no_peak)
    peaks_o[2] = jnp.maximum(peaks_o[2], top)
    save("n1")
    save("rs1")
    save("hq")
    reuse("aq", "sl")

    chunks = ff // CHUNK

    def up_chunk(c):
        def piece_of(k):
            def run():
                part = dot_nn(hq_s[...], w_up[:, pl.ds(c * CHUNK + k * PIECE, PIECE)])
                up_s[c % 2, :, pl.ds(k * PIECE, PIECE)] = part

            return run

        return [piece_of(k) for k in range(CHUNK // PIECE)]

    def act_chunk(c):
        cols = pl.ds(c * CHUNK, CHUNK)

        def body(start, at, carry):
            act, low, slope = activation(up_s[c % 2, at, :] + b_up[:, cols], m3, i3)
            aq_s[at, cols] = low.astype(BF16)
            sl_s[at, cols] = slope.astype(BF16)
            size = jnp.abs(act)
            top = size[:, 0:128]
            for i in range(128, CHUNK, 128):
                top = jnp.maximum(top, size[:, i : i + 128])
            amax_s[at, :] = top if c == 0 else jnp.maximum(amax_s[at, :], top)
            return carry

        return body

    def down_chunk(c):
        def piece_of(k):
            def run():
                cols = pl.ds(k * PIECE, PIECE)
                part = dot_nn(aq_s[:, pl.ds(c * CHUNK, CHUNK)], w_down[pl.ds(c * CHUNK, CHUNK), cols])
                acc[:, cols] = part if c == 0 else acc[:, cols] + part

            return run

        return [piece_of(k) for k in range(width // PIECE)]

    weight_ready(2)
    weight_ready(3)
    for dot in up_chunk(0):
        dot()
    for c in range(chunks):
        dots = []
        if c + 1 < chunks:
            dots += up_chunk(c + 1)
        if c > 0:
            dots += down_chunk(c - 1)
        weave(dots, BLOCK, act_chunk(c))
    peaks_o[3] = jnp.maximum(peaks_o[3], masked_peak(amax_s[...], 0))
    save("aq")
    save("sl")
    reuse("n2", "rs2")

    def norm_two(start, at, c):
        s = hid[at, :] + (acc[at, :] + b_down[...])
        center = s - jnp.mean(s, -1, keepdims=True)
        rs = lax.rsqrt(jnp.mean(center * center, -1, keepdims=True) + EPS)
        n = center * rs
        n2_s[at, :] = n.astype(BF16)
        rs2_s[at, :] = jnp.broadcast_to(rs, (BLOCK, 128))
        xout[r, at, :] = (n * gain[1:2, :] + shift[1:2, :]).astype(BF16)
        return c

    def down_last(k):
        def run():
            at, cols = pl.ds(k * PIECE, PIECE), pl.ds((chunks - 1) * CHUNK, CHUNK)
            acc[at, :] += dot_nn(aq_s[at, cols], w_down[cols, :])

        return run

    down_last(0)()
    weave([down_last(k) for k in range(1, seq // PIECE)] + [lambda: None], BLOCK, norm_two)
    save("n2")
    save("rs2")

    @pl.when(jnp.logical_not(last))
    def _():
        hop(r).start()

    @pl.when(last)
    def _():
        for p in range(count - 1):
            mix_part(r, p).start()
        mix_own(r).start()

    @pl.when(r == rows - 1)
    def _():
        for name in order:
            save_copy(name).wait()

        @pl.when(jnp.logical_not(last))
        def _():
            for i in range(row_count):
                hop(i).wait_send()
            for i in range(row_count):
                mix_part(i, 0).wait_recv()

        @pl.when(last)
        def _():
            for i in range(row_count):
                for p in range(count - 1):
                    mix_part(i, p).wait_send()
                mix_own(i).wait()


def bwd_kernel(count, *refs):
    (
        lens, scales, seeds, h_qkv, h_out, h_up, h_down, gain, shift, left_i,
        x_i, qkv_i, lse_i, ctx_i, n1_i, rs1_i, sl_i, n2_i, rs2_i,
        dproj_o, dbr_o, dup_o, ddn_o, gtok_o, left_o, small_o,
        w_qkv, w_out, w_up, w_down, w_sem, turn_in, turn_out, turn_in_sem, turn_out_sem,
        gin, gout, x_s, qkv_s, lse_s, ctx_s, n1_s, rs1_s, sl_s, n2_s, rs2_s,
        dproj_s, dbr_s, dup_s, ddn_s, dctx_s, acc, dr,
        up_s, ops_s, s_s, g_s, p_s, ds_s, gv_s, gk_s, gq_s, k_t, in_s, inner_s,
        load_sem, save_sem, in_sem, send_sem, recv_sem, tok_send,
    ) = refs
    r = pl.program_id(0)
    rows = pl.num_programs(0)
    row_count = seeds.shape[0]
    seq, width = seeds.shape[1], seeds.shape[2]
    ff = w_up.shape[1]
    piece = seq // count
    stage = lax.axis_index("pipe")
    first = stage == 0
    last = stage == count - 1

    loaded = {
        "n2": (n2_i, n2_s), "rs2": (rs2_i, rs2_s), "sl": (sl_i, sl_s), "n1": (n1_i, n1_s),
        "rs1": (rs1_i, rs1_s), "ctx": (ctx_i, ctx_s), "qkv": (qkv_i, qkv_s), "lse": (lse_i, lse_s),
        "x": (x_i, x_s),
    }
    load_order = list(loaded)
    staged = {
        "ddn": (ddn_s, ddn_o), "dup": (dup_s, dup_o), "dbr": (dbr_s, dbr_o), "dproj": (dproj_s, dproj_o),
    }
    save_order = list(staged)

    def load_copy(name, i):
        src, dst = loaded[name]
        return pltpu.make_async_copy(src.at[i], dst, load_sem.at[load_order.index(name)])

    def fetch_next(*names):
        @pl.when(r + 1 < rows)
        def _():
            for name in names:
                load_copy(name, r + 1).start()

    def ready(*names):
        for name in names:
            load_copy(name, r).wait()

    def save_copy(name):
        src, dst = staged[name]
        return pltpu.make_async_copy(src, dst.at[r], save_sem.at[save_order.index(name)])

    def save(name):
        save_copy(name).start()

    def reuse(*names):
        @pl.when(r > 0)
        def _():
            for name in names:
                save_copy(name).wait()

    def seed_copy(i):
        return pltpu.make_async_copy(seeds.at[i], gin.at[i], in_sem.at[i])

    def hop(i):
        return pltpu.make_async_remote_copy(
            src_ref=gout.at[i], dst_ref=gin.at[i], send_sem=send_sem.at[i], recv_sem=recv_sem.at[i],
            device_id={"pipe": lax.rem(stage + count - 1, count)}, device_id_type=LOGICAL,
        )

    def tok_copy(i):
        return pltpu.make_async_copy(gout.at[i], gtok_o.at[i], tok_send.at[i])

    fetches = [(h_down, w_down), (h_up, w_up), (h_out, w_out), (h_qkv, w_qkv)]

    def weight_copy(k):
        return pltpu.make_async_copy(fetches[k][0], fetches[k][1], w_sem.at[k])

    def weight_ready(k):
        @pl.when(r == 0)
        def _():
            weight_copy(k).wait()

    parts = left_i.shape[2] // width
    turns = row_count * parts

    def turn_load(i):
        cols = pl.ds(pl.multiple_of(i % parts * width, 128), width)
        return pltpu.make_async_copy(left_i.at[i // parts, :, cols], turn_in.at[i % 2], turn_in_sem.at[i % 2])

    def turn_store(i):
        rows_at = pl.ds(pl.multiple_of(i % parts * width, 128), width)
        cols = pl.ds(pl.multiple_of(i // parts * seq, 128), seq)
        return pltpu.make_async_copy(turn_out.at[i % 2], left_o.at[rows_at, cols], turn_out_sem.at[i % 2])

    def turn_left():
        turn_load(0).start()

        def body(i, c):
            @pl.when(i + 1 < turns)
            def _():
                turn_load(i + 1).start()

            turn_load(i).wait()

            @pl.when(i >= 2)
            def _():
                turn_store(i - 2).wait()

            turn_out[i % 2] = turn_in[i % 2].T
            turn_store(i).start()
            return c

        lax.fori_loop(0, turns, body, 0)
        turn_store(turns - 2).wait()
        turn_store(turns - 1).wait()

    @pl.when(r == 0)
    def _():
        greet(stage, count)
        small_o[...] = jnp.zeros_like(small_o)

        @pl.when(last)
        def _():
            for i in range(row_count):
                seed_copy(i).start()

        for name in ("n2", "rs2"):
            load_copy(name, 0).start()
        weight_copy(0).start()
        load_copy("sl", 0).start()
        for k in (1, 2, 3):
            weight_copy(k).start()
        for name in load_order[3:]:
            load_copy(name, 0).start()

        @pl.when(stage < count - 2)
        def _():
            turn_left()

    @pl.when(last)
    def _():
        seed_copy(r).wait()

    @pl.when(jnp.logical_not(last))
    def _():
        hop(r).wait_recv()

    length = lens[r]
    m0, m1, m2 = scales[0, 0], scales[0, 1], scales[0, 2]
    i0, i1, i2 = 1.0 / m0, 1.0 / m1, 1.0 / m2

    offsets = {}
    at_col = 0
    for name, size in (
        ("gain0", width), ("gain1", width), ("shift0", width), ("shift1", width),
        ("out", width), ("down", width), ("up", ff), ("qkv", 3 * width),
    ):
        offsets[name] = at_col
        at_col += size

    def blocks(size, body, init=0, begin=0, end=seq):
        step = lambda i, c: body(i * size, pl.ds(i * size, size), c)
        return lax.fori_loop(begin // size, end // size, step, init, unroll=True)

    def weave(dots, size, body, init=0):
        total, cut = seq // size, 0
        for k, dot in enumerate(dots):
            dot()
            begin, cut = cut, total * (k + 1) // len(dots)
            init = blocks(size, body, init, begin * size, cut * size)
        return init

    def row_mask(start, size):
        return (start + lax.broadcasted_iota(jnp.int32, (size, 1), 0)) < length

    def put_small(name, v, col=0):
        small_o[:, pl.ds(offsets[name] + col, v.shape[1])] += v

    no_sum = jnp.zeros((8, width), F32)

    ready("n2", "rs2")
    reuse("ddn")

    def norm_two(start, at, sums):
        dy = jnp.where(row_mask(start, BLOCK), gin[r, at, :].astype(F32), 0.0)
        n = n2_s[at, :].astype(F32)
        e = dy * gain[1:2, :]
        mean_e = jnp.mean(e, -1, keepdims=True)
        mean_en = jnp.mean(e * n, -1, keepdims=True)
        d = (e - mean_e - n * mean_en) * rs2_s[at, 0:1]
        dr[at, :] = d
        ddn_s[at, :] = d.astype(BF16)
        return sums[0] + fold_rows(dy * n), sums[1] + fold_rows(dy), sums[2] + fold_rows(d)

    for name, v in zip(("gain1", "shift1", "down"), blocks(BLOCK, norm_two, (no_sum,) * 3)):
        put_small(name, v)
    save("ddn")
    fetch_next("n2", "rs2")
    ready("sl")
    reuse("dup")

    chunks = ff // CHUNK

    def dact_chunk(c):
        def piece_of(k):
            def run():
                at = pl.ds(c * CHUNK + k * PIECE, PIECE)
                up_s[c % 2, :, pl.ds(k * PIECE, PIECE)] = dot_nt(ddn_s[...], w_down[at, :])

            return run

        return [piece_of(k) for k in range(CHUNK // PIECE)]

    def slope_chunk(c):
        cols = pl.ds(c * CHUNK, CHUNK)

        def body(start, at, total):
            d = up_s[c % 2, at, :] * sl_s[at, cols].astype(F32)
            dup_s[at, cols] = d.astype(BF16)
            return total + fold_rows(d)

        return body

    def dhid_chunk(c):
        cols = pl.ds(c * CHUNK, CHUNK)

        def piece_of(k):
            def run():
                at = pl.ds(k * PIECE, PIECE)
                part = dot_nt(dup_s[:, cols], w_up[at, cols])
                acc[:, at] = part if c == 0 else acc[:, at] + part

            return run

        return [piece_of(k) for k in range(width // PIECE)]

    weight_ready(0)
    weight_ready(1)
    for dot in dact_chunk(0):
        dot()
    for c in range(chunks):
        dots = []
        if c + 1 < chunks:
            dots += dact_chunk(c + 1)
        if c > 0:
            dots += dhid_chunk(c - 1)
        put_small("up", weave(dots, BLOCK, slope_chunk(c), jnp.zeros((8, CHUNK), F32)), c * CHUNK)
    save("dup")
    fetch_next("sl")
    ready("n1", "rs1")
    reuse("dbr")

    def norm_one(start, at, sums):
        n = n1_s[at, :].astype(F32)
        t = jnp.tanh((n * gain[0:1, :] + shift[0:1, :]) * i2)
        dy = dr[at, :] + acc[at, :] * (1.0 - t * t)
        e = dy * gain[0:1, :]
        mean_e = jnp.mean(e, -1, keepdims=True)
        mean_en = jnp.mean(e * n, -1, keepdims=True)
        d = (e - mean_e - n * mean_en) * rs1_s[at, 0:1]
        dr[at, :] = d
        dbr_s[at, :] = d.astype(BF16)
        return sums[0] + fold_rows(dy * n), sums[1] + fold_rows(dy), sums[2] + fold_rows(d)

    def dhid_last(k):
        def run():
            at, cols = pl.ds(k * PIECE, PIECE), pl.ds((chunks - 1) * CHUNK, CHUNK)
            acc[at, :] += dot_nt(dup_s[at, cols], w_up[:, cols])

        return run

    dhid_last(0)()
    dots = [dhid_last(k) for k in range(1, seq // PIECE)] + [lambda: None]
    for name, v in zip(("gain0", "shift0", "out"), weave(dots, BLOCK, norm_one, (no_sum,) * 3)):
        put_small(name, v)
    save("dbr")
    fetch_next("n1", "rs1")
    ready("ctx")
    weight_ready(2)
    for k in range(width // PIECE):
        acc[:, pl.ds(k * PIECE, PIECE)] = dot_nt(dbr_s[...], w_out[pl.ds(k * PIECE, PIECE), :])
    ready("qkv", "lse")
    reuse("dproj")

    one = jnp.ones((), BF16)
    zero = jnp.zeros((), BF16)
    head_scale = jnp.asarray(HEAD_DIM ** -0.5, BF16)
    pick = lax.broadcasted_iota(jnp.int32, (16, PAIR), 0)
    side_of = lax.broadcasted_iota(jnp.int32, (16, PAIR), 1) // HEAD_DIM
    sum_lanes = jnp.where(pick == side_of, 1.0, 0.0).astype(BF16)

    def prepare(p):
        slot = p % 2
        cols = slice(p * PAIR, (p + 1) * PAIR)

        def body(start, at, c):
            lane = lax.broadcasted_iota(jnp.int32, (OPS, PAIR), 1)
            lo = lane < HEAD_DIM
            spot = jnp.where(lo, lane, lane - HEAD_DIM)
            ctx = ctx_s[at, cols]
            t = jnp.tanh(ctx * i1)
            low = (acc[at, cols] * (1.0 - t * t)).astype(BF16)
            dctx_s[slot, at, :] = low
            inner = low.astype(F32) * ctx
            hi = inner.astype(BF16)
            in_s[0, at, :] = hi
            in_s[1, at, :] = (inner - hi.astype(F32)).astype(BF16)
            bias = jnp.where(row_mask(start, OPS), 0.0, MASKED)
            extra = jnp.where(spot == 0, jnp.broadcast_to(bias, (OPS, PAIR)), 0.0).astype(BF16)
            q2 = qkv_s[at, p * PAIR : (p + 1) * PAIR] * head_scale
            k2 = qkv_s[at, width + p * PAIR : width + (p + 1) * PAIR]
            v2 = qkv_s[at, 2 * width + p * PAIR : 2 * width + (p + 1) * PAIR]
            ops_s[slot, 0, at, :] = jnp.where(lo, q2, one)
            ops_s[slot, 1, at, :] = jnp.where(lo, one, q2)
            ops_s[slot, 2, at, :] = jnp.where(lo, k2, extra)
            ops_s[slot, 3, at, :] = jnp.where(lo, extra, k2)
            ops_s[slot, 4, at, :] = jnp.where(lo, v2, zero)
            ops_s[slot, 5, at, :] = jnp.where(lo, zero, v2)
            ops_s[slot, 6, at, :] = q2
            return c

        blocks(OPS, body)
        inner_s[slot] = dot_nt(sum_lanes, in_s[0]) + dot_nt(sum_lanes, in_s[1])
        k_t[slot] = qkv_s[:, width + p * PAIR : width + (p + 1) * PAIR].T

    def scores(h):
        slot, side = h // 2 % 2, h % 2

        def piece_of(k, out, left, right):
            def run():
                queries = pl.ds(k * PIECE, PIECE)
                out[side, :, queries] = dot_nt(left[...], right[queries, :])

            return run

        pairs = [
            (s_s, ops_s.at[slot, 2 + side], ops_s.at[slot, side]),
            (g_s, ops_s.at[slot, 4 + side], dctx_s.at[slot]),
        ]
        return [piece_of(k, *pair) for pair in pairs for k in range(seq // PIECE)]

    def soften(h):
        slot, side = h // 2 % 2, h % 2

        def body(start, at, c):
            prob = jnp.exp(s_s[side, at, :] - lse_s[h : h + 1, :])
            p_s[side, at, :] = prob.astype(BF16)
            ds_s[side, at, :] = (prob * (g_s[side, at, :] - inner_s[slot, side : side + 1, :])).astype(BF16)
            return c

        return body

    def collect(h):
        slot, side = h // 2 % 2, h % 2
        rows = slice(side * HEAD_DIM, (side + 1) * HEAD_DIM)

        def grad_v():
            gv_s[side] = dot_nn(p_s[side], dctx_s[slot])

        def grad_k():
            gk_s[side] = dot_nn(ds_s[side], ops_s[slot, 6])

        def grad_q(k):
            def run():
                queries = pl.ds(k * PIECE, PIECE)
                gq_s[rows, queries] = dot_nn(k_t[slot, rows, :], ds_s[side, :, queries])

            return run

        return [grad_v, grad_k] + [grad_q(k) for k in range(seq // PIECE)]

    def settle(p):
        dproj_s[:, p * PAIR : (p + 1) * PAIR] = (gq_s[...].T * (HEAD_DIM ** -0.5)).astype(BF16)

        def body(start, at, c):
            lo = lax.broadcasted_iota(jnp.int32, (OPS, PAIR), 1) < HEAD_DIM
            k = jnp.where(lo, gk_s[0, at, :], gk_s[1, at, :])
            v = jnp.where(lo, gv_s[0, at, :], gv_s[1, at, :])
            dproj_s[at, width + p * PAIR : width + (p + 1) * PAIR] = k.astype(BF16)
            dproj_s[at, 2 * width + p * PAIR : 2 * width + (p + 1) * PAIR] = v.astype(BF16)
            return c

        blocks(OPS, body)

    heads = 2 * (width // PAIR)
    prepare(0)
    for dot in scores(0):
        dot()
    for h in range(heads):
        dots = []
        if h + 1 < heads:
            if (h + 1) % 2 == 0:
                prepare((h + 1) // 2)
            dots += scores(h + 1)
        if h > 0:
            dots += collect(h - 1)
        weave(dots, BLOCK, soften(h))
        if h > 0 and h % 2 == 0:
            settle(h // 2 - 1)
    for dot in collect(heads - 1):
        dot()
    settle(heads // 2 - 1)
    save("dproj")
    fetch_next("ctx", "qkv", "lse")
    weight_ready(3)
    ready("x")

    def dx_piece(k):
        def run():
            at = pl.ds(k * PIECE, PIECE)
            acc[:, at] = dot_nt(dproj_s[...], w_qkv[at, :])

        return run

    def quant_in(k):
        cols = pl.ds(k * PIECE, PIECE)
        values = pl.ds(2 * width + k * PIECE, PIECE)

        def body(start, at, sums):
            t = jnp.tanh(x_s[at, cols].astype(F32) * i0)
            gout[r, at, cols] = (dr[at, cols] + acc[at, cols] * (1.0 - t * t)).astype(BF16)
            return (
                sums[0] + fold_rows(dproj_s[at, cols].astype(F32)),
                sums[1] + fold_rows(dproj_s[at, values].astype(F32)),
            )

        return body

    dx_piece(0)()
    pieces = width // PIECE
    for k in range(pieces):
        dots = [dx_piece(k + 1)] if k + 1 < pieces else [lambda: None]
        sums = weave(dots, BLOCK, quant_in(k), (jnp.zeros((8, PIECE), F32),) * 2)
        put_small("qkv", sums[0], k * PIECE)
        put_small("qkv", sums[1], 2 * width + k * PIECE)
    fetch_next("x")

    @pl.when(jnp.logical_not(first))
    def _():
        hop(r).start()

    @pl.when(first)
    def _():
        tok_copy(r).start()

    @pl.when(r == rows - 1)
    def _():
        @pl.when(stage >= count - 2)
        def _():
            turn_left()

        for name in save_order:
            save_copy(name).wait()

        @pl.when(jnp.logical_not(first))
        def _():
            for i in range(row_count):
                hop(i).wait_send()

        @pl.when(first)
        def _():
            for i in range(row_count):
                tok_copy(i).wait()


def whole(a):
    return pl.BlockSpec(a.shape, lambda r, n=a.ndim: (0,) * n, pipeline_mode=pl.Buffered(1))


ANYWHERE = pl.BlockSpec(memory_space=pl.ANY)
SCALAR = pl.BlockSpec(memory_space=pltpu.SMEM)
VMEM_LIMIT = 60 * 1024 * 1024


def run_forward(count, tokens, lengths, scales, weights):
    w_qkv, b_qkv, w_out, b_out, w_up, b_up, w_down, b_down, gain, shift = weights
    rows, seq, width = tokens.shape
    ff = w_up.shape[1]
    big = lambda n, t: jax.ShapeDtypeStruct((rows, seq, n), t)
    saves = [
        (width, BF16), (3 * width, BF16), (None, F32), (width, F32), (width, BF16), (128, F32),
        (ff, BF16), (width, BF16), (128, F32),
    ]
    heads = 16 * pl.cdiv(width // HEAD_DIM, 16)
    room = lambda n: (heads, seq) if n is None else (seq, n)
    lefts = [(ff, BF16), (width, BF16), (width, BF16), (width, BF16)]
    heavy = (w_qkv, w_out, w_up, w_down)
    dense = (b_qkv, b_out, b_up, b_down, gain, shift)
    tok = rows * seq
    return pl.pallas_call(
        lambda *refs: fwd_kernel(count, *refs),
        grid=(rows,),
        in_specs=[SCALAR, SCALAR, ANYWHERE] + [ANYWHERE] * 4 + [whole(a) for a in dense],
        out_specs=[ANYWHERE] * 11 + [pl.BlockSpec((4, 8, 128), lambda r: (0, 0, 0))],
        out_shape=[jax.ShapeDtypeStruct((rows, *room(n)), t) for n, t in saves]
        + [
            big(ff + 3 * width, BF16),
            jax.ShapeDtypeStruct((rows, seq // count, width), BF16),
            jax.ShapeDtypeStruct((4, 8, 128), F32),
        ],
        scratch_shapes=[pltpu.VMEM(a.shape, a.dtype) for a in heavy]
        + [pltpu.SemaphoreType.DMA((4,))]
        + [pltpu.VMEM((rows, seq, width), BF16), pltpu.VMEM((rows, seq, width), BF16)]
        + [pltpu.VMEM(room(n), t) for n, t in saves[1:] + lefts]
        + [
            pltpu.VMEM((seq, width), F32),
            pltpu.VMEM((seq, width), F32),
            pltpu.VMEM((2, seq, CHUNK), F32),
            pltpu.VMEM((2, 6, seq, PAIR), BF16),
            pltpu.VMEM((2, seq, seq), F32),
            pltpu.VMEM((2, seq, seq), BF16),
            pltpu.VMEM((2, seq, PAIR), F32),
            pltpu.VMEM((4, seq, PAIR), F32),
            pltpu.VMEM((seq, 128), F32),
            pltpu.VMEM((seq, PAIR), F32),
            pltpu.SemaphoreType.DMA((13,)),
            pltpu.SemaphoreType.DMA((rows,)),
            pltpu.SemaphoreType.DMA((rows,)),
            pltpu.SemaphoreType.DMA((rows,)),
            pltpu.SemaphoreType.DMA((rows, count)),
            pltpu.SemaphoreType.DMA((rows,)),
        ],
        compiler_params=pltpu.CompilerParams(
            collective_id=0, has_side_effects=True, vmem_limit_bytes=VMEM_LIMIT,
            dimension_semantics=("arbitrary",),
        ),
        cost_estimate=pl.CostEstimate(
            flops=2 * tok * (4 * width * width + 2 * width * ff + 2 * seq * width),
            bytes_accessed=tok * 28000, transcendentals=tok * 3 * ff,
        ),
    )(lengths, scales, tokens, *heavy, *dense)


def run_backward(count, seeds, lengths, scales, weights, kept):
    w_qkv, b_qkv, w_out, b_out, w_up, b_up, w_down, b_down, gain, shift = weights
    *loads, left = kept
    rows, seq, width = seeds.shape
    ff = w_up.shape[1]
    big = lambda n, t: jax.ShapeDtypeStruct((rows, seq, n), t)
    saves = [(3 * width, BF16), (width, BF16), (ff, BF16), (width, BF16)]
    heavy = (w_qkv, w_out, w_up, w_down)
    dense = (gain, shift)
    tok = rows * seq
    small = 6 * width + ff + 3 * width
    return pl.pallas_call(
        lambda *refs: bwd_kernel(count, *refs),
        grid=(rows,),
        in_specs=[SCALAR, SCALAR, ANYWHERE] + [ANYWHERE] * 4 + [whole(a) for a in dense] + [ANYWHERE] * 10,
        out_specs=[ANYWHERE] * 6 + [pl.BlockSpec((8, small), lambda r: (0, 0))],
        out_shape=[big(n, t) for n, t in saves]
        + [
            big(width, BF16), jax.ShapeDtypeStruct((left.shape[2], rows * seq), BF16),
            jax.ShapeDtypeStruct((8, small), F32),
        ],
        scratch_shapes=[pltpu.VMEM(a.shape, a.dtype) for a in heavy]
        + [
            pltpu.SemaphoreType.DMA((4,)),
            pltpu.VMEM((2, seq, width), BF16),
            pltpu.VMEM((2, width, seq), BF16),
            pltpu.SemaphoreType.DMA((2,)),
            pltpu.SemaphoreType.DMA((2,)),
        ]
        + [pltpu.VMEM((rows, seq, width), BF16), pltpu.VMEM((rows, seq, width), BF16)]
        + [pltpu.VMEM(a.shape[1:], a.dtype) for a in loads]
        + [pltpu.VMEM((seq, n), t) for n, t in saves]
        + [
            pltpu.VMEM((2, seq, PAIR), BF16),
            pltpu.VMEM((seq, width), F32),
            pltpu.VMEM((seq, width), F32),
            pltpu.VMEM((2, seq, CHUNK), F32),
            pltpu.VMEM((2, 7, seq, PAIR), BF16),
            pltpu.VMEM((2, seq, seq), F32),
            pltpu.VMEM((2, seq, seq), F32),
            pltpu.VMEM((2, seq, seq), BF16),
            pltpu.VMEM((2, seq, seq), BF16),
            pltpu.VMEM((2, seq, PAIR), F32),
            pltpu.VMEM((2, seq, PAIR), F32),
            pltpu.VMEM((PAIR, seq), F32),
            pltpu.VMEM((2, PAIR, seq), BF16),
            pltpu.VMEM((2, seq, PAIR), BF16),
            pltpu.VMEM((2, 16, seq), F32),
            pltpu.SemaphoreType.DMA((9,)),
            pltpu.SemaphoreType.DMA((4,)),
            pltpu.SemaphoreType.DMA((rows,)),
            pltpu.SemaphoreType.DMA((rows,)),
            pltpu.SemaphoreType.DMA((rows,)),
            pltpu.SemaphoreType.DMA((rows,)),
        ],
        compiler_params=pltpu.CompilerParams(
            collective_id=1, has_side_effects=True, vmem_limit_bytes=VMEM_LIMIT,
            dimension_semantics=("arbitrary",),
        ),
        cost_estimate=pl.CostEstimate(
            flops=2 * tok * (4 * width * width + 2 * width * ff + 5 * seq * width),
            bytes_accessed=tok * 28000, transcendentals=tok * ff,
        ),
    )(lengths, scales, seeds, *heavy, *dense, left, *loads)


def ring_to_dp(pos, n):
    return jnp.where(pos < n // 2, 2 * pos, 2 * (n - pos) - 1)


def dp_to_ring(j, n):
    return jnp.where(j % 2 == 0, j // 2, n - 1 - j // 2)


def grad_kernel(count, n, *refs):
    (
        left, ddn, dup, dproj, dbr, small, g0,
        gq_o, go_o, gu_o, gd_o, small_o, gtok_o,
        slots_d, slots_u, slots_q, slots_s, wide_v, thin_v, ddn_v, dup_v, dpo_v,
        wide_sem, thin_sem, right_sem,
        send_d, recv_d, send_u, recv_u, send_q, recv_q, send_s, recv_s, tok_send, tok_recv,
    ) = refs
    width = ddn.shape[1]
    ff = dup.shape[1]
    shard, shard_ff = width // n, ff // n
    row_count, seq = g0.shape[0], g0.shape[1]
    piece = seq // count
    stage = lax.axis_index("pipe")
    me = lax.axis_index("dp")
    pos = dp_to_ring(me, n)
    first = stage == 0
    ahead = ring_to_dp(lax.rem(pos + 1, n), n)
    behind = ring_to_dp(lax.rem(pos + n - 1, n), n)
    target = (ahead, behind)

    def chunk(d, step):
        at = pos + 2 * n - 1 - step if d == 0 else pos + 1 + step
        return ring_to_dp(lax.rem(at, n), n)

    def wide_copy(d, step):
        rows = pl.ds(pl.multiple_of(chunk(d, step) * shard_ff, 16), shard_ff)
        return pltpu.make_async_copy(left.at[rows, :], wide_v.at[d], wide_sem.at[d])

    def thin_copy(k, d, step):
        rows = pl.ds(pl.multiple_of(ff + k * width + chunk(d, step) * shard, 16), shard)
        return pltpu.make_async_copy(left.at[rows, :], thin_v.at[k, d], thin_sem.at[k, d])

    rights = [
        (ddn, ddn_v), (dup, dup_v), (dproj, dpo_v.at[:, pl.ds(0, 3 * width)]),
        (dbr, dpo_v.at[:, pl.ds(3 * width, width)]),
    ]

    def right_copy(k):
        return pltpu.make_async_copy(rights[k][0], rights[k][1], right_sem.at[k])

    for d in range(2):
        wide_copy(d, 0).start()
    right_copy(0).start()
    right_copy(1).start()
    for d in range(2):
        thin_copy(0, d, 0).start()
    right_copy(2).start()
    right_copy(3).start()
    for d in range(2):
        thin_copy(1, d, 0).start()
        if d == 1:
            thin_copy(2, d, 0).start()

    barrier = pltpu.get_barrier_semaphore()
    for peer in target:
        pl.semaphore_signal(barrier, inc=1, device_id={"dp": peer}, device_id_type=LOGICAL)

    @pl.when(first)
    def _():
        pl.semaphore_wait(barrier, 1 + count)

    @pl.when(jnp.logical_not(first))
    def _():
        pl.semaphore_signal(barrier, inc=1, device_id={"pipe": jnp.int32(0)}, device_id_type=LOGICAL)
        pl.semaphore_wait(barrier, 2)

    def tok_part(i, p):
        return pltpu.make_async_remote_copy(
            src_ref=g0.at[i, pl.ds(p * piece, piece)], dst_ref=gtok_o.at[i],
            send_sem=tok_send.at[i, p], recv_sem=tok_recv.at[i],
            device_id={"pipe": jnp.int32(p)}, device_id_type=LOGICAL,
        )

    def tok_own(i):
        return pltpu.make_async_copy(g0.at[i, pl.ds(0, piece)], gtok_o.at[i], tok_send.at[i, 0])

    @pl.when(first)
    def _():
        for i in range(row_count):
            for p in range(1, count):
                tok_part(i, p).start()
            tok_own(i).start()

    def message(slots, send, recv, d, at):
        return pltpu.make_async_remote_copy(
            src_ref=slots.at[d, at], dst_ref=slots.at[d, jnp.minimum(at + 1, n - 1)],
            send_sem=send.at[d, at], recv_sem=recv.at[d, jnp.minimum(at + 1, n - 1)],
            device_id={"dp": target[d]}, device_id_type=LOGICAL,
        )

    def arrived(slots, send, recv, d, at):
        return pltpu.make_async_remote_copy(
            src_ref=slots.at[d, at], dst_ref=slots.at[d, at],
            send_sem=send.at[d, at], recv_sem=recv.at[d, at],
            device_id={"dp": target[d]}, device_id_type=LOGICAL,
        )

    def lane(slots, send, recv, d, step, mine, finish):
        @pl.when(step == 0)
        def _():
            slots[d, 0] = mine.astype(BF16)

        @pl.when(step > 0)
        def _():
            arrived(slots, send, recv, d, step).wait_recv()

            @pl.when(step < n - 1)
            def _():
                slots[d, step] = (slots[d, step].astype(F32) + mine).astype(BF16)

            @pl.when(step == n - 1)
            def _():
                finish(slots[d, step].astype(F32) + mine)

        @pl.when(step < n - 1)
        def _():
            message(slots, send, recv, d, step).start()

    def small_message(at):
        return pltpu.make_async_remote_copy(
            src_ref=slots_s.at[at], dst_ref=slots_s.at[jnp.minimum(at + 1, n - 1)],
            send_sem=send_s.at[at], recv_sem=recv_s.at[jnp.minimum(at + 1, n - 1)],
            device_id={"dp": target[0]}, device_id_type=LOGICAL,
        )

    def small_arrived(at):
        return pltpu.make_async_remote_copy(
            src_ref=slots_s.at[at], dst_ref=slots_s.at[at], send_sem=send_s.at[at],
            recv_sem=recv_s.at[at], device_id={"dp": target[0]}, device_id_type=LOGICAL,
        )

    sum_rows = lax.broadcasted_iota(jnp.int32, (16, 128), 0) < 9

    def small_step(step):
        mine = small[chunk(0, step)]

        @pl.when(step == 0)
        def _():
            slots_s[0] = mine

        @pl.when(step > 0)
        def _():
            small_arrived(step).wait_recv()
            got = slots_s[step]
            slots_s[step] = jnp.where(sum_rows, got + mine, jnp.maximum(got, mine))

        @pl.when(step < n - 1)
        def _():
            small_message(step).start()

        @pl.when(step == n - 1)
        def _():
            small_o[...] = slots_s[step]

    half, half_ff = width // 2, ff // 2

    def fetched(copy, step, *args):
        copy(*args, step).wait()

    def refill(copy, step, *args):
        @pl.when(step < n - 1)
        def _():
            copy(*args, step + 1).start()

    def right_ready(k, step):
        @pl.when(step == 0)
        def _():
            right_copy(k).wait()

    def turn(step, _):
        right_ready(0, step)
        for d in range(2):
            cols = slice(d * half, (d + 1) * half)
            fetched(wide_copy, step, d)
            mine = dot_nn(wide_v[d], ddn_v[:, cols])
            refill(wide_copy, step, d)

            def finish_down(total):
                gd_o[:, cols] = total

            lane(slots_d, send_d, recv_d, d, step, mine, finish_down)
        small_step(step)
        right_ready(1, step)
        for d in range(2):
            cols = slice(d * half_ff, (d + 1) * half_ff)
            fetched(thin_copy, step, 0, d)
            mine = dot_nn(thin_v[0, d], dup_v[:, cols])
            refill(thin_copy, step, 0, d)

            def finish_up(total):
                gu_o[:, cols] = total

            lane(slots_u, send_u, recv_u, d, step, mine, finish_up)
        right_ready(2, step)
        right_ready(3, step)
        fetched(thin_copy, step, 1, 0)
        mine = dot_nn(thin_v[1, 0], dpo_v[:, 0 : 2 * width])
        refill(thin_copy, step, 1, 0)

        def finish_ahead(total):
            gq_o[:, 0 : 2 * width] = total

        lane(slots_q, send_q, recv_q, 0, step, mine, finish_ahead)
        fetched(thin_copy, step, 1, 1)
        fetched(thin_copy, step, 2, 1)
        mine = jnp.concatenate(
            [
                dot_nn(thin_v[1, 1], dpo_v[:, 2 * width : 3 * width]),
                dot_nn(thin_v[2, 1], dpo_v[:, 3 * width : 4 * width]),
            ],
            1,
        )
        refill(thin_copy, step, 1, 1)
        refill(thin_copy, step, 2, 1)

        def finish_behind(total):
            gq_o[:, 2 * width : 3 * width] = total[:, 0:width]
            go_o[...] = total[:, width : 2 * width]

        lane(slots_q, send_q, recv_q, 1, step, mine, finish_behind)
        return 0

    lax.fori_loop(0, n, turn, 0)

    def drain(at, _):
        for d in range(2):
            message(slots_d, send_d, recv_d, d, at).wait_send()
            message(slots_u, send_u, recv_u, d, at).wait_send()
            message(slots_q, send_q, recv_q, d, at).wait_send()
        small_message(at).wait_send()
        return 0

    lax.fori_loop(0, n - 1, drain, 0)

    @pl.when(first)
    def _():
        for i in range(row_count):
            for p in range(1, count):
                tok_part(i, p).wait_send()
            tok_own(i).wait()

    @pl.when(jnp.logical_not(first))
    def _():
        for i in range(row_count):
            tok_part(i, 1).wait_recv()


def run_grads(count, n, left, dproj, dbr, dup, ddn, g0, small):
    rows, seq, width = g0.shape
    ff = dup.shape[2]
    flat = lambda a: a.reshape(rows * seq, a.shape[2])
    tok = rows * seq
    shard, shard_ff = width // n, ff // n
    ops = [left] + [flat(a) for a in (ddn, dup, dproj, dbr)]
    vmem = pl.BlockSpec(memory_space=pltpu.VMEM)
    sem = pltpu.SemaphoreType.DMA
    return pl.pallas_call(
        lambda *refs: grad_kernel(count, n, *refs),
        in_specs=[ANYWHERE] * 5 + [vmem, ANYWHERE],
        out_specs=[vmem] * 5 + [ANYWHERE],
        out_shape=[
            jax.ShapeDtypeStruct((shard, 3 * width), F32),
            jax.ShapeDtypeStruct((shard, width), F32),
            jax.ShapeDtypeStruct((shard, ff), F32),
            jax.ShapeDtypeStruct((shard_ff, width), F32),
            jax.ShapeDtypeStruct((16, 128), F32),
            jax.ShapeDtypeStruct((rows, seq // count, width), BF16),
        ],
        scratch_shapes=[
            pltpu.VMEM((2, n, shard_ff, width // 2), BF16),
            pltpu.VMEM((2, n, shard, ff // 2), BF16),
            pltpu.VMEM((2, n, shard, 2 * width), BF16),
            pltpu.VMEM((n, 16, 128), F32),
            pltpu.VMEM((2, shard_ff, tok), BF16),
            pltpu.VMEM((3, 2, shard, tok), BF16),
            pltpu.VMEM((tok, width), BF16),
            pltpu.VMEM((tok, ff), BF16),
            pltpu.VMEM((tok, 4 * width), BF16),
            sem((2,)), sem((3, 2)), sem((4,)),
            sem((2, n)), sem((2, n)), sem((2, n)), sem((2, n)), sem((2, n)), sem((2, n)),
            sem((n,)), sem((n,)), sem((rows, count)), sem((rows,)),
        ],
        compiler_params=pltpu.CompilerParams(
            collective_id=2, has_side_effects=True, vmem_limit_bytes=VMEM_LIMIT,
        ),
        cost_estimate=pl.CostEstimate(
            flops=2 * tok * (4 * width * width + 2 * width * ff), bytes_accessed=tok * 25000, transcendentals=0,
        ),
    )(*ops, small, g0)


def weight_grad(left, right):
    g = jnp.einsum("rsd,rse->de", left, right, preferred_element_type=F32).astype(BF16)
    return lax.psum_scatter(g, "dp", scatter_dimension=0, tiled=True).astype(F32)


def share_pieces(whole_rows, count, stage):
    piece = whole_rows.shape[1] // count
    mine = whole_rows[:, :piece]
    for p in range(1, count):
        got = lax.ppermute(whole_rows[:, p * piece : (p + 1) * piece], "pipe", [(0, p)])
        mine = jnp.where(stage == p, got, mine)
    return mine


def shards(
    tokens, lengths, ema_scales, w_qkv, bias_qv, w_out, bias_out, w_up, bias_up, w_down, bias_down,
    ln_gain, ln_bias, cotangent,
):
    count = lax.axis_size("pipe")
    n = lax.axis_size("dp")
    width = tokens.shape[2]
    ff = w_up.shape[2]
    b_qkv = jnp.concatenate([bias_qv[:, :width], jnp.zeros_like(bias_qv[:, :width]), bias_qv[:, width:]], 1)
    weights = (
        w_qkv[0], b_qkv, w_out[0], bias_out, w_up[0], bias_up, w_down[0], bias_down, ln_gain[0], ln_bias[0],
    )
    *kept, mixed, peaks = run_forward(count, tokens, lengths, ema_scales, weights)
    left = kept[-1]
    dproj, dbr, dup, ddn, g0, turned, small = run_backward(
        count, cotangent, lengths, ema_scales, weights, kept
    )
    sums = jnp.sum(small, 0)
    parts, at = [], 0
    for size in (width, width, width, width, width, width, ff, width, width, width):
        parts.append(sums[at : at + size])
        at += size
    parts[7:] = [jnp.concatenate([parts[7], parts[9]])]
    packed = jnp.concatenate([v.reshape(n, -1) for v in parts], 1)
    peak = jnp.max(peaks, (1, 2))
    sums_width = packed.shape[1]
    if n >= 4 and n % 2 == 0 and width // n % 16 == 0 and ff // n % 128 == 0 and sums_width == 9 * 128:
        top = jnp.broadcast_to(jnp.pad(peak, (0, 124))[None, None], (n, 7, 128))
        with_peak = jnp.concatenate([packed.reshape(n, 9, 128), top], 1)
        g_qkv, g_out, g_up, g_down, small_sum, grad_tokens = run_grads(
            count, n, turned, dproj, dbr, dup, ddn, g0, with_peak
        )
        mine = small_sum[:9].reshape(1, sums_width)
        batch_max = small_sum[9:10, :4]
    else:
        g_down = weight_grad(left[:, :, :ff], ddn)
        g_up = weight_grad(left[:, :, ff : ff + width], dup)
        g_qkv = weight_grad(left[:, :, ff + width : ff + 2 * width], dproj)
        g_out = weight_grad(left[:, :, ff + 2 * width :], dbr)
        mine = lax.psum_scatter(packed, "dp", scatter_dimension=0, tiled=True)
        batch_max = lax.pmax(peak, "dp")[None]
        grad_tokens = share_pieces(g0, count, lax.axis_index("pipe"))
    outs, at = [], 0
    for size in (width, width, width, width, width, width, ff, 2 * width):
        outs.append(mine[:, at : at + size // n])
        at += size // n
    gain0, gain1, shift0, shift1, s_out, s_down, s_up, s_qv = outs
    g_gain = jnp.stack([gain0, gain1], 1)
    g_shift = jnp.stack([shift0, shift1], 1)
    return (
        mixed, grad_tokens, g_qkv[None], s_qv, g_out[None], s_out, g_up[None], s_up, g_down[None], s_down,
        g_gain, g_shift, batch_max,
    )


def solution(mesh):
    return jax.shard_map(
        shards,
        mesh=mesh,
        in_specs=(
            P("dp", None, None), P("dp"), P("pipe", None), P("pipe", None, None), P("pipe", None),
            P("pipe", None, None), P("pipe", None), P("pipe", None, None), P("pipe", None),
            P("pipe", None, None), P("pipe", None), P("pipe", None, None), P("pipe", None, None),
            P("dp", None, None),
        ),
        out_specs=(
            P("dp", "pipe", None), P("dp", "pipe", None), P("pipe", "dp", None), P("pipe", "dp"),
            P("pipe", "dp", None), P("pipe", "dp"), P("pipe", "dp", None), P("pipe", "dp"),
            P("pipe", "dp", None), P("pipe", "dp"), P("pipe", None, "dp"), P("pipe", None, "dp"),
            P("pipe", None),
        ),
        check_vma=False,
    )
```

```python
import jax
import jax.numpy as jnp
from jax import lax
from jax.experimental import pallas as pl
from jax.experimental.pallas import tpu as pltpu
from jax.sharding import PartitionSpec as P

HEAD_DIM = 64
PAIR = 2 * HEAD_DIM
EPS = 1e-06
MASKED = -1000000000.0
CHUNK = 512
PIECE = 256
BLOCK = 16
OPS = 64
LOGICAL = pl.DeviceIdType.MESH
F32 = jnp.float32
BF16 = jnp.bfloat16

ERF_POLY = (
    0.7978823511659165,
    0.03634481045269742,
    -4.5110171354091134e-05,
    -5.02654469142584e-05,
    3.0867937984305273e-06,
    -6.60140005994544e-08,
)
ERF_CLAMP = 5.2 * 5.2
HALF_LOG2E = -0.7213475204444817
LOG2_DENSITY = -1.3257480647361593


def dot_nn(a, b):
    return jnp.dot(a, b, preferred_element_type=F32)


def dot_nt(a, b):
    return lax.dot_general(a, b, (((1,), (1,)), ((), ())), preferred_element_type=F32)


def dot_tn(a, b):
    return lax.dot_general(a, b, (((0,), (0,)), ((), ())), preferred_element_type=F32)


def fold_rows(v):
    return jnp.sum(v.reshape(v.shape[0] // 8, 8, v.shape[1]), 0)


def peak_rows(v):
    tiles = [v[:, i : i + 128] for i in range(0, v.shape[1], 128)]
    top = tiles[0]
    for tile in tiles[1:]:
        top = jnp.maximum(top, tile)
    return jnp.max(top.reshape(v.shape[0] // 8, 8, 128), 0)


def greet(stage, count):
    barrier = pltpu.get_barrier_semaphore()
    for step in range(1, count):
        peer = lax.rem(stage + step, count)
        pl.semaphore_signal(barrier, inc=1, device_id={"pipe": peer}, device_id_type=LOGICAL)
    pl.semaphore_wait(barrier, count - 1)


def activation(u, ceiling, inv_ceiling):
    square = u * u
    w = jnp.minimum(square, ERF_CLAMP)
    poly = w * ERF_POLY[-1] + ERF_POLY[-2]
    for coef in ERF_POLY[-3::-1]:
        poly = poly * w + coef
    t = jnp.tanh(u * poly)
    half = 0.5 * u
    act = half + half * t
    ratio = jnp.tanh(act * inv_ceiling)
    density = jnp.exp2(square * HALF_LOG2E + LOG2_DENSITY)
    slope = (1.0 - ratio * ratio) * ((0.5 + 0.5 * t) + u * density)
    return act, ceiling * ratio, slope


def fwd_kernel(count, *refs):
    (
        lens, vec_i, tokens, h_qkv, h_out, h_up, h_down,
        x_o, qkv_o, lse_o, ctx_o, n1_o, rs1_o, sl_o, n2_o, rs2_o, left_o,
        mixed_o, peaks_o, vecs_o, o_qkv, o_out, o_up, o_down,
        w_qkv, w_out, w_up, w_down, w_sem, give_sem, take_sem, vec_s, vec_sem, peaks_s, peak_in, peak_sem,
        xs, qkv_s, lse_s, ctx_s, n1_s, rs1_s, sl_s, n2_s, rs2_s, aq_s, hq_s, xq_s, cq_s,
        acc, hid, up_s, ops_s, s_s, e_s, o_s, top_s, amax_s, lcol_s,
        save_sem, left_recv, in_sem, send_sem, recv_sem, mix_send, mix_recv,
    ) = refs
    r = pl.program_id(0)
    passes = pl.num_programs(0)
    row_count = tokens.shape[0]
    held = row_count // 2
    seq, width = tokens.shape[1], tokens.shape[2]
    ff = w_up.shape[1]
    piece = seq // count
    stage = lax.axis_index("pipe")
    side, group = lax.rem(stage, 2), lax.div(stage, 2)
    partner = stage + 1 - 2 * side
    first = group == 0
    last = group == count // 2 - 1
    a, k = lax.div(r, 2), lax.rem(r, 2)
    mine = k == side
    theirs = jnp.logical_not(mine)
    inlet = xs.at[r]

    left = {"aq": (0, ff), "hq": (ff, width), "xq": (ff + width, width), "cq": (ff + 2 * width, width)}
    left_order = list(left)
    staged = {
        "x": (None, x_o), "qkv": (qkv_s, qkv_o), "lse": (lse_s, lse_o), "ctx": (ctx_s, ctx_o),
        "n1": (n1_s, n1_o), "rs1": (rs1_s, rs1_o), "sl": (sl_s, sl_o), "n2": (n2_s, n2_o),
        "rs2": (rs2_s, rs2_o), "aq": (aq_s, left_o), "hq": (hq_s, left_o), "xq": (xq_s, left_o),
        "cq": (cq_s, left_o),
    }
    order = list(staged)
    owned = [h_qkv, h_out, h_up, h_down]
    lent = [o_qkv, o_out, o_up, o_down]
    resident = [w_qkv, w_out, w_up, w_down]

    def give(m):
        return pltpu.make_async_remote_copy(
            src_ref=owned[m], dst_ref=lent[m], send_sem=give_sem.at[m], recv_sem=take_sem.at[m],
            device_id={"pipe": partner}, device_id_type=LOGICAL,
        )

    def fetch(m, own_layer):
        @pl.when(own_layer)
        def _():
            pltpu.make_async_copy(owned[m], resident[m], w_sem.at[m]).start()

        @pl.when(jnp.logical_not(own_layer))
        def _():
            pltpu.make_async_copy(lent[m], resident[m], w_sem.at[m]).start()

    def weight_ready(m):
        pltpu.make_async_copy(owned[m], resident[m], w_sem.at[m]).wait()

    def fetch_next(*which):
        @pl.when(r + 1 < passes)
        def _():
            @pl.when(jnp.logical_and(r == 0, mine))
            def _():
                for m in which:
                    give(m).wait_recv()

            for m in which:
                fetch(m, theirs)

    def fetch_first(m):
        @pl.when(jnp.logical_and(r == 0, theirs))
        def _():
            give(m).wait_recv()
            pltpu.make_async_copy(lent[m], resident[m], w_sem.at[m]).start()

    def give_vec():
        return pltpu.make_async_remote_copy(
            src_ref=vec_i, dst_ref=vec_s.at[side], send_sem=vec_sem.at[0], recv_sem=vec_sem.at[1],
            device_id={"pipe": partner}, device_id_type=LOGICAL,
        )

    def take_vec():
        return pltpu.make_async_remote_copy(
            src_ref=vec_i, dst_ref=vec_s.at[1 - side], send_sem=vec_sem.at[0], recv_sem=vec_sem.at[1],
            device_id={"pipe": partner}, device_id_type=LOGICAL,
        )

    def give_peaks():
        return pltpu.make_async_remote_copy(
            src_ref=peaks_s.at[1 - side], dst_ref=peak_in, send_sem=peak_sem.at[0], recv_sem=peak_sem.at[1],
            device_id={"pipe": partner}, device_id_type=LOGICAL,
        )

    def save_copy(name, at):
        src, dst = staged[name]
        src = xs.at[at] if src is None else src
        if name in left:
            dst = dst.at[side * held + lax.div(at, 2), :, pl.ds(*left[name])]
        else:
            dst = dst.at[at]
        return pltpu.make_async_copy(src, dst, save_sem.at[order.index(name)])

    def left_send(name, at):
        row = lax.div(at, 2)
        return pltpu.make_async_remote_copy(
            src_ref=staged[name][0], dst_ref=left_o.at[side * held + row, :, pl.ds(*left[name])],
            send_sem=save_sem.at[order.index(name)], recv_sem=left_recv.at[left_order.index(name), row],
            device_id={"pipe": partner}, device_id_type=LOGICAL,
        )

    def left_take(name, row):
        return pltpu.make_async_remote_copy(
            src_ref=staged[name][0], dst_ref=left_o.at[(1 - side) * held + row, :, pl.ds(*left[name])],
            send_sem=save_sem.at[order.index(name)], recv_sem=left_recv.at[left_order.index(name), row],
            device_id={"pipe": partner}, device_id_type=LOGICAL,
        )

    def save(name):
        if name not in left:
            save_copy(name, r).start()
            return

        @pl.when(mine)
        def _():
            save_copy(name, r).start()

        @pl.when(theirs)
        def _():
            left_send(name, r).start()

    def saved(name, at, own_layer):
        if name not in left:
            save_copy(name, at).wait()
            return

        @pl.when(own_layer)
        def _():
            save_copy(name, at).wait()

        @pl.when(jnp.logical_not(own_layer))
        def _():
            left_send(name, at).wait_send()

    def reuse(*names):
        @pl.when(r > 0)
        def _():
            for name in names:
                saved(name, r - 1, theirs)

    def token_copy(i):
        return pltpu.make_async_copy(tokens.at[side * held + i], xs.at[2 * i], in_sem.at[i])

    def hop(i):
        return pltpu.make_async_remote_copy(
            src_ref=xs.at[2 * held + i], dst_ref=xs.at[2 * i], send_sem=send_sem.at[i], recv_sem=recv_sem.at[i],
            device_id={"pipe": lax.rem(stage + 2, count)}, device_id_type=LOGICAL,
        )

    def mix_part(i, p):
        row = side * held + i
        return pltpu.make_async_remote_copy(
            src_ref=xs.at[2 * held + i, pl.ds(p * piece, piece)], dst_ref=mixed_o.at[row],
            send_sem=mix_send.at[i, p], recv_sem=mix_recv.at[row],
            device_id={"pipe": jnp.int32(p)}, device_id_type=LOGICAL,
        )

    def mix_take(row):
        return pltpu.make_async_remote_copy(
            src_ref=xs.at[2 * held, pl.ds(0, piece)], dst_ref=mixed_o.at[row],
            send_sem=mix_send.at[0, 0], recv_sem=mix_recv.at[row],
            device_id={"pipe": partner}, device_id_type=LOGICAL,
        )

    def mix_own(i, p):
        return pltpu.make_async_copy(
            xs.at[2 * held + i, pl.ds(p * piece, piece)], mixed_o.at[side * held + i], mix_send.at[i, p]
        )

    @pl.when(r == 0)
    def _():
        greet(stage, count)
        give_vec().start()
        for m in range(4):
            give(m).start()

        @pl.when(mine)
        def _():
            for m in range(4):
                pltpu.make_async_copy(owned[m], resident[m], w_sem.at[m]).start()

        @pl.when(first)
        def _():
            for i in range(held):
                token_copy(i).start()

        vec_s[side] = vec_i[...]
        peaks_s[...] = jnp.zeros_like(peaks_s)

    @pl.when(jnp.logical_or(jnp.logical_and(r == 0, theirs), jnp.logical_and(r == 1, theirs)))
    def _():
        take_vec().wait_recv()

    @pl.when(jnp.logical_and(first, k == 0))
    def _():
        token_copy(a).wait()

    @pl.when(jnp.logical_and(jnp.logical_not(first), k == 0))
    def _():
        hop(a).wait_recv()

    length = lens[side * held + a]

    def vec(i, size):
        return vec_s[k, i : i + 1, 0:size]

    b_qkv, b_out, b_up, b_down = vec(0, 3 * width), vec(1, width), vec(2, ff), vec(3, width)
    gain = [vec(4, width), vec(5, width)]
    shift = [vec(6, width), vec(7, width)]
    m0, m1, m2, m3 = vec(8, width), vec(9, PAIR), vec(10, width), vec(11, CHUNK)
    i0, i1, i2, i3 = vec(12, width), vec(13, PAIR), vec(14, width), vec(15, CHUNK)

    def row_mask(start, size):
        return (start + lax.broadcasted_iota(jnp.int32, (size, 1), 0)) < length

    def blocks(size, body, init=0, begin=0, end=seq):
        step = lambda i, c: body(i * size, pl.ds(i * size, size), c)
        return lax.fori_loop(begin // size, end // size, step, init, unroll=True)

    def weave(dots, size, body, init=0):
        total, cut = seq // size, 0
        for k, dot in enumerate(dots):
            dot()
            begin, cut = cut, total * (k + 1) // len(dots)
            init = blocks(size, body, init, begin * size, cut * size)
        return init

    no_peak = jnp.zeros((8, 128), F32)

    reuse("x")
    save("x")
    reuse("xq", "qkv", "lse", "ctx", "cq")

    def quant_in(start, at, top):
        x = inlet[at, :].astype(F32)
        xq_s[at, :] = (m0 * jnp.tanh(x * i0)).astype(BF16)
        return jnp.maximum(top, masked_peak(x, start))

    def masked_peak(v, start):
        return peak_rows(jnp.where(row_mask(start, v.shape[0]), jnp.abs(v), 0.0))

    peaks_s[k, 0] = jnp.maximum(peaks_s[k, 0], blocks(BLOCK, quant_in, no_peak))
    save("xq")

    fetch_first(0)
    weight_ready(0)
    for j in range(3):
        cols = pl.ds(j * width, width)
        proj = dot_nn(xq_s[...], w_qkv[:, cols]) + b_qkv[:, j * width : (j + 1) * width]
        qkv_s[:, cols] = proj.astype(BF16)
    save("qkv")
    fetch_first(1)

    one = jnp.ones((), BF16)
    zero = jnp.zeros((), BF16)
    head_scale = jnp.asarray(HEAD_DIM ** -0.5, BF16)

    def prepare(p):
        slot = p % 2

        def body(start, at, c):
            lane = lax.broadcasted_iota(jnp.int32, (OPS, PAIR), 1)
            lo = lane < HEAD_DIM
            spot = jnp.where(lo, lane, lane - HEAD_DIM)
            bias = jnp.where(row_mask(start, OPS), 0.0, MASKED)
            extra = jnp.where(spot == 0, jnp.broadcast_to(bias, (OPS, PAIR)), 0.0).astype(BF16)
            q2 = qkv_s[at, p * PAIR : (p + 1) * PAIR] * head_scale
            k2 = qkv_s[at, width + p * PAIR : width + (p + 1) * PAIR]
            v2 = qkv_s[at, 2 * width + p * PAIR : 2 * width + (p + 1) * PAIR]
            ops_s[slot, 0, at, :] = jnp.where(lo, q2, one)
            ops_s[slot, 1, at, :] = jnp.where(lo, one, q2)
            ops_s[slot, 2, at, :] = jnp.where(lo, k2, extra)
            ops_s[slot, 3, at, :] = jnp.where(lo, extra, k2)
            ops_s[slot, 4, at, :] = jnp.where(lo, v2, one)
            ops_s[slot, 5, at, :] = jnp.where(lo, one, v2)
            return c

        blocks(OPS, body)

    def scores(h):
        p, side = h // 2, h % 2

        def piece_of(k):
            def run():
                keys = pl.ds(k * PIECE, PIECE)
                s_s[side, :, keys] = dot_nt(ops_s[p % 2, side], ops_s[p % 2, 2 + side, keys, :])

            return run

        return [piece_of(k) for k in range(seq // PIECE)]

    def soften(h):
        side = h % 2

        def body(start, at, c):
            s = s_s[side, at, :]
            top = jnp.max(s, -1, keepdims=True)
            e_s[side, at, :] = jnp.exp(s - top).astype(BF16)
            top_s[h % 4, at, :] = jnp.broadcast_to(top, (BLOCK, PAIR))
            return c

        return body

    def collect(h):
        p, side = h // 2, h % 2

        def piece_of(k):
            def run():
                queries = pl.ds(k * PIECE, PIECE)
                o_s[side, queries, :] = dot_nn(e_s[side, queries, :], ops_s[p % 2, 4 + side])

            return run

        return [piece_of(k) for k in range(seq // PIECE)]

    def settle(p, peak):
        cols = slice(p * PAIR, (p + 1) * PAIR)

        def body(start, at, top):
            lo = lax.broadcasted_iota(jnp.int32, (OPS, PAIR), 1) < HEAD_DIM
            o_a, o_b = o_s[0, at, :], o_s[1, at, :]
            total = pltpu.roll(jnp.where(lo, o_b, o_a), HEAD_DIM, 1)
            c = jnp.where(lo, o_a, o_b) / total
            ctx_s[at, cols] = c
            lcol_s[at, :] = jnp.where(lo, top_s[2 * p % 4, at, :], top_s[(2 * p + 1) % 4, at, :]) + jnp.log(total)
            cq_s[at, cols] = (m1 * jnp.tanh(c * i1)).astype(BF16)
            return jnp.maximum(top, masked_peak(c, start))

        peak = blocks(OPS, body, peak)
        flipped = lcol_s[...].T
        lse_s[2 * p : 2 * p + 1, :] = flipped[0:1, :]
        lse_s[2 * p + 1 : 2 * p + 2, :] = flipped[HEAD_DIM : HEAD_DIM + 1, :]
        return peak

    heads = 2 * (width // PAIR)
    peak = no_peak
    prepare(0)
    for dot in scores(0):
        dot()
    for h in range(heads):
        dots = []
        if h + 1 < heads:
            if (h + 1) % 2 == 0:
                prepare((h + 1) // 2)
            dots += scores(h + 1)
        if h > 0:
            dots += collect(h - 1)
        weave(dots, BLOCK, soften(h))
        if h > 0 and h % 2 == 0:
            peak = settle(h // 2 - 1, peak)
    for dot in collect(heads - 1):
        dot()
    peak = settle(heads // 2 - 1, peak)
    peaks_s[k, 1] = jnp.maximum(peaks_s[k, 1], peak)
    fetch_first(2)
    save("lse")
    save("ctx")
    save("cq")
    weight_ready(1)
    reuse("n1", "rs1", "hq")

    def out_piece(k):
        def run():
            at = pl.ds(k * PIECE, PIECE)
            acc[at, :] = dot_nn(cq_s[at, :], w_out[...])

        return run

    def norm_one(start, at, top):
        s = inlet[at, :].astype(F32) + (acc[at, :] + b_out)
        center = s - jnp.mean(s, -1, keepdims=True)
        rs = lax.rsqrt(jnp.mean(center * center, -1, keepdims=True) + EPS)
        n = center * rs
        h = n * gain[0] + shift[0]
        n1_s[at, :] = n.astype(BF16)
        rs1_s[at, :] = jnp.broadcast_to(rs, (BLOCK, 128))
        hid[at, :] = h
        hq_s[at, :] = (m2 * jnp.tanh(h * i2)).astype(BF16)
        return jnp.maximum(top, masked_peak(h, start))

    out_piece(0)()
    top = weave([out_piece(k) for k in range(1, seq // PIECE)] + [lambda: None], BLOCK, norm_one, no_peak)
    peaks_s[k, 2] = jnp.maximum(peaks_s[k, 2], top)
    fetch_first(3)
    fetch_next(0, 1)
    save("n1")
    save("rs1")
    save("hq")
    reuse("aq", "sl")

    chunks = ff // CHUNK

    def up_chunk(c):
        def piece_of(k):
            def run():
                part = dot_nn(hq_s[...], w_up[:, pl.ds(c * CHUNK + k * PIECE, PIECE)])
                up_s[c % 2, :, pl.ds(k * PIECE, PIECE)] = part

            return run

        return [piece_of(k) for k in range(CHUNK // PIECE)]

    def act_chunk(c):
        cols = pl.ds(c * CHUNK, CHUNK)

        def body(start, at, carry):
            act, low, slope = activation(up_s[c % 2, at, :] + b_up[:, c * CHUNK : (c + 1) * CHUNK], m3, i3)
            aq_s[at, cols] = low.astype(BF16)
            sl_s[at, cols] = slope.astype(BF16)
            size = jnp.abs(act)
            top = size[:, 0:128]
            for i in range(128, CHUNK, 128):
                top = jnp.maximum(top, size[:, i : i + 128])
            amax_s[at, :] = top if c == 0 else jnp.maximum(amax_s[at, :], top)
            return carry

        return body

    def down_chunk(c):
        def piece_of(k):
            def run():
                cols = pl.ds(k * PIECE, PIECE)
                part = dot_nn(aq_s[:, pl.ds(c * CHUNK, CHUNK)], w_down[pl.ds(c * CHUNK, CHUNK), cols])
                acc[:, cols] = part if c == 0 else acc[:, cols] + part

            return run

        return [piece_of(k) for k in range(width // PIECE)]

    weight_ready(2)
    weight_ready(3)
    for dot in up_chunk(0):
        dot()
    for c in range(chunks):
        dots = []
        if c + 1 < chunks:
            dots += up_chunk(c + 1)
        if c > 0:
            dots += down_chunk(c - 1)
        weave(dots, BLOCK, act_chunk(c))
    peaks_s[k, 3] = jnp.maximum(peaks_s[k, 3], masked_peak(amax_s[...], 0))
    save("aq")
    save("sl")
    reuse("n2", "rs2")
    outlet = jnp.where(k == 0, r + 1, 2 * held + a)

    def norm_two(start, at, c):
        s = hid[at, :] + (acc[at, :] + b_down)
        center = s - jnp.mean(s, -1, keepdims=True)
        rs = lax.rsqrt(jnp.mean(center * center, -1, keepdims=True) + EPS)
        n = center * rs
        n2_s[at, :] = n.astype(BF16)
        rs2_s[at, :] = jnp.broadcast_to(rs, (BLOCK, 128))
        xs[outlet, at, :] = (n * gain[1] + shift[1]).astype(BF16)
        return c

    def down_last(k):
        def run():
            at, cols = pl.ds(k * PIECE, PIECE), pl.ds((chunks - 1) * CHUNK, CHUNK)
            acc[at, :] += dot_nn(aq_s[at, cols], w_down[cols, :])

        return run

    down_last(0)()
    weave([down_last(k) for k in range(1, seq // PIECE)] + [lambda: None], BLOCK, norm_two)
    save("n2")
    save("rs2")
    fetch_next(2, 3)

    @pl.when(jnp.logical_and(k == 1, jnp.logical_not(last)))
    def _():
        hop(a).start()

    @pl.when(jnp.logical_and(k == 1, last))
    def _():
        for p in range(count):
            @pl.when(stage == p)
            def _():
                mix_own(a, p).start()

            @pl.when(stage != p)
            def _():
                mix_part(a, p).start()

    @pl.when(r == passes - 1)
    def _():
        give_peaks().start()
        vecs_o[...] = vec_s[...]
        for name in order:
            saved(name, r, mine)
        for name in left_order:
            for i in range(held):
                left_take(name, i).wait_recv()
        give_vec().wait_send()
        for m in range(4):
            give(m).wait_send()
        give_peaks().wait_send()
        give_peaks().wait_recv()
        peaks_o[...] = jnp.maximum(peaks_s[side], peak_in[...])

        @pl.when(jnp.logical_not(last))
        def _():
            for i in range(held):
                hop(i).wait_send()
            for row in range(row_count):
                mix_take(row).wait_recv()

        @pl.when(last)
        def _():
            for i in range(held):
                for p in range(count):
                    @pl.when(stage == p)
                    def _():
                        mix_own(i, p).wait()

                    @pl.when(stage != p)
                    def _():
                        mix_part(i, p).wait_send()
                mix_take((1 - side) * held + i).wait_recv()


def bwd_kernel(count, *refs):
    (
        lens, vecs, seeds, h_qkv, h_out, h_up, h_down, o_qkv, o_out, o_up, o_down, left_i,
        x_i, qkv_i, lse_i, ctx_i, n1_i, rs1_i, sl_i, n2_i, rs2_i,
        dproj_o, dbr_o, dup_o, ddn_o, gtok_o, left_o, small_o,
        w_qkv, w_out, w_up, w_down, w_sem, turn_in, turn_out, turn_in_sem, turn_out_sem,
        small_s, small_in, small_sem,
        gs, x_s, qkv_s, lse_s, ctx_s, n1_s, rs1_s, sl_s, n2_s, rs2_s,
        dproj_s, dbr_s, dup_s, ddn_s, dctx_s, acc, dr,
        up_s, ops_s, s_s, g_s, p_s, ds_s, gv_s, gk_s, gq_s, k_t, in_s, inner_s,
        load_sem, save_sem, right_recv, in_sem, send_sem, recv_sem, tok_send,
    ) = refs
    r = pl.program_id(0)
    passes = pl.num_programs(0)
    row_count = seeds.shape[0]
    held = row_count // 2
    seq, width = seeds.shape[1], seeds.shape[2]
    ff = w_up.shape[1]
    stage = lax.axis_index("pipe")
    side, group = lax.rem(stage, 2), lax.div(stage, 2)
    partner = stage + 1 - 2 * side
    first = group == 0
    last = group == count // 2 - 1
    a, k = lax.div(r, 2), 1 - lax.rem(r, 2)
    mine = k == side
    theirs = jnp.logical_not(mine)

    loaded = {
        "n2": (n2_i, n2_s), "rs2": (rs2_i, rs2_s), "sl": (sl_i, sl_s), "n1": (n1_i, n1_s),
        "rs1": (rs1_i, rs1_s), "ctx": (ctx_i, ctx_s), "qkv": (qkv_i, qkv_s), "lse": (lse_i, lse_s),
        "x": (x_i, x_s),
    }
    load_order = list(loaded)
    staged = {
        "ddn": (ddn_s, ddn_o), "dup": (dup_s, dup_o), "dbr": (dbr_s, dbr_o), "dproj": (dproj_s, dproj_o),
    }
    save_order = list(staged)

    def load_copy(name, at):
        src, dst = loaded[name]
        forward_pass = 2 * lax.div(at, 2) + 1 - lax.rem(at, 2)
        return pltpu.make_async_copy(src.at[forward_pass], dst, load_sem.at[load_order.index(name)])

    def fetch_next(*names):
        @pl.when(r + 1 < passes)
        def _():
            for name in names:
                load_copy(name, r + 1).start()

    def ready(*names):
        for name in names:
            load_copy(name, r).wait()

    def save_copy(name, at):
        src, dst = staged[name]
        dst = dst.at[side * held + lax.div(at, 2)]
        return pltpu.make_async_copy(src, dst, save_sem.at[save_order.index(name)])

    def save_send(name, at):
        src, dst = staged[name]
        row = lax.div(at, 2)
        return pltpu.make_async_remote_copy(
            src_ref=src, dst_ref=dst.at[side * held + row], send_sem=save_sem.at[save_order.index(name)],
            recv_sem=right_recv.at[save_order.index(name), row],
            device_id={"pipe": partner}, device_id_type=LOGICAL,
        )

    def save_take(name, row):
        src, dst = staged[name]
        return pltpu.make_async_remote_copy(
            src_ref=src, dst_ref=dst.at[(1 - side) * held + row], send_sem=save_sem.at[save_order.index(name)],
            recv_sem=right_recv.at[save_order.index(name), row],
            device_id={"pipe": partner}, device_id_type=LOGICAL,
        )

    def save(name):
        @pl.when(mine)
        def _():
            save_copy(name, r).start()

        @pl.when(theirs)
        def _():
            save_send(name, r).start()

    def saved(name, at, own_layer):
        @pl.when(own_layer)
        def _():
            save_copy(name, at).wait()

        @pl.when(jnp.logical_not(own_layer))
        def _():
            save_send(name, at).wait_send()

    def reuse(*names):
        @pl.when(r > 0)
        def _():
            for name in names:
                saved(name, r - 1, theirs)

    def seed_copy(i):
        return pltpu.make_async_copy(seeds.at[side * held + i], gs.at[2 * i], in_sem.at[i])

    def hop(i):
        return pltpu.make_async_remote_copy(
            src_ref=gs.at[2 * held + i], dst_ref=gs.at[2 * i], send_sem=send_sem.at[i], recv_sem=recv_sem.at[i],
            device_id={"pipe": lax.rem(stage + count - 2, count)}, device_id_type=LOGICAL,
        )

    def tok_copy(i):
        return pltpu.make_async_copy(gs.at[2 * held + i], gtok_o.at[i], tok_send.at[i])

    def give_small():
        return pltpu.make_async_remote_copy(
            src_ref=small_s.at[1 - side], dst_ref=small_in, send_sem=small_sem.at[0], recv_sem=small_sem.at[1],
            device_id={"pipe": partner}, device_id_type=LOGICAL,
        )

    owned = [h_down, h_up, h_out, h_qkv]
    lent = [o_down, o_up, o_out, o_qkv]
    resident = [w_down, w_up, w_out, w_qkv]

    def fetch(m, own_layer):
        @pl.when(own_layer)
        def _():
            pltpu.make_async_copy(owned[m], resident[m], w_sem.at[m]).start()

        @pl.when(jnp.logical_not(own_layer))
        def _():
            pltpu.make_async_copy(lent[m], resident[m], w_sem.at[m]).start()

    def weight_ready(m):
        pltpu.make_async_copy(owned[m], resident[m], w_sem.at[m]).wait()

    def weight_next(*which):
        @pl.when(r + 1 < passes)
        def _():
            for m in which:
                fetch(m, theirs)

    parts = left_i.shape[2] // width
    turns = row_count * parts

    def turn_load(i):
        cols = pl.ds(pl.multiple_of(i % parts * width, 128), width)
        return pltpu.make_async_copy(left_i.at[i // parts, :, cols], turn_in.at[i % 2], turn_in_sem.at[i % 2])

    def turn_store(i):
        rows_at = pl.ds(pl.multiple_of(i % parts * width, 128), width)
        cols = pl.ds(pl.multiple_of(i // parts * seq, 128), seq)
        return pltpu.make_async_copy(turn_out.at[i % 2], left_o.at[rows_at, cols], turn_out_sem.at[i % 2])

    def turn_left():
        turn_load(0).start()

        def body(i, c):
            @pl.when(i + 1 < turns)
            def _():
                turn_load(i + 1).start()

            turn_load(i).wait()

            @pl.when(i >= 2)
            def _():
                turn_store(i - 2).wait()

            turn_out[i % 2] = turn_in[i % 2].T
            turn_store(i).start()
            return c

        lax.fori_loop(0, turns, body, 0)
        turn_store(turns - 2).wait()
        turn_store(turns - 1).wait()

    @pl.when(r == 0)
    def _():
        greet(stage, count)

        @pl.when(last)
        def _():
            for i in range(held):
                seed_copy(i).start()

        for name in ("n2", "rs2"):
            load_copy(name, 0).start()
        fetch(0, mine)
        load_copy("sl", 0).start()
        for m in (1, 2, 3):
            fetch(m, mine)
        for name in load_order[3:]:
            load_copy(name, 0).start()
        small_s[...] = jnp.zeros_like(small_s)

        @pl.when(jnp.logical_not(last))
        def _():
            turn_left()

    @pl.when(jnp.logical_and(last, k == 1))
    def _():
        seed_copy(a).wait()

    @pl.when(jnp.logical_and(jnp.logical_not(last), k == 1))
    def _():
        hop(a).wait_recv()

    length = lens[side * held + a]

    def vec(i, size):
        return vecs[k, i : i + 1, 0:size]

    gain = [vec(4, width), vec(5, width)]
    shift = [vec(6, width), vec(7, width)]
    i0, i1, i2 = vec(12, PIECE), vec(13, PAIR), vec(14, width)

    offsets = {}
    at_col = 0
    for name, size in (
        ("gain0", width), ("gain1", width), ("shift0", width), ("shift1", width),
        ("out", width), ("down", width), ("up", ff), ("qkv", 3 * width),
    ):
        offsets[name] = at_col
        at_col += size

    def blocks(size, body, init=0, begin=0, end=seq):
        step = lambda i, c: body(i * size, pl.ds(i * size, size), c)
        return lax.fori_loop(begin // size, end // size, step, init, unroll=True)

    def weave(dots, size, body, init=0):
        total, cut = seq // size, 0
        for k, dot in enumerate(dots):
            dot()
            begin, cut = cut, total * (k + 1) // len(dots)
            init = blocks(size, body, init, begin * size, cut * size)
        return init

    def row_mask(start, size):
        return (start + lax.broadcasted_iota(jnp.int32, (size, 1), 0)) < length

    def put_small(name, v, col=0):
        small_s[k, :, pl.ds(offsets[name] + col, v.shape[1])] += v

    no_sum = jnp.zeros((8, width), F32)

    ready("n2", "rs2")
    reuse("ddn")

    def norm_two(start, at, sums):
        dy = jnp.where(row_mask(start, BLOCK), gs[r, at, :].astype(F32), 0.0)
        n = n2_s[at, :].astype(F32)
        e = dy * gain[1]
        mean_e = jnp.mean(e, -1, keepdims=True)
        mean_en = jnp.mean(e * n, -1, keepdims=True)
        d = (e - mean_e - n * mean_en) * rs2_s[at, 0:1]
        dr[at, :] = d
        ddn_s[at, :] = d.astype(BF16)
        return sums[0] + fold_rows(dy * n), sums[1] + fold_rows(dy), sums[2] + fold_rows(d)

    for name, v in zip(("gain1", "shift1", "down"), blocks(BLOCK, norm_two, (no_sum,) * 3)):
        put_small(name, v)
    save("ddn")
    fetch_next("n2", "rs2")
    ready("sl")
    reuse("dup")

    chunks = ff // CHUNK

    def dact_chunk(c):
        def piece_of(k):
            def run():
                at = pl.ds(c * CHUNK + k * PIECE, PIECE)
                up_s[c % 2, :, pl.ds(k * PIECE, PIECE)] = dot_nt(ddn_s[...], w_down[at, :])

            return run

        return [piece_of(k) for k in range(CHUNK // PIECE)]

    def slope_chunk(c):
        cols = pl.ds(c * CHUNK, CHUNK)

        def body(start, at, total):
            d = up_s[c % 2, at, :] * sl_s[at, cols].astype(F32)
            dup_s[at, cols] = d.astype(BF16)
            return total + fold_rows(d)

        return body

    def dhid_chunk(c):
        cols = pl.ds(c * CHUNK, CHUNK)

        def piece_of(k):
            def run():
                at = pl.ds(k * PIECE, PIECE)
                part = dot_nt(dup_s[:, cols], w_up[at, cols])
                acc[:, at] = part if c == 0 else acc[:, at] + part

            return run

        return [piece_of(k) for k in range(width // PIECE)]

    weight_ready(0)
    weight_ready(1)
    for dot in dact_chunk(0):
        dot()
    for c in range(chunks):
        dots = []
        if c + 1 < chunks:
            dots += dact_chunk(c + 1)
        if c > 0:
            dots += dhid_chunk(c - 1)
        put_small("up", weave(dots, BLOCK, slope_chunk(c), jnp.zeros((8, CHUNK), F32)), c * CHUNK)
    save("dup")
    fetch_next("sl")
    ready("n1", "rs1")
    reuse("dbr")

    def norm_one(start, at, sums):
        n = n1_s[at, :].astype(F32)
        t = jnp.tanh((n * gain[0] + shift[0]) * i2)
        dy = dr[at, :] + acc[at, :] * (1.0 - t * t)
        e = dy * gain[0]
        mean_e = jnp.mean(e, -1, keepdims=True)
        mean_en = jnp.mean(e * n, -1, keepdims=True)
        d = (e - mean_e - n * mean_en) * rs1_s[at, 0:1]
        dr[at, :] = d
        dbr_s[at, :] = d.astype(BF16)
        return sums[0] + fold_rows(dy * n), sums[1] + fold_rows(dy), sums[2] + fold_rows(d)

    def dhid_last(k):
        def run():
            at, cols = pl.ds(k * PIECE, PIECE), pl.ds((chunks - 1) * CHUNK, CHUNK)
            acc[at, :] += dot_nt(dup_s[at, cols], w_up[:, cols])

        return run

    dhid_last(0)()
    dots = [dhid_last(k) for k in range(1, seq // PIECE)] + [lambda: None]
    for name, v in zip(("gain0", "shift0", "out"), weave(dots, BLOCK, norm_one, (no_sum,) * 3)):
        put_small(name, v)
    save("dbr")
    weight_next(0, 1)
    fetch_next("n1", "rs1")
    ready("ctx")
    weight_ready(2)
    for j in range(width // PIECE):
        acc[:, pl.ds(j * PIECE, PIECE)] = dot_nt(dbr_s[...], w_out[pl.ds(j * PIECE, PIECE), :])
    weight_next(2)
    ready("qkv", "lse")
    reuse("dproj")

    one = jnp.ones((), BF16)
    zero = jnp.zeros((), BF16)
    head_scale = jnp.asarray(HEAD_DIM ** -0.5, BF16)
    pick = lax.broadcasted_iota(jnp.int32, (16, PAIR), 0)
    side_of = lax.broadcasted_iota(jnp.int32, (16, PAIR), 1) // HEAD_DIM
    sum_lanes = jnp.where(pick == side_of, 1.0, 0.0).astype(BF16)

    def prepare(p):
        slot = p % 2
        cols = slice(p * PAIR, (p + 1) * PAIR)

        def body(start, at, c):
            lane = lax.broadcasted_iota(jnp.int32, (OPS, PAIR), 1)
            lo = lane < HEAD_DIM
            spot = jnp.where(lo, lane, lane - HEAD_DIM)
            ctx = ctx_s[at, cols]
            t = jnp.tanh(ctx * i1)
            low = (acc[at, cols] * (1.0 - t * t)).astype(BF16)
            dctx_s[slot, at, :] = low
            inner = low.astype(F32) * ctx
            hi = inner.astype(BF16)
            in_s[0, at, :] = hi
            in_s[1, at, :] = (inner - hi.astype(F32)).astype(BF16)
            bias = jnp.where(row_mask(start, OPS), 0.0, MASKED)
            extra = jnp.where(spot == 0, jnp.broadcast_to(bias, (OPS, PAIR)), 0.0).astype(BF16)
            q2 = qkv_s[at, p * PAIR : (p + 1) * PAIR] * head_scale
            k2 = qkv_s[at, width + p * PAIR : width + (p + 1) * PAIR]
            v2 = qkv_s[at, 2 * width + p * PAIR : 2 * width + (p + 1) * PAIR]
            ops_s[slot, 0, at, :] = jnp.where(lo, q2, one)
            ops_s[slot, 1, at, :] = jnp.where(lo, one, q2)
            ops_s[slot, 2, at, :] = jnp.where(lo, k2, extra)
            ops_s[slot, 3, at, :] = jnp.where(lo, extra, k2)
            ops_s[slot, 4, at, :] = jnp.where(lo, v2, zero)
            ops_s[slot, 5, at, :] = jnp.where(lo, zero, v2)
            ops_s[slot, 6, at, :] = q2
            return c

        blocks(OPS, body)
        inner_s[slot] = dot_nt(sum_lanes, in_s[0]) + dot_nt(sum_lanes, in_s[1])
        k_t[slot] = qkv_s[:, width + p * PAIR : width + (p + 1) * PAIR].T

    def scores(h):
        slot, side = h // 2 % 2, h % 2

        def piece_of(k, out, left, right):
            def run():
                queries = pl.ds(k * PIECE, PIECE)
                out[side, :, queries] = dot_nt(left[...], right[queries, :])

            return run

        pairs = [
            (s_s, ops_s.at[slot, 2 + side], ops_s.at[slot, side]),
            (g_s, ops_s.at[slot, 4 + side], dctx_s.at[slot]),
        ]
        return [piece_of(k, *pair) for pair in pairs for k in range(seq // PIECE)]

    def soften(h):
        slot, side = h // 2 % 2, h % 2

        def body(start, at, c):
            prob = jnp.exp(s_s[side, at, :] - lse_s[h : h + 1, :])
            p_s[side, at, :] = prob.astype(BF16)
            ds_s[side, at, :] = (prob * (g_s[side, at, :] - inner_s[slot, side : side + 1, :])).astype(BF16)
            return c

        return body

    def collect(h):
        slot, side = h // 2 % 2, h % 2
        rows = slice(side * HEAD_DIM, (side + 1) * HEAD_DIM)

        def grad_v():
            gv_s[side] = dot_nn(p_s[side], dctx_s[slot])

        def grad_k():
            gk_s[side] = dot_nn(ds_s[side], ops_s[slot, 6])

        def grad_q(k):
            def run():
                queries = pl.ds(k * PIECE, PIECE)
                gq_s[rows, queries] = dot_nn(k_t[slot, rows, :], ds_s[side, :, queries])

            return run

        return [grad_v, grad_k] + [grad_q(k) for k in range(seq // PIECE)]

    def settle(p):
        dproj_s[:, p * PAIR : (p + 1) * PAIR] = (gq_s[...].T * (HEAD_DIM ** -0.5)).astype(BF16)

        def body(start, at, c):
            lo = lax.broadcasted_iota(jnp.int32, (OPS, PAIR), 1) < HEAD_DIM
            k = jnp.where(lo, gk_s[0, at, :], gk_s[1, at, :])
            v = jnp.where(lo, gv_s[0, at, :], gv_s[1, at, :])
            dproj_s[at, width + p * PAIR : width + (p + 1) * PAIR] = k.astype(BF16)
            dproj_s[at, 2 * width + p * PAIR : 2 * width + (p + 1) * PAIR] = v.astype(BF16)
            return c

        blocks(OPS, body)

    heads = 2 * (width // PAIR)
    prepare(0)
    for dot in scores(0):
        dot()
    for h in range(heads):
        dots = []
        if h + 1 < heads:
            if (h + 1) % 2 == 0:
                prepare((h + 1) // 2)
            dots += scores(h + 1)
        if h > 0:
            dots += collect(h - 1)
        weave(dots, BLOCK, soften(h))
        if h > 0 and h % 2 == 0:
            settle(h // 2 - 1)
    for dot in collect(heads - 1):
        dot()
    settle(heads // 2 - 1)
    save("dproj")
    fetch_next("ctx", "qkv", "lse")
    weight_ready(3)
    ready("x")
    outlet = jnp.where(k == 1, r + 1, 2 * held + a)

    def dx_piece(k):
        def run():
            at = pl.ds(k * PIECE, PIECE)
            acc[:, at] = dot_nt(dproj_s[...], w_qkv[at, :])

        return run

    def quant_in(k):
        cols = pl.ds(k * PIECE, PIECE)
        values = pl.ds(2 * width + k * PIECE, PIECE)

        def body(start, at, sums):
            t = jnp.tanh(x_s[at, cols].astype(F32) * i0)
            gs[outlet, at, cols] = (dr[at, cols] + acc[at, cols] * (1.0 - t * t)).astype(BF16)
            return (
                sums[0] + fold_rows(dproj_s[at, cols].astype(F32)),
                sums[1] + fold_rows(dproj_s[at, values].astype(F32)),
            )

        return body

    dx_piece(0)()
    pieces = width // PIECE
    for j in range(pieces):
        dots = [dx_piece(j + 1)] if j + 1 < pieces else [lambda: None]
        sums = weave(dots, BLOCK, quant_in(j), (jnp.zeros((8, PIECE), F32),) * 2)
        put_small("qkv", sums[0], j * PIECE)
        put_small("qkv", sums[1], 2 * width + j * PIECE)
    fetch_next("x")
    weight_next(3)

    @pl.when(jnp.logical_and(k == 0, jnp.logical_not(first)))
    def _():
        hop(a).start()

    @pl.when(jnp.logical_and(k == 0, first))
    def _():
        tok_copy(a).start()

    @pl.when(r == passes - 1)
    def _():
        give_small().start()

        @pl.when(last)
        def _():
            turn_left()

        for name in save_order:
            saved(name, r, mine)
        for name in save_order:
            for i in range(held):
                save_take(name, i).wait_recv()
        give_small().wait_send()
        give_small().wait_recv()
        small_o[...] = small_s[side] + small_in[...]

        @pl.when(jnp.logical_not(first))
        def _():
            for i in range(held):
                hop(i).wait_send()

        @pl.when(first)
        def _():
            for i in range(held):
                tok_copy(i).wait()


def whole(a):
    return pl.BlockSpec(a.shape, lambda r, n=a.ndim: (0,) * n, pipeline_mode=pl.Buffered(1))


ANYWHERE = pl.BlockSpec(memory_space=pl.ANY)
SCALAR = pl.BlockSpec(memory_space=pltpu.SMEM)
VMEM_LIMIT = 60 * 1024 * 1024


def run_forward(count, tokens, lengths, vec, heavy):
    rows, seq, width = tokens.shape
    ff = heavy[2].shape[1]
    held = rows // 2
    saves = [
        (width, BF16), (3 * width, BF16), (None, F32), (width, F32), (width, BF16), (128, F32),
        (ff, BF16), (width, BF16), (128, F32),
    ]
    heads = 16 * pl.cdiv(width // HEAD_DIM, 16)
    room = lambda n: (heads, seq) if n is None else (seq, n)
    lefts = [(ff, BF16), (width, BF16), (width, BF16), (width, BF16)]
    tok = rows * seq
    sem = pltpu.SemaphoreType.DMA
    return pl.pallas_call(
        lambda *refs: fwd_kernel(count, *refs),
        grid=(2 * held,),
        in_specs=[SCALAR, whole(vec)] + [ANYWHERE] * 5,
        out_specs=[ANYWHERE] * 11
        + [pl.BlockSpec((4, 8, 128), lambda r: (0, 0, 0)), pl.BlockSpec((2, *vec.shape), lambda r: (0, 0, 0))]
        + [ANYWHERE] * 4,
        out_shape=[jax.ShapeDtypeStruct((2 * held, *room(n)), t) for n, t in saves]
        + [
            jax.ShapeDtypeStruct((rows, seq, ff + 3 * width), BF16),
            jax.ShapeDtypeStruct((rows, seq // count, width), BF16),
            jax.ShapeDtypeStruct((4, 8, 128), F32),
            jax.ShapeDtypeStruct((2, *vec.shape), F32),
        ]
        + [jax.ShapeDtypeStruct(w.shape, w.dtype) for w in heavy],
        scratch_shapes=[pltpu.VMEM(w.shape, w.dtype) for w in heavy]
        + [
            sem((4,)), sem((4,)), sem((4,)),
            pltpu.VMEM((2, *vec.shape), F32),
            sem((2,)),
            pltpu.VMEM((2, 4, 8, 128), F32),
            pltpu.VMEM((4, 8, 128), F32),
            sem((2,)),
            pltpu.VMEM((3 * held, seq, width), BF16),
        ]
        + [pltpu.VMEM(room(n), t) for n, t in saves[1:] + lefts]
        + [
            pltpu.VMEM((seq, width), F32),
            pltpu.VMEM((seq, width), F32),
            pltpu.VMEM((2, seq, CHUNK), F32),
            pltpu.VMEM((2, 6, seq, PAIR), BF16),
            pltpu.VMEM((2, seq, seq), F32),
            pltpu.VMEM((2, seq, seq), BF16),
            pltpu.VMEM((2, seq, PAIR), F32),
            pltpu.VMEM((4, seq, PAIR), F32),
            pltpu.VMEM((seq, 128), F32),
            pltpu.VMEM((seq, PAIR), F32),
            sem((13,)), sem((4, held)), sem((held,)), sem((held,)), sem((held,)), sem((held, count)), sem((rows,)),
        ],
        compiler_params=pltpu.CompilerParams(
            collective_id=0, has_side_effects=True, vmem_limit_bytes=VMEM_LIMIT,
            dimension_semantics=("arbitrary",),
        ),
        cost_estimate=pl.CostEstimate(
            flops=2 * tok * (4 * width * width + 2 * width * ff + 2 * seq * width),
            bytes_accessed=tok * 28000, transcendentals=tok * 3 * ff,
        ),
    )(lengths, vec, tokens, *heavy)


def run_backward(count, seeds, lengths, vecs, heavy, lent, kept):
    *loads, left = kept
    rows, seq, width = seeds.shape
    ff = heavy[2].shape[1]
    held = rows // 2
    big = lambda n, t: jax.ShapeDtypeStruct((rows, seq, n), t)
    saves = [(3 * width, BF16), (width, BF16), (ff, BF16), (width, BF16)]
    tok = rows * seq
    small = 6 * width + ff + 3 * width
    sem = pltpu.SemaphoreType.DMA
    return pl.pallas_call(
        lambda *refs: bwd_kernel(count, *refs),
        grid=(2 * held,),
        in_specs=[SCALAR, whole(vecs)] + [ANYWHERE] * 19,
        out_specs=[ANYWHERE] * 6 + [pl.BlockSpec((8, small), lambda r: (0, 0))],
        out_shape=[big(n, t) for n, t in saves]
        + [
            jax.ShapeDtypeStruct((held, seq, width), BF16),
            jax.ShapeDtypeStruct((left.shape[2], rows * seq), BF16),
            jax.ShapeDtypeStruct((8, small), F32),
        ],
        scratch_shapes=[pltpu.VMEM(w.shape, w.dtype) for w in heavy]
        + [
            sem((4,)),
            pltpu.VMEM((2, seq, width), BF16),
            pltpu.VMEM((2, width, seq), BF16),
            sem((2,)), sem((2,)),
            pltpu.VMEM((2, 8, small), F32),
            pltpu.VMEM((8, small), F32),
            sem((2,)),
            pltpu.VMEM((3 * held, seq, width), BF16),
        ]
        + [pltpu.VMEM(x.shape[1:], x.dtype) for x in loads]
        + [pltpu.VMEM((seq, n), t) for n, t in saves]
        + [
            pltpu.VMEM((2, seq, PAIR), BF16),
            pltpu.VMEM((seq, width), F32),
            pltpu.VMEM((seq, width), F32),
            pltpu.VMEM((2, seq, CHUNK), F32),
            pltpu.VMEM((2, 7, seq, PAIR), BF16),
            pltpu.VMEM((2, seq, seq), F32),
            pltpu.VMEM((2, seq, seq), F32),
            pltpu.VMEM((2, seq, seq), BF16),
            pltpu.VMEM((2, seq, seq), BF16),
            pltpu.VMEM((2, seq, PAIR), F32),
            pltpu.VMEM((2, seq, PAIR), F32),
            pltpu.VMEM((PAIR, seq), F32),
            pltpu.VMEM((2, PAIR, seq), BF16),
            pltpu.VMEM((2, seq, PAIR), BF16),
            pltpu.VMEM((2, 16, seq), F32),
            sem((9,)), sem((4,)), sem((4, held)), sem((held,)), sem((held,)), sem((held,)), sem((held,)),
        ],
        compiler_params=pltpu.CompilerParams(
            collective_id=1, has_side_effects=True, vmem_limit_bytes=VMEM_LIMIT,
            dimension_semantics=("arbitrary",),
        ),
        cost_estimate=pl.CostEstimate(
            flops=2 * tok * (4 * width * width + 2 * width * ff + 5 * seq * width),
            bytes_accessed=tok * 28000, transcendentals=tok * ff,
        ),
    )(lengths, vecs, seeds, *heavy, *lent, left, *loads)


def ring_to_dp(pos, n):
    return jnp.where(pos < n // 2, 2 * pos, 2 * (n - pos) - 1)


def dp_to_ring(j, n):
    return jnp.where(j % 2 == 0, j // 2, n - 1 - j // 2)


def grad_kernel(count, n, *refs):
    (
        left, ddn, dup, dproj, dbr, small, g0,
        gq_o, go_o, gu_o, gd_o, small_o, gtok_o,
        slots_d, slots_u, slots_q, slots_s, wide_v, thin_v, ddn_v, dup_v, dpo_v,
        wide_sem, thin_sem, right_sem,
        send_d, recv_d, send_u, recv_u, send_q, recv_q, send_s, recv_s, tok_send, tok_recv,
    ) = refs
    width = ddn.shape[1]
    ff = dup.shape[1]
    shard, shard_ff = width // n, ff // n
    held, seq = g0.shape[0], g0.shape[1]
    piece = seq // count
    stage = lax.axis_index("pipe")
    side = lax.rem(stage, 2)
    me = lax.axis_index("dp")
    pos = dp_to_ring(me, n)
    first = stage < 2
    ahead = ring_to_dp(lax.rem(pos + 1, n), n)
    behind = ring_to_dp(lax.rem(pos + n - 1, n), n)
    target = (ahead, behind)

    def chunk(d, step):
        at = pos + 2 * n - 1 - step if d == 0 else pos + 1 + step
        return ring_to_dp(lax.rem(at, n), n)

    def wide_copy(d, step):
        rows = pl.ds(pl.multiple_of(chunk(d, step) * shard_ff, 16), shard_ff)
        return pltpu.make_async_copy(left.at[rows, :], wide_v.at[d], wide_sem.at[d])

    def thin_copy(k, d, step):
        rows = pl.ds(pl.multiple_of(ff + k * width + chunk(d, step) * shard, 16), shard)
        return pltpu.make_async_copy(left.at[rows, :], thin_v.at[k, d], thin_sem.at[k, d])

    rights = [
        (ddn, ddn_v), (dup, dup_v), (dproj, dpo_v.at[:, pl.ds(0, 3 * width)]),
        (dbr, dpo_v.at[:, pl.ds(3 * width, width)]),
    ]

    def right_copy(k):
        return pltpu.make_async_copy(rights[k][0], rights[k][1], right_sem.at[k])

    for d in range(2):
        wide_copy(d, 0).start()
    right_copy(0).start()
    right_copy(1).start()
    for d in range(2):
        thin_copy(0, d, 0).start()
    right_copy(2).start()
    right_copy(3).start()
    for d in range(2):
        thin_copy(1, d, 0).start()
        if d == 1:
            thin_copy(2, d, 0).start()

    barrier = pltpu.get_barrier_semaphore()
    for peer in target:
        pl.semaphore_signal(barrier, inc=1, device_id={"dp": peer}, device_id_type=LOGICAL)

    for p in range(2):
        @pl.when(stage != p)
        def _():
            pl.semaphore_signal(barrier, inc=1, device_id={"pipe": jnp.int32(p)}, device_id_type=LOGICAL)

    @pl.when(first)
    def _():
        pl.semaphore_wait(barrier, 1 + count)

    @pl.when(jnp.logical_not(first))
    def _():
        pl.semaphore_wait(barrier, 2)

    def tok_part(i, p):
        row = side * held + i
        return pltpu.make_async_remote_copy(
            src_ref=g0.at[i, pl.ds(p * piece, piece)], dst_ref=gtok_o.at[row],
            send_sem=tok_send.at[i, p], recv_sem=tok_recv.at[row],
            device_id={"pipe": jnp.int32(p)}, device_id_type=LOGICAL,
        )

    def tok_take(row):
        return pltpu.make_async_remote_copy(
            src_ref=g0.at[0, pl.ds(0, piece)], dst_ref=gtok_o.at[row],
            send_sem=tok_send.at[0, 0], recv_sem=tok_recv.at[row],
            device_id={"pipe": jnp.int32(0)}, device_id_type=LOGICAL,
        )

    def tok_own(i, p):
        return pltpu.make_async_copy(
            g0.at[i, pl.ds(p * piece, piece)], gtok_o.at[side * held + i], tok_send.at[i, p]
        )

    @pl.when(first)
    def _():
        for i in range(held):
            for p in range(count):
                @pl.when(stage == p)
                def _():
                    tok_own(i, p).start()

                @pl.when(stage != p)
                def _():
                    tok_part(i, p).start()

    def message(slots, send, recv, d, at):
        return pltpu.make_async_remote_copy(
            src_ref=slots.at[d, at], dst_ref=slots.at[d, jnp.minimum(at + 1, n - 1)],
            send_sem=send.at[d, at], recv_sem=recv.at[d, jnp.minimum(at + 1, n - 1)],
            device_id={"dp": target[d]}, device_id_type=LOGICAL,
        )

    def arrived(slots, send, recv, d, at):
        return pltpu.make_async_remote_copy(
            src_ref=slots.at[d, at], dst_ref=slots.at[d, at],
            send_sem=send.at[d, at], recv_sem=recv.at[d, at],
            device_id={"dp": target[d]}, device_id_type=LOGICAL,
        )

    def lane(slots, send, recv, d, step, mine, finish):
        @pl.when(step == 0)
        def _():
            slots[d, 0] = mine.astype(BF16)

        @pl.when(step > 0)
        def _():
            arrived(slots, send, recv, d, step).wait_recv()

            @pl.when(step < n - 1)
            def _():
                slots[d, step] = (slots[d, step].astype(F32) + mine).astype(BF16)

            @pl.when(step == n - 1)
            def _():
                finish(slots[d, step].astype(F32) + mine)

        @pl.when(step < n - 1)
        def _():
            message(slots, send, recv, d, step).start()

    def small_message(at):
        return pltpu.make_async_remote_copy(
            src_ref=slots_s.at[at], dst_ref=slots_s.at[jnp.minimum(at + 1, n - 1)],
            send_sem=send_s.at[at], recv_sem=recv_s.at[jnp.minimum(at + 1, n - 1)],
            device_id={"dp": target[0]}, device_id_type=LOGICAL,
        )

    def small_arrived(at):
        return pltpu.make_async_remote_copy(
            src_ref=slots_s.at[at], dst_ref=slots_s.at[at], send_sem=send_s.at[at],
            recv_sem=recv_s.at[at], device_id={"dp": target[0]}, device_id_type=LOGICAL,
        )

    sum_rows = lax.broadcasted_iota(jnp.int32, (16, 128), 0) < 9

    def small_step(step):
        mine = small[chunk(0, step)]

        @pl.when(step == 0)
        def _():
            slots_s[0] = mine

        @pl.when(step > 0)
        def _():
            small_arrived(step).wait_recv()
            got = slots_s[step]
            slots_s[step] = jnp.where(sum_rows, got + mine, jnp.maximum(got, mine))

        @pl.when(step < n - 1)
        def _():
            small_message(step).start()

        @pl.when(step == n - 1)
        def _():
            small_o[...] = slots_s[step]

    half, half_ff = width // 2, ff // 2

    def fetched(copy, step, *args):
        copy(*args, step).wait()

    def refill(copy, step, *args):
        @pl.when(step < n - 1)
        def _():
            copy(*args, step + 1).start()

    def right_ready(k, step):
        @pl.when(step == 0)
        def _():
            right_copy(k).wait()

    def turn(step, _):
        right_ready(0, step)
        for d in range(2):
            cols = slice(d * half, (d + 1) * half)
            fetched(wide_copy, step, d)
            mine = dot_nn(wide_v[d], ddn_v[:, cols])
            refill(wide_copy, step, d)

            def finish_down(total):
                gd_o[:, cols] = total

            lane(slots_d, send_d, recv_d, d, step, mine, finish_down)
        small_step(step)
        right_ready(1, step)
        for d in range(2):
            cols = slice(d * half_ff, (d + 1) * half_ff)
            fetched(thin_copy, step, 0, d)
            mine = dot_nn(thin_v[0, d], dup_v[:, cols])
            refill(thin_copy, step, 0, d)

            def finish_up(total):
                gu_o[:, cols] = total

            lane(slots_u, send_u, recv_u, d, step, mine, finish_up)
        right_ready(2, step)
        right_ready(3, step)
        fetched(thin_copy, step, 1, 0)
        mine = dot_nn(thin_v[1, 0], dpo_v[:, 0 : 2 * width])
        refill(thin_copy, step, 1, 0)

        def finish_ahead(total):
            gq_o[:, 0 : 2 * width] = total

        lane(slots_q, send_q, recv_q, 0, step, mine, finish_ahead)
        fetched(thin_copy, step, 1, 1)
        fetched(thin_copy, step, 2, 1)
        mine = jnp.concatenate(
            [
                dot_nn(thin_v[1, 1], dpo_v[:, 2 * width : 3 * width]),
                dot_nn(thin_v[2, 1], dpo_v[:, 3 * width : 4 * width]),
            ],
            1,
        )
        refill(thin_copy, step, 1, 1)
        refill(thin_copy, step, 2, 1)

        def finish_behind(total):
            gq_o[:, 2 * width : 3 * width] = total[:, 0:width]
            go_o[...] = total[:, width : 2 * width]

        lane(slots_q, send_q, recv_q, 1, step, mine, finish_behind)
        return 0

    lax.fori_loop(0, n, turn, 0)

    def drain(at, _):
        for d in range(2):
            message(slots_d, send_d, recv_d, d, at).wait_send()
            message(slots_u, send_u, recv_u, d, at).wait_send()
            message(slots_q, send_q, recv_q, d, at).wait_send()
        small_message(at).wait_send()
        return 0

    lax.fori_loop(0, n - 1, drain, 0)

    @pl.when(first)
    def _():
        for i in range(held):
            for p in range(count):
                @pl.when(stage == p)
                def _():
                    tok_own(i, p).wait()

                @pl.when(stage != p)
                def _():
                    tok_part(i, p).wait_send()
            tok_take((1 - side) * held + i).wait_recv()

    @pl.when(jnp.logical_not(first))
    def _():
        for row in range(2 * held):
            tok_take(row).wait_recv()


def run_grads(count, n, left, dproj, dbr, dup, ddn, g0, small):
    held, seq, width = g0.shape
    rows = 2 * held
    ff = dup.shape[2]
    flat = lambda a: a.reshape(rows * seq, a.shape[2])
    tok = rows * seq
    shard, shard_ff = width // n, ff // n
    ops = [left] + [flat(a) for a in (ddn, dup, dproj, dbr)]
    vmem = pl.BlockSpec(memory_space=pltpu.VMEM)
    sem = pltpu.SemaphoreType.DMA
    return pl.pallas_call(
        lambda *refs: grad_kernel(count, n, *refs),
        in_specs=[ANYWHERE] * 5 + [vmem, ANYWHERE],
        out_specs=[vmem] * 5 + [ANYWHERE],
        out_shape=[
            jax.ShapeDtypeStruct((shard, 3 * width), F32),
            jax.ShapeDtypeStruct((shard, width), F32),
            jax.ShapeDtypeStruct((shard, ff), F32),
            jax.ShapeDtypeStruct((shard_ff, width), F32),
            jax.ShapeDtypeStruct((16, 128), F32),
            jax.ShapeDtypeStruct((rows, seq // count, width), BF16),
        ],
        scratch_shapes=[
            pltpu.VMEM((2, n, shard_ff, width // 2), BF16),
            pltpu.VMEM((2, n, shard, ff // 2), BF16),
            pltpu.VMEM((2, n, shard, 2 * width), BF16),
            pltpu.VMEM((n, 16, 128), F32),
            pltpu.VMEM((2, shard_ff, tok), BF16),
            pltpu.VMEM((3, 2, shard, tok), BF16),
            pltpu.VMEM((tok, width), BF16),
            pltpu.VMEM((tok, ff), BF16),
            pltpu.VMEM((tok, 4 * width), BF16),
            sem((2,)), sem((3, 2)), sem((4,)),
            sem((2, n)), sem((2, n)), sem((2, n)), sem((2, n)), sem((2, n)), sem((2, n)),
            sem((n,)), sem((n,)), sem((held, count)), sem((rows,)),
        ],
        compiler_params=pltpu.CompilerParams(
            collective_id=2, has_side_effects=True, vmem_limit_bytes=VMEM_LIMIT,
        ),
        cost_estimate=pl.CostEstimate(
            flops=2 * tok * (4 * width * width + 2 * width * ff), bytes_accessed=tok * 25000, transcendentals=0,
        ),
    )(*ops, small, g0)


def weight_grad(left, right):
    g = jnp.einsum("rsd,rse->de", left, right, preferred_element_type=F32).astype(BF16)
    return lax.psum_scatter(g, "dp", scatter_dimension=0, tiled=True).astype(F32)


def share_pieces(held_rows, count, stage):
    piece = held_rows.shape[1] // count
    sides = []
    for source in range(2):
        mine = held_rows[:, :piece]
        for p in range(count):
            part = held_rows[:, p * piece : (p + 1) * piece]
            got = part if p == source else lax.ppermute(part, "pipe", [(source, p)])
            mine = jnp.where(stage == p, got, mine)
        sides.append(mine)
    return jnp.concatenate(sides, 0)


def shards(
    tokens, lengths, ema_scales, w_qkv, bias_qv, w_out, bias_out, w_up, bias_up, w_down, bias_down,
    ln_gain, ln_bias, cotangent,
):
    count = lax.axis_size("pipe")
    n = lax.axis_size("dp")
    width = tokens.shape[2]
    ff = w_up.shape[2]
    fill = lambda v: jnp.pad(v, ((0, 0), (0, ff - v.shape[1])))
    b_qkv = jnp.concatenate([bias_qv[:, :width], jnp.zeros_like(bias_qv[:, :width]), bias_qv[:, width:]], 1)
    ranges = jnp.broadcast_to(ema_scales[0][:, None], (4, ff))
    vec = jnp.concatenate(
        [
            fill(b_qkv), fill(bias_out), bias_up, fill(bias_down), fill(ln_gain[0]), fill(ln_bias[0]),
            ranges, 1.0 / ranges,
        ],
        0,
    )
    heavy = (w_qkv[0], w_out[0], w_up[0], w_down[0])
    *kept, mixed, peaks, vecs, l_qkv, l_out, l_up, l_down = run_forward(count, tokens, lengths, vec, heavy)
    left = kept[-1]
    dproj, dbr, dup, ddn, g0, turned, small = run_backward(
        count, cotangent, lengths, vecs, heavy, (l_qkv, l_out, l_up, l_down), kept
    )
    sums = jnp.sum(small, 0)
    parts, at = [], 0
    for size in (width, width, width, width, width, width, ff, width, width, width):
        parts.append(sums[at : at + size])
        at += size
    parts[7:] = [jnp.concatenate([parts[7], parts[9]])]
    packed = jnp.concatenate([v.reshape(n, -1) for v in parts], 1)
    peak = jnp.max(peaks, (1, 2))
    sums_width = packed.shape[1]
    if n >= 4 and n % 2 == 0 and width // n % 16 == 0 and ff // n % 128 == 0 and sums_width == 9 * 128:
        top = jnp.broadcast_to(jnp.pad(peak, (0, 124))[None, None], (n, 7, 128))
        with_peak = jnp.concatenate([packed.reshape(n, 9, 128), top], 1)
        g_qkv, g_out, g_up, g_down, small_sum, grad_tokens = run_grads(
            count, n, turned, dproj, dbr, dup, ddn, g0, with_peak
        )
        mine = small_sum[:9].reshape(1, sums_width)
        batch_max = small_sum[9:10, :4]
    else:
        g_down = weight_grad(left[:, :, :ff], ddn)
        g_up = weight_grad(left[:, :, ff : ff + width], dup)
        g_qkv = weight_grad(left[:, :, ff + width : ff + 2 * width], dproj)
        g_out = weight_grad(left[:, :, ff + 2 * width :], dbr)
        mine = lax.psum_scatter(packed, "dp", scatter_dimension=0, tiled=True)
        batch_max = lax.pmax(peak, "dp")[None]
        grad_tokens = share_pieces(g0, count, lax.axis_index("pipe"))
    outs, at = [], 0
    for size in (width, width, width, width, width, width, ff, 2 * width):
        outs.append(mine[:, at : at + size // n])
        at += size // n
    gain0, gain1, shift0, shift1, s_out, s_down, s_up, s_qv = outs
    g_gain = jnp.stack([gain0, gain1], 1)
    g_shift = jnp.stack([shift0, shift1], 1)
    return (
        mixed, grad_tokens, g_qkv[None], s_qv, g_out[None], s_out, g_up[None], s_up, g_down[None], s_down,
        g_gain, g_shift, batch_max,
    )


def solution(mesh):
    return jax.shard_map(
        shards,
        mesh=mesh,
        in_specs=(
            P("dp", None, None), P("dp"), P("pipe", None), P("pipe", None, None), P("pipe", None),
            P("pipe", None, None), P("pipe", None), P("pipe", None, None), P("pipe", None),
            P("pipe", None, None), P("pipe", None), P("pipe", None, None), P("pipe", None, None),
            P("dp", None, None),
        ),
        out_specs=(
            P("dp", "pipe", None), P("dp", "pipe", None), P("pipe", "dp", None), P("pipe", "dp"),
            P("pipe", "dp", None), P("pipe", "dp"), P("pipe", "dp", None), P("pipe", "dp"),
            P("pipe", "dp", None), P("pipe", "dp"), P("pipe", None, "dp"), P("pipe", None, "dp"),
            P("pipe", None),
        ),
        check_vma=False,
    )
```

```python
import jax
import jax.numpy as jnp
from jax import lax
from jax.experimental import pallas as pl
from jax.experimental.pallas import tpu as pltpu
from jax.sharding import PartitionSpec as P

HEAD_DIM = 64
PAIR = 2 * HEAD_DIM
EPS = 1e-06
MASKED = -1000000000.0
CHUNK = 512
PIECE = 256
BLOCK = 16
OPS = 64
LOGICAL = pl.DeviceIdType.MESH
F32 = jnp.float32
BF16 = jnp.bfloat16

ERF_POLY = (
    0.7978823511659165,
    0.03634481045269742,
    -4.5110171354091134e-05,
    -5.02654469142584e-05,
    3.0867937984305273e-06,
    -6.60140005994544e-08,
)
ERF_CLAMP = 5.2 * 5.2
HALF_LOG2E = -0.7213475204444817
LOG2_DENSITY = -1.3257480647361593


def dot_nn(a, b):
    return jnp.dot(a, b, preferred_element_type=F32)


def dot_nt(a, b):
    return lax.dot_general(a, b, (((1,), (1,)), ((), ())), preferred_element_type=F32)


def dot_tn(a, b):
    return lax.dot_general(a, b, (((0,), (0,)), ((), ())), preferred_element_type=F32)


def fold_rows(v):
    return jnp.sum(v.reshape(v.shape[0] // 8, 8, v.shape[1]), 0)


def peak_rows(v):
    tiles = [v[:, i : i + 128] for i in range(0, v.shape[1], 128)]
    top = tiles[0]
    for tile in tiles[1:]:
        top = jnp.maximum(top, tile)
    return jnp.max(top.reshape(v.shape[0] // 8, 8, 128), 0)


def greet(stage, count):
    barrier = pltpu.get_barrier_semaphore()
    for step in range(1, count):
        peer = lax.rem(stage + step, count)
        pl.semaphore_signal(barrier, inc=1, device_id={"pipe": peer}, device_id_type=LOGICAL)
    pl.semaphore_wait(barrier, count - 1)


def activation(u, ceiling, inv_ceiling):
    square = u * u
    w = jnp.minimum(square, ERF_CLAMP)
    poly = w * ERF_POLY[-1] + ERF_POLY[-2]
    for coef in ERF_POLY[-3::-1]:
        poly = poly * w + coef
    t = jnp.tanh(u * poly)
    half = 0.5 * u
    act = half + half * t
    ratio = jnp.tanh(act * inv_ceiling)
    density = jnp.exp2(square * HALF_LOG2E + LOG2_DENSITY)
    slope = (1.0 - ratio * ratio) * ((0.5 + 0.5 * t) + u * density)
    return act, ceiling * ratio, slope


def fwd_kernel(count, *refs):
    (
        lens, scales, tokens, h_qkv, h_out, h_up, h_down, b_qkv, b_out, b_up, b_down, gain, shift,
        x_o, qkv_o, inv_o, ctx_o, n1_o, rs1_o, sl_o, n2_o, rs2_o, left_o, exp_o,
        mixed_o, peaks_o,
        w_qkv, w_out, w_up, w_down, w_sem,
        xin, xout, qkv_s, inv_s, ctx_s, n1_s, rs1_s, sl_s, n2_s, rs2_s, aq_s, hq_s, xq_s, cq_s,
        acc, hid, up_s, ops_s, s_s, e_s, o_s, amax_s,
        exp_sem, save_sem, in_sem, send_sem, recv_sem, mix_send, mix_recv,
    ) = refs
    r = pl.program_id(0)
    rows = pl.num_programs(0)
    row_count = tokens.shape[0]
    seq, width = tokens.shape[1], tokens.shape[2]
    ff = w_up.shape[1]
    piece = seq // count
    stage = lax.axis_index("pipe")
    first = stage == 0
    last = stage == count - 1

    left = {"aq": (0, ff), "hq": (ff, width), "xq": (ff + width, width), "cq": (ff + 2 * width, width)}
    staged = {
        "x": (xin.at[r], x_o), "qkv": (qkv_s, qkv_o), "inv": (inv_s, inv_o), "ctx": (ctx_s, ctx_o),
        "n1": (n1_s, n1_o), "rs1": (rs1_s, rs1_o), "sl": (sl_s, sl_o), "n2": (n2_s, n2_o),
        "rs2": (rs2_s, rs2_o), "aq": (aq_s, left_o), "hq": (hq_s, left_o), "xq": (xq_s, left_o),
        "cq": (cq_s, left_o),
    }
    order = list(staged)
    fetches = [(h_qkv, w_qkv), (h_out, w_out), (h_up, w_up), (h_down, w_down)]

    def weight_copy(k):
        return pltpu.make_async_copy(fetches[k][0], fetches[k][1], w_sem.at[k])

    def weight_ready(k):
        @pl.when(r == 0)
        def _():
            weight_copy(k).wait()

    def save_copy(name):
        src, dst = staged[name]
        dst = dst.at[r]
        if name in left:
            dst = dst.at[:, pl.ds(*left[name])]
        return pltpu.make_async_copy(src, dst, save_sem.at[order.index(name)])

    def save(name):
        save_copy(name).start()

    def reuse(*names):
        @pl.when(r > 0)
        def _():
            for name in names:
                save_copy(name).wait()

    def token_copy(i):
        return pltpu.make_async_copy(tokens.at[i], xin.at[i], in_sem.at[i])

    def hop(i):
        return pltpu.make_async_remote_copy(
            src_ref=xout.at[i], dst_ref=xin.at[i], send_sem=send_sem.at[i], recv_sem=recv_sem.at[i],
            device_id={"pipe": lax.rem(stage + 1, count)}, device_id_type=LOGICAL,
        )

    def mix_part(i, p):
        return pltpu.make_async_remote_copy(
            src_ref=xout.at[i, pl.ds(p * piece, piece)], dst_ref=mixed_o.at[i],
            send_sem=mix_send.at[i, p], recv_sem=mix_recv.at[i],
            device_id={"pipe": jnp.int32(p)}, device_id_type=LOGICAL,
        )

    def mix_own(i):
        return pltpu.make_async_copy(
            xout.at[i, pl.ds((count - 1) * piece, piece)], mixed_o.at[i], mix_send.at[i, count - 1]
        )

    @pl.when(r == 0)
    def _():
        greet(stage, count)
        peaks_o[...] = jnp.zeros_like(peaks_o)
        for k in range(4):
            weight_copy(k).start()

        @pl.when(first)
        def _():
            for i in range(row_count):
                token_copy(i).start()

    @pl.when(first)
    def _():
        token_copy(r).wait()

    @pl.when(jnp.logical_not(first))
    def _():
        hop(r).wait_recv()

    length = lens[r]
    m0, m1, m2, m3 = scales[0, 0], scales[0, 1], scales[0, 2], scales[0, 3]
    i0, i1, i2, i3 = 1.0 / m0, 1.0 / m1, 1.0 / m2, 1.0 / m3

    def row_mask(start, size):
        return (start + lax.broadcasted_iota(jnp.int32, (size, 1), 0)) < length

    def blocks(size, body, init=0, begin=0, end=seq):
        step = lambda i, c: body(i * size, pl.ds(i * size, size), c)
        return lax.fori_loop(begin // size, end // size, step, init, unroll=True)

    def weave(dots, size, body, init=0):
        total, cut = seq // size, 0
        for k, dot in enumerate(dots):
            dot()
            begin, cut = cut, total * (k + 1) // len(dots)
            init = blocks(size, body, init, begin * size, cut * size)
        return init

    no_peak = jnp.zeros((8, 128), F32)

    @pl.when(r > 0)
    def _():
        save_copy("x").wait()

    save("x")
    reuse("xq", "qkv", "inv", "ctx", "cq")

    def quant_in(start, at, top):
        x = xin[r, at, :].astype(F32)
        xq_s[at, :] = (m0 * jnp.tanh(x * i0)).astype(BF16)
        return jnp.maximum(top, masked_peak(x, start))

    def masked_peak(v, start):
        return peak_rows(jnp.where(row_mask(start, v.shape[0]), jnp.abs(v), 0.0))

    peaks_o[0] = jnp.maximum(peaks_o[0], blocks(BLOCK, quant_in, no_peak))
    save("xq")

    weight_ready(0)
    for j in range(3):
        cols = pl.ds(j * width, width)
        proj = dot_nn(xq_s[...], w_qkv[:, cols]) + b_qkv[:, cols]
        qkv_s[:, cols] = proj.astype(BF16)
    save("qkv")

    one = jnp.ones((), BF16)
    zero = jnp.zeros((), BF16)
    head_scale = jnp.asarray(HEAD_DIM ** -0.5, BF16)

    def prepare(p):
        slot = p % 2

        def body(start, at, c):
            lane = lax.broadcasted_iota(jnp.int32, (OPS, PAIR), 1)
            lo = lane < HEAD_DIM
            spot = jnp.where(lo, lane, lane - HEAD_DIM)
            bias = jnp.where(row_mask(start, OPS), 0.0, MASKED)
            extra = jnp.where(spot == 0, jnp.broadcast_to(bias, (OPS, PAIR)), 0.0).astype(BF16)
            q2 = qkv_s[at, p * PAIR : (p + 1) * PAIR] * head_scale
            k2 = qkv_s[at, width + p * PAIR : width + (p + 1) * PAIR]
            v2 = qkv_s[at, 2 * width + p * PAIR : 2 * width + (p + 1) * PAIR]
            ops_s[slot, 0, at, :] = jnp.where(lo, q2, one)
            ops_s[slot, 1, at, :] = jnp.where(lo, one, q2)
            ops_s[slot, 2, at, :] = jnp.where(lo, k2, extra)
            ops_s[slot, 3, at, :] = jnp.where(lo, extra, k2)
            ops_s[slot, 4, at, :] = jnp.where(lo, v2, one)
            ops_s[slot, 5, at, :] = jnp.where(lo, one, v2)
            return c

        blocks(OPS, body)

    def scores(h):
        p, side = h // 2, h % 2

        def piece_of(k):
            def run():
                keys = pl.ds(k * PIECE, PIECE)
                s_s[side, :, keys] = dot_nt(ops_s[p % 2, side], ops_s[p % 2, 2 + side, keys, :])

            return run

        return [piece_of(k) for k in range(seq // PIECE)]

    def exp_copy(h):
        return pltpu.make_async_copy(e_s.at[h % 4], exp_o.at[r, h], exp_sem.at[h % 4])

    def soften(h):
        def body(start, at, c):
            s = s_s[h % 2, at, :]
            e_s[h % 4, at, :] = jnp.exp(s - jnp.max(s, -1, keepdims=True)).astype(BF16)
            return c

        return body

    def collect(h):
        p, side = h // 2, h % 2

        def piece_of(k):
            def run():
                queries = pl.ds(k * PIECE, PIECE)
                o_s[side, queries, :] = dot_nn(e_s[h % 4, queries, :], ops_s[p % 2, 4 + side])

            return run

        return [piece_of(k) for k in range(seq // PIECE)]

    def settle(p, peak):
        cols = slice(p * PAIR, (p + 1) * PAIR)

        def body(start, at, top):
            lo = lax.broadcasted_iota(jnp.int32, (OPS, PAIR), 1) < HEAD_DIM
            o_a, o_b = o_s[0, at, :], o_s[1, at, :]
            total = pltpu.roll(jnp.where(lo, o_b, o_a), HEAD_DIM, 1)
            inverse = 1.0 / total
            c = jnp.where(lo, o_a, o_b) * inverse
            inv_s[at, cols] = inverse
            ctx_s[at, cols] = c
            cq_s[at, cols] = (m1 * jnp.tanh(c * i1)).astype(BF16)
            return jnp.maximum(top, masked_peak(c, start))

        return blocks(OPS, body, peak)

    heads = 2 * (width // PAIR)
    peak = no_peak
    prepare(0)
    for dot in scores(0):
        dot()
    for h in range(heads):
        dots = []
        if h + 1 < heads:
            if (h + 1) % 2 == 0:
                prepare((h + 1) // 2)
            dots += scores(h + 1)
        if h > 0:
            dots += collect(h - 1)
        if h >= 4:
            exp_copy(h).wait()
        else:
            @pl.when(r > 0)
            def _():
                exp_copy(h).wait()

        weave(dots, BLOCK, soften(h))
        exp_copy(h).start()
        if h > 0 and h % 2 == 0:
            peak = settle(h // 2 - 1, peak)
    for dot in collect(heads - 1):
        dot()
    peak = settle(heads // 2 - 1, peak)
    peaks_o[1] = jnp.maximum(peaks_o[1], peak)
    save("inv")
    save("ctx")
    save("cq")
    weight_ready(1)
    reuse("n1", "rs1", "hq")

    def out_piece(k):
        def run():
            at = pl.ds(k * PIECE, PIECE)
            acc[at, :] = dot_nn(cq_s[at, :], w_out[...])

        return run

    def norm_one(start, at, top):
        s = xin[r, at, :].astype(F32) + (acc[at, :] + b_out[...])
        center = s - jnp.mean(s, -1, keepdims=True)
        rs = lax.rsqrt(jnp.mean(center * center, -1, keepdims=True) + EPS)
        n = center * rs
        h = n * gain[0:1, :] + shift[0:1, :]
        n1_s[at, :] = n.astype(BF16)
        rs1_s[at, :] = jnp.broadcast_to(rs, (BLOCK, 128))
        hid[at, :] = h
        hq_s[at, :] = (m2 * jnp.tanh(h * i2)).astype(BF16)
        return jnp.maximum(top, masked_peak(h, start))

    out_piece(0)()
    top = weave([out_piece(k) for k in range(1, seq // PIECE)] + [lambda: None], BLOCK, norm_one, no_peak)
    peaks_o[2] = jnp.maximum(peaks_o[2], top)
    save("n1")
    save("rs1")
    save("hq")
    reuse("aq", "sl")

    chunks = ff // CHUNK

    def up_chunk(c):
        def piece_of(k):
            def run():
                part = dot_nn(hq_s[...], w_up[:, pl.ds(c * CHUNK + k * PIECE, PIECE)])
                up_s[c % 2, :, pl.ds(k * PIECE, PIECE)] = part

            return run

        return [piece_of(k) for k in range(CHUNK // PIECE)]

    def act_chunk(c):
        cols = pl.ds(c * CHUNK, CHUNK)

        def body(start, at, carry):
            act, low, slope = activation(up_s[c % 2, at, :] + b_up[:, cols], m3, i3)
            aq_s[at, cols] = low.astype(BF16)
            sl_s[at, cols] = slope.astype(BF16)
            size = jnp.abs(act)
            top = size[:, 0:128]
            for i in range(128, CHUNK, 128):
                top = jnp.maximum(top, size[:, i : i + 128])
            amax_s[at, :] = top if c == 0 else jnp.maximum(amax_s[at, :], top)
            return carry

        return body

    def down_chunk(c):
        def piece_of(k):
            def run():
                cols = pl.ds(k * PIECE, PIECE)
                part = dot_nn(aq_s[:, pl.ds(c * CHUNK, CHUNK)], w_down[pl.ds(c * CHUNK, CHUNK), cols])
                acc[:, cols] = part if c == 0 else acc[:, cols] + part

            return run

        return [piece_of(k) for k in range(width // PIECE)]

    weight_ready(2)
    weight_ready(3)
    for dot in up_chunk(0):
        dot()
    for c in range(chunks):
        dots = []
        if c + 1 < chunks:
            dots += up_chunk(c + 1)
        if c > 0:
            dots += down_chunk(c - 1)
        weave(dots, BLOCK, act_chunk(c))
    peaks_o[3] = jnp.maximum(peaks_o[3], masked_peak(amax_s[...], 0))
    save("aq")
    save("sl")
    reuse("n2", "rs2")

    def norm_two(start, at, c):
        s = hid[at, :] + (acc[at, :] + b_down[...])
        center = s - jnp.mean(s, -1, keepdims=True)
        rs = lax.rsqrt(jnp.mean(center * center, -1, keepdims=True) + EPS)
        n = center * rs
        n2_s[at, :] = n.astype(BF16)
        rs2_s[at, :] = jnp.broadcast_to(rs, (BLOCK, 128))
        xout[r, at, :] = (n * gain[1:2, :] + shift[1:2, :]).astype(BF16)
        return c

    def down_last(k):
        def run():
            at, cols = pl.ds(k * PIECE, PIECE), pl.ds((chunks - 1) * CHUNK, CHUNK)
            acc[at, :] += dot_nn(aq_s[at, cols], w_down[cols, :])

        return run

    down_last(0)()
    weave([down_last(k) for k in range(1, seq // PIECE)] + [lambda: None], BLOCK, norm_two)
    save("n2")
    save("rs2")

    @pl.when(jnp.logical_not(last))
    def _():
        hop(r).start()

    @pl.when(last)
    def _():
        for p in range(count - 1):
            mix_part(r, p).start()
        mix_own(r).start()

    @pl.when(r == rows - 1)
    def _():
        for name in order:
            save_copy(name).wait()
        for h in range(heads - 4, heads):
            exp_copy(h).wait()

        @pl.when(jnp.logical_not(last))
        def _():
            for i in range(row_count):
                hop(i).wait_send()
            for i in range(row_count):
                mix_part(i, 0).wait_recv()

        @pl.when(last)
        def _():
            for i in range(row_count):
                for p in range(count - 1):
                    mix_part(i, p).wait_send()
                mix_own(i).wait()


def bwd_kernel(count, *refs):
    (
        lens, scales, seeds, h_qkv, h_out, h_up, h_down, gain, shift, left_i,
        x_i, qkv_i, inv_i, ctx_i, n1_i, rs1_i, sl_i, n2_i, rs2_i, exp_i,
        dproj_o, dbr_o, dup_o, ddn_o, gtok_o, left_o, small_o,
        w_qkv, w_out, w_up, w_down, w_sem, turn_in, turn_out, turn_in_sem, turn_out_sem,
        gin, gout, x_s, qkv_s, inv_s, ctx_s, n1_s, rs1_s, sl_s, n2_s, rs2_s,
        dproj_s, dbr_s, dup_s, ddn_s, dctx_s, acc, dr,
        up_s, ops_s, e_s, g_s, ds_s, gv_s, gk_s, gq_s, q_t, do_t, inner_s,
        exp_sem, load_sem, save_sem, in_sem, send_sem, recv_sem, tok_send,
    ) = refs
    r = pl.program_id(0)
    rows = pl.num_programs(0)
    row_count = seeds.shape[0]
    seq, width = seeds.shape[1], seeds.shape[2]
    ff = w_up.shape[1]
    piece = seq // count
    stage = lax.axis_index("pipe")
    first = stage == 0
    last = stage == count - 1

    loaded = {
        "n2": (n2_i, n2_s), "rs2": (rs2_i, rs2_s), "sl": (sl_i, sl_s), "n1": (n1_i, n1_s),
        "rs1": (rs1_i, rs1_s), "ctx": (ctx_i, ctx_s), "qkv": (qkv_i, qkv_s), "inv": (inv_i, inv_s),
        "x": (x_i, x_s),
    }
    load_order = list(loaded)
    staged = {
        "ddn": (ddn_s, ddn_o), "dup": (dup_s, dup_o), "dbr": (dbr_s, dbr_o), "dproj": (dproj_s, dproj_o),
    }
    save_order = list(staged)

    def load_copy(name, i):
        src, dst = loaded[name]
        return pltpu.make_async_copy(src.at[i], dst, load_sem.at[load_order.index(name)])

    def exp_copy(h, i):
        return pltpu.make_async_copy(exp_i.at[i, h], e_s.at[h % 4], exp_sem.at[h % 4])

    def fetch_next(*names):
        @pl.when(r + 1 < rows)
        def _():
            for name in names:
                load_copy(name, r + 1).start()

    def ready(*names):
        for name in names:
            load_copy(name, r).wait()

    def save_copy(name):
        src, dst = staged[name]
        return pltpu.make_async_copy(src, dst.at[r], save_sem.at[save_order.index(name)])

    def save(name):
        save_copy(name).start()

    def reuse(*names):
        @pl.when(r > 0)
        def _():
            for name in names:
                save_copy(name).wait()

    def seed_copy(i):
        return pltpu.make_async_copy(seeds.at[i], gin.at[i], in_sem.at[i])

    def hop(i):
        return pltpu.make_async_remote_copy(
            src_ref=gout.at[i], dst_ref=gin.at[i], send_sem=send_sem.at[i], recv_sem=recv_sem.at[i],
            device_id={"pipe": lax.rem(stage + count - 1, count)}, device_id_type=LOGICAL,
        )

    def tok_copy(i):
        return pltpu.make_async_copy(gout.at[i], gtok_o.at[i], tok_send.at[i])

    fetches = [(h_down, w_down), (h_up, w_up), (h_out, w_out), (h_qkv, w_qkv)]

    def weight_copy(k):
        return pltpu.make_async_copy(fetches[k][0], fetches[k][1], w_sem.at[k])

    def weight_ready(k):
        @pl.when(r == 0)
        def _():
            weight_copy(k).wait()

    parts = left_i.shape[2] // width
    turns = row_count * parts

    def turn_load(i):
        cols = pl.ds(pl.multiple_of(i % parts * width, 128), width)
        return pltpu.make_async_copy(left_i.at[i // parts, :, cols], turn_in.at[i % 2], turn_in_sem.at[i % 2])

    def turn_store(i):
        rows_at = pl.ds(pl.multiple_of(i % parts * width, 128), width)
        cols = pl.ds(pl.multiple_of(i // parts * seq, 128), seq)
        return pltpu.make_async_copy(turn_out.at[i % 2], left_o.at[rows_at, cols], turn_out_sem.at[i % 2])

    def turn_left():
        turn_load(0).start()

        def body(i, c):
            @pl.when(i + 1 < turns)
            def _():
                turn_load(i + 1).start()

            turn_load(i).wait()

            @pl.when(i >= 2)
            def _():
                turn_store(i - 2).wait()

            turn_out[i % 2] = turn_in[i % 2].T
            turn_store(i).start()
            return c

        lax.fori_loop(0, turns, body, 0)
        turn_store(turns - 2).wait()
        turn_store(turns - 1).wait()

    @pl.when(r == 0)
    def _():
        greet(stage, count)
        small_o[...] = jnp.zeros_like(small_o)

        @pl.when(last)
        def _():
            for i in range(row_count):
                seed_copy(i).start()

        for name in ("n2", "rs2"):
            load_copy(name, 0).start()
        weight_copy(0).start()
        load_copy("sl", 0).start()
        for k in (1, 2, 3):
            weight_copy(k).start()
        for name in load_order[3:]:
            load_copy(name, 0).start()
        for h in range(4):
            exp_copy(h, 0).start()

        @pl.when(stage < count - 2)
        def _():
            turn_left()

    @pl.when(last)
    def _():
        seed_copy(r).wait()

    @pl.when(jnp.logical_not(last))
    def _():
        hop(r).wait_recv()

    length = lens[r]
    m0, m1, m2 = scales[0, 0], scales[0, 1], scales[0, 2]
    i0, i1, i2 = 1.0 / m0, 1.0 / m1, 1.0 / m2

    offsets = {}
    at_col = 0
    for name, size in (
        ("gain0", width), ("gain1", width), ("shift0", width), ("shift1", width),
        ("out", width), ("down", width), ("up", ff), ("qkv", 3 * width),
    ):
        offsets[name] = at_col
        at_col += size

    def blocks(size, body, init=0, begin=0, end=seq):
        step = lambda i, c: body(i * size, pl.ds(i * size, size), c)
        return lax.fori_loop(begin // size, end // size, step, init, unroll=True)

    def weave(dots, size, body, init=0):
        total, cut = seq // size, 0
        for k, dot in enumerate(dots):
            dot()
            begin, cut = cut, total * (k + 1) // len(dots)
            init = blocks(size, body, init, begin * size, cut * size)
        return init

    def row_mask(start, size):
        return (start + lax.broadcasted_iota(jnp.int32, (size, 1), 0)) < length

    def put_small(name, v, col=0):
        small_o[:, pl.ds(offsets[name] + col, v.shape[1])] += v

    no_sum = jnp.zeros((8, width), F32)

    ready("n2", "rs2")
    reuse("ddn")

    def norm_two(start, at, sums):
        dy = jnp.where(row_mask(start, BLOCK), gin[r, at, :].astype(F32), 0.0)
        n = n2_s[at, :].astype(F32)
        e = dy * gain[1:2, :]
        mean_e = jnp.mean(e, -1, keepdims=True)
        mean_en = jnp.mean(e * n, -1, keepdims=True)
        d = (e - mean_e - n * mean_en) * rs2_s[at, 0:1]
        dr[at, :] = d
        ddn_s[at, :] = d.astype(BF16)
        return sums[0] + fold_rows(dy * n), sums[1] + fold_rows(dy), sums[2] + fold_rows(d)

    for name, v in zip(("gain1", "shift1", "down"), blocks(BLOCK, norm_two, (no_sum,) * 3)):
        put_small(name, v)
    save("ddn")
    fetch_next("n2", "rs2")
    ready("sl")
    reuse("dup")

    chunks = ff // CHUNK

    def dact_chunk(c):
        def piece_of(k):
            def run():
                at = pl.ds(c * CHUNK + k * PIECE, PIECE)
                up_s[c % 2, :, pl.ds(k * PIECE, PIECE)] = dot_nt(ddn_s[...], w_down[at, :])

            return run

        return [piece_of(k) for k in range(CHUNK // PIECE)]

    def slope_chunk(c):
        cols = pl.ds(c * CHUNK, CHUNK)

        def body(start, at, total):
            d = up_s[c % 2, at, :] * sl_s[at, cols].astype(F32)
            dup_s[at, cols] = d.astype(BF16)
            return total + fold_rows(d)

        return body

    def dhid_chunk(c):
        cols = pl.ds(c * CHUNK, CHUNK)

        def piece_of(k):
            def run():
                at = pl.ds(k * PIECE, PIECE)
                part = dot_nt(dup_s[:, cols], w_up[at, cols])
                acc[:, at] = part if c == 0 else acc[:, at] + part

            return run

        return [piece_of(k) for k in range(width // PIECE)]

    weight_ready(0)
    weight_ready(1)
    for dot in dact_chunk(0):
        dot()
    for c in range(chunks):
        dots = []
        if c + 1 < chunks:
            dots += dact_chunk(c + 1)
        if c > 0:
            dots += dhid_chunk(c - 1)
        put_small("up", weave(dots, BLOCK, slope_chunk(c), jnp.zeros((8, CHUNK), F32)), c * CHUNK)
    save("dup")
    fetch_next("sl")
    ready("n1", "rs1")
    reuse("dbr")

    def norm_one(start, at, sums):
        n = n1_s[at, :].astype(F32)
        t = jnp.tanh((n * gain[0:1, :] + shift[0:1, :]) * i2)
        dy = dr[at, :] + acc[at, :] * (1.0 - t * t)
        e = dy * gain[0:1, :]
        mean_e = jnp.mean(e, -1, keepdims=True)
        mean_en = jnp.mean(e * n, -1, keepdims=True)
        d = (e - mean_e - n * mean_en) * rs1_s[at, 0:1]
        dr[at, :] = d
        dbr_s[at, :] = d.astype(BF16)
        return sums[0] + fold_rows(dy * n), sums[1] + fold_rows(dy), sums[2] + fold_rows(d)

    def dhid_last(k):
        def run():
            at, cols = pl.ds(k * PIECE, PIECE), pl.ds((chunks - 1) * CHUNK, CHUNK)
            acc[at, :] += dot_nt(dup_s[at, cols], w_up[:, cols])

        return run

    dhid_last(0)()
    dots = [dhid_last(k) for k in range(1, seq // PIECE)] + [lambda: None]
    for name, v in zip(("gain0", "shift0", "out"), weave(dots, BLOCK, norm_one, (no_sum,) * 3)):
        put_small(name, v)
    save("dbr")
    fetch_next("n1", "rs1")
    ready("ctx")
    weight_ready(2)
    for k in range(width // PIECE):
        acc[:, pl.ds(k * PIECE, PIECE)] = dot_nt(dbr_s[...], w_out[pl.ds(k * PIECE, PIECE), :])
    ready("qkv", "inv")
    reuse("dproj")

    zero = jnp.zeros((), BF16)
    head_scale = jnp.asarray(HEAD_DIM ** -0.5, BF16)

    def prepare(p):
        slot = p % 2
        cols = slice(p * PAIR, (p + 1) * PAIR)

        def body(start, at, c):
            lo = lax.broadcasted_iota(jnp.int32, (OPS, PAIR), 1) < HEAD_DIM
            ctx = ctx_s[at, cols]
            t = jnp.tanh(ctx * i1)
            low = (acc[at, cols] * (1.0 - t * t) * inv_s[at, cols]).astype(BF16)
            dctx_s[slot, at, :] = low
            inner = low.astype(F32) * ctx
            whole_sum = jnp.sum(inner, -1, keepdims=True)
            lower = jnp.sum(jnp.where(lo, inner, 0.0), -1, keepdims=True)
            inner_s[slot, 0, at, :] = jnp.broadcast_to(lower, (OPS, PAIR))
            inner_s[slot, 1, at, :] = jnp.broadcast_to(whole_sum - lower, (OPS, PAIR))
            v2 = qkv_s[at, 2 * width + p * PAIR : 2 * width + (p + 1) * PAIR]
            ops_s[slot, 0, at, :] = jnp.where(lo, v2, zero)
            ops_s[slot, 1, at, :] = jnp.where(lo, zero, v2)
            return c

        blocks(OPS, body)
        q_t[slot] = (qkv_s[:, cols] * head_scale).T
        do_t[slot] = dctx_s[slot].T

    def scores(h):
        slot, side = h // 2 % 2, h % 2

        def piece_of(k):
            def run():
                keys = pl.ds(k * PIECE, PIECE)
                g_s[side, :, keys] = dot_nt(dctx_s[slot], ops_s[slot, side, keys, :])

            return run

        return [piece_of(k) for k in range(seq // PIECE)]

    def soften(h):
        slot, side = h // 2 % 2, h % 2

        def body(start, at, c):
            inner = jnp.concatenate([inner_s[slot, side, at, :]] * (seq // PAIR), 1)
            ds_s[side, at, :] = (e_s[h % 4, at, :].astype(F32) * (g_s[side, at, :] - inner)).astype(BF16)
            return c

        return body

    def collect(h):
        slot, side = h // 2 % 2, h % 2
        rows_at = slice(side * HEAD_DIM, (side + 1) * HEAD_DIM)

        def grad_v(k):
            def run():
                keys = pl.ds(k * PIECE, PIECE)
                gv_s[rows_at, keys] = dot_nn(do_t[slot, rows_at, :], e_s[h % 4, :, keys])

            return run

        def grad_k(k):
            def run():
                keys = pl.ds(k * PIECE, PIECE)
                gk_s[rows_at, keys] = dot_nn(q_t[slot, rows_at, :], ds_s[side, :, keys])

            return run

        def grad_q(k):
            def run():
                queries = pl.ds(k * PIECE, PIECE)
                keys_low = qkv_s[:, width + h // 2 * PAIR : width + (h // 2 + 1) * PAIR]
                gq_s[side, queries, :] = dot_nn(ds_s[side, queries, :], keys_low)

            return run

        return [make(k) for make in (grad_v, grad_k, grad_q) for k in range(seq // PIECE)]

    def settle(p):
        def body(start, at, c):
            lo = lax.broadcasted_iota(jnp.int32, (OPS, PAIR), 1) < HEAD_DIM
            q = jnp.where(lo, gq_s[0, at, :], gq_s[1, at, :]) * (HEAD_DIM ** -0.5)
            dproj_s[at, p * PAIR : (p + 1) * PAIR] = q.astype(BF16)
            return c

        blocks(OPS, body)
        dproj_s[:, width + p * PAIR : width + (p + 1) * PAIR] = gk_s[...].astype(BF16).T
        dproj_s[:, 2 * width + p * PAIR : 2 * width + (p + 1) * PAIR] = gv_s[...].astype(BF16).T

    heads = 2 * (width // PAIR)
    prepare(0)
    for dot in scores(0):
        dot()
    for h in range(heads):
        dots = []
        if h + 1 < heads:
            if (h + 1) % 2 == 0:
                prepare((h + 1) // 2)
            dots += scores(h + 1)
        if h > 0:
            dots += collect(h - 1)
        exp_copy(h, r).wait()
        weave(dots, BLOCK, soften(h))
        if 0 < h and h + 3 < heads:
            exp_copy(h + 3, r).start()
        if h > 0 and h % 2 == 0:
            settle(h // 2 - 1)
    for dot in collect(heads - 1):
        dot()
    settle(heads // 2 - 1)
    save("dproj")
    fetch_next("ctx", "qkv", "inv")

    @pl.when(r + 1 < rows)
    def _():
        for h in range(4):
            exp_copy(h, r + 1).start()

    weight_ready(3)
    ready("x")

    def dx_piece(k):
        def run():
            at = pl.ds(k * PIECE, PIECE)
            acc[:, at] = dot_nt(dproj_s[...], w_qkv[at, :])

        return run

    def quant_in(k):
        cols = pl.ds(k * PIECE, PIECE)
        values = pl.ds(2 * width + k * PIECE, PIECE)

        def body(start, at, sums):
            t = jnp.tanh(x_s[at, cols].astype(F32) * i0)
            gout[r, at, cols] = (dr[at, cols] + acc[at, cols] * (1.0 - t * t)).astype(BF16)
            return (
                sums[0] + fold_rows(dproj_s[at, cols].astype(F32)),
                sums[1] + fold_rows(dproj_s[at, values].astype(F32)),
            )

        return body

    dx_piece(0)()
    pieces = width // PIECE
    for k in range(pieces):
        dots = [dx_piece(k + 1)] if k + 1 < pieces else [lambda: None]
        sums = weave(dots, BLOCK, quant_in(k), (jnp.zeros((8, PIECE), F32),) * 2)
        put_small("qkv", sums[0], k * PIECE)
        put_small("qkv", sums[1], 2 * width + k * PIECE)
    fetch_next("x")

    @pl.when(jnp.logical_not(first))
    def _():
        hop(r).start()

    @pl.when(first)
    def _():
        tok_copy(r).start()

    @pl.when(r == rows - 1)
    def _():
        @pl.when(stage >= count - 2)
        def _():
            turn_left()

        for name in save_order:
            save_copy(name).wait()

        @pl.when(jnp.logical_not(first))
        def _():
            for i in range(row_count):
                hop(i).wait_send()

        @pl.when(first)
        def _():
            for i in range(row_count):
                tok_copy(i).wait()


def whole(a):
    return pl.BlockSpec(a.shape, lambda r, n=a.ndim: (0,) * n, pipeline_mode=pl.Buffered(1))


ANYWHERE = pl.BlockSpec(memory_space=pl.ANY)
SCALAR = pl.BlockSpec(memory_space=pltpu.SMEM)
VMEM_LIMIT = 60 * 1024 * 1024


def run_forward(count, tokens, lengths, scales, weights):
    w_qkv, b_qkv, w_out, b_out, w_up, b_up, w_down, b_down, gain, shift = weights
    rows, seq, width = tokens.shape
    ff = w_up.shape[1]
    big = lambda n, t: jax.ShapeDtypeStruct((rows, seq, n), t)
    saves = [
        (width, BF16), (3 * width, BF16), (width, F32), (width, F32), (width, BF16), (128, F32),
        (ff, BF16), (width, BF16), (128, F32),
    ]
    heads = width // HEAD_DIM
    lefts = [(ff, BF16), (width, BF16), (width, BF16), (width, BF16)]
    heavy = (w_qkv, w_out, w_up, w_down)
    dense = (b_qkv, b_out, b_up, b_down, gain, shift)
    tok = rows * seq
    return pl.pallas_call(
        lambda *refs: fwd_kernel(count, *refs),
        grid=(rows,),
        in_specs=[SCALAR, SCALAR, ANYWHERE] + [ANYWHERE] * 4 + [whole(a) for a in dense],
        out_specs=[ANYWHERE] * 12 + [pl.BlockSpec((4, 8, 128), lambda r: (0, 0, 0))],
        out_shape=[big(n, t) for n, t in saves]
        + [
            big(ff + 3 * width, BF16),
            jax.ShapeDtypeStruct((rows, heads, seq, seq), BF16),
            jax.ShapeDtypeStruct((rows, seq // count, width), BF16),
            jax.ShapeDtypeStruct((4, 8, 128), F32),
        ],
        scratch_shapes=[pltpu.VMEM(a.shape, a.dtype) for a in heavy]
        + [pltpu.SemaphoreType.DMA((4,))]
        + [pltpu.VMEM((rows, seq, width), BF16), pltpu.VMEM((rows, seq, width), BF16)]
        + [pltpu.VMEM((seq, n), t) for n, t in saves[1:] + lefts]
        + [
            pltpu.VMEM((seq, width), F32),
            pltpu.VMEM((seq, width), F32),
            pltpu.VMEM((2, seq, CHUNK), F32),
            pltpu.VMEM((2, 6, seq, PAIR), BF16),
            pltpu.VMEM((2, seq, seq), F32),
            pltpu.VMEM((4, seq, seq), BF16),
            pltpu.VMEM((2, seq, PAIR), F32),
            pltpu.VMEM((seq, 128), F32),
            pltpu.SemaphoreType.DMA((4,)),
            pltpu.SemaphoreType.DMA((13,)),
            pltpu.SemaphoreType.DMA((rows,)),
            pltpu.SemaphoreType.DMA((rows,)),
            pltpu.SemaphoreType.DMA((rows,)),
            pltpu.SemaphoreType.DMA((rows, count)),
            pltpu.SemaphoreType.DMA((rows,)),
        ],
        compiler_params=pltpu.CompilerParams(
            collective_id=0, has_side_effects=True, vmem_limit_bytes=VMEM_LIMIT,
            dimension_semantics=("arbitrary",),
        ),
        cost_estimate=pl.CostEstimate(
            flops=2 * tok * (4 * width * width + 2 * width * ff + 2 * seq * width),
            bytes_accessed=tok * 28000, transcendentals=tok * 3 * ff,
        ),
    )(lengths, scales, tokens, *heavy, *dense)


def run_backward(count, seeds, lengths, scales, weights, kept):
    w_qkv, b_qkv, w_out, b_out, w_up, b_up, w_down, b_down, gain, shift = weights
    *loads, left, exps = kept
    rows, seq, width = seeds.shape
    ff = w_up.shape[1]
    big = lambda n, t: jax.ShapeDtypeStruct((rows, seq, n), t)
    saves = [(3 * width, BF16), (width, BF16), (ff, BF16), (width, BF16)]
    heavy = (w_qkv, w_out, w_up, w_down)
    dense = (gain, shift)
    tok = rows * seq
    small = 6 * width + ff + 3 * width
    return pl.pallas_call(
        lambda *refs: bwd_kernel(count, *refs),
        grid=(rows,),
        in_specs=[SCALAR, SCALAR, ANYWHERE] + [ANYWHERE] * 4 + [whole(a) for a in dense] + [ANYWHERE] * 11,
        out_specs=[ANYWHERE] * 6 + [pl.BlockSpec((8, small), lambda r: (0, 0))],
        out_shape=[big(n, t) for n, t in saves]
        + [
            big(width, BF16), jax.ShapeDtypeStruct((left.shape[2], rows * seq), BF16),
            jax.ShapeDtypeStruct((8, small), F32),
        ],
        scratch_shapes=[pltpu.VMEM(a.shape, a.dtype) for a in heavy]
        + [
            pltpu.SemaphoreType.DMA((4,)),
            pltpu.VMEM((2, seq, width), BF16),
            pltpu.VMEM((2, width, seq), BF16),
            pltpu.SemaphoreType.DMA((2,)),
            pltpu.SemaphoreType.DMA((2,)),
        ]
        + [pltpu.VMEM((rows, seq, width), BF16), pltpu.VMEM((rows, seq, width), BF16)]
        + [pltpu.VMEM(a.shape[1:], a.dtype) for a in loads]
        + [pltpu.VMEM((seq, n), t) for n, t in saves]
        + [
            pltpu.VMEM((2, seq, PAIR), BF16),
            pltpu.VMEM((seq, width), F32),
            pltpu.VMEM((seq, width), F32),
            pltpu.VMEM((2, seq, CHUNK), F32),
            pltpu.VMEM((2, 2, seq, PAIR), BF16),
            pltpu.VMEM((4, seq, seq), BF16),
            pltpu.VMEM((2, seq, seq), F32),
            pltpu.VMEM((2, seq, seq), BF16),
            pltpu.VMEM((PAIR, seq), F32),
            pltpu.VMEM((PAIR, seq), F32),
            pltpu.VMEM((2, seq, PAIR), F32),
            pltpu.VMEM((2, PAIR, seq), BF16),
            pltpu.VMEM((2, PAIR, seq), BF16),
            pltpu.VMEM((2, 2, seq, PAIR), F32),
            pltpu.SemaphoreType.DMA((4,)),
            pltpu.SemaphoreType.DMA((9,)),
            pltpu.SemaphoreType.DMA((4,)),
            pltpu.SemaphoreType.DMA((rows,)),
            pltpu.SemaphoreType.DMA((rows,)),
            pltpu.SemaphoreType.DMA((rows,)),
            pltpu.SemaphoreType.DMA((rows,)),
        ],
        compiler_params=pltpu.CompilerParams(
            collective_id=1, has_side_effects=True, vmem_limit_bytes=VMEM_LIMIT,
            dimension_semantics=("arbitrary",),
        ),
        cost_estimate=pl.CostEstimate(
            flops=2 * tok * (4 * width * width + 2 * width * ff + 5 * seq * width),
            bytes_accessed=tok * 28000, transcendentals=tok * ff,
        ),
    )(lengths, scales, seeds, *heavy, *dense, left, *loads, exps)


def ring_to_dp(pos, n):
    return jnp.where(pos < n // 2, 2 * pos, 2 * (n - pos) - 1)


def dp_to_ring(j, n):
    return jnp.where(j % 2 == 0, j // 2, n - 1 - j // 2)


def grad_kernel(count, n, *refs):
    (
        left, ddn, dup, dproj, dbr, small, g0,
        gq_o, go_o, gu_o, gd_o, small_o, gtok_o,
        slots_d, slots_u, slots_q, slots_s, wide_v, thin_v, ddn_v, dup_v, dpo_v,
        wide_sem, thin_sem, right_sem,
        send_d, recv_d, send_u, recv_u, send_q, recv_q, send_s, recv_s, tok_send, tok_recv,
    ) = refs
    width = ddn.shape[1]
    ff = dup.shape[1]
    shard, shard_ff = width // n, ff // n
    row_count, seq = g0.shape[0], g0.shape[1]
    piece = seq // count
    stage = lax.axis_index("pipe")
    me = lax.axis_index("dp")
    pos = dp_to_ring(me, n)
    first = stage == 0
    ahead = ring_to_dp(lax.rem(pos + 1, n), n)
    behind = ring_to_dp(lax.rem(pos + n - 1, n), n)
    target = (ahead, behind)

    def chunk(d, step):
        at = pos + 2 * n - 1 - step if d == 0 else pos + 1 + step
        return ring_to_dp(lax.rem(at, n), n)

    def wide_copy(d, step):
        rows = pl.ds(pl.multiple_of(chunk(d, step) * shard_ff, 16), shard_ff)
        return pltpu.make_async_copy(left.at[rows, :], wide_v.at[d], wide_sem.at[d])

    def thin_copy(k, d, step):
        rows = pl.ds(pl.multiple_of(ff + k * width + chunk(d, step) * shard, 16), shard)
        return pltpu.make_async_copy(left.at[rows, :], thin_v.at[k, d], thin_sem.at[k, d])

    rights = [
        (ddn, ddn_v), (dup, dup_v), (dproj, dpo_v.at[:, pl.ds(0, 3 * width)]),
        (dbr, dpo_v.at[:, pl.ds(3 * width, width)]),
    ]

    def right_copy(k):
        return pltpu.make_async_copy(rights[k][0], rights[k][1], right_sem.at[k])

    for d in range(2):
        wide_copy(d, 0).start()
    right_copy(0).start()
    right_copy(1).start()
    for d in range(2):
        thin_copy(0, d, 0).start()
    right_copy(2).start()
    right_copy(3).start()
    for d in range(2):
        thin_copy(1, d, 0).start()
        if d == 1:
            thin_copy(2, d, 0).start()

    barrier = pltpu.get_barrier_semaphore()
    for peer in target:
        pl.semaphore_signal(barrier, inc=1, device_id={"dp": peer}, device_id_type=LOGICAL)

    @pl.when(first)
    def _():
        pl.semaphore_wait(barrier, 1 + count)

    @pl.when(jnp.logical_not(first))
    def _():
        pl.semaphore_signal(barrier, inc=1, device_id={"pipe": jnp.int32(0)}, device_id_type=LOGICAL)
        pl.semaphore_wait(barrier, 2)

    def tok_part(i, p):
        return pltpu.make_async_remote_copy(
            src_ref=g0.at[i, pl.ds(p * piece, piece)], dst_ref=gtok_o.at[i],
            send_sem=tok_send.at[i, p], recv_sem=tok_recv.at[i],
            device_id={"pipe": jnp.int32(p)}, device_id_type=LOGICAL,
        )

    def tok_own(i):
        return pltpu.make_async_copy(g0.at[i, pl.ds(0, piece)], gtok_o.at[i], tok_send.at[i, 0])

    @pl.when(first)
    def _():
        for i in range(row_count):
            for p in range(1, count):
                tok_part(i, p).start()
            tok_own(i).start()

    def message(slots, send, recv, d, at):
        return pltpu.make_async_remote_copy(
            src_ref=slots.at[d, at], dst_ref=slots.at[d, jnp.minimum(at + 1, n - 1)],
            send_sem=send.at[d, at], recv_sem=recv.at[d, jnp.minimum(at + 1, n - 1)],
            device_id={"dp": target[d]}, device_id_type=LOGICAL,
        )

    def arrived(slots, send, recv, d, at):
        return pltpu.make_async_remote_copy(
            src_ref=slots.at[d, at], dst_ref=slots.at[d, at],
            send_sem=send.at[d, at], recv_sem=recv.at[d, at],
            device_id={"dp": target[d]}, device_id_type=LOGICAL,
        )

    def lane(slots, send, recv, d, step, mine, finish):
        @pl.when(step == 0)
        def _():
            slots[d, 0] = mine.astype(BF16)

        @pl.when(step > 0)
        def _():
            arrived(slots, send, recv, d, step).wait_recv()

            @pl.when(step < n - 1)
            def _():
                slots[d, step] = (slots[d, step].astype(F32) + mine).astype(BF16)

            @pl.when(step == n - 1)
            def _():
                finish(slots[d, step].astype(F32) + mine)

        @pl.when(step < n - 1)
        def _():
            message(slots, send, recv, d, step).start()

    def small_message(at):
        return pltpu.make_async_remote_copy(
            src_ref=slots_s.at[at], dst_ref=slots_s.at[jnp.minimum(at + 1, n - 1)],
            send_sem=send_s.at[at], recv_sem=recv_s.at[jnp.minimum(at + 1, n - 1)],
            device_id={"dp": target[0]}, device_id_type=LOGICAL,
        )

    def small_arrived(at):
        return pltpu.make_async_remote_copy(
            src_ref=slots_s.at[at], dst_ref=slots_s.at[at], send_sem=send_s.at[at],
            recv_sem=recv_s.at[at], device_id={"dp": target[0]}, device_id_type=LOGICAL,
        )

    sum_rows = lax.broadcasted_iota(jnp.int32, (16, 128), 0) < 9

    def small_step(step):
        mine = small[chunk(0, step)]

        @pl.when(step == 0)
        def _():
            slots_s[0] = mine

        @pl.when(step > 0)
        def _():
            small_arrived(step).wait_recv()
            got = slots_s[step]
            slots_s[step] = jnp.where(sum_rows, got + mine, jnp.maximum(got, mine))

        @pl.when(step < n - 1)
        def _():
            small_message(step).start()

        @pl.when(step == n - 1)
        def _():
            small_o[...] = slots_s[step]

    half, half_ff = width // 2, ff // 2

    def fetched(copy, step, *args):
        copy(*args, step).wait()

    def refill(copy, step, *args):
        @pl.when(step < n - 1)
        def _():
            copy(*args, step + 1).start()

    def right_ready(k, step):
        @pl.when(step == 0)
        def _():
            right_copy(k).wait()

    def turn(step, _):
        right_ready(0, step)
        for d in range(2):
            cols = slice(d * half, (d + 1) * half)
            fetched(wide_copy, step, d)
            mine = dot_nn(wide_v[d], ddn_v[:, cols])
            refill(wide_copy, step, d)

            def finish_down(total):
                gd_o[:, cols] = total

            lane(slots_d, send_d, recv_d, d, step, mine, finish_down)
        small_step(step)
        right_ready(1, step)
        for d in range(2):
            cols = slice(d * half_ff, (d + 1) * half_ff)
            fetched(thin_copy, step, 0, d)
            mine = dot_nn(thin_v[0, d], dup_v[:, cols])
            refill(thin_copy, step, 0, d)

            def finish_up(total):
                gu_o[:, cols] = total

            lane(slots_u, send_u, recv_u, d, step, mine, finish_up)
        right_ready(2, step)
        right_ready(3, step)
        fetched(thin_copy, step, 1, 0)
        mine = dot_nn(thin_v[1, 0], dpo_v[:, 0 : 2 * width])
        refill(thin_copy, step, 1, 0)

        def finish_ahead(total):
            gq_o[:, 0 : 2 * width] = total

        lane(slots_q, send_q, recv_q, 0, step, mine, finish_ahead)
        fetched(thin_copy, step, 1, 1)
        fetched(thin_copy, step, 2, 1)
        mine = jnp.concatenate(
            [
                dot_nn(thin_v[1, 1], dpo_v[:, 2 * width : 3 * width]),
                dot_nn(thin_v[2, 1], dpo_v[:, 3 * width : 4 * width]),
            ],
            1,
        )
        refill(thin_copy, step, 1, 1)
        refill(thin_copy, step, 2, 1)

        def finish_behind(total):
            gq_o[:, 2 * width : 3 * width] = total[:, 0:width]
            go_o[...] = total[:, width : 2 * width]

        lane(slots_q, send_q, recv_q, 1, step, mine, finish_behind)
        return 0

    lax.fori_loop(0, n, turn, 0)

    def drain(at, _):
        for d in range(2):
            message(slots_d, send_d, recv_d, d, at).wait_send()
            message(slots_u, send_u, recv_u, d, at).wait_send()
            message(slots_q, send_q, recv_q, d, at).wait_send()
        small_message(at).wait_send()
        return 0

    lax.fori_loop(0, n - 1, drain, 0)

    @pl.when(first)
    def _():
        for i in range(row_count):
            for p in range(1, count):
                tok_part(i, p).wait_send()
            tok_own(i).wait()

    @pl.when(jnp.logical_not(first))
    def _():
        for i in range(row_count):
            tok_part(i, 1).wait_recv()


def run_grads(count, n, left, dproj, dbr, dup, ddn, g0, small):
    rows, seq, width = g0.shape
    ff = dup.shape[2]
    flat = lambda a: a.reshape(rows * seq, a.shape[2])
    tok = rows * seq
    shard, shard_ff = width // n, ff // n
    ops = [left] + [flat(a) for a in (ddn, dup, dproj, dbr)]
    vmem = pl.BlockSpec(memory_space=pltpu.VMEM)
    sem = pltpu.SemaphoreType.DMA
    return pl.pallas_call(
        lambda *refs: grad_kernel(count, n, *refs),
        in_specs=[ANYWHERE] * 5 + [vmem, ANYWHERE],
        out_specs=[vmem] * 5 + [ANYWHERE],
        out_shape=[
            jax.ShapeDtypeStruct((shard, 3 * width), F32),
            jax.ShapeDtypeStruct((shard, width), F32),
            jax.ShapeDtypeStruct((shard, ff), F32),
            jax.ShapeDtypeStruct((shard_ff, width), F32),
            jax.ShapeDtypeStruct((16, 128), F32),
            jax.ShapeDtypeStruct((rows, seq // count, width), BF16),
        ],
        scratch_shapes=[
            pltpu.VMEM((2, n, shard_ff, width // 2), BF16),
            pltpu.VMEM((2, n, shard, ff // 2), BF16),
            pltpu.VMEM((2, n, shard, 2 * width), BF16),
            pltpu.VMEM((n, 16, 128), F32),
            pltpu.VMEM((2, shard_ff, tok), BF16),
            pltpu.VMEM((3, 2, shard, tok), BF16),
            pltpu.VMEM((tok, width), BF16),
            pltpu.VMEM((tok, ff), BF16),
            pltpu.VMEM((tok, 4 * width), BF16),
            sem((2,)), sem((3, 2)), sem((4,)),
            sem((2, n)), sem((2, n)), sem((2, n)), sem((2, n)), sem((2, n)), sem((2, n)),
            sem((n,)), sem((n,)), sem((rows, count)), sem((rows,)),
        ],
        compiler_params=pltpu.CompilerParams(
            collective_id=2, has_side_effects=True, vmem_limit_bytes=VMEM_LIMIT,
        ),
        cost_estimate=pl.CostEstimate(
            flops=2 * tok * (4 * width * width + 2 * width * ff), bytes_accessed=tok * 25000, transcendentals=0,
        ),
    )(*ops, small, g0)


def weight_grad(left, right):
    g = jnp.einsum("rsd,rse->de", left, right, preferred_element_type=F32).astype(BF16)
    return lax.psum_scatter(g, "dp", scatter_dimension=0, tiled=True).astype(F32)


def share_pieces(whole_rows, count, stage):
    piece = whole_rows.shape[1] // count
    mine = whole_rows[:, :piece]
    for p in range(1, count):
        got = lax.ppermute(whole_rows[:, p * piece : (p + 1) * piece], "pipe", [(0, p)])
        mine = jnp.where(stage == p, got, mine)
    return mine


def shards(
    tokens, lengths, ema_scales, w_qkv, bias_qv, w_out, bias_out, w_up, bias_up, w_down, bias_down,
    ln_gain, ln_bias, cotangent,
):
    count = lax.axis_size("pipe")
    n = lax.axis_size("dp")
    width = tokens.shape[2]
    ff = w_up.shape[2]
    b_qkv = jnp.concatenate([bias_qv[:, :width], jnp.zeros_like(bias_qv[:, :width]), bias_qv[:, width:]], 1)
    weights = (
        w_qkv[0], b_qkv, w_out[0], bias_out, w_up[0], bias_up, w_down[0], bias_down, ln_gain[0], ln_bias[0],
    )
    *kept, mixed, peaks = run_forward(count, tokens, lengths, ema_scales, weights)
    left = kept[-2]
    dproj, dbr, dup, ddn, g0, turned, small = run_backward(
        count, cotangent, lengths, ema_scales, weights, kept
    )
    sums = jnp.sum(small, 0)
    parts, at = [], 0
    for size in (width, width, width, width, width, width, ff, width, width, width):
        parts.append(sums[at : at + size])
        at += size
    parts[7:] = [jnp.concatenate([parts[7], parts[9]])]
    packed = jnp.concatenate([v.reshape(n, -1) for v in parts], 1)
    peak = jnp.max(peaks, (1, 2))
    sums_width = packed.shape[1]
    if n >= 4 and n % 2 == 0 and width // n % 16 == 0 and ff // n % 128 == 0 and sums_width == 9 * 128:
        top = jnp.broadcast_to(jnp.pad(peak, (0, 124))[None, None], (n, 7, 128))
        with_peak = jnp.concatenate([packed.reshape(n, 9, 128), top], 1)
        g_qkv, g_out, g_up, g_down, small_sum, grad_tokens = run_grads(
            count, n, turned, dproj, dbr, dup, ddn, g0, with_peak
        )
        mine = small_sum[:9].reshape(1, sums_width)
        batch_max = small_sum[9:10, :4]
    else:
        g_down = weight_grad(left[:, :, :ff], ddn)
        g_up = weight_grad(left[:, :, ff : ff + width], dup)
        g_qkv = weight_grad(left[:, :, ff + width : ff + 2 * width], dproj)
        g_out = weight_grad(left[:, :, ff + 2 * width :], dbr)
        mine = lax.psum_scatter(packed, "dp", scatter_dimension=0, tiled=True)
        batch_max = lax.pmax(peak, "dp")[None]
        grad_tokens = share_pieces(g0, count, lax.axis_index("pipe"))
    outs, at = [], 0
    for size in (width, width, width, width, width, width, ff, 2 * width):
        outs.append(mine[:, at : at + size // n])
        at += size // n
    gain0, gain1, shift0, shift1, s_out, s_down, s_up, s_qv = outs
    g_gain = jnp.stack([gain0, gain1], 1)
    g_shift = jnp.stack([shift0, shift1], 1)
    return (
        mixed, grad_tokens, g_qkv[None], s_qv, g_out[None], s_out, g_up[None], s_up, g_down[None], s_down,
        g_gain, g_shift, batch_max,
    )


def solution(mesh):
    return jax.shard_map(
        shards,
        mesh=mesh,
        in_specs=(
            P("dp", None, None), P("dp"), P("pipe", None), P("pipe", None, None), P("pipe", None),
            P("pipe", None, None), P("pipe", None), P("pipe", None, None), P("pipe", None),
            P("pipe", None, None), P("pipe", None), P("pipe", None, None), P("pipe", None, None),
            P("dp", None, None),
        ),
        out_specs=(
            P("dp", "pipe", None), P("dp", "pipe", None), P("pipe", "dp", None), P("pipe", "dp"),
            P("pipe", "dp", None), P("pipe", "dp"), P("pipe", "dp", None), P("pipe", "dp"),
            P("pipe", "dp", None), P("pipe", "dp"), P("pipe", None, "dp"), P("pipe", None, "dp"),
            P("pipe", None),
        ),
        check_vma=False,
    )
```

```python
import jax
import jax.numpy as jnp
from jax import lax
from jax.experimental import pallas as pl
from jax.experimental.pallas import tpu as pltpu
from jax.sharding import PartitionSpec as P

HEAD_DIM = 64
PAIR = 2 * HEAD_DIM
EPS = 1e-06
MASKED = -1000000000.0
CHUNK = 512
PIECE = 256
BLOCK = 16
OPS = 64
LOGICAL = pl.DeviceIdType.MESH
F32 = jnp.float32
BF16 = jnp.bfloat16

ERF_POLY = (
    0.7978823511659165,
    0.03634481045269742,
    -4.5110171354091134e-05,
    -5.02654469142584e-05,
    3.0867937984305273e-06,
    -6.60140005994544e-08,
)
ERF_CLAMP = 5.2 * 5.2
HALF_LOG2E = -0.7213475204444817
LOG2_DENSITY = -1.3257480647361593


def dot_nn(a, b):
    return jnp.dot(a, b, preferred_element_type=F32)


def dot_nt(a, b):
    return lax.dot_general(a, b, (((1,), (1,)), ((), ())), preferred_element_type=F32)


def dot_tn(a, b):
    return lax.dot_general(a, b, (((0,), (0,)), ((), ())), preferred_element_type=F32)


def fold_rows(v):
    return jnp.sum(v.reshape(v.shape[0] // 8, 8, v.shape[1]), 0)


def peak_rows(v):
    tiles = [v[:, i : i + 128] for i in range(0, v.shape[1], 128)]
    top = tiles[0]
    for tile in tiles[1:]:
        top = jnp.maximum(top, tile)
    return jnp.max(top.reshape(v.shape[0] // 8, 8, 128), 0)


def greet(stage, count):
    barrier = pltpu.get_barrier_semaphore()
    for step in range(1, count):
        peer = lax.rem(stage + step, count)
        pl.semaphore_signal(barrier, inc=1, device_id={"pipe": peer}, device_id_type=LOGICAL)
    pl.semaphore_wait(barrier, count - 1)


def activation(u, ceiling, inv_ceiling):
    square = u * u
    w = jnp.minimum(square, ERF_CLAMP)
    poly = w * ERF_POLY[-1] + ERF_POLY[-2]
    for coef in ERF_POLY[-3::-1]:
        poly = poly * w + coef
    t = jnp.tanh(u * poly)
    half = 0.5 * u
    act = half + half * t
    ratio = jnp.tanh(act * inv_ceiling)
    density = jnp.exp2(square * HALF_LOG2E + LOG2_DENSITY)
    slope = (1.0 - ratio * ratio) * ((0.5 + 0.5 * t) + u * density)
    return act, ceiling * ratio, slope


def fwd_kernel(count, *refs):
    (
        lens, scales, tokens, h_qkv, h_out, h_up, h_down, b_qkv, b_out, b_up, b_down, gain, shift,
        x_o, qkv_o, inv_o, ctx_o, n1_o, rs1_o, sl_o, n2_o, rs2_o, left_o, exp_o,
        mixed_o, peaks_o,
        w_qkv, w_out, w_up, w_down, w_sem,
        xin, xout, qkv_s, inv_s, ctx_s, n1_s, rs1_s, sl_s, n2_s, rs2_s, aq_s, hq_s, xq_s, cq_s,
        acc, hid, up_s, ops_s, s_s, e_s, o_s, amax_s,
        save_sem, in_sem, send_sem, recv_sem, mix_send, mix_recv,
    ) = refs
    r = pl.program_id(0)
    rows = pl.num_programs(0)
    row_count = tokens.shape[0]
    seq, width = tokens.shape[1], tokens.shape[2]
    ff = w_up.shape[1]
    piece = seq // count
    stage = lax.axis_index("pipe")
    first = stage == 0
    last = stage == count - 1

    left = {"aq": (0, ff), "hq": (ff, width), "xq": (ff + width, width), "cq": (ff + 2 * width, width)}
    staged = {
        "x": (xin.at[r], x_o), "qkv": (qkv_s, qkv_o), "inv": (inv_s, inv_o), "ctx": (ctx_s, ctx_o),
        "n1": (n1_s, n1_o), "rs1": (rs1_s, rs1_o), "sl": (sl_s, sl_o), "n2": (n2_s, n2_o),
        "rs2": (rs2_s, rs2_o), "aq": (aq_s, left_o), "hq": (hq_s, left_o), "xq": (xq_s, left_o),
        "cq": (cq_s, left_o), "exp": (e_s, exp_o),
    }
    order = list(staged)
    early = ("x", "xq", "qkv", "inv", "ctx", "cq", "exp")
    late = ("n1", "rs1", "hq", "aq", "sl", "n2", "rs2")
    fetches = [(h_qkv, w_qkv), (h_out, w_out), (h_up, w_up), (h_down, w_down)]

    def weight_copy(k):
        return pltpu.make_async_copy(fetches[k][0], fetches[k][1], w_sem.at[k])

    def save_copy(name):
        src, dst = staged[name]
        dst = dst.at[r]
        if name in left:
            dst = dst.at[:, pl.ds(*left[name])]
        return pltpu.make_async_copy(src, dst, save_sem.at[order.index(name)])

    def token_copy(i):
        return pltpu.make_async_copy(tokens.at[i], xin.at[i], in_sem.at[i])

    def hop(i):
        return pltpu.make_async_remote_copy(
            src_ref=xout.at[i], dst_ref=xin.at[i], send_sem=send_sem.at[i], recv_sem=recv_sem.at[i],
            device_id={"pipe": lax.rem(stage + 1, count)}, device_id_type=LOGICAL,
        )

    def mix_part(i, p):
        return pltpu.make_async_remote_copy(
            src_ref=xout.at[i, pl.ds(p * piece, piece)], dst_ref=mixed_o.at[i],
            send_sem=mix_send.at[i, p], recv_sem=mix_recv.at[i],
            device_id={"pipe": jnp.int32(p)}, device_id_type=LOGICAL,
        )

    def mix_own(i):
        return pltpu.make_async_copy(
            xout.at[i, pl.ds((count - 1) * piece, piece)], mixed_o.at[i], mix_send.at[i, count - 1]
        )

    @pl.when(r == 0)
    def _():
        greet(stage, count)
        peaks_o[...] = jnp.zeros_like(peaks_o)
        for k in range(4):
            weight_copy(k).start()

        @pl.when(first)
        def _():
            for i in range(row_count):
                token_copy(i).start()

    @pl.when(first)
    def _():
        token_copy(r).wait()

    @pl.when(jnp.logical_not(first))
    def _():
        hop(r).wait_recv()

    length = lens[r]
    m0, m1, m2, m3 = scales[0, 0], scales[0, 1], scales[0, 2], scales[0, 3]
    i0, i1, i2, i3 = 1.0 / m0, 1.0 / m1, 1.0 / m2, 1.0 / m3

    def row_mask(start, size):
        return (start + lax.broadcasted_iota(jnp.int32, (size, 1), 0)) < length

    def blocks(size, body, init=0, begin=0, end=seq):
        step = lambda i, c: body(i * size, pl.ds(i * size, size), c)
        return lax.fori_loop(begin // size, end // size, step, init, unroll=True)

    def weave(dots, size, body, init=0):
        total, cut = seq // size, 0
        for k, dot in enumerate(dots):
            dot()
            begin, cut = cut, total * (k + 1) // len(dots)
            init = blocks(size, body, init, begin * size, cut * size)
        return init

    no_peak = jnp.zeros((8, 128), F32)

    @pl.when(r > 0)
    def _():
        for name in early:
            save_copy(name).wait()

    @pl.when(r == 0)
    def _():
        weight_copy(0).wait()

    def quant_in(start, at, top):
        x = xin[r, at, :].astype(F32)
        xq_s[at, :] = (m0 * jnp.tanh(x * i0)).astype(BF16)
        return jnp.maximum(top, masked_peak(x, start))

    def masked_peak(v, start):
        return peak_rows(jnp.where(row_mask(start, v.shape[0]), jnp.abs(v), 0.0))

    peaks_o[0] = jnp.maximum(peaks_o[0], blocks(BLOCK, quant_in, no_peak))
    for j in range(3):
        cols = pl.ds(j * width, width)
        proj = dot_nn(xq_s[...], w_qkv[:, cols]) + b_qkv[:, cols]
        qkv_s[:, cols] = proj.astype(BF16)

    one = jnp.ones((), BF16)
    zero = jnp.zeros((), BF16)
    head_scale = jnp.asarray(HEAD_DIM ** -0.5, BF16)

    def prepare(p):
        slot = p % 2

        def body(start, at, c):
            lane = lax.broadcasted_iota(jnp.int32, (OPS, PAIR), 1)
            lo = lane < HEAD_DIM
            spot = jnp.where(lo, lane, lane - HEAD_DIM)
            bias = jnp.where(row_mask(start, OPS), 0.0, MASKED)
            extra = jnp.where(spot == 0, jnp.broadcast_to(bias, (OPS, PAIR)), 0.0).astype(BF16)
            q2 = qkv_s[at, p * PAIR : (p + 1) * PAIR] * head_scale
            k2 = qkv_s[at, width + p * PAIR : width + (p + 1) * PAIR]
            v2 = qkv_s[at, 2 * width + p * PAIR : 2 * width + (p + 1) * PAIR]
            ops_s[slot, 0, at, :] = jnp.where(lo, q2, one)
            ops_s[slot, 1, at, :] = jnp.where(lo, one, q2)
            ops_s[slot, 2, at, :] = jnp.where(lo, k2, extra)
            ops_s[slot, 3, at, :] = jnp.where(lo, extra, k2)
            ops_s[slot, 4, at, :] = jnp.where(lo, v2, one)
            ops_s[slot, 5, at, :] = jnp.where(lo, one, v2)
            return c

        blocks(OPS, body)

    def scores(h):
        p, side = h // 2, h % 2

        def piece_of(k):
            def run():
                keys = pl.ds(k * PIECE, PIECE)
                s_s[side, :, keys] = dot_nt(ops_s[p % 2, side], ops_s[p % 2, 2 + side, keys, :])

            return run

        return [piece_of(k) for k in range(seq // PIECE)]

    def soften(h):
        def body(start, at, c):
            s = s_s[h % 2, at, :]
            e_s[h, at, :] = jnp.exp(s - jnp.max(s, -1, keepdims=True)).astype(BF16)
            return c

        return body

    def collect(h):
        p, side = h // 2, h % 2

        def piece_of(k):
            def run():
                queries = pl.ds(k * PIECE, PIECE)
                o_s[side, queries, :] = dot_nn(e_s[h, queries, :], ops_s[p % 2, 4 + side])

            return run

        return [piece_of(k) for k in range(seq // PIECE)]

    def settle(p, peak):
        cols = slice(p * PAIR, (p + 1) * PAIR)

        def body(start, at, top):
            lo = lax.broadcasted_iota(jnp.int32, (OPS, PAIR), 1) < HEAD_DIM
            o_a, o_b = o_s[0, at, :], o_s[1, at, :]
            total = pltpu.roll(jnp.where(lo, o_b, o_a), HEAD_DIM, 1)
            inverse = 1.0 / total
            c = jnp.where(lo, o_a, o_b) * inverse
            inv_s[at, cols] = inverse
            ctx_s[at, cols] = c
            cq_s[at, cols] = (m1 * jnp.tanh(c * i1)).astype(BF16)
            return jnp.maximum(top, masked_peak(c, start))

        return blocks(OPS, body, peak)

    heads = 2 * (width // PAIR)
    peak = no_peak
    prepare(0)
    for dot in scores(0):
        dot()
    for h in range(heads):
        dots = []
        if h + 1 < heads:
            if (h + 1) % 2 == 0:
                prepare((h + 1) // 2)
            dots += scores(h + 1)
        if h > 0:
            dots += collect(h - 1)
        weave(dots, BLOCK, soften(h))
        if h > 0 and h % 2 == 0:
            peak = settle(h // 2 - 1, peak)
    for dot in collect(heads - 1):
        dot()
    peak = settle(heads // 2 - 1, peak)
    peaks_o[1] = jnp.maximum(peaks_o[1], peak)

    for name in early:
        save_copy(name).start()

    @pl.when(r > 0)
    def _():
        for name in late:
            save_copy(name).wait()

    @pl.when(r == 0)
    def _():
        for k in (1, 2, 3):
            weight_copy(k).wait()

    def out_piece(k):
        def run():
            at = pl.ds(k * PIECE, PIECE)
            acc[at, :] = dot_nn(cq_s[at, :], w_out[...])

        return run

    def norm_one(start, at, top):
        s = xin[r, at, :].astype(F32) + (acc[at, :] + b_out[...])
        center = s - jnp.mean(s, -1, keepdims=True)
        rs = lax.rsqrt(jnp.mean(center * center, -1, keepdims=True) + EPS)
        n = center * rs
        h = n * gain[0:1, :] + shift[0:1, :]
        n1_s[at, :] = n.astype(BF16)
        rs1_s[at, :] = jnp.broadcast_to(rs, (BLOCK, 128))
        hid[at, :] = h
        hq_s[at, :] = (m2 * jnp.tanh(h * i2)).astype(BF16)
        return jnp.maximum(top, masked_peak(h, start))

    out_piece(0)()
    top = weave([out_piece(k) for k in range(1, seq // PIECE)] + [lambda: None], BLOCK, norm_one, no_peak)
    peaks_o[2] = jnp.maximum(peaks_o[2], top)

    chunks = ff // CHUNK

    def up_chunk(c):
        def piece_of(k):
            def run():
                part = dot_nn(hq_s[...], w_up[:, pl.ds(c * CHUNK + k * PIECE, PIECE)])
                up_s[c % 2, :, pl.ds(k * PIECE, PIECE)] = part

            return run

        return [piece_of(k) for k in range(CHUNK // PIECE)]

    def act_chunk(c):
        cols = pl.ds(c * CHUNK, CHUNK)

        def body(start, at, carry):
            act, low, slope = activation(up_s[c % 2, at, :] + b_up[:, cols], m3, i3)
            aq_s[at, cols] = low.astype(BF16)
            sl_s[at, cols] = slope.astype(BF16)
            size = jnp.abs(act)
            top = size[:, 0:128]
            for i in range(128, CHUNK, 128):
                top = jnp.maximum(top, size[:, i : i + 128])
            amax_s[at, :] = top if c == 0 else jnp.maximum(amax_s[at, :], top)
            return carry

        return body

    def down_chunk(c):
        def piece_of(k):
            def run():
                cols = pl.ds(k * PIECE, PIECE)
                part = dot_nn(aq_s[:, pl.ds(c * CHUNK, CHUNK)], w_down[pl.ds(c * CHUNK, CHUNK), cols])
                acc[:, cols] = part if c == 0 else acc[:, cols] + part

            return run

        return [piece_of(k) for k in range(width // PIECE)]

    for dot in up_chunk(0):
        dot()
    for c in range(chunks):
        dots = []
        if c + 1 < chunks:
            dots += up_chunk(c + 1)
        if c > 0:
            dots += down_chunk(c - 1)
        weave(dots, BLOCK, act_chunk(c))
    peaks_o[3] = jnp.maximum(peaks_o[3], masked_peak(amax_s[...], 0))

    def norm_two(start, at, c):
        s = hid[at, :] + (acc[at, :] + b_down[...])
        center = s - jnp.mean(s, -1, keepdims=True)
        rs = lax.rsqrt(jnp.mean(center * center, -1, keepdims=True) + EPS)
        n = center * rs
        n2_s[at, :] = n.astype(BF16)
        rs2_s[at, :] = jnp.broadcast_to(rs, (BLOCK, 128))
        xout[r, at, :] = (n * gain[1:2, :] + shift[1:2, :]).astype(BF16)
        return c

    def down_last(k):
        def run():
            at, cols = pl.ds(k * PIECE, PIECE), pl.ds((chunks - 1) * CHUNK, CHUNK)
            acc[at, :] += dot_nn(aq_s[at, cols], w_down[cols, :])

        return run

    down_last(0)()
    weave([down_last(k) for k in range(1, seq // PIECE)] + [lambda: None], BLOCK, norm_two)
    for name in late:
        save_copy(name).start()

    @pl.when(jnp.logical_not(last))
    def _():
        hop(r).start()

    @pl.when(last)
    def _():
        for p in range(count - 1):
            mix_part(r, p).start()
        mix_own(r).start()

    @pl.when(r == rows - 1)
    def _():
        for name in order:
            save_copy(name).wait()

        @pl.when(jnp.logical_not(last))
        def _():
            for i in range(row_count):
                hop(i).wait_send()
            for i in range(row_count):
                mix_part(i, 0).wait_recv()

        @pl.when(last)
        def _():
            for i in range(row_count):
                for p in range(count - 1):
                    mix_part(i, p).wait_send()
                mix_own(i).wait()


def bwd_kernel(count, *refs):
    (
        lens, scales, seeds, h_qkv, h_out, h_up, h_down, gain, shift, left_i,
        x_i, qkv_i, inv_i, ctx_i, n1_i, rs1_i, sl_i, n2_i, rs2_i, exp_i,
        dproj_o, dbr_o, dup_o, ddn_o, gtok_o, left_o, small_o,
        w_qkv, w_out, w_up, w_down, w_sem, turn_in, turn_out, turn_in_sem, turn_out_sem,
        gin, x_s, qkv_s, inv_s, ctx_s, n1_s, rs1_s, sl_s, n2_s, rs2_s, e_s,
        dproj_s, dbr_s, dup_s, ddn_s, dctx_s, acc, dr,
        up_s, ops_s, g_s, ds_s, gv_s, gk_s, gq_s, q_t, do_t, inner_s,
        load_sem, save_sem, in_sem, send_sem, recv_sem, tok_send,
    ) = refs
    r = pl.program_id(0)
    rows = pl.num_programs(0)
    row_count = seeds.shape[0]
    seq, width = seeds.shape[1], seeds.shape[2]
    ff = w_up.shape[1]
    piece = seq // count
    stage = lax.axis_index("pipe")
    first = stage == 0
    last = stage == count - 1

    loaded = {
        "n2": (n2_i, n2_s), "rs2": (rs2_i, rs2_s), "sl": (sl_i, sl_s), "n1": (n1_i, n1_s),
        "rs1": (rs1_i, rs1_s), "ctx": (ctx_i, ctx_s), "qkv": (qkv_i, qkv_s), "inv": (inv_i, inv_s),
        "x": (x_i, x_s), "exp": (exp_i, e_s),
    }
    load_order = list(loaded)
    early = ("n2", "rs2", "sl", "n1", "rs1")
    late = ("ctx", "qkv", "inv", "exp", "x")
    staged = {
        "ddn": (ddn_s, ddn_o), "dup": (dup_s, dup_o), "dbr": (dbr_s, dbr_o), "dproj": (dproj_s, dproj_o),
    }
    save_order = list(staged)

    def load_copy(name, i):
        src, dst = loaded[name]
        return pltpu.make_async_copy(src.at[i], dst, load_sem.at[load_order.index(name)])

    def save_copy(name):
        src, dst = staged[name]
        return pltpu.make_async_copy(src, dst.at[r], save_sem.at[save_order.index(name)])

    def seed_copy(i):
        return pltpu.make_async_copy(seeds.at[i], gin.at[i], in_sem.at[i])

    def hop(i):
        return pltpu.make_async_remote_copy(
            src_ref=gin.at[i], dst_ref=gin.at[i], send_sem=send_sem.at[i], recv_sem=recv_sem.at[i],
            device_id={"pipe": lax.rem(stage + count - 1, count)}, device_id_type=LOGICAL,
        )

    def tok_copy(i):
        return pltpu.make_async_copy(gin.at[i], gtok_o.at[i], tok_send.at[i])

    fetches = [(h_down, w_down), (h_up, w_up), (h_out, w_out), (h_qkv, w_qkv)]

    def weight_copy(k):
        return pltpu.make_async_copy(fetches[k][0], fetches[k][1], w_sem.at[k])

    parts = left_i.shape[2] // width
    turns = row_count * parts

    def turn_load(i):
        cols = pl.ds(pl.multiple_of(i % parts * width, 128), width)
        return pltpu.make_async_copy(left_i.at[i // parts, :, cols], turn_in.at[i % 2], turn_in_sem.at[i % 2])

    def turn_store(i):
        rows_at = pl.ds(pl.multiple_of(i % parts * width, 128), width)
        cols = pl.ds(pl.multiple_of(i // parts * seq, 128), seq)
        return pltpu.make_async_copy(turn_out.at[i % 2], left_o.at[rows_at, cols], turn_out_sem.at[i % 2])

    def turn_left():
        turn_load(0).start()

        def body(i, c):
            @pl.when(i + 1 < turns)
            def _():
                turn_load(i + 1).start()

            turn_load(i).wait()

            @pl.when(i >= 2)
            def _():
                turn_store(i - 2).wait()

            turn_out[i % 2] = turn_in[i % 2].T
            turn_store(i).start()
            return c

        lax.fori_loop(0, turns, body, 0)
        turn_store(turns - 2).wait()
        turn_store(turns - 1).wait()

    @pl.when(r == 0)
    def _():
        greet(stage, count)
        small_o[...] = jnp.zeros_like(small_o)

        @pl.when(last)
        def _():
            for i in range(row_count):
                seed_copy(i).start()

        for name in ("n2", "rs2"):
            load_copy(name, 0).start()
        weight_copy(0).start()
        for name in early[2:]:
            load_copy(name, 0).start()
        for k in (1, 2, 3):
            weight_copy(k).start()
        for name in late:
            load_copy(name, 0).start()

        @pl.when(stage < count - 2)
        def _():
            turn_left()

    @pl.when(last)
    def _():
        seed_copy(r).wait()

    @pl.when(jnp.logical_not(last))
    def _():
        hop(r).wait_recv()

    length = lens[r]
    m0, m1, m2 = scales[0, 0], scales[0, 1], scales[0, 2]
    i0, i1, i2 = 1.0 / m0, 1.0 / m1, 1.0 / m2

    offsets = {}
    at_col = 0
    for name, size in (
        ("gain0", width), ("gain1", width), ("shift0", width), ("shift1", width),
        ("out", width), ("down", width), ("up", ff), ("qkv", 3 * width),
    ):
        offsets[name] = at_col
        at_col += size

    def blocks(size, body, init=0, begin=0, end=seq):
        step = lambda i, c: body(i * size, pl.ds(i * size, size), c)
        return lax.fori_loop(begin // size, end // size, step, init, unroll=True)

    def weave(dots, size, body, init=0):
        total, cut = seq // size, 0
        for k, dot in enumerate(dots):
            dot()
            begin, cut = cut, total * (k + 1) // len(dots)
            init = blocks(size, body, init, begin * size, cut * size)
        return init

    def row_mask(start, size):
        return (start + lax.broadcasted_iota(jnp.int32, (size, 1), 0)) < length

    def put_small(name, v, col=0):
        small_o[:, pl.ds(offsets[name] + col, v.shape[1])] += v

    no_sum = jnp.zeros((8, width), F32)

    for name in early:
        load_copy(name, r).wait()

    @pl.when(r > 0)
    def _():
        for name in ("ddn", "dup", "dbr"):
            save_copy(name).wait()

    @pl.when(r == 0)
    def _():
        for k in (0, 1):
            weight_copy(k).wait()

    def norm_two(start, at, sums):
        dy = jnp.where(row_mask(start, BLOCK), gin[r, at, :].astype(F32), 0.0)
        n = n2_s[at, :].astype(F32)
        e = dy * gain[1:2, :]
        mean_e = jnp.mean(e, -1, keepdims=True)
        mean_en = jnp.mean(e * n, -1, keepdims=True)
        d = (e - mean_e - n * mean_en) * rs2_s[at, 0:1]
        dr[at, :] = d
        ddn_s[at, :] = d.astype(BF16)
        return sums[0] + fold_rows(dy * n), sums[1] + fold_rows(dy), sums[2] + fold_rows(d)

    for name, v in zip(("gain1", "shift1", "down"), blocks(BLOCK, norm_two, (no_sum,) * 3)):
        put_small(name, v)

    chunks = ff // CHUNK

    def dact_chunk(c):
        def piece_of(k):
            def run():
                at = pl.ds(c * CHUNK + k * PIECE, PIECE)
                up_s[c % 2, :, pl.ds(k * PIECE, PIECE)] = dot_nt(ddn_s[...], w_down[at, :])

            return run

        return [piece_of(k) for k in range(CHUNK // PIECE)]

    def slope_chunk(c):
        cols = pl.ds(c * CHUNK, CHUNK)

        def body(start, at, total):
            d = up_s[c % 2, at, :] * sl_s[at, cols].astype(F32)
            dup_s[at, cols] = d.astype(BF16)
            return total + fold_rows(d)

        return body

    def dhid_chunk(c):
        cols = pl.ds(c * CHUNK, CHUNK)

        def piece_of(k):
            def run():
                at = pl.ds(k * PIECE, PIECE)
                part = dot_nt(dup_s[:, cols], w_up[at, cols])
                acc[:, at] = part if c == 0 else acc[:, at] + part

            return run

        return [piece_of(k) for k in range(width // PIECE)]

    for dot in dact_chunk(0):
        dot()
    for c in range(chunks):
        dots = []
        if c + 1 < chunks:
            dots += dact_chunk(c + 1)
        if c > 0:
            dots += dhid_chunk(c - 1)
        put_small("up", weave(dots, BLOCK, slope_chunk(c), jnp.zeros((8, CHUNK), F32)), c * CHUNK)

    def norm_one(start, at, sums):
        n = n1_s[at, :].astype(F32)
        t = jnp.tanh((n * gain[0:1, :] + shift[0:1, :]) * i2)
        dy = dr[at, :] + acc[at, :] * (1.0 - t * t)
        e = dy * gain[0:1, :]
        mean_e = jnp.mean(e, -1, keepdims=True)
        mean_en = jnp.mean(e * n, -1, keepdims=True)
        d = (e - mean_e - n * mean_en) * rs1_s[at, 0:1]
        dr[at, :] = d
        dbr_s[at, :] = d.astype(BF16)
        return sums[0] + fold_rows(dy * n), sums[1] + fold_rows(dy), sums[2] + fold_rows(d)

    def dhid_last(k):
        def run():
            at, cols = pl.ds(k * PIECE, PIECE), pl.ds((chunks - 1) * CHUNK, CHUNK)
            acc[at, :] += dot_nt(dup_s[at, cols], w_up[:, cols])

        return run

    dhid_last(0)()
    dots = [dhid_last(k) for k in range(1, seq // PIECE)] + [lambda: None]
    for name, v in zip(("gain0", "shift0", "out"), weave(dots, BLOCK, norm_one, (no_sum,) * 3)):
        put_small(name, v)

    for name in ("ddn", "dup", "dbr"):
        save_copy(name).start()

    @pl.when(r + 1 < rows)
    def _():
        for name in early:
            load_copy(name, r + 1).start()

    for name in late:
        load_copy(name, r).wait()

    @pl.when(r > 0)
    def _():
        save_copy("dproj").wait()

    @pl.when(r == 0)
    def _():
        for k in (2, 3):
            weight_copy(k).wait()

    for k in range(width // PIECE):
        acc[:, pl.ds(k * PIECE, PIECE)] = dot_nt(dbr_s[...], w_out[pl.ds(k * PIECE, PIECE), :])

    zero = jnp.zeros((), BF16)
    head_scale = jnp.asarray(HEAD_DIM ** -0.5, BF16)

    def prepare(p):
        slot = p % 2
        cols = slice(p * PAIR, (p + 1) * PAIR)

        def body(start, at, c):
            lo = lax.broadcasted_iota(jnp.int32, (OPS, PAIR), 1) < HEAD_DIM
            ctx = ctx_s[at, cols]
            t = jnp.tanh(ctx * i1)
            low = (acc[at, cols] * (1.0 - t * t) * inv_s[at, cols]).astype(BF16)
            dctx_s[slot, at, :] = low
            inner = low.astype(F32) * ctx
            whole_sum = jnp.sum(inner, -1, keepdims=True)
            lower = jnp.sum(jnp.where(lo, inner, 0.0), -1, keepdims=True)
            inner_s[slot, 0, at, :] = jnp.broadcast_to(lower, (OPS, PAIR))
            inner_s[slot, 1, at, :] = jnp.broadcast_to(whole_sum - lower, (OPS, PAIR))
            v2 = qkv_s[at, 2 * width + p * PAIR : 2 * width + (p + 1) * PAIR]
            ops_s[slot, 0, at, :] = jnp.where(lo, v2, zero)
            ops_s[slot, 1, at, :] = jnp.where(lo, zero, v2)
            return c

        blocks(OPS, body)
        q_t[slot] = (qkv_s[:, cols] * head_scale).T
        do_t[slot] = dctx_s[slot].T

    def scores(h):
        slot, side = h // 2 % 2, h % 2

        def piece_of(k):
            def run():
                keys = pl.ds(k * PIECE, PIECE)
                g_s[side, :, keys] = dot_nt(dctx_s[slot], ops_s[slot, side, keys, :])

            return run

        return [piece_of(k) for k in range(seq // PIECE)]

    def soften(h):
        slot, side = h // 2 % 2, h % 2

        def body(start, at, c):
            inner = jnp.concatenate([inner_s[slot, side, at, :]] * (seq // PAIR), 1)
            ds_s[side, at, :] = (e_s[h, at, :].astype(F32) * (g_s[side, at, :] - inner)).astype(BF16)
            return c

        return body

    def collect(h):
        slot, side = h // 2 % 2, h % 2
        rows_at = slice(side * HEAD_DIM, (side + 1) * HEAD_DIM)

        def grad_v(k):
            def run():
                keys = pl.ds(k * PIECE, PIECE)
                gv_s[rows_at, keys] = dot_nn(do_t[slot, rows_at, :], e_s[h, :, keys])

            return run

        def grad_k(k):
            def run():
                keys = pl.ds(k * PIECE, PIECE)
                gk_s[rows_at, keys] = dot_nn(q_t[slot, rows_at, :], ds_s[side, :, keys])

            return run

        def grad_q(k):
            def run():
                queries = pl.ds(k * PIECE, PIECE)
                keys_low = qkv_s[:, width + h // 2 * PAIR : width + (h // 2 + 1) * PAIR]
                gq_s[side, queries, :] = dot_nn(ds_s[side, queries, :], keys_low)

            return run

        return [make(k) for make in (grad_v, grad_k, grad_q) for k in range(seq // PIECE)]

    def settle(p):
        def body(start, at, c):
            lo = lax.broadcasted_iota(jnp.int32, (OPS, PAIR), 1) < HEAD_DIM
            q = jnp.where(lo, gq_s[0, at, :], gq_s[1, at, :]) * (HEAD_DIM ** -0.5)
            dproj_s[at, p * PAIR : (p + 1) * PAIR] = q.astype(BF16)
            return c

        blocks(OPS, body)
        dproj_s[:, width + p * PAIR : width + (p + 1) * PAIR] = gk_s[...].astype(BF16).T
        dproj_s[:, 2 * width + p * PAIR : 2 * width + (p + 1) * PAIR] = gv_s[...].astype(BF16).T

    heads = 2 * (width // PAIR)
    prepare(0)
    for dot in scores(0):
        dot()
    for h in range(heads):
        dots = []
        if h + 1 < heads:
            if (h + 1) % 2 == 0:
                prepare((h + 1) // 2)
            dots += scores(h + 1)
        if h > 0:
            dots += collect(h - 1)
        weave(dots, BLOCK, soften(h))
        if h > 0 and h % 2 == 0:
            settle(h // 2 - 1)
    for dot in collect(heads - 1):
        dot()
    settle(heads // 2 - 1)
    def dx_piece(k):
        def run():
            at = pl.ds(k * PIECE, PIECE)
            acc[:, at] = dot_nt(dproj_s[...], w_qkv[at, :])

        return run

    def quant_in(k):
        cols = pl.ds(k * PIECE, PIECE)
        values = pl.ds(2 * width + k * PIECE, PIECE)

        def body(start, at, sums):
            t = jnp.tanh(x_s[at, cols].astype(F32) * i0)
            gin[r, at, cols] = (dr[at, cols] + acc[at, cols] * (1.0 - t * t)).astype(BF16)
            return (
                sums[0] + fold_rows(dproj_s[at, cols].astype(F32)),
                sums[1] + fold_rows(dproj_s[at, values].astype(F32)),
            )

        return body

    dx_piece(0)()
    pieces = width // PIECE
    for k in range(pieces):
        dots = [dx_piece(k + 1)] if k + 1 < pieces else [lambda: None]
        sums = weave(dots, BLOCK, quant_in(k), (jnp.zeros((8, PIECE), F32),) * 2)
        put_small("qkv", sums[0], k * PIECE)
        put_small("qkv", sums[1], 2 * width + k * PIECE)
    save_copy("dproj").start()

    @pl.when(r + 1 < rows)
    def _():
        for name in late:
            load_copy(name, r + 1).start()

    @pl.when(jnp.logical_not(first))
    def _():
        hop(r).start()

    @pl.when(first)
    def _():
        tok_copy(r).start()

    @pl.when(r == rows - 1)
    def _():
        @pl.when(stage >= count - 2)
        def _():
            turn_left()

        for name in save_order:
            save_copy(name).wait()

        @pl.when(jnp.logical_not(first))
        def _():
            for i in range(row_count):
                hop(i).wait_send()

        @pl.when(first)
        def _():
            for i in range(row_count):
                tok_copy(i).wait()


def whole(a):
    return pl.BlockSpec(a.shape, lambda r, n=a.ndim: (0,) * n, pipeline_mode=pl.Buffered(1))


ANYWHERE = pl.BlockSpec(memory_space=pl.ANY)
SCALAR = pl.BlockSpec(memory_space=pltpu.SMEM)
VMEM_LIMIT = 60 * 1024 * 1024


def run_forward(count, tokens, lengths, scales, weights):
    w_qkv, b_qkv, w_out, b_out, w_up, b_up, w_down, b_down, gain, shift = weights
    rows, seq, width = tokens.shape
    ff = w_up.shape[1]
    big = lambda n, t: jax.ShapeDtypeStruct((rows, seq, n), t)
    saves = [
        (width, BF16), (3 * width, BF16), (width, F32), (width, F32), (width, BF16), (128, F32),
        (ff, BF16), (width, BF16), (128, F32),
    ]
    heads = width // HEAD_DIM
    lefts = [(ff, BF16), (width, BF16), (width, BF16), (width, BF16)]
    heavy = (w_qkv, w_out, w_up, w_down)
    dense = (b_qkv, b_out, b_up, b_down, gain, shift)
    tok = rows * seq
    return pl.pallas_call(
        lambda *refs: fwd_kernel(count, *refs),
        grid=(rows,),
        in_specs=[SCALAR, SCALAR, ANYWHERE] + [ANYWHERE] * 4 + [whole(a) for a in dense],
        out_specs=[ANYWHERE] * 12 + [pl.BlockSpec((4, 8, 128), lambda r: (0, 0, 0))],
        out_shape=[big(n, t) for n, t in saves]
        + [
            big(ff + 3 * width, BF16),
            jax.ShapeDtypeStruct((rows, heads, seq, seq), BF16),
            jax.ShapeDtypeStruct((rows, seq // count, width), BF16),
            jax.ShapeDtypeStruct((4, 8, 128), F32),
        ],
        scratch_shapes=[pltpu.VMEM(a.shape, a.dtype) for a in heavy]
        + [pltpu.SemaphoreType.DMA((4,))]
        + [pltpu.VMEM((rows, seq, width), BF16), pltpu.VMEM((rows, seq, width), BF16)]
        + [pltpu.VMEM((seq, n), t) for n, t in saves[1:] + lefts]
        + [
            pltpu.VMEM((seq, width), F32),
            pltpu.VMEM((seq, width), F32),
            pltpu.VMEM((2, seq, CHUNK), F32),
            pltpu.VMEM((2, 6, seq, PAIR), BF16),
            pltpu.VMEM((2, seq, seq), F32),
            pltpu.VMEM((heads, seq, seq), BF16),
            pltpu.VMEM((2, seq, PAIR), F32),
            pltpu.VMEM((seq, 128), F32),
            pltpu.SemaphoreType.DMA((14,)),
            pltpu.SemaphoreType.DMA((rows,)),
            pltpu.SemaphoreType.DMA((rows,)),
            pltpu.SemaphoreType.DMA((rows,)),
            pltpu.SemaphoreType.DMA((rows, count)),
            pltpu.SemaphoreType.DMA((rows,)),
        ],
        compiler_params=pltpu.CompilerParams(
            collective_id=0, has_side_effects=True, vmem_limit_bytes=VMEM_LIMIT,
            dimension_semantics=("arbitrary",),
        ),
        cost_estimate=pl.CostEstimate(
            flops=2 * tok * (4 * width * width + 2 * width * ff + 2 * seq * width),
            bytes_accessed=tok * 28000, transcendentals=tok * 3 * ff,
        ),
    )(lengths, scales, tokens, *heavy, *dense)


def run_backward(count, seeds, lengths, scales, weights, kept):
    w_qkv, b_qkv, w_out, b_out, w_up, b_up, w_down, b_down, gain, shift = weights
    *loads, left, exps = kept
    loads.append(exps)
    rows, seq, width = seeds.shape
    ff = w_up.shape[1]
    big = lambda n, t: jax.ShapeDtypeStruct((rows, seq, n), t)
    saves = [(3 * width, BF16), (width, BF16), (ff, BF16), (width, BF16)]
    heavy = (w_qkv, w_out, w_up, w_down)
    dense = (gain, shift)
    tok = rows * seq
    small = 6 * width + ff + 3 * width
    return pl.pallas_call(
        lambda *refs: bwd_kernel(count, *refs),
        grid=(rows,),
        in_specs=[SCALAR, SCALAR, ANYWHERE] + [ANYWHERE] * 4 + [whole(a) for a in dense] + [ANYWHERE] * 11,
        out_specs=[ANYWHERE] * 6 + [pl.BlockSpec((8, small), lambda r: (0, 0))],
        out_shape=[big(n, t) for n, t in saves]
        + [
            big(width, BF16), jax.ShapeDtypeStruct((left.shape[2], rows * seq), BF16),
            jax.ShapeDtypeStruct((8, small), F32),
        ],
        scratch_shapes=[pltpu.VMEM(a.shape, a.dtype) for a in heavy]
        + [
            pltpu.SemaphoreType.DMA((4,)),
            pltpu.VMEM((2, seq, width), BF16),
            pltpu.VMEM((2, width, seq), BF16),
            pltpu.SemaphoreType.DMA((2,)),
            pltpu.SemaphoreType.DMA((2,)),
        ]
        + [pltpu.VMEM((rows, seq, width), BF16)]
        + [pltpu.VMEM(a.shape[1:], a.dtype) for a in loads]
        + [pltpu.VMEM((seq, n), t) for n, t in saves]
        + [
            pltpu.VMEM((2, seq, PAIR), BF16),
            pltpu.VMEM((seq, width), F32),
            pltpu.VMEM((seq, width), F32),
            pltpu.VMEM((2, seq, CHUNK), F32),
            pltpu.VMEM((2, 2, seq, PAIR), BF16),
            pltpu.VMEM((2, seq, seq), F32),
            pltpu.VMEM((2, seq, seq), BF16),
            pltpu.VMEM((PAIR, seq), F32),
            pltpu.VMEM((PAIR, seq), F32),
            pltpu.VMEM((2, seq, PAIR), F32),
            pltpu.VMEM((2, PAIR, seq), BF16),
            pltpu.VMEM((2, PAIR, seq), BF16),
            pltpu.VMEM((2, 2, seq, PAIR), F32),
            pltpu.SemaphoreType.DMA((10,)),
            pltpu.SemaphoreType.DMA((4,)),
            pltpu.SemaphoreType.DMA((rows,)),
            pltpu.SemaphoreType.DMA((rows,)),
            pltpu.SemaphoreType.DMA((rows,)),
            pltpu.SemaphoreType.DMA((rows,)),
        ],
        compiler_params=pltpu.CompilerParams(
            collective_id=1, has_side_effects=True, vmem_limit_bytes=VMEM_LIMIT,
            dimension_semantics=("arbitrary",),
        ),
        cost_estimate=pl.CostEstimate(
            flops=2 * tok * (4 * width * width + 2 * width * ff + 5 * seq * width),
            bytes_accessed=tok * 28000, transcendentals=tok * ff,
        ),
    )(lengths, scales, seeds, *heavy, *dense, left, *loads)


def ring_to_dp(pos, n):
    return jnp.where(pos < n // 2, 2 * pos, 2 * (n - pos) - 1)


def dp_to_ring(j, n):
    return jnp.where(j % 2 == 0, j // 2, n - 1 - j // 2)


def grad_kernel(count, n, *refs):
    (
        left, ddn, dup, dproj, dbr, small, g0,
        gq_o, go_o, gu_o, gd_o, small_o, gtok_o,
        slots_d, slots_u, slots_q, slots_s, wide_v, thin_v, ddn_v, dup_v, dpo_v,
        wide_sem, thin_sem, right_sem,
        send_d, recv_d, send_u, recv_u, send_q, recv_q, send_s, recv_s, tok_send, tok_recv,
    ) = refs
    width = ddn.shape[1]
    ff = dup.shape[1]
    shard, shard_ff = width // n, ff // n
    row_count, seq = g0.shape[0], g0.shape[1]
    piece = seq // count
    stage = lax.axis_index("pipe")
    me = lax.axis_index("dp")
    pos = dp_to_ring(me, n)
    first = stage == 0
    ahead = ring_to_dp(lax.rem(pos + 1, n), n)
    behind = ring_to_dp(lax.rem(pos + n - 1, n), n)
    target = (ahead, behind)

    def chunk(d, step):
        at = pos + 2 * n - 1 - step if d == 0 else pos + 1 + step
        return ring_to_dp(lax.rem(at, n), n)

    def wide_copy(d, step):
        rows = pl.ds(pl.multiple_of(chunk(d, step) * shard_ff, 16), shard_ff)
        return pltpu.make_async_copy(left.at[rows, :], wide_v.at[d], wide_sem.at[d])

    def thin_copy(k, d, step):
        rows = pl.ds(pl.multiple_of(ff + k * width + chunk(d, step) * shard, 16), shard)
        return pltpu.make_async_copy(left.at[rows, :], thin_v.at[k, d], thin_sem.at[k, d])

    rights = [
        (ddn, ddn_v), (dup, dup_v), (dproj, dpo_v.at[:, pl.ds(0, 3 * width)]),
        (dbr, dpo_v.at[:, pl.ds(3 * width, width)]),
    ]

    def right_copy(k):
        return pltpu.make_async_copy(rights[k][0], rights[k][1], right_sem.at[k])

    for d in range(2):
        wide_copy(d, 0).start()
    right_copy(0).start()
    right_copy(1).start()
    for d in range(2):
        thin_copy(0, d, 0).start()
    right_copy(2).start()
    right_copy(3).start()
    for d in range(2):
        thin_copy(1, d, 0).start()
        if d == 1:
            thin_copy(2, d, 0).start()

    barrier = pltpu.get_barrier_semaphore()
    for peer in target:
        pl.semaphore_signal(barrier, inc=1, device_id={"dp": peer}, device_id_type=LOGICAL)

    @pl.when(first)
    def _():
        pl.semaphore_wait(barrier, 1 + count)

    @pl.when(jnp.logical_not(first))
    def _():
        pl.semaphore_signal(barrier, inc=1, device_id={"pipe": jnp.int32(0)}, device_id_type=LOGICAL)
        pl.semaphore_wait(barrier, 2)

    def tok_part(i, p):
        return pltpu.make_async_remote_copy(
            src_ref=g0.at[i, pl.ds(p * piece, piece)], dst_ref=gtok_o.at[i],
            send_sem=tok_send.at[i, p], recv_sem=tok_recv.at[i],
            device_id={"pipe": jnp.int32(p)}, device_id_type=LOGICAL,
        )

    def tok_own(i):
        return pltpu.make_async_copy(g0.at[i, pl.ds(0, piece)], gtok_o.at[i], tok_send.at[i, 0])

    @pl.when(first)
    def _():
        for i in range(row_count):
            for p in range(1, count):
                tok_part(i, p).start()
            tok_own(i).start()

    def message(slots, send, recv, d, at):
        return pltpu.make_async_remote_copy(
            src_ref=slots.at[d, at], dst_ref=slots.at[d, jnp.minimum(at + 1, n - 1)],
            send_sem=send.at[d, at], recv_sem=recv.at[d, jnp.minimum(at + 1, n - 1)],
            device_id={"dp": target[d]}, device_id_type=LOGICAL,
        )

    def arrived(slots, send, recv, d, at):
        return pltpu.make_async_remote_copy(
            src_ref=slots.at[d, at], dst_ref=slots.at[d, at],
            send_sem=send.at[d, at], recv_sem=recv.at[d, at],
            device_id={"dp": target[d]}, device_id_type=LOGICAL,
        )

    def lane(slots, send, recv, d, step, mine, finish):
        @pl.when(step == 0)
        def _():
            slots[d, 0] = mine.astype(BF16)

        @pl.when(step > 0)
        def _():
            arrived(slots, send, recv, d, step).wait_recv()

            @pl.when(step < n - 1)
            def _():
                slots[d, step] = (slots[d, step].astype(F32) + mine).astype(BF16)

            @pl.when(step == n - 1)
            def _():
                finish(slots[d, step].astype(F32) + mine)

        @pl.when(step < n - 1)
        def _():
            message(slots, send, recv, d, step).start()

    def small_message(at):
        return pltpu.make_async_remote_copy(
            src_ref=slots_s.at[at], dst_ref=slots_s.at[jnp.minimum(at + 1, n - 1)],
            send_sem=send_s.at[at], recv_sem=recv_s.at[jnp.minimum(at + 1, n - 1)],
            device_id={"dp": target[0]}, device_id_type=LOGICAL,
        )

    def small_arrived(at):
        return pltpu.make_async_remote_copy(
            src_ref=slots_s.at[at], dst_ref=slots_s.at[at], send_sem=send_s.at[at],
            recv_sem=recv_s.at[at], device_id={"dp": target[0]}, device_id_type=LOGICAL,
        )

    sum_rows = lax.broadcasted_iota(jnp.int32, (16, 128), 0) < 9

    def small_step(step):
        mine = small[chunk(0, step)]

        @pl.when(step == 0)
        def _():
            slots_s[0] = mine

        @pl.when(step > 0)
        def _():
            small_arrived(step).wait_recv()
            got = slots_s[step]
            slots_s[step] = jnp.where(sum_rows, got + mine, jnp.maximum(got, mine))

        @pl.when(step < n - 1)
        def _():
            small_message(step).start()

        @pl.when(step == n - 1)
        def _():
            small_o[...] = slots_s[step]

    half, half_ff = width // 2, ff // 2

    def fetched(copy, step, *args):
        copy(*args, step).wait()

    def refill(copy, step, *args):
        @pl.when(step < n - 1)
        def _():
            copy(*args, step + 1).start()

    def right_ready(k, step):
        @pl.when(step == 0)
        def _():
            right_copy(k).wait()

    def turn(step, _):
        right_ready(0, step)
        for d in range(2):
            cols = slice(d * half, (d + 1) * half)
            fetched(wide_copy, step, d)
            mine = dot_nn(wide_v[d], ddn_v[:, cols])
            refill(wide_copy, step, d)

            def finish_down(total):
                gd_o[:, cols] = total

            lane(slots_d, send_d, recv_d, d, step, mine, finish_down)
        small_step(step)
        right_ready(1, step)
        for d in range(2):
            cols = slice(d * half_ff, (d + 1) * half_ff)
            fetched(thin_copy, step, 0, d)
            mine = dot_nn(thin_v[0, d], dup_v[:, cols])
            refill(thin_copy, step, 0, d)

            def finish_up(total):
                gu_o[:, cols] = total

            lane(slots_u, send_u, recv_u, d, step, mine, finish_up)
        right_ready(2, step)
        right_ready(3, step)
        fetched(thin_copy, step, 1, 0)
        mine = dot_nn(thin_v[1, 0], dpo_v[:, 0 : 2 * width])
        refill(thin_copy, step, 1, 0)

        def finish_ahead(total):
            gq_o[:, 0 : 2 * width] = total

        lane(slots_q, send_q, recv_q, 0, step, mine, finish_ahead)
        fetched(thin_copy, step, 1, 1)
        fetched(thin_copy, step, 2, 1)
        mine = jnp.concatenate(
            [
                dot_nn(thin_v[1, 1], dpo_v[:, 2 * width : 3 * width]),
                dot_nn(thin_v[2, 1], dpo_v[:, 3 * width : 4 * width]),
            ],
            1,
        )
        refill(thin_copy, step, 1, 1)
        refill(thin_copy, step, 2, 1)

        def finish_behind(total):
            gq_o[:, 2 * width : 3 * width] = total[:, 0:width]
            go_o[...] = total[:, width : 2 * width]

        lane(slots_q, send_q, recv_q, 1, step, mine, finish_behind)
        return 0

    lax.fori_loop(0, n, turn, 0)

    def drain(at, _):
        for d in range(2):
            message(slots_d, send_d, recv_d, d, at).wait_send()
            message(slots_u, send_u, recv_u, d, at).wait_send()
            message(slots_q, send_q, recv_q, d, at).wait_send()
        small_message(at).wait_send()
        return 0

    lax.fori_loop(0, n - 1, drain, 0)

    @pl.when(first)
    def _():
        for i in range(row_count):
            for p in range(1, count):
                tok_part(i, p).wait_send()
            tok_own(i).wait()

    @pl.when(jnp.logical_not(first))
    def _():
        for i in range(row_count):
            tok_part(i, 1).wait_recv()


def run_grads(count, n, left, dproj, dbr, dup, ddn, g0, small):
    rows, seq, width = g0.shape
    ff = dup.shape[2]
    flat = lambda a: a.reshape(rows * seq, a.shape[2])
    tok = rows * seq
    shard, shard_ff = width // n, ff // n
    ops = [left] + [flat(a) for a in (ddn, dup, dproj, dbr)]
    vmem = pl.BlockSpec(memory_space=pltpu.VMEM)
    sem = pltpu.SemaphoreType.DMA
    return pl.pallas_call(
        lambda *refs: grad_kernel(count, n, *refs),
        in_specs=[ANYWHERE] * 5 + [vmem, ANYWHERE],
        out_specs=[vmem] * 5 + [ANYWHERE],
        out_shape=[
            jax.ShapeDtypeStruct((shard, 3 * width), F32),
            jax.ShapeDtypeStruct((shard, width), F32),
            jax.ShapeDtypeStruct((shard, ff), F32),
            jax.ShapeDtypeStruct((shard_ff, width), F32),
            jax.ShapeDtypeStruct((16, 128), F32),
            jax.ShapeDtypeStruct((rows, seq // count, width), BF16),
        ],
        scratch_shapes=[
            pltpu.VMEM((2, n, shard_ff, width // 2), BF16),
            pltpu.VMEM((2, n, shard, ff // 2), BF16),
            pltpu.VMEM((2, n, shard, 2 * width), BF16),
            pltpu.VMEM((n, 16, 128), F32),
            pltpu.VMEM((2, shard_ff, tok), BF16),
            pltpu.VMEM((3, 2, shard, tok), BF16),
            pltpu.VMEM((tok, width), BF16),
            pltpu.VMEM((tok, ff), BF16),
            pltpu.VMEM((tok, 4 * width), BF16),
            sem((2,)), sem((3, 2)), sem((4,)),
            sem((2, n)), sem((2, n)), sem((2, n)), sem((2, n)), sem((2, n)), sem((2, n)),
            sem((n,)), sem((n,)), sem((rows, count)), sem((rows,)),
        ],
        compiler_params=pltpu.CompilerParams(
            collective_id=2, has_side_effects=True, vmem_limit_bytes=VMEM_LIMIT,
        ),
        cost_estimate=pl.CostEstimate(
            flops=2 * tok * (4 * width * width + 2 * width * ff), bytes_accessed=tok * 25000, transcendentals=0,
        ),
    )(*ops, small, g0)


def weight_grad(left, right):
    g = jnp.einsum("rsd,rse->de", left, right, preferred_element_type=F32).astype(BF16)
    return lax.psum_scatter(g, "dp", scatter_dimension=0, tiled=True).astype(F32)


def share_pieces(whole_rows, count, stage):
    piece = whole_rows.shape[1] // count
    mine = whole_rows[:, :piece]
    for p in range(1, count):
        got = lax.ppermute(whole_rows[:, p * piece : (p + 1) * piece], "pipe", [(0, p)])
        mine = jnp.where(stage == p, got, mine)
    return mine


def shards(
    tokens, lengths, ema_scales, w_qkv, bias_qv, w_out, bias_out, w_up, bias_up, w_down, bias_down,
    ln_gain, ln_bias, cotangent,
):
    count = lax.axis_size("pipe")
    n = lax.axis_size("dp")
    width = tokens.shape[2]
    ff = w_up.shape[2]
    b_qkv = jnp.concatenate([bias_qv[:, :width], jnp.zeros_like(bias_qv[:, :width]), bias_qv[:, width:]], 1)
    weights = (
        w_qkv[0], b_qkv, w_out[0], bias_out, w_up[0], bias_up, w_down[0], bias_down, ln_gain[0], ln_bias[0],
    )
    *kept, mixed, peaks = run_forward(count, tokens, lengths, ema_scales, weights)
    left = kept[-2]
    dproj, dbr, dup, ddn, g0, turned, small = run_backward(
        count, cotangent, lengths, ema_scales, weights, kept
    )
    sums = jnp.sum(small, 0)
    parts, at = [], 0
    for size in (width, width, width, width, width, width, ff, width, width, width):
        parts.append(sums[at : at + size])
        at += size
    parts[7:] = [jnp.concatenate([parts[7], parts[9]])]
    packed = jnp.concatenate([v.reshape(n, -1) for v in parts], 1)
    peak = jnp.max(peaks, (1, 2))
    sums_width = packed.shape[1]
    if n >= 4 and n % 2 == 0 and width // n % 16 == 0 and ff // n % 128 == 0 and sums_width == 9 * 128:
        top = jnp.broadcast_to(jnp.pad(peak, (0, 124))[None, None], (n, 7, 128))
        with_peak = jnp.concatenate([packed.reshape(n, 9, 128), top], 1)
        g_qkv, g_out, g_up, g_down, small_sum, grad_tokens = run_grads(
            count, n, turned, dproj, dbr, dup, ddn, g0, with_peak
        )
        mine = small_sum[:9].reshape(1, sums_width)
        batch_max = small_sum[9:10, :4]
    else:
        g_down = weight_grad(left[:, :, :ff], ddn)
        g_up = weight_grad(left[:, :, ff : ff + width], dup)
        g_qkv = weight_grad(left[:, :, ff + width : ff + 2 * width], dproj)
        g_out = weight_grad(left[:, :, ff + 2 * width :], dbr)
        mine = lax.psum_scatter(packed, "dp", scatter_dimension=0, tiled=True)
        batch_max = lax.pmax(peak, "dp")[None]
        grad_tokens = share_pieces(g0, count, lax.axis_index("pipe"))
    outs, at = [], 0
    for size in (width, width, width, width, width, width, ff, 2 * width):
        outs.append(mine[:, at : at + size // n])
        at += size // n
    gain0, gain1, shift0, shift1, s_out, s_down, s_up, s_qv = outs
    g_gain = jnp.stack([gain0, gain1], 1)
    g_shift = jnp.stack([shift0, shift1], 1)
    return (
        mixed, grad_tokens, g_qkv[None], s_qv, g_out[None], s_out, g_up[None], s_up, g_down[None], s_down,
        g_gain, g_shift, batch_max,
    )


def solution(mesh):
    return jax.shard_map(
        shards,
        mesh=mesh,
        in_specs=(
            P("dp", None, None), P("dp"), P("pipe", None), P("pipe", None, None), P("pipe", None),
            P("pipe", None, None), P("pipe", None), P("pipe", None, None), P("pipe", None),
            P("pipe", None, None), P("pipe", None), P("pipe", None, None), P("pipe", None, None),
            P("dp", None, None),
        ),
        out_specs=(
            P("dp", "pipe", None), P("dp", "pipe", None), P("pipe", "dp", None), P("pipe", "dp"),
            P("pipe", "dp", None), P("pipe", "dp"), P("pipe", "dp", None), P("pipe", "dp"),
            P("pipe", "dp", None), P("pipe", "dp"), P("pipe", None, "dp"), P("pipe", None, "dp"),
            P("pipe", None),
        ),
        check_vma=False,
    )
```

```python
import jax
import jax.numpy as jnp
from jax import lax
from jax.experimental import pallas as pl
from jax.experimental.pallas import tpu as pltpu
from jax.sharding import PartitionSpec as P

HEAD_DIM = 64
PAIR = 2 * HEAD_DIM
EPS = 1e-06
MASKED = -1000000000.0
CHUNK = 512
PIECE = 256
BLOCK = 16
OPS = 64
LOGICAL = pl.DeviceIdType.MESH
F32 = jnp.float32
BF16 = jnp.bfloat16

ERF_POLY = (
    0.7978823511659165,
    0.03634481045269742,
    -4.5110171354091134e-05,
    -5.02654469142584e-05,
    3.0867937984305273e-06,
    -6.60140005994544e-08,
)
ERF_CLAMP = 5.2 * 5.2
HALF_LOG2E = -0.7213475204444817
LOG2_TWICE_DENSITY = -0.3257480647361593


def dot_nn(a, b):
    return jnp.dot(a, b, preferred_element_type=F32)


def dot_nt(a, b):
    return lax.dot_general(a, b, (((1,), (1,)), ((), ())), preferred_element_type=F32)


def dot_tn(a, b):
    return lax.dot_general(a, b, (((0,), (0,)), ((), ())), preferred_element_type=F32)


def fold_rows(v):
    return jnp.sum(v.reshape(v.shape[0] // 8, 8, v.shape[1]), 0)


def peak_rows(v):
    tiles = [v[:, i : i + 128] for i in range(0, v.shape[1], 128)]
    top = tiles[0]
    for tile in tiles[1:]:
        top = jnp.maximum(top, tile)
    return jnp.max(top.reshape(v.shape[0] // 8, 8, 128), 0)


def greet(stage, count):
    barrier = pltpu.get_barrier_semaphore()
    for step in range(1, count):
        peer = lax.rem(stage + step, count)
        pl.semaphore_signal(barrier, inc=1, device_id={"pipe": peer}, device_id_type=LOGICAL)
    pl.semaphore_wait(barrier, count - 1)


def activation(u, ceiling, inv_ceiling):
    square = u * u
    w = jnp.minimum(square, ERF_CLAMP)
    poly = w * ERF_POLY[-1] + ERF_POLY[-2]
    for coef in ERF_POLY[-3::-1]:
        poly = poly * w + coef
    twice_cdf = 1.0 + jnp.tanh(u * poly)
    act = (0.5 * u) * twice_cdf
    ratio = jnp.tanh(act * inv_ceiling)
    twice_density = jnp.exp2(square * HALF_LOG2E + LOG2_TWICE_DENSITY)
    twice_slope = (1.0 - ratio * ratio) * (twice_cdf + u * twice_density)
    return act, ceiling * ratio, twice_slope


def fwd_kernel(count, *refs):
    (
        lens, scales, tokens, h_qkv, h_out, h_up, h_down, b_qkv, b_out, b_up, b_down, gain, shift,
        x_o, qkv_o, inv_o, ctx_o, n1_o, rs1_o, sl_o, n2_o, rs2_o, left_o, exp_o,
        mixed_o, peaks_o,
        w_qkv, w_out, w_up, w_down, w_sem,
        xin, xout, qkv_s, inv_s, ctx_s, n1_s, rs1_s, sl_s, n2_s, rs2_s, aq_s, hq_s, xq_s, cq_s,
        acc, hid, up_s, ops_s, s_s, e_s, o_s, amax_s,
        save_sem, in_sem, send_sem, recv_sem, mix_send, mix_recv,
    ) = refs
    r = pl.program_id(0)
    rows = pl.num_programs(0)
    row_count = tokens.shape[0]
    seq, width = tokens.shape[1], tokens.shape[2]
    ff = w_up.shape[1]
    piece = seq // count
    stage = lax.axis_index("pipe")
    first = stage == 0
    last = stage == count - 1

    left = {"aq": (0, ff), "hq": (ff, width), "xq": (ff + width, width), "cq": (ff + 2 * width, width)}
    staged = {
        "x": (xin.at[r], x_o), "qkv": (qkv_s, qkv_o), "inv": (inv_s, inv_o), "ctx": (ctx_s, ctx_o),
        "n1": (n1_s, n1_o), "rs1": (rs1_s, rs1_o), "sl": (sl_s, sl_o), "n2": (n2_s, n2_o),
        "rs2": (rs2_s, rs2_o), "aq": (aq_s, left_o), "hq": (hq_s, left_o), "xq": (xq_s, left_o),
        "cq": (cq_s, left_o), "exp": (e_s, exp_o),
    }
    order = list(staged)
    early = ("x", "xq", "qkv", "inv", "ctx", "cq", "exp")
    late = ("n1", "rs1", "hq", "aq", "sl", "n2", "rs2")
    fetches = [(h_qkv, w_qkv), (h_out, w_out), (h_up, w_up), (h_down, w_down)]

    def weight_copy(k):
        return pltpu.make_async_copy(fetches[k][0], fetches[k][1], w_sem.at[k])

    def save_copy(name):
        src, dst = staged[name]
        dst = dst.at[r]
        if name in left:
            dst = dst.at[:, pl.ds(*left[name])]
        return pltpu.make_async_copy(src, dst, save_sem.at[order.index(name)])

    def token_copy(i):
        return pltpu.make_async_copy(tokens.at[i], xin.at[i], in_sem.at[i])

    def hop(i):
        return pltpu.make_async_remote_copy(
            src_ref=xout.at[i], dst_ref=xin.at[i], send_sem=send_sem.at[i], recv_sem=recv_sem.at[i],
            device_id={"pipe": lax.rem(stage + 1, count)}, device_id_type=LOGICAL,
        )

    def mix_part(i, p):
        return pltpu.make_async_remote_copy(
            src_ref=xout.at[i, pl.ds(p * piece, piece)], dst_ref=mixed_o.at[i],
            send_sem=mix_send.at[i, p], recv_sem=mix_recv.at[i],
            device_id={"pipe": jnp.int32(p)}, device_id_type=LOGICAL,
        )

    def mix_own(i):
        return pltpu.make_async_copy(
            xout.at[i, pl.ds((count - 1) * piece, piece)], mixed_o.at[i], mix_send.at[i, count - 1]
        )

    @pl.when(r == 0)
    def _():
        greet(stage, count)
        peaks_o[...] = jnp.zeros_like(peaks_o)
        for k in range(4):
            weight_copy(k).start()

        @pl.when(first)
        def _():
            for i in range(row_count):
                token_copy(i).start()

    @pl.when(first)
    def _():
        token_copy(r).wait()

    @pl.when(jnp.logical_not(first))
    def _():
        hop(r).wait_recv()

    length = lens[r]
    m0, m1, m2, m3 = scales[0, 0], scales[0, 1], scales[0, 2], scales[0, 3]
    i0, i1, i2, i3 = 1.0 / m0, 1.0 / m1, 1.0 / m2, 1.0 / m3

    def row_mask(start, size):
        return (start + lax.broadcasted_iota(jnp.int32, (size, 1), 0)) < length

    def blocks(size, body, init=0, begin=0, end=seq):
        step = lambda i, c: body(i * size, pl.ds(i * size, size), c)
        return lax.fori_loop(begin // size, end // size, step, init, unroll=True)

    def weave(dots, size, body, init=0):
        total, cut = seq // size, 0
        for k, dot in enumerate(dots):
            dot()
            begin, cut = cut, total * (k + 1) // len(dots)
            init = blocks(size, body, init, begin * size, cut * size)
        return init

    no_peak = jnp.zeros((8, 128), F32)

    @pl.when(r > 0)
    def _():
        for name in early:
            save_copy(name).wait()

    @pl.when(r == 0)
    def _():
        for k in (0, 1):
            weight_copy(k).wait()

    def quant_in(start, at, top):
        x = xin[r, at, :].astype(F32)
        xq_s[at, :] = (m0 * jnp.tanh(x * i0)).astype(BF16)
        return jnp.maximum(top, masked_peak(x, start))

    def masked_peak(v, start):
        return peak_rows(jnp.where(row_mask(start, v.shape[0]), jnp.abs(v), 0.0))

    peaks_o[0] = jnp.maximum(peaks_o[0], blocks(BLOCK, quant_in, no_peak))
    def project(g):
        def piece_of(part):
            def run():
                cols = slice(part * width + g * PIECE, part * width + (g + 1) * PIECE)
                proj = dot_nn(xq_s[...], w_qkv[:, cols]) + b_qkv[:, cols]
                qkv_s[:, cols] = proj.astype(BF16)

            return run

        return [piece_of(part) for part in range(3)]

    def project_out(g):
        def piece_of(k):
            def run():
                rows_at, cols = slice(g * PIECE, (g + 1) * PIECE), slice(k * PIECE, (k + 1) * PIECE)
                part = dot_nn(cq_s[:, rows_at], w_out[rows_at, cols])
                acc[:, cols] = part if g == 0 else acc[:, cols] + part

            return run

        return [piece_of(k) for k in range(width // PIECE)]

    one = jnp.ones((), BF16)
    zero = jnp.zeros((), BF16)
    head_scale = jnp.asarray(HEAD_DIM ** -0.5, BF16)

    def prepare(p):
        slot = p % 2

        def body(start, at, c):
            lane = lax.broadcasted_iota(jnp.int32, (OPS, PAIR), 1)
            lo = lane < HEAD_DIM
            spot = jnp.where(lo, lane, lane - HEAD_DIM)
            bias = jnp.where(row_mask(start, OPS), 0.0, MASKED)
            extra = jnp.where(spot == 0, jnp.broadcast_to(bias, (OPS, PAIR)), 0.0).astype(BF16)
            q2 = qkv_s[at, p * PAIR : (p + 1) * PAIR] * head_scale
            k2 = qkv_s[at, width + p * PAIR : width + (p + 1) * PAIR]
            v2 = qkv_s[at, 2 * width + p * PAIR : 2 * width + (p + 1) * PAIR]
            ops_s[slot, 0, at, :] = jnp.where(lo, q2, one)
            ops_s[slot, 1, at, :] = jnp.where(lo, one, q2)
            ops_s[slot, 2, at, :] = jnp.where(lo, k2, extra)
            ops_s[slot, 3, at, :] = jnp.where(lo, extra, k2)
            ops_s[slot, 4, at, :] = jnp.where(lo, v2, one)
            ops_s[slot, 5, at, :] = jnp.where(lo, one, v2)
            return c

        blocks(OPS, body)

    def scores(h):
        p, side = h // 2, h % 2

        def piece_of(k):
            def run():
                keys = pl.ds(k * PIECE, PIECE)
                s_s[side, :, keys] = dot_nt(ops_s[p % 2, side], ops_s[p % 2, 2 + side, keys, :])

            return run

        return [piece_of(k) for k in range(seq // PIECE)]

    def soften(h):
        def body(start, at, c):
            s = s_s[h % 2, at, :]
            e_s[h, at, :] = jnp.exp(s - jnp.max(s, -1, keepdims=True)).astype(BF16)
            return c

        return body

    def collect(h):
        p, side = h // 2, h % 2

        def piece_of(k):
            def run():
                queries = pl.ds(k * PIECE, PIECE)
                o_s[side, queries, :] = dot_nn(e_s[h, queries, :], ops_s[p % 2, 4 + side])

            return run

        return [piece_of(k) for k in range(seq // PIECE)]

    def settle(p, peak):
        cols = slice(p * PAIR, (p + 1) * PAIR)

        def body(start, at, top):
            lo = lax.broadcasted_iota(jnp.int32, (OPS, PAIR), 1) < HEAD_DIM
            o_a, o_b = o_s[0, at, :], o_s[1, at, :]
            total = pltpu.roll(jnp.where(lo, o_b, o_a), HEAD_DIM, 1)
            inverse = 1.0 / total
            c = jnp.where(lo, o_a, o_b) * inverse
            inv_s[at, cols] = inverse
            ctx_s[at, cols] = c
            cq_s[at, cols] = (m1 * jnp.tanh(c * i1)).astype(BF16)
            return jnp.maximum(top, masked_peak(c, start))

        return blocks(OPS, body, peak)

    heads = 2 * (width // PAIR)
    groups = width // PIECE
    span = heads // groups
    peak = no_peak
    for dot in project(0):
        dot()
    prepare(0)
    for dot in scores(0):
        dot()
    for h in range(heads):
        g, turn = h // span, h % span
        dots = []
        if h + 1 < heads:
            if (h + 1) % 2 == 0:
                prepare((h + 1) // 2)
            dots += scores(h + 1)
        if h > 0:
            dots += collect(h - 1)
        if g + 1 < groups and turn < 3:
            dots.append(project(g + 1)[turn])
        if g > 0 and turn > 0:
            dots.append(project_out(g - 1)[turn - 1])
        weave(dots, BLOCK, soften(h))
        if h > 0 and h % 2 == 0:
            peak = settle(h // 2 - 1, peak)
    for dot in collect(heads - 1):
        dot()
    peak = settle(heads // 2 - 1, peak)
    peaks_o[1] = jnp.maximum(peaks_o[1], peak)

    for name in early:
        save_copy(name).start()

    @pl.when(r > 0)
    def _():
        for name in late:
            save_copy(name).wait()

    @pl.when(r == 0)
    def _():
        for k in (2, 3):
            weight_copy(k).wait()

    def out_piece(k):
        def run():
            at, cols = pl.ds(k * PIECE, PIECE), slice((groups - 1) * PIECE, groups * PIECE)
            acc[at, :] += dot_nn(cq_s[at, cols], w_out[cols, :])

        return run

    def norm_one(start, at, top):
        s = xin[r, at, :].astype(F32) + (acc[at, :] + b_out[...])
        center = s - jnp.mean(s, -1, keepdims=True)
        rs = lax.rsqrt(jnp.mean(center * center, -1, keepdims=True) + EPS)
        n = center * rs
        h = n * gain[0:1, :] + shift[0:1, :]
        n1_s[at, :] = n.astype(BF16)
        rs1_s[at, :] = jnp.broadcast_to(rs, (BLOCK, 128))
        hid[at, :] = h
        hq_s[at, :] = (m2 * jnp.tanh(h * i2)).astype(BF16)
        return jnp.maximum(top, masked_peak(h, start))

    out_piece(0)()
    top = weave([out_piece(k) for k in range(1, seq // PIECE)] + [lambda: None], BLOCK, norm_one, no_peak)
    peaks_o[2] = jnp.maximum(peaks_o[2], top)

    chunks = ff // CHUNK

    def up_chunk(c):
        def piece_of(k):
            def run():
                part = dot_nn(hq_s[...], w_up[:, pl.ds(c * CHUNK + k * PIECE, PIECE)])
                up_s[c % 2, :, pl.ds(k * PIECE, PIECE)] = part

            return run

        return [piece_of(k) for k in range(CHUNK // PIECE)]

    def act_chunk(c):
        cols = pl.ds(c * CHUNK, CHUNK)

        def body(start, at, carry):
            act, low, slope = activation(up_s[c % 2, at, :] + b_up[:, cols], m3, i3)
            aq_s[at, cols] = low.astype(BF16)
            sl_s[at, cols] = slope.astype(BF16)
            size = jnp.abs(act)
            top = size[:, 0:128]
            for i in range(128, CHUNK, 128):
                top = jnp.maximum(top, size[:, i : i + 128])
            amax_s[at, :] = top if c == 0 else jnp.maximum(amax_s[at, :], top)
            return carry

        return body

    def down_chunk(c):
        def piece_of(k):
            def run():
                cols = pl.ds(k * PIECE, PIECE)
                part = dot_nn(aq_s[:, pl.ds(c * CHUNK, CHUNK)], w_down[pl.ds(c * CHUNK, CHUNK), cols])
                acc[:, cols] = part if c == 0 else acc[:, cols] + part

            return run

        return [piece_of(k) for k in range(width // PIECE)]

    for dot in up_chunk(0):
        dot()
    for c in range(chunks):
        dots = []
        if c + 1 < chunks:
            dots += up_chunk(c + 1)
        if c > 0:
            dots += down_chunk(c - 1)
        weave(dots, BLOCK, act_chunk(c))
    peaks_o[3] = jnp.maximum(peaks_o[3], masked_peak(amax_s[...], 0))

    def norm_two(start, at, c):
        s = hid[at, :] + (acc[at, :] + b_down[...])
        center = s - jnp.mean(s, -1, keepdims=True)
        rs = lax.rsqrt(jnp.mean(center * center, -1, keepdims=True) + EPS)
        n = center * rs
        n2_s[at, :] = n.astype(BF16)
        rs2_s[at, :] = jnp.broadcast_to(rs, (BLOCK, 128))
        xout[r, at, :] = (n * gain[1:2, :] + shift[1:2, :]).astype(BF16)
        return c

    def down_last(k):
        def run():
            at, cols = pl.ds(k * PIECE, PIECE), pl.ds((chunks - 1) * CHUNK, CHUNK)
            acc[at, :] += dot_nn(aq_s[at, cols], w_down[cols, :])

        return run

    down_last(0)()
    weave([down_last(k) for k in range(1, seq // PIECE)] + [lambda: None], BLOCK, norm_two)
    for name in late:
        save_copy(name).start()

    @pl.when(jnp.logical_not(last))
    def _():
        hop(r).start()

    @pl.when(last)
    def _():
        for p in range(count - 1):
            mix_part(r, p).start()
        mix_own(r).start()

    @pl.when(r == rows - 1)
    def _():
        for name in order:
            save_copy(name).wait()

        @pl.when(jnp.logical_not(last))
        def _():
            for i in range(row_count):
                hop(i).wait_send()
            for i in range(row_count):
                mix_part(i, 0).wait_recv()

        @pl.when(last)
        def _():
            for i in range(row_count):
                for p in range(count - 1):
                    mix_part(i, p).wait_send()
                mix_own(i).wait()


def bwd_kernel(count, *refs):
    (
        lens, scales, seeds, h_qkv, h_out, h_up, h_down, gain, shift, left_i,
        x_i, qkv_i, inv_i, ctx_i, n1_i, rs1_i, sl_i, n2_i, rs2_i, exp_i,
        dproj_o, dbr_o, dup_o, ddn_o, gtok_o, left_o, small_o,
        w_qkv, w_out, w_up, w_down, w_sem, turn_in, turn_out, turn_in_sem, turn_out_sem,
        gin, x_s, qkv_s, inv_s, ctx_s, n1_s, rs1_s, sl_s, n2_s, rs2_s, e_s,
        dproj_s, dbr_s, dup_s, ddn_s, dctx_s, acc, dr, dx,
        up_s, ops_s, g_s, ds_s, gv_s, gk_s, gq_s, q_t, k_t, do_t, inner_s,
        load_sem, save_sem, in_sem, send_sem, recv_sem, tok_send,
    ) = refs
    r = pl.program_id(0)
    rows = pl.num_programs(0)
    row_count = seeds.shape[0]
    seq, width = seeds.shape[1], seeds.shape[2]
    ff = w_up.shape[1]
    piece = seq // count
    stage = lax.axis_index("pipe")
    first = stage == 0
    last = stage == count - 1

    loaded = {
        "n2": (n2_i, n2_s), "rs2": (rs2_i, rs2_s), "sl": (sl_i, sl_s), "n1": (n1_i, n1_s),
        "rs1": (rs1_i, rs1_s), "ctx": (ctx_i, ctx_s), "qkv": (qkv_i, qkv_s), "inv": (inv_i, inv_s),
        "x": (x_i, x_s), "exp": (exp_i, e_s),
    }
    load_order = list(loaded)
    early = ("n2", "rs2", "sl", "n1", "rs1")
    late = ("ctx", "qkv", "inv", "exp", "x")
    staged = {
        "ddn": (ddn_s, ddn_o), "dup": (dup_s, dup_o), "dbr": (dbr_s, dbr_o), "dproj": (dproj_s, dproj_o),
    }
    save_order = list(staged)

    def load_copy(name, i):
        src, dst = loaded[name]
        return pltpu.make_async_copy(src.at[i], dst, load_sem.at[load_order.index(name)])

    def save_copy(name):
        src, dst = staged[name]
        return pltpu.make_async_copy(src, dst.at[r], save_sem.at[save_order.index(name)])

    def seed_copy(i):
        return pltpu.make_async_copy(seeds.at[i], gin.at[i], in_sem.at[i])

    def hop(i):
        return pltpu.make_async_remote_copy(
            src_ref=gin.at[i], dst_ref=gin.at[i], send_sem=send_sem.at[i], recv_sem=recv_sem.at[i],
            device_id={"pipe": lax.rem(stage + count - 1, count)}, device_id_type=LOGICAL,
        )

    def tok_copy(i):
        return pltpu.make_async_copy(gin.at[i], gtok_o.at[i], tok_send.at[i])

    fetches = [(h_down, w_down), (h_up, w_up), (h_out, w_out), (h_qkv, w_qkv)]

    def weight_copy(k):
        return pltpu.make_async_copy(fetches[k][0], fetches[k][1], w_sem.at[k])

    parts = left_i.shape[2] // width
    turns = row_count * parts

    def turn_load(i):
        cols = pl.ds(pl.multiple_of(i % parts * width, 128), width)
        return pltpu.make_async_copy(left_i.at[i // parts, :, cols], turn_in.at[i % 2], turn_in_sem.at[i % 2])

    def turn_store(i):
        rows_at = pl.ds(pl.multiple_of(i % parts * width, 128), width)
        cols = pl.ds(pl.multiple_of(i // parts * seq, 128), seq)
        return pltpu.make_async_copy(turn_out.at[i % 2], left_o.at[rows_at, cols], turn_out_sem.at[i % 2])

    def turn_left():
        turn_load(0).start()

        def body(i, c):
            @pl.when(i + 1 < turns)
            def _():
                turn_load(i + 1).start()

            turn_load(i).wait()

            @pl.when(i >= 2)
            def _():
                turn_store(i - 2).wait()

            turn_out[i % 2] = turn_in[i % 2].T
            turn_store(i).start()
            return c

        lax.fori_loop(0, turns, body, 0)
        turn_store(turns - 2).wait()
        turn_store(turns - 1).wait()

    @pl.when(r == 0)
    def _():
        greet(stage, count)
        small_o[...] = jnp.zeros_like(small_o)

        @pl.when(last)
        def _():
            for i in range(row_count):
                seed_copy(i).start()

        for name in ("n2", "rs2"):
            load_copy(name, 0).start()
        weight_copy(0).start()
        for name in early[2:]:
            load_copy(name, 0).start()
        for k in (1, 2, 3):
            weight_copy(k).start()
        for name in late:
            load_copy(name, 0).start()

        @pl.when(stage < count - 2)
        def _():
            turn_left()

    @pl.when(last)
    def _():
        seed_copy(r).wait()

    @pl.when(jnp.logical_not(last))
    def _():
        hop(r).wait_recv()

    length = lens[r]
    m0, m1, m2 = scales[0, 0], scales[0, 1], scales[0, 2]
    i0, i1, i2 = 1.0 / m0, 1.0 / m1, 1.0 / m2

    offsets = {}
    at_col = 0
    for name, size in (
        ("gain0", width), ("gain1", width), ("shift0", width), ("shift1", width),
        ("out", width), ("down", width), ("up", ff), ("qkv", 3 * width),
    ):
        offsets[name] = at_col
        at_col += size

    def blocks(size, body, init=0, begin=0, end=seq):
        step = lambda i, c: body(i * size, pl.ds(i * size, size), c)
        return lax.fori_loop(begin // size, end // size, step, init, unroll=True)

    def weave(dots, size, body, init=0):
        total, cut = seq // size, 0
        for k, dot in enumerate(dots):
            dot()
            begin, cut = cut, total * (k + 1) // len(dots)
            init = blocks(size, body, init, begin * size, cut * size)
        return init

    def row_mask(start, size):
        return (start + lax.broadcasted_iota(jnp.int32, (size, 1), 0)) < length

    def put_small(name, v, col=0):
        small_o[:, pl.ds(offsets[name] + col, v.shape[1])] += v

    no_sum = jnp.zeros((8, width), F32)

    for name in early:
        load_copy(name, r).wait()

    @pl.when(r > 0)
    def _():
        for name in ("ddn", "dup", "dbr"):
            save_copy(name).wait()

    @pl.when(r == 0)
    def _():
        for k in (0, 1):
            weight_copy(k).wait()

    def norm_two(start, at, sums):
        dy = jnp.where(row_mask(start, BLOCK), gin[r, at, :].astype(F32), 0.0)
        n = n2_s[at, :].astype(F32)
        e = dy * gain[1:2, :]
        mean_e = jnp.mean(e, -1, keepdims=True)
        mean_en = jnp.mean(e * n, -1, keepdims=True)
        d = (e - mean_e - n * mean_en) * rs2_s[at, 0:1]
        dr[at, :] = d
        ddn_s[at, :] = d.astype(BF16)
        return sums[0] + fold_rows(dy * n), sums[1] + fold_rows(dy), sums[2] + fold_rows(d)

    for name, v in zip(("gain1", "shift1", "down"), blocks(BLOCK, norm_two, (no_sum,) * 3)):
        put_small(name, v)

    chunks = ff // CHUNK

    def dact_chunk(c):
        def piece_of(k):
            def run():
                at = pl.ds(c * CHUNK + k * PIECE, PIECE)
                up_s[c % 2, :, pl.ds(k * PIECE, PIECE)] = dot_nt(ddn_s[...], w_down[at, :])

            return run

        return [piece_of(k) for k in range(CHUNK // PIECE)]

    def slope_chunk(c):
        cols = pl.ds(c * CHUNK, CHUNK)

        def body(start, at, total):
            d = (0.5 * up_s[c % 2, at, :]) * sl_s[at, cols].astype(F32)
            dup_s[at, cols] = d.astype(BF16)
            return total + fold_rows(d)

        return body

    def dhid_chunk(c):
        cols = pl.ds(c * CHUNK, CHUNK)

        def piece_of(k):
            def run():
                at = pl.ds(k * PIECE, PIECE)
                part = dot_nt(dup_s[:, cols], w_up[at, cols])
                acc[:, at] = part if c == 0 else acc[:, at] + part

            return run

        return [piece_of(k) for k in range(width // PIECE)]

    for dot in dact_chunk(0):
        dot()
    for c in range(chunks):
        dots = []
        if c + 1 < chunks:
            dots += dact_chunk(c + 1)
        if c > 0:
            dots += dhid_chunk(c - 1)
        put_small("up", weave(dots, BLOCK, slope_chunk(c), jnp.zeros((8, CHUNK), F32)), c * CHUNK)

    def norm_one(start, at, sums):
        n = n1_s[at, :].astype(F32)
        t = jnp.tanh((n * gain[0:1, :] + shift[0:1, :]) * i2)
        dy = dr[at, :] + acc[at, :] * (1.0 - t * t)
        e = dy * gain[0:1, :]
        mean_e = jnp.mean(e, -1, keepdims=True)
        mean_en = jnp.mean(e * n, -1, keepdims=True)
        d = (e - mean_e - n * mean_en) * rs1_s[at, 0:1]
        dr[at, :] = d
        dbr_s[at, :] = d.astype(BF16)
        return sums[0] + fold_rows(dy * n), sums[1] + fold_rows(dy), sums[2] + fold_rows(d)

    def dhid_last(k):
        def run():
            at, cols = pl.ds(k * PIECE, PIECE), pl.ds((chunks - 1) * CHUNK, CHUNK)
            acc[at, :] += dot_nt(dup_s[at, cols], w_up[:, cols])

        return run

    dhid_last(0)()
    dots = [dhid_last(k) for k in range(1, seq // PIECE)] + [lambda: None]
    for name, v in zip(("gain0", "shift0", "out"), weave(dots, BLOCK, norm_one, (no_sum,) * 3)):
        put_small(name, v)

    for name in ("ddn", "dup", "dbr"):
        save_copy(name).start()

    @pl.when(r + 1 < rows)
    def _():
        for name in early:
            load_copy(name, r + 1).start()

    for name in late:
        load_copy(name, r).wait()

    @pl.when(r > 0)
    def _():
        save_copy("dproj").wait()

    @pl.when(r == 0)
    def _():
        for k in (2, 3):
            weight_copy(k).wait()

    def dctx_piece(g):
        def run():
            at = pl.ds(g * PIECE, PIECE)
            acc[:, at] = dot_nt(dbr_s[...], w_out[at, :])

        return run

    def dx_part(g, k):
        def run():
            at = pl.ds(k * PIECE, PIECE)
            total = None
            for part in range(3):
                cols = slice(part * width + g * PIECE, part * width + (g + 1) * PIECE)
                piece = dot_nt(dproj_s[:, cols], w_qkv[at, cols])
                total = piece if total is None else total + piece
            dx[:, at] = total if g == 0 else dx[:, at] + total

        return run

    zero = jnp.zeros((), BF16)
    head_scale = jnp.asarray(HEAD_DIM ** -0.5, BF16)

    def prepare(p):
        slot = p % 2
        cols = slice(p * PAIR, (p + 1) * PAIR)

        def body(start, at, c):
            lo = lax.broadcasted_iota(jnp.int32, (OPS, PAIR), 1) < HEAD_DIM
            ctx = ctx_s[at, cols]
            t = jnp.tanh(ctx * i1)
            low = (acc[at, cols] * (1.0 - t * t) * inv_s[at, cols]).astype(BF16)
            dctx_s[slot, at, :] = low
            inner = low.astype(F32) * ctx
            whole_sum = jnp.sum(inner, -1, keepdims=True)
            lower = jnp.sum(jnp.where(lo, inner, 0.0), -1, keepdims=True)
            inner_s[slot, 0, at, :] = jnp.broadcast_to(lower, (OPS, PAIR))
            inner_s[slot, 1, at, :] = jnp.broadcast_to(whole_sum - lower, (OPS, PAIR))
            v2 = qkv_s[at, 2 * width + p * PAIR : 2 * width + (p + 1) * PAIR]
            ops_s[slot, 0, at, :] = jnp.where(lo, v2, zero)
            ops_s[slot, 1, at, :] = jnp.where(lo, zero, v2)
            return c

        blocks(OPS, body)
        q_t[slot] = (qkv_s[:, cols] * head_scale).T
        k_t[slot] = qkv_s[:, width + p * PAIR : width + (p + 1) * PAIR].T
        do_t[slot] = dctx_s[slot].T

    def scores(h):
        slot, side = h // 2 % 2, h % 2

        def piece_of(k):
            def run():
                keys = pl.ds(k * PIECE, PIECE)
                g_s[side, :, keys] = dot_nt(dctx_s[slot], ops_s[slot, side, keys, :])

            return run

        return [piece_of(k) for k in range(seq // PIECE)]

    def soften(h):
        slot, side = h // 2 % 2, h % 2

        def body(start, at, c):
            inner = jnp.concatenate([inner_s[slot, side, at, :]] * (seq // PAIR), 1)
            ds_s[side, at, :] = (e_s[h, at, :].astype(F32) * (g_s[side, at, :] - inner)).astype(BF16)
            return c

        return body

    def collect(h):
        slot, side = h // 2 % 2, h % 2
        rows_at = slice(side * HEAD_DIM, (side + 1) * HEAD_DIM)

        def grad_v(k):
            def run():
                keys = pl.ds(k * PIECE, PIECE)
                gv_s[rows_at, keys] = dot_nn(do_t[slot, rows_at, :], e_s[h, :, keys])

            return run

        def grad_k(k):
            def run():
                keys = pl.ds(k * PIECE, PIECE)
                gk_s[rows_at, keys] = dot_nn(q_t[slot, rows_at, :], ds_s[side, :, keys])

            return run

        def grad_q(k):
            def run():
                queries = pl.ds(k * PIECE, PIECE)
                gq_s[rows_at, queries] = dot_nt(k_t[slot, rows_at, :], ds_s[side, queries, :])

            return run

        return [make(k) for make in (grad_v, grad_k, grad_q) for k in range(seq // PIECE)]

    def settle(p):
        for part, grad in enumerate((gq_s[...] * (HEAD_DIM ** -0.5), gk_s[...], gv_s[...])):
            dproj_s[:, part * width + p * PAIR : part * width + (p + 1) * PAIR] = grad.astype(BF16).T

    heads = 2 * (width // PAIR)
    groups = width // PIECE
    span = heads // groups
    dctx_piece(0)()
    prepare(0)
    for dot in scores(0):
        dot()
    for h in range(heads):
        g, turn = h // span, h % span
        dots = []
        if h + 1 < heads:
            if (h + 1) % 2 == 0:
                prepare((h + 1) // 2)
            dots += scores(h + 1)
        if h > 0:
            dots += collect(h - 1)
        if g + 1 < groups and turn == 0:
            dots.append(dctx_piece(g + 1))
        if g > 0 and turn > 0:
            dots.append(dx_part(g - 1, turn - 1))
        weave(dots, BLOCK, soften(h))
        if h > 0 and h % 2 == 0:
            settle(h // 2 - 1)
    for dot in collect(heads - 1):
        dot()
    settle(heads // 2 - 1)

    def quant_in(k):
        cols = pl.ds(k * PIECE, PIECE)
        values = pl.ds(2 * width + k * PIECE, PIECE)

        def body(start, at, sums):
            t = jnp.tanh(x_s[at, cols].astype(F32) * i0)
            gin[r, at, cols] = (dr[at, cols] + dx[at, cols] * (1.0 - t * t)).astype(BF16)
            return (
                sums[0] + fold_rows(dproj_s[at, cols].astype(F32)),
                sums[1] + fold_rows(dproj_s[at, values].astype(F32)),
            )

        return body

    dx_part(groups - 1, 0)()
    pieces = width // PIECE
    for k in range(pieces):
        dots = [dx_part(groups - 1, k + 1)] if k + 1 < pieces else [lambda: None]
        sums = weave(dots, BLOCK, quant_in(k), (jnp.zeros((8, PIECE), F32),) * 2)
        put_small("qkv", sums[0], k * PIECE)
        put_small("qkv", sums[1], 2 * width + k * PIECE)
    save_copy("dproj").start()

    @pl.when(r + 1 < rows)
    def _():
        for name in late:
            load_copy(name, r + 1).start()

    @pl.when(jnp.logical_not(first))
    def _():
        hop(r).start()

    @pl.when(first)
    def _():
        tok_copy(r).start()

    @pl.when(r == rows - 1)
    def _():
        @pl.when(stage >= count - 2)
        def _():
            turn_left()

        for name in save_order:
            save_copy(name).wait()

        @pl.when(jnp.logical_not(first))
        def _():
            for i in range(row_count):
                hop(i).wait_send()

        @pl.when(first)
        def _():
            for i in range(row_count):
                tok_copy(i).wait()


def whole(a):
    return pl.BlockSpec(a.shape, lambda r, n=a.ndim: (0,) * n, pipeline_mode=pl.Buffered(1))


ANYWHERE = pl.BlockSpec(memory_space=pl.ANY)
SCALAR = pl.BlockSpec(memory_space=pltpu.SMEM)
VMEM_LIMIT = 60 * 1024 * 1024


def run_forward(count, tokens, lengths, scales, weights):
    w_qkv, b_qkv, w_out, b_out, w_up, b_up, w_down, b_down, gain, shift = weights
    rows, seq, width = tokens.shape
    ff = w_up.shape[1]
    big = lambda n, t: jax.ShapeDtypeStruct((rows, seq, n), t)
    saves = [
        (width, BF16), (3 * width, BF16), (width, F32), (width, F32), (width, BF16), (128, F32),
        (ff, BF16), (width, BF16), (128, F32),
    ]
    heads = width // HEAD_DIM
    lefts = [(ff, BF16), (width, BF16), (width, BF16), (width, BF16)]
    heavy = (w_qkv, w_out, w_up, w_down)
    dense = (b_qkv, b_out, b_up, b_down, gain, shift)
    tok = rows * seq
    return pl.pallas_call(
        lambda *refs: fwd_kernel(count, *refs),
        grid=(rows,),
        in_specs=[SCALAR, SCALAR, ANYWHERE] + [ANYWHERE] * 4 + [whole(a) for a in dense],
        out_specs=[ANYWHERE] * 12 + [pl.BlockSpec((4, 8, 128), lambda r: (0, 0, 0))],
        out_shape=[big(n, t) for n, t in saves]
        + [
            big(ff + 3 * width, BF16),
            jax.ShapeDtypeStruct((rows, heads, seq, seq), BF16),
            jax.ShapeDtypeStruct((rows, seq // count, width), BF16),
            jax.ShapeDtypeStruct((4, 8, 128), F32),
        ],
        scratch_shapes=[pltpu.VMEM(a.shape, a.dtype) for a in heavy]
        + [pltpu.SemaphoreType.DMA((4,))]
        + [pltpu.VMEM((rows, seq, width), BF16), pltpu.VMEM((rows, seq, width), BF16)]
        + [pltpu.VMEM((seq, n), t) for n, t in saves[1:] + lefts]
        + [
            pltpu.VMEM((seq, width), F32),
            pltpu.VMEM((seq, width), F32),
            pltpu.VMEM((2, seq, CHUNK), F32),
            pltpu.VMEM((2, 6, seq, PAIR), BF16),
            pltpu.VMEM((2, seq, seq), F32),
            pltpu.VMEM((heads, seq, seq), BF16),
            pltpu.VMEM((2, seq, PAIR), F32),
            pltpu.VMEM((seq, 128), F32),
            pltpu.SemaphoreType.DMA((14,)),
            pltpu.SemaphoreType.DMA((rows,)),
            pltpu.SemaphoreType.DMA((rows,)),
            pltpu.SemaphoreType.DMA((rows,)),
            pltpu.SemaphoreType.DMA((rows, count)),
            pltpu.SemaphoreType.DMA((rows,)),
        ],
        compiler_params=pltpu.CompilerParams(
            collective_id=0, has_side_effects=True, vmem_limit_bytes=VMEM_LIMIT,
            dimension_semantics=("arbitrary",),
        ),
        cost_estimate=pl.CostEstimate(
            flops=2 * tok * (4 * width * width + 2 * width * ff + 2 * seq * width),
            bytes_accessed=tok * 28000, transcendentals=tok * 3 * ff,
        ),
    )(lengths, scales, tokens, *heavy, *dense)


def run_backward(count, seeds, lengths, scales, weights, kept):
    w_qkv, b_qkv, w_out, b_out, w_up, b_up, w_down, b_down, gain, shift = weights
    *loads, left, exps = kept
    loads.append(exps)
    rows, seq, width = seeds.shape
    ff = w_up.shape[1]
    big = lambda n, t: jax.ShapeDtypeStruct((rows, seq, n), t)
    saves = [(3 * width, BF16), (width, BF16), (ff, BF16), (width, BF16)]
    heavy = (w_qkv, w_out, w_up, w_down)
    dense = (gain, shift)
    tok = rows * seq
    small = 6 * width + ff + 3 * width
    return pl.pallas_call(
        lambda *refs: bwd_kernel(count, *refs),
        grid=(rows,),
        in_specs=[SCALAR, SCALAR, ANYWHERE] + [ANYWHERE] * 4 + [whole(a) for a in dense] + [ANYWHERE] * 11,
        out_specs=[ANYWHERE] * 6 + [pl.BlockSpec((8, small), lambda r: (0, 0))],
        out_shape=[big(n, t) for n, t in saves]
        + [
            big(width, BF16), jax.ShapeDtypeStruct((left.shape[2], rows * seq), BF16),
            jax.ShapeDtypeStruct((8, small), F32),
        ],
        scratch_shapes=[pltpu.VMEM(a.shape, a.dtype) for a in heavy]
        + [
            pltpu.SemaphoreType.DMA((4,)),
            pltpu.VMEM((2, seq, width), BF16),
            pltpu.VMEM((2, width, seq), BF16),
            pltpu.SemaphoreType.DMA((2,)),
            pltpu.SemaphoreType.DMA((2,)),
        ]
        + [pltpu.VMEM((rows, seq, width), BF16)]
        + [pltpu.VMEM(a.shape[1:], a.dtype) for a in loads]
        + [pltpu.VMEM((seq, n), t) for n, t in saves]
        + [
            pltpu.VMEM((2, seq, PAIR), BF16),
            pltpu.VMEM((seq, width), F32),
            pltpu.VMEM((seq, width), F32),
            pltpu.VMEM((seq, width), F32),
            pltpu.VMEM((2, seq, CHUNK), F32),
            pltpu.VMEM((2, 2, seq, PAIR), BF16),
            pltpu.VMEM((2, seq, seq), F32),
            pltpu.VMEM((2, seq, seq), BF16),
            pltpu.VMEM((PAIR, seq), F32),
            pltpu.VMEM((PAIR, seq), F32),
            pltpu.VMEM((PAIR, seq), F32),
            pltpu.VMEM((2, PAIR, seq), BF16),
            pltpu.VMEM((2, PAIR, seq), BF16),
            pltpu.VMEM((2, PAIR, seq), BF16),
            pltpu.VMEM((2, 2, seq, PAIR), F32),
            pltpu.SemaphoreType.DMA((10,)),
            pltpu.SemaphoreType.DMA((4,)),
            pltpu.SemaphoreType.DMA((rows,)),
            pltpu.SemaphoreType.DMA((rows,)),
            pltpu.SemaphoreType.DMA((rows,)),
            pltpu.SemaphoreType.DMA((rows,)),
        ],
        compiler_params=pltpu.CompilerParams(
            collective_id=1, has_side_effects=True, vmem_limit_bytes=VMEM_LIMIT,
            dimension_semantics=("arbitrary",),
        ),
        cost_estimate=pl.CostEstimate(
            flops=2 * tok * (4 * width * width + 2 * width * ff + 5 * seq * width),
            bytes_accessed=tok * 28000, transcendentals=tok * ff,
        ),
    )(lengths, scales, seeds, *heavy, *dense, left, *loads)


def ring_to_dp(pos, n):
    return jnp.where(pos < n // 2, 2 * pos, 2 * (n - pos) - 1)


def dp_to_ring(j, n):
    return jnp.where(j % 2 == 0, j // 2, n - 1 - j // 2)


def grad_kernel(count, n, *refs):
    (
        left, ddn, dup, dproj, dbr, small, g0,
        gq_o, go_o, gu_o, gd_o, small_o, gtok_o,
        slots_d, slots_u, slots_q, slots_s, wide_v, thin_v, ddn_v, dup_v, dpo_v,
        wide_sem, thin_sem, right_sem,
        send_d, recv_d, send_u, recv_u, send_q, recv_q, send_s, recv_s, tok_send, tok_recv,
    ) = refs
    width = ddn.shape[1]
    ff = dup.shape[1]
    shard, shard_ff = width // n, ff // n
    row_count, seq = g0.shape[0], g0.shape[1]
    piece = seq // count
    stage = lax.axis_index("pipe")
    me = lax.axis_index("dp")
    pos = dp_to_ring(me, n)
    first = stage == 0
    ahead = ring_to_dp(lax.rem(pos + 1, n), n)
    behind = ring_to_dp(lax.rem(pos + n - 1, n), n)
    target = (ahead, behind)

    def chunk(d, step):
        at = pos + 2 * n - 1 - step if d == 0 else pos + 1 + step
        return ring_to_dp(lax.rem(at, n), n)

    def wide_copy(d, step):
        rows = pl.ds(pl.multiple_of(chunk(d, step) * shard_ff, 16), shard_ff)
        return pltpu.make_async_copy(left.at[rows, :], wide_v.at[d], wide_sem.at[d])

    def thin_copy(k, d, step):
        rows = pl.ds(pl.multiple_of(ff + k * width + chunk(d, step) * shard, 16), shard)
        return pltpu.make_async_copy(left.at[rows, :], thin_v.at[k, d], thin_sem.at[k, d])

    rights = [
        (ddn, ddn_v), (dup, dup_v), (dproj, dpo_v.at[:, pl.ds(0, 3 * width)]),
        (dbr, dpo_v.at[:, pl.ds(3 * width, width)]),
    ]

    def right_copy(k):
        return pltpu.make_async_copy(rights[k][0], rights[k][1], right_sem.at[k])

    for d in range(2):
        wide_copy(d, 0).start()
    right_copy(0).start()
    right_copy(1).start()
    for d in range(2):
        thin_copy(0, d, 0).start()
    right_copy(2).start()
    right_copy(3).start()
    for d in range(2):
        thin_copy(1, d, 0).start()
        if d == 1:
            thin_copy(2, d, 0).start()

    barrier = pltpu.get_barrier_semaphore()
    for peer in target:
        pl.semaphore_signal(barrier, inc=1, device_id={"dp": peer}, device_id_type=LOGICAL)

    @pl.when(first)
    def _():
        pl.semaphore_wait(barrier, 1 + count)

    @pl.when(jnp.logical_not(first))
    def _():
        pl.semaphore_signal(barrier, inc=1, device_id={"pipe": jnp.int32(0)}, device_id_type=LOGICAL)
        pl.semaphore_wait(barrier, 2)

    def tok_part(i, p):
        return pltpu.make_async_remote_copy(
            src_ref=g0.at[i, pl.ds(p * piece, piece)], dst_ref=gtok_o.at[i],
            send_sem=tok_send.at[i, p], recv_sem=tok_recv.at[i],
            device_id={"pipe": jnp.int32(p)}, device_id_type=LOGICAL,
        )

    def tok_own(i):
        return pltpu.make_async_copy(g0.at[i, pl.ds(0, piece)], gtok_o.at[i], tok_send.at[i, 0])

    @pl.when(first)
    def _():
        for i in range(row_count):
            for p in range(1, count):
                tok_part(i, p).start()
            tok_own(i).start()

    def message(slots, send, recv, d, at):
        return pltpu.make_async_remote_copy(
            src_ref=slots.at[d, at], dst_ref=slots.at[d, jnp.minimum(at + 1, n - 1)],
            send_sem=send.at[d, at], recv_sem=recv.at[d, jnp.minimum(at + 1, n - 1)],
            device_id={"dp": target[d]}, device_id_type=LOGICAL,
        )

    def arrived(slots, send, recv, d, at):
        return pltpu.make_async_remote_copy(
            src_ref=slots.at[d, at], dst_ref=slots.at[d, at],
            send_sem=send.at[d, at], recv_sem=recv.at[d, at],
            device_id={"dp": target[d]}, device_id_type=LOGICAL,
        )

    def lane(slots, send, recv, d, step, mine, finish):
        @pl.when(step == 0)
        def _():
            slots[d, 0] = mine.astype(BF16)

        @pl.when(step > 0)
        def _():
            arrived(slots, send, recv, d, step).wait_recv()

            @pl.when(step < n - 1)
            def _():
                slots[d, step] = (slots[d, step].astype(F32) + mine).astype(BF16)

            @pl.when(step == n - 1)
            def _():
                finish(slots[d, step].astype(F32) + mine)

        @pl.when(step < n - 1)
        def _():
            message(slots, send, recv, d, step).start()

    def small_message(at):
        return pltpu.make_async_remote_copy(
            src_ref=slots_s.at[at], dst_ref=slots_s.at[jnp.minimum(at + 1, n - 1)],
            send_sem=send_s.at[at], recv_sem=recv_s.at[jnp.minimum(at + 1, n - 1)],
            device_id={"dp": target[0]}, device_id_type=LOGICAL,
        )

    def small_arrived(at):
        return pltpu.make_async_remote_copy(
            src_ref=slots_s.at[at], dst_ref=slots_s.at[at], send_sem=send_s.at[at],
            recv_sem=recv_s.at[at], device_id={"dp": target[0]}, device_id_type=LOGICAL,
        )

    sum_rows = lax.broadcasted_iota(jnp.int32, (16, 128), 0) < 9

    def small_step(step):
        mine = small[chunk(0, step)]

        @pl.when(step == 0)
        def _():
            slots_s[0] = mine

        @pl.when(step > 0)
        def _():
            small_arrived(step).wait_recv()
            got = slots_s[step]
            slots_s[step] = jnp.where(sum_rows, got + mine, jnp.maximum(got, mine))

        @pl.when(step < n - 1)
        def _():
            small_message(step).start()

        @pl.when(step == n - 1)
        def _():
            small_o[...] = slots_s[step]

    half, half_ff = width // 2, ff // 2

    def fetched(copy, step, *args):
        copy(*args, step).wait()

    def refill(copy, step, *args):
        @pl.when(step < n - 1)
        def _():
            copy(*args, step + 1).start()

    def right_ready(k, step):
        @pl.when(step == 0)
        def _():
            right_copy(k).wait()

    def turn(step, _):
        right_ready(0, step)
        for d in range(2):
            cols = slice(d * half, (d + 1) * half)
            fetched(wide_copy, step, d)
            mine = dot_nn(wide_v[d], ddn_v[:, cols])
            refill(wide_copy, step, d)

            def finish_down(total):
                gd_o[:, cols] = total

            lane(slots_d, send_d, recv_d, d, step, mine, finish_down)
        small_step(step)
        right_ready(1, step)
        for d in range(2):
            cols = slice(d * half_ff, (d + 1) * half_ff)
            fetched(thin_copy, step, 0, d)
            mine = dot_nn(thin_v[0, d], dup_v[:, cols])
            refill(thin_copy, step, 0, d)

            def finish_up(total):
                gu_o[:, cols] = total

            lane(slots_u, send_u, recv_u, d, step, mine, finish_up)
        right_ready(2, step)
        right_ready(3, step)
        fetched(thin_copy, step, 1, 0)
        mine = dot_nn(thin_v[1, 0], dpo_v[:, 0 : 2 * width])
        refill(thin_copy, step, 1, 0)

        def finish_ahead(total):
            gq_o[:, 0 : 2 * width] = total

        lane(slots_q, send_q, recv_q, 0, step, mine, finish_ahead)
        fetched(thin_copy, step, 1, 1)
        fetched(thin_copy, step, 2, 1)
        mine = jnp.concatenate(
            [
                dot_nn(thin_v[1, 1], dpo_v[:, 2 * width : 3 * width]),
                dot_nn(thin_v[2, 1], dpo_v[:, 3 * width : 4 * width]),
            ],
            1,
        )
        refill(thin_copy, step, 1, 1)
        refill(thin_copy, step, 2, 1)

        def finish_behind(total):
            gq_o[:, 2 * width : 3 * width] = total[:, 0:width]
            go_o[...] = total[:, width : 2 * width]

        lane(slots_q, send_q, recv_q, 1, step, mine, finish_behind)
        return 0

    lax.fori_loop(0, n, turn, 0)

    def drain(at, _):
        for d in range(2):
            message(slots_d, send_d, recv_d, d, at).wait_send()
            message(slots_u, send_u, recv_u, d, at).wait_send()
            message(slots_q, send_q, recv_q, d, at).wait_send()
        small_message(at).wait_send()
        return 0

    lax.fori_loop(0, n - 1, drain, 0)

    @pl.when(first)
    def _():
        for i in range(row_count):
            for p in range(1, count):
                tok_part(i, p).wait_send()
            tok_own(i).wait()

    @pl.when(jnp.logical_not(first))
    def _():
        for i in range(row_count):
            tok_part(i, 1).wait_recv()


def run_grads(count, n, left, dproj, dbr, dup, ddn, g0, small):
    rows, seq, width = g0.shape
    ff = dup.shape[2]
    flat = lambda a: a.reshape(rows * seq, a.shape[2])
    tok = rows * seq
    shard, shard_ff = width // n, ff // n
    ops = [left] + [flat(a) for a in (ddn, dup, dproj, dbr)]
    vmem = pl.BlockSpec(memory_space=pltpu.VMEM)
    sem = pltpu.SemaphoreType.DMA
    return pl.pallas_call(
        lambda *refs: grad_kernel(count, n, *refs),
        in_specs=[ANYWHERE] * 5 + [vmem, ANYWHERE],
        out_specs=[vmem] * 5 + [ANYWHERE],
        out_shape=[
            jax.ShapeDtypeStruct((shard, 3 * width), F32),
            jax.ShapeDtypeStruct((shard, width), F32),
            jax.ShapeDtypeStruct((shard, ff), F32),
            jax.ShapeDtypeStruct((shard_ff, width), F32),
            jax.ShapeDtypeStruct((16, 128), F32),
            jax.ShapeDtypeStruct((rows, seq // count, width), BF16),
        ],
        scratch_shapes=[
            pltpu.VMEM((2, n, shard_ff, width // 2), BF16),
            pltpu.VMEM((2, n, shard, ff // 2), BF16),
            pltpu.VMEM((2, n, shard, 2 * width), BF16),
            pltpu.VMEM((n, 16, 128), F32),
            pltpu.VMEM((2, shard_ff, tok), BF16),
            pltpu.VMEM((3, 2, shard, tok), BF16),
            pltpu.VMEM((tok, width), BF16),
            pltpu.VMEM((tok, ff), BF16),
            pltpu.VMEM((tok, 4 * width), BF16),
            sem((2,)), sem((3, 2)), sem((4,)),
            sem((2, n)), sem((2, n)), sem((2, n)), sem((2, n)), sem((2, n)), sem((2, n)),
            sem((n,)), sem((n,)), sem((rows, count)), sem((rows,)),
        ],
        compiler_params=pltpu.CompilerParams(
            collective_id=2, has_side_effects=True, vmem_limit_bytes=VMEM_LIMIT,
        ),
        cost_estimate=pl.CostEstimate(
            flops=2 * tok * (4 * width * width + 2 * width * ff), bytes_accessed=tok * 25000, transcendentals=0,
        ),
    )(*ops, small, g0)


def weight_grad(left, right):
    g = jnp.einsum("rsd,rse->de", left, right, preferred_element_type=F32).astype(BF16)
    return lax.psum_scatter(g, "dp", scatter_dimension=0, tiled=True).astype(F32)


def share_pieces(whole_rows, count, stage):
    piece = whole_rows.shape[1] // count
    mine = whole_rows[:, :piece]
    for p in range(1, count):
        got = lax.ppermute(whole_rows[:, p * piece : (p + 1) * piece], "pipe", [(0, p)])
        mine = jnp.where(stage == p, got, mine)
    return mine


def shards(
    tokens, lengths, ema_scales, w_qkv, bias_qv, w_out, bias_out, w_up, bias_up, w_down, bias_down,
    ln_gain, ln_bias, cotangent,
):
    count = lax.axis_size("pipe")
    n = lax.axis_size("dp")
    width = tokens.shape[2]
    ff = w_up.shape[2]
    b_qkv = jnp.concatenate([bias_qv[:, :width], jnp.zeros_like(bias_qv[:, :width]), bias_qv[:, width:]], 1)
    weights = (
        w_qkv[0], b_qkv, w_out[0], bias_out, w_up[0], bias_up, w_down[0], bias_down, ln_gain[0], ln_bias[0],
    )
    *kept, mixed, peaks = run_forward(count, tokens, lengths, ema_scales, weights)
    left = kept[-2]
    dproj, dbr, dup, ddn, g0, turned, small = run_backward(
        count, cotangent, lengths, ema_scales, weights, kept
    )
    sums = jnp.sum(small, 0)
    parts, at = [], 0
    for size in (width, width, width, width, width, width, ff, width, width, width):
        parts.append(sums[at : at + size])
        at += size
    parts[7:] = [jnp.concatenate([parts[7], parts[9]])]
    packed = jnp.concatenate([v.reshape(n, -1) for v in parts], 1)
    peak = jnp.max(peaks, (1, 2))
    sums_width = packed.shape[1]
    if n >= 4 and n % 2 == 0 and width // n % 16 == 0 and ff // n % 128 == 0 and sums_width == 9 * 128:
        top = jnp.broadcast_to(jnp.pad(peak, (0, 124))[None, None], (n, 7, 128))
        with_peak = jnp.concatenate([packed.reshape(n, 9, 128), top], 1)
        g_qkv, g_out, g_up, g_down, small_sum, grad_tokens = run_grads(
            count, n, turned, dproj, dbr, dup, ddn, g0, with_peak
        )
        mine = small_sum[:9].reshape(1, sums_width)
        batch_max = small_sum[9:10, :4]
    else:
        g_down = weight_grad(left[:, :, :ff], ddn)
        g_up = weight_grad(left[:, :, ff : ff + width], dup)
        g_qkv = weight_grad(left[:, :, ff + width : ff + 2 * width], dproj)
        g_out = weight_grad(left[:, :, ff + 2 * width :], dbr)
        mine = lax.psum_scatter(packed, "dp", scatter_dimension=0, tiled=True)
        batch_max = lax.pmax(peak, "dp")[None]
        grad_tokens = share_pieces(g0, count, lax.axis_index("pipe"))
    outs, at = [], 0
    for size in (width, width, width, width, width, width, ff, 2 * width):
        outs.append(mine[:, at : at + size // n])
        at += size // n
    gain0, gain1, shift0, shift1, s_out, s_down, s_up, s_qv = outs
    g_gain = jnp.stack([gain0, gain1], 1)
    g_shift = jnp.stack([shift0, shift1], 1)
    return (
        mixed, grad_tokens, g_qkv[None], s_qv, g_out[None], s_out, g_up[None], s_up, g_down[None], s_down,
        g_gain, g_shift, batch_max,
    )


def solution(mesh):
    return jax.shard_map(
        shards,
        mesh=mesh,
        in_specs=(
            P("dp", None, None), P("dp"), P("pipe", None), P("pipe", None, None), P("pipe", None),
            P("pipe", None, None), P("pipe", None), P("pipe", None, None), P("pipe", None),
            P("pipe", None, None), P("pipe", None), P("pipe", None, None), P("pipe", None, None),
            P("dp", None, None),
        ),
        out_specs=(
            P("dp", "pipe", None), P("dp", "pipe", None), P("pipe", "dp", None), P("pipe", "dp"),
            P("pipe", "dp", None), P("pipe", "dp"), P("pipe", "dp", None), P("pipe", "dp"),
            P("pipe", "dp", None), P("pipe", "dp"), P("pipe", None, "dp"), P("pipe", None, "dp"),
            P("pipe", None),
        ),
        check_vma=False,
    )
```

```python
import jax
import jax.numpy as jnp
from jax import lax
from jax.experimental import pallas as pl
from jax.experimental.pallas import tpu as pltpu
from jax.sharding import PartitionSpec as P

HEAD_DIM = 64
PAIR = 2 * HEAD_DIM
EPS = 1e-06
MASKED = -1000000000.0
CHUNK = 512
PIECE = 256
BLOCK = 16
OPS = 64
LOGICAL = pl.DeviceIdType.MESH
F32 = jnp.float32
BF16 = jnp.bfloat16

ERF_POLY = (
    0.7978823511659165,
    0.03634481045269742,
    -4.5110171354091134e-05,
    -5.02654469142584e-05,
    3.0867937984305273e-06,
    -6.60140005994544e-08,
)
ERF_CLAMP = 5.2 * 5.2
HALF_LOG2E = -0.7213475204444817
LOG2_TWICE_DENSITY = -0.3257480647361593


def dot_nn(a, b):
    return jnp.dot(a, b, preferred_element_type=F32)


def dot_nt(a, b):
    return lax.dot_general(a, b, (((1,), (1,)), ((), ())), preferred_element_type=F32)


def dot_tn(a, b):
    return lax.dot_general(a, b, (((0,), (0,)), ((), ())), preferred_element_type=F32)


def fold_rows(v):
    return jnp.sum(v.reshape(v.shape[0] // 8, 8, v.shape[1]), 0)


def peak_rows(v):
    tiles = [v[:, i : i + 128] for i in range(0, v.shape[1], 128)]
    top = tiles[0]
    for tile in tiles[1:]:
        top = jnp.maximum(top, tile)
    return jnp.max(top.reshape(v.shape[0] // 8, 8, 128), 0)


def greet(stage, count):
    barrier = pltpu.get_barrier_semaphore()
    for step in range(1, count):
        peer = lax.rem(stage + step, count)
        pl.semaphore_signal(barrier, inc=1, device_id={"pipe": peer}, device_id_type=LOGICAL)
    pl.semaphore_wait(barrier, count - 1)


def activation(u, ceiling, inv_ceiling):
    square = u * u
    w = jnp.minimum(square, ERF_CLAMP)
    poly = w * ERF_POLY[-1] + ERF_POLY[-2]
    for coef in ERF_POLY[-3::-1]:
        poly = poly * w + coef
    twice_cdf = 1.0 + jnp.tanh(u * poly)
    act = (0.5 * u) * twice_cdf
    ratio = jnp.tanh(act * inv_ceiling)
    twice_density = jnp.exp2(square * HALF_LOG2E + LOG2_TWICE_DENSITY)
    twice_slope = (1.0 - ratio * ratio) * (twice_cdf + u * twice_density)
    return act, ceiling * ratio, twice_slope


def fwd_kernel(count, *refs):
    (
        lens, scales, tokens, h_qkv, h_out, h_up, h_down, b_qkv, b_out, b_up, b_down, gain, shift,
        x_o, qkv_o, inv_o, ctx_o, n1_o, rs1_o, sl_o, n2_o, rs2_o, left_o, exp_o,
        mixed_o, peaks_o,
        w_qkv, w_out, w_up, w_down, w_sem,
        xin, xout, qkv_s, inv_s, ctx_s, n1_s, rs1_s, sl_s, n2_s, rs2_s, aq_s, hq_s, xq_s, cq_s,
        acc, hid, up_s, ops_s, s_s, e_s, o_s, amax_s,
        save_sem, in_sem, send_sem, recv_sem, mix_send, mix_recv,
    ) = refs
    r = pl.program_id(0)
    rows = pl.num_programs(0)
    row_count = tokens.shape[0]
    seq, width = tokens.shape[1], tokens.shape[2]
    ff = w_up.shape[1]
    piece = seq // count
    stage = lax.axis_index("pipe")
    first = stage == 0
    last = stage == count - 1

    left = {"aq": (0, ff), "hq": (ff, width), "xq": (ff + width, width), "cq": (ff + 2 * width, width)}
    staged = {
        "x": (xin.at[r], x_o), "qkv": (qkv_s, qkv_o), "inv": (inv_s, inv_o), "ctx": (ctx_s, ctx_o),
        "n1": (n1_s, n1_o), "rs1": (rs1_s, rs1_o), "sl": (sl_s, sl_o), "n2": (n2_s, n2_o),
        "rs2": (rs2_s, rs2_o), "aq": (aq_s, left_o), "hq": (hq_s, left_o), "xq": (xq_s, left_o),
        "cq": (cq_s, left_o), "exp": (e_s, exp_o),
    }
    order = list(staged)
    early = ("x", "xq", "qkv", "inv", "ctx", "cq", "exp")
    late = ("n1", "rs1", "hq", "aq", "sl", "n2", "rs2")
    fetches = [(h_qkv, w_qkv), (h_out, w_out), (h_up, w_up), (h_down, w_down)]

    def weight_copy(k):
        return pltpu.make_async_copy(fetches[k][0], fetches[k][1], w_sem.at[k])

    def save_copy(name):
        src, dst = staged[name]
        dst = dst.at[r]
        if name in left:
            dst = dst.at[:, pl.ds(*left[name])]
        return pltpu.make_async_copy(src, dst, save_sem.at[order.index(name)])

    def token_copy(i):
        return pltpu.make_async_copy(tokens.at[i], xin.at[i], in_sem.at[i])

    def hop(i):
        return pltpu.make_async_remote_copy(
            src_ref=xout.at[i], dst_ref=xin.at[i], send_sem=send_sem.at[i], recv_sem=recv_sem.at[i],
            device_id={"pipe": lax.rem(stage + 1, count)}, device_id_type=LOGICAL,
        )

    def mix_part(i, p):
        return pltpu.make_async_remote_copy(
            src_ref=xout.at[i, pl.ds(p * piece, piece)], dst_ref=mixed_o.at[i],
            send_sem=mix_send.at[i, p], recv_sem=mix_recv.at[i],
            device_id={"pipe": jnp.int32(p)}, device_id_type=LOGICAL,
        )

    def mix_own(i):
        return pltpu.make_async_copy(
            xout.at[i, pl.ds((count - 1) * piece, piece)], mixed_o.at[i], mix_send.at[i, count - 1]
        )

    @pl.when(r == 0)
    def _():
        greet(stage, count)
        peaks_o[...] = jnp.zeros_like(peaks_o)
        for k in range(4):
            weight_copy(k).start()

        @pl.when(first)
        def _():
            for i in range(row_count):
                token_copy(i).start()

    @pl.when(first)
    def _():
        token_copy(r).wait()

    @pl.when(jnp.logical_not(first))
    def _():
        hop(r).wait_recv()

    length = lens[r]
    m0, m1, m2, m3 = scales[0, 0], scales[0, 1], scales[0, 2], scales[0, 3]
    i0, i1, i2, i3 = 1.0 / m0, 1.0 / m1, 1.0 / m2, 1.0 / m3

    def row_mask(start, size):
        return (start + lax.broadcasted_iota(jnp.int32, (size, 1), 0)) < length

    def blocks(size, body, init=0, begin=0, end=seq):
        step = lambda i, c: body(i * size, pl.ds(i * size, size), c)
        return lax.fori_loop(begin // size, end // size, step, init, unroll=True)

    def weave(dots, size, body, init=0):
        total, cut = seq // size, 0
        for k, dot in enumerate(dots):
            dot()
            begin, cut = cut, total * (k + 1) // len(dots)
            init = blocks(size, body, init, begin * size, cut * size)
        return init

    no_peak = jnp.zeros((8, 128), F32)

    @pl.when(r > 0)
    def _():
        for name in early:
            save_copy(name).wait()

    @pl.when(r == 0)
    def _():
        weight_copy(0).wait()

    def quant_in(start, at, top):
        x = xin[r, at, :].astype(F32)
        xq_s[at, :] = (m0 * jnp.tanh(x * i0)).astype(BF16)
        return jnp.maximum(top, masked_peak(x, start))

    def masked_peak(v, start):
        return peak_rows(jnp.where(row_mask(start, v.shape[0]), jnp.abs(v), 0.0))

    peaks_o[0] = jnp.maximum(peaks_o[0], blocks(BLOCK, quant_in, no_peak))
    for j in range(3):
        cols = pl.ds(j * width, width)
        proj = dot_nn(xq_s[...], w_qkv[:, cols]) + b_qkv[:, cols]
        qkv_s[:, cols] = proj.astype(BF16)

    one = jnp.ones((), BF16)
    zero = jnp.zeros((), BF16)
    head_scale = jnp.asarray(HEAD_DIM ** -0.5, BF16)

    def prepare(p):
        slot = p % 2

        def body(start, at, c):
            lane = lax.broadcasted_iota(jnp.int32, (OPS, PAIR), 1)
            lo = lane < HEAD_DIM
            spot = jnp.where(lo, lane, lane - HEAD_DIM)
            bias = jnp.where(row_mask(start, OPS), 0.0, MASKED)
            extra = jnp.where(spot == 0, jnp.broadcast_to(bias, (OPS, PAIR)), 0.0).astype(BF16)
            q2 = qkv_s[at, p * PAIR : (p + 1) * PAIR] * head_scale
            k2 = qkv_s[at, width + p * PAIR : width + (p + 1) * PAIR]
            v2 = qkv_s[at, 2 * width + p * PAIR : 2 * width + (p + 1) * PAIR]
            ops_s[slot, 0, at, :] = jnp.where(lo, q2, one)
            ops_s[slot, 1, at, :] = jnp.where(lo, one, q2)
            ops_s[slot, 2, at, :] = jnp.where(lo, k2, extra)
            ops_s[slot, 3, at, :] = jnp.where(lo, extra, k2)
            ops_s[slot, 4, at, :] = jnp.where(lo, v2, one)
            ops_s[slot, 5, at, :] = jnp.where(lo, one, v2)
            return c

        blocks(OPS, body)

    def scores(h):
        p, side = h // 2, h % 2

        def piece_of(k):
            def run():
                keys = pl.ds(k * PIECE, PIECE)
                s_s[side, :, keys] = dot_nt(ops_s[p % 2, side], ops_s[p % 2, 2 + side, keys, :])

            return run

        return [piece_of(k) for k in range(seq // PIECE)]

    def soften(h):
        def body(start, at, c):
            s = s_s[h % 2, at, :]
            e_s[h, at, :] = jnp.exp(s - jnp.max(s, -1, keepdims=True)).astype(BF16)
            return c

        return body

    def collect(h):
        p, side = h // 2, h % 2

        def run():
            o_s[side] = dot_nn(e_s[h], ops_s[p % 2, 4 + side])

        return [run]

    def settle(p, peak):
        cols = slice(p * PAIR, (p + 1) * PAIR)

        def body(start, at, top):
            lo = lax.broadcasted_iota(jnp.int32, (OPS, PAIR), 1) < HEAD_DIM
            o_a, o_b = o_s[0, at, :], o_s[1, at, :]
            total = pltpu.roll(jnp.where(lo, o_b, o_a), HEAD_DIM, 1)
            inverse = 1.0 / total
            c = jnp.where(lo, o_a, o_b) * inverse
            inv_s[at, cols] = inverse
            ctx_s[at, cols] = c
            cq_s[at, cols] = (m1 * jnp.tanh(c * i1)).astype(BF16)
            return jnp.maximum(top, masked_peak(c, start))

        return blocks(OPS, body, peak)

    heads = 2 * (width // PAIR)
    peak = no_peak
    prepare(0)
    for dot in scores(0):
        dot()
    for h in range(heads):
        dots = []
        if h + 1 < heads:
            if (h + 1) % 2 == 0:
                prepare((h + 1) // 2)
            dots += scores(h + 1)
        if h > 0:
            dots += collect(h - 1)
        weave(dots, BLOCK, soften(h))
        if h > 0 and h % 2 == 0:
            peak = settle(h // 2 - 1, peak)
    for dot in collect(heads - 1):
        dot()
    peak = settle(heads // 2 - 1, peak)
    peaks_o[1] = jnp.maximum(peaks_o[1], peak)

    for name in early:
        save_copy(name).start()

    @pl.when(r > 0)
    def _():
        for name in late:
            save_copy(name).wait()

    @pl.when(r == 0)
    def _():
        for k in (1, 2, 3):
            weight_copy(k).wait()

    for k in range(width // PIECE):
        cols = slice(k * PIECE, (k + 1) * PIECE)
        acc[:, cols] = dot_nn(cq_s[...], w_out[:, cols])

    def norm_one(start, at, top):
        s = xin[r, at, :].astype(F32) + (acc[at, :] + b_out[...])
        center = s - jnp.mean(s, -1, keepdims=True)
        rs = lax.rsqrt(jnp.mean(center * center, -1, keepdims=True) + EPS)
        n = center * rs
        h = n * gain[0:1, :] + shift[0:1, :]
        n1_s[at, :] = n.astype(BF16)
        rs1_s[at, :] = jnp.broadcast_to(rs, (BLOCK, 128))
        hid[at, :] = h
        hq_s[at, :] = (m2 * jnp.tanh(h * i2)).astype(BF16)
        return jnp.maximum(top, masked_peak(h, start))

    peaks_o[2] = jnp.maximum(peaks_o[2], blocks(BLOCK, norm_one, no_peak))

    chunks = ff // CHUNK

    def up_chunk(c):
        def piece_of(k):
            def run():
                part = dot_nn(hq_s[...], w_up[:, pl.ds(c * CHUNK + k * PIECE, PIECE)])
                up_s[c % 2, :, pl.ds(k * PIECE, PIECE)] = part

            return run

        return [piece_of(k) for k in range(CHUNK // PIECE)]

    def act_chunk(c):
        cols = pl.ds(c * CHUNK, CHUNK)

        def body(start, at, carry):
            act, low, slope = activation(up_s[c % 2, at, :] + b_up[:, cols], m3, i3)
            aq_s[at, cols] = low.astype(BF16)
            sl_s[at, cols] = slope.astype(BF16)
            size = jnp.abs(act)
            top = size[:, 0:128]
            for i in range(128, CHUNK, 128):
                top = jnp.maximum(top, size[:, i : i + 128])
            amax_s[at, :] = top if c == 0 else jnp.maximum(amax_s[at, :], top)
            return carry

        return body

    def down_chunk(c):
        def piece_of(k):
            def run():
                cols, hidden_at = pl.ds(k * PIECE, PIECE), pl.ds((c - 1) * CHUNK, 2 * CHUNK)
                part = dot_nn(aq_s[:, hidden_at], w_down[hidden_at, cols])
                acc[:, cols] = part if c == 1 else acc[:, cols] + part

            return run

        return [piece_of(k) for k in range(width // PIECE)]

    for dot in up_chunk(0):
        dot()
    for c in range(chunks):
        dots = []
        if c + 1 < chunks:
            dots += up_chunk(c + 1)
        if c > 0 and c % 2 == 0:
            dots += down_chunk(c - 1)
        weave(dots or [lambda: None], BLOCK, act_chunk(c))
    for dot in down_chunk(chunks - 1):
        dot()
    peaks_o[3] = jnp.maximum(peaks_o[3], masked_peak(amax_s[...], 0))

    def norm_two(start, at, c):
        s = hid[at, :] + (acc[at, :] + b_down[...])
        center = s - jnp.mean(s, -1, keepdims=True)
        rs = lax.rsqrt(jnp.mean(center * center, -1, keepdims=True) + EPS)
        n = center * rs
        n2_s[at, :] = n.astype(BF16)
        rs2_s[at, :] = jnp.broadcast_to(rs, (BLOCK, 128))
        xout[r, at, :] = (n * gain[1:2, :] + shift[1:2, :]).astype(BF16)
        return c

    blocks(BLOCK, norm_two)
    for name in late:
        save_copy(name).start()

    @pl.when(jnp.logical_not(last))
    def _():
        hop(r).start()

    @pl.when(last)
    def _():
        for p in range(count - 1):
            mix_part(r, p).start()
        mix_own(r).start()

    @pl.when(r == rows - 1)
    def _():
        for name in order:
            save_copy(name).wait()

        @pl.when(jnp.logical_not(last))
        def _():
            for i in range(row_count):
                hop(i).wait_send()
            for i in range(row_count):
                mix_part(i, 0).wait_recv()

        @pl.when(last)
        def _():
            for i in range(row_count):
                for p in range(count - 1):
                    mix_part(i, p).wait_send()
                mix_own(i).wait()


def bwd_kernel(count, *refs):
    (
        lens, scales, seeds, h_qkv, h_out, h_up, h_down, gain, shift, left_i,
        x_i, qkv_i, inv_i, ctx_i, n1_i, rs1_i, sl_i, n2_i, rs2_i, exp_i,
        dproj_o, dbr_o, dup_o, ddn_o, gtok_o, left_o, small_o,
        w_qkv, w_out, w_up, w_down, w_sem, turn_in, turn_out, turn_in_sem, turn_out_sem,
        gin, x_s, qkv_s, inv_s, ctx_s, n1_s, rs1_s, sl_s, n2_s, rs2_s, e_s,
        dproj_s, dbr_s, dup_s, ddn_s, dctx_s, acc, dr,
        up_s, ops_s, g_s, ds_s, gv_s, gk_s, gq_s, q_t, do_t, inner_s, small_s,
        load_sem, save_sem, in_sem, send_sem, recv_sem, tok_send,
    ) = refs
    r = pl.program_id(0)
    rows = pl.num_programs(0)
    row_count = seeds.shape[0]
    seq, width = seeds.shape[1], seeds.shape[2]
    ff = w_up.shape[1]
    piece = seq // count
    stage = lax.axis_index("pipe")
    first = stage == 0
    last = stage == count - 1

    loaded = {
        "n2": (n2_i, n2_s), "rs2": (rs2_i, rs2_s), "sl": (sl_i, sl_s), "n1": (n1_i, n1_s),
        "rs1": (rs1_i, rs1_s), "ctx": (ctx_i, ctx_s), "qkv": (qkv_i, qkv_s), "inv": (inv_i, inv_s),
        "x": (x_i, x_s), "exp": (exp_i, e_s),
    }
    load_order = list(loaded)
    early = ("n2", "rs2", "sl", "n1", "rs1")
    late = ("ctx", "qkv", "inv", "exp", "x")
    staged = {
        "ddn": (ddn_s, ddn_o), "dup": (dup_s, dup_o), "dbr": (dbr_s, dbr_o), "dproj": (dproj_s, dproj_o),
    }
    save_order = list(staged)

    def load_copy(name, i):
        src, dst = loaded[name]
        return pltpu.make_async_copy(src.at[i], dst, load_sem.at[load_order.index(name)])

    def save_copy(name):
        src, dst = staged[name]
        return pltpu.make_async_copy(src, dst.at[r], save_sem.at[save_order.index(name)])

    def seed_copy(i):
        return pltpu.make_async_copy(seeds.at[i], gin.at[i], in_sem.at[i])

    def hop(i):
        return pltpu.make_async_remote_copy(
            src_ref=gin.at[i], dst_ref=gin.at[i], send_sem=send_sem.at[i], recv_sem=recv_sem.at[i],
            device_id={"pipe": lax.rem(stage + count - 1, count)}, device_id_type=LOGICAL,
        )

    def tok_copy(i):
        return pltpu.make_async_copy(gin.at[i], gtok_o.at[i], tok_send.at[i])

    fetches = [(h_down, w_down), (h_up, w_up), (h_out, w_out), (h_qkv, w_qkv)]

    def weight_copy(k):
        return pltpu.make_async_copy(fetches[k][0], fetches[k][1], w_sem.at[k])

    parts = left_i.shape[2] // width
    turns = row_count * parts

    def turn_load(i):
        cols = pl.ds(pl.multiple_of(i % parts * width, 128), width)
        return pltpu.make_async_copy(left_i.at[i // parts, :, cols], turn_in.at[i % 2], turn_in_sem.at[i % 2])

    def turn_store(i):
        rows_at = pl.ds(pl.multiple_of(i % parts * width, 128), width)
        cols = pl.ds(pl.multiple_of(i // parts * seq, 128), seq)
        return pltpu.make_async_copy(turn_out.at[i % 2], left_o.at[rows_at, cols], turn_out_sem.at[i % 2])

    def turn_left():
        turn_load(0).start()

        def body(i, c):
            @pl.when(i + 1 < turns)
            def _():
                turn_load(i + 1).start()

            turn_load(i).wait()

            @pl.when(i >= 2)
            def _():
                turn_store(i - 2).wait()

            turn_out[i % 2] = turn_in[i % 2].T
            turn_store(i).start()
            return c

        lax.fori_loop(0, turns, body, 0)
        turn_store(turns - 2).wait()
        turn_store(turns - 1).wait()

    @pl.when(r == 0)
    def _():
        greet(stage, count)
        small_s[...] = jnp.zeros_like(small_s)

        @pl.when(last)
        def _():
            for i in range(row_count):
                seed_copy(i).start()

        for name in ("n2", "rs2"):
            load_copy(name, 0).start()
        weight_copy(0).start()
        for name in early[2:]:
            load_copy(name, 0).start()
        for k in (1, 2, 3):
            weight_copy(k).start()
        for name in late:
            load_copy(name, 0).start()

        @pl.when(stage < count - 2)
        def _():
            turn_left()

    @pl.when(last)
    def _():
        seed_copy(r).wait()

    @pl.when(jnp.logical_not(last))
    def _():
        hop(r).wait_recv()

    length = lens[r]
    m0, m1, m2 = scales[0, 0], scales[0, 1], scales[0, 2]
    i0, i1, i2 = 1.0 / m0, 1.0 / m1, 1.0 / m2

    offsets = {}
    at_col = 0
    for name, size in (
        ("gain0", width), ("gain1", width), ("shift0", width), ("shift1", width),
        ("out", width), ("down", width), ("up", ff), ("qkv", 3 * width),
    ):
        offsets[name] = at_col
        at_col += size

    def blocks(size, body, init=0, begin=0, end=seq):
        step = lambda i, c: body(i * size, pl.ds(i * size, size), c)
        return lax.fori_loop(begin // size, end // size, step, init, unroll=True)

    def weave(dots, size, body, init=0):
        total, cut = seq // size, 0
        for k, dot in enumerate(dots):
            dot()
            begin, cut = cut, total * (k + 1) // len(dots)
            init = blocks(size, body, init, begin * size, cut * size)
        return init

    def row_mask(start, size):
        return (start + lax.broadcasted_iota(jnp.int32, (size, 1), 0)) < length

    def put_small(name, v, col=0):
        small_s[:, pl.ds(offsets[name] + col, v.shape[1])] += v

    no_sum = jnp.zeros((8, width), F32)

    for name in early:
        load_copy(name, r).wait()

    @pl.when(r > 0)
    def _():
        for name in ("ddn", "dup", "dbr"):
            save_copy(name).wait()

    @pl.when(r == 0)
    def _():
        for k in (0, 1):
            weight_copy(k).wait()

    def norm_two(start, at, sums):
        dy = jnp.where(row_mask(start, BLOCK), gin[r, at, :].astype(F32), 0.0)
        n = n2_s[at, :].astype(F32)
        e = dy * gain[1:2, :]
        mean_e = jnp.mean(e, -1, keepdims=True)
        mean_en = jnp.mean(e * n, -1, keepdims=True)
        d = (e - mean_e - n * mean_en) * rs2_s[at, 0:1]
        dr[at, :] = d
        ddn_s[at, :] = d.astype(BF16)
        return sums[0] + fold_rows(dy * n), sums[1] + fold_rows(dy), sums[2] + fold_rows(d)

    for name, v in zip(("gain1", "shift1", "down"), blocks(BLOCK, norm_two, (no_sum,) * 3)):
        put_small(name, v)

    chunks = ff // CHUNK

    def dact_chunk(c):
        def piece_of(k):
            def run():
                at = pl.ds(c * CHUNK + k * PIECE, PIECE)
                up_s[c % 2, :, pl.ds(k * PIECE, PIECE)] = dot_nt(ddn_s[...], w_down[at, :])

            return run

        return [piece_of(k) for k in range(CHUNK // PIECE)]

    def slope_chunk(c):
        cols = pl.ds(c * CHUNK, CHUNK)

        def body(start, at, total):
            d = (0.5 * up_s[c % 2, at, :]) * sl_s[at, cols].astype(F32)
            dup_s[at, cols] = d.astype(BF16)
            return total + fold_rows(d)

        return body

    def dhid_chunk(c):
        def piece_of(k):
            def run():
                at, hidden_at = pl.ds(k * PIECE, PIECE), pl.ds((c - 1) * CHUNK, 2 * CHUNK)
                part = dot_nt(dup_s[:, hidden_at], w_up[at, hidden_at])
                acc[:, at] = part if c == 1 else acc[:, at] + part

            return run

        return [piece_of(k) for k in range(width // PIECE)]

    for dot in dact_chunk(0):
        dot()
    for c in range(chunks):
        dots = []
        if c + 1 < chunks:
            dots += dact_chunk(c + 1)
        if c > 0 and c % 2 == 0:
            dots += dhid_chunk(c - 1)
        total = weave(dots or [lambda: None], BLOCK, slope_chunk(c), jnp.zeros((8, CHUNK), F32))
        put_small("up", total, c * CHUNK)
    for dot in dhid_chunk(chunks - 1):
        dot()

    def norm_one(start, at, sums):
        n = n1_s[at, :].astype(F32)
        t = jnp.tanh((n * gain[0:1, :] + shift[0:1, :]) * i2)
        dy = dr[at, :] + acc[at, :] * (1.0 - t * t)
        e = dy * gain[0:1, :]
        mean_e = jnp.mean(e, -1, keepdims=True)
        mean_en = jnp.mean(e * n, -1, keepdims=True)
        d = (e - mean_e - n * mean_en) * rs1_s[at, 0:1]
        dr[at, :] = d
        dbr_s[at, :] = d.astype(BF16)
        return sums[0] + fold_rows(dy * n), sums[1] + fold_rows(dy), sums[2] + fold_rows(d)

    for name, v in zip(("gain0", "shift0", "out"), blocks(BLOCK, norm_one, (no_sum,) * 3)):
        put_small(name, v)

    for name in ("ddn", "dup", "dbr"):
        save_copy(name).start()

    @pl.when(r + 1 < rows)
    def _():
        for name in early:
            load_copy(name, r + 1).start()

    for name in late:
        load_copy(name, r).wait()

    @pl.when(r > 0)
    def _():
        save_copy("dproj").wait()

    @pl.when(r == 0)
    def _():
        for k in (2, 3):
            weight_copy(k).wait()

    for k in range(width // PIECE):
        acc[:, pl.ds(k * PIECE, PIECE)] = dot_nt(dbr_s[...], w_out[pl.ds(k * PIECE, PIECE), :])

    zero = jnp.zeros((), BF16)
    head_scale = jnp.asarray(HEAD_DIM ** -0.5, BF16)

    def prepare(p):
        slot = p % 2
        cols = slice(p * PAIR, (p + 1) * PAIR)

        def body(start, at, c):
            lo = lax.broadcasted_iota(jnp.int32, (OPS, PAIR), 1) < HEAD_DIM
            ctx = ctx_s[at, cols]
            t = jnp.tanh(ctx * i1)
            low = (acc[at, cols] * (1.0 - t * t) * inv_s[at, cols]).astype(BF16)
            dctx_s[slot, at, :] = low
            inner = low.astype(F32) * ctx
            whole_sum = jnp.sum(inner, -1, keepdims=True)
            lower = jnp.sum(jnp.where(lo, inner, 0.0), -1, keepdims=True)
            inner_s[slot, 0, at, :] = jnp.broadcast_to(lower, (OPS, PAIR))
            inner_s[slot, 1, at, :] = jnp.broadcast_to(whole_sum - lower, (OPS, PAIR))
            v2 = qkv_s[at, 2 * width + p * PAIR : 2 * width + (p + 1) * PAIR]
            ops_s[slot, 0, at, :] = jnp.where(lo, v2, zero)
            ops_s[slot, 1, at, :] = jnp.where(lo, zero, v2)
            return c

        blocks(OPS, body)
        q_t[slot] = (qkv_s[:, cols] * head_scale).T
        do_t[slot] = dctx_s[slot].T

    def scores(h):
        slot, side = h // 2 % 2, h % 2

        def piece_of(k):
            def run():
                keys = pl.ds(k * PIECE, PIECE)
                g_s[side, :, keys] = dot_nt(dctx_s[slot], ops_s[slot, side, keys, :])

            return run

        return [piece_of(k) for k in range(seq // PIECE)]

    def soften(h):
        slot, side = h // 2 % 2, h % 2

        def body(start, at, c):
            inner = jnp.concatenate([inner_s[slot, side, at, :]] * (seq // PAIR), 1)
            ds_s[side, at, :] = (e_s[h, at, :].astype(F32) * (g_s[side, at, :] - inner)).astype(BF16)
            return c

        return body

    def collect(h):
        slot, side = h // 2 % 2, h % 2
        rows_at = slice(side * HEAD_DIM, (side + 1) * HEAD_DIM)

        def grad_v(k):
            def run():
                keys = pl.ds(k * PIECE, PIECE)
                gv_s[rows_at, keys] = dot_nn(do_t[slot, rows_at, :], e_s[h, :, keys])

            return run

        def grad_k(k):
            def run():
                keys = pl.ds(k * PIECE, PIECE)
                gk_s[rows_at, keys] = dot_nn(q_t[slot, rows_at, :], ds_s[side, :, keys])

            return run

        def grad_q():
            keys_low = qkv_s[:, width + h // 2 * PAIR : width + (h // 2 + 1) * PAIR]
            gq_s[side] = dot_nn(ds_s[side], keys_low)

        return [make(k) for make in (grad_v, grad_k) for k in range(seq // PIECE)] + [grad_q]

    def settle(p):
        def body(start, at, c):
            lo = lax.broadcasted_iota(jnp.int32, (OPS, PAIR), 1) < HEAD_DIM
            q = jnp.where(lo, gq_s[0, at, :], gq_s[1, at, :]) * (HEAD_DIM ** -0.5)
            dproj_s[at, p * PAIR : (p + 1) * PAIR] = q.astype(BF16)
            return c

        blocks(OPS, body)
        dproj_s[:, width + p * PAIR : width + (p + 1) * PAIR] = gk_s[...].astype(BF16).T
        dproj_s[:, 2 * width + p * PAIR : 2 * width + (p + 1) * PAIR] = gv_s[...].astype(BF16).T

    heads = 2 * (width // PAIR)
    prepare(0)
    for dot in scores(0):
        dot()
    for h in range(heads):
        dots = []
        if h + 1 < heads:
            if (h + 1) % 2 == 0:
                prepare((h + 1) // 2)
            dots += scores(h + 1)
        if h > 0:
            dots += collect(h - 1)
        weave(dots, BLOCK, soften(h))
        if h > 0 and h % 2 == 0:
            settle(h // 2 - 1)
    for dot in collect(heads - 1):
        dot()
    settle(heads // 2 - 1)
    def dx_piece(k):
        def run():
            at = pl.ds(k * PIECE, PIECE)
            acc[:, at] = dot_nt(dproj_s[...], w_qkv[at, :])

        return run

    def quant_in(k):
        cols = pl.ds(k * PIECE, PIECE)
        values = pl.ds(2 * width + k * PIECE, PIECE)

        def body(start, at, sums):
            t = jnp.tanh(x_s[at, cols].astype(F32) * i0)
            gin[r, at, cols] = (dr[at, cols] + acc[at, cols] * (1.0 - t * t)).astype(BF16)
            return (
                sums[0] + fold_rows(dproj_s[at, cols].astype(F32)),
                sums[1] + fold_rows(dproj_s[at, values].astype(F32)),
            )

        return body

    dx_piece(0)()
    pieces = width // PIECE
    for k in range(pieces):
        dots = [dx_piece(k + 1)] if k + 1 < pieces else [lambda: None]
        sums = weave(dots, BLOCK, quant_in(k), (jnp.zeros((8, PIECE), F32),) * 2)
        put_small("qkv", sums[0], k * PIECE)
        put_small("qkv", sums[1], 2 * width + k * PIECE)
    save_copy("dproj").start()

    @pl.when(r + 1 < rows)
    def _():
        for name in late:
            load_copy(name, r + 1).start()

    @pl.when(jnp.logical_not(first))
    def _():
        hop(r).start()

    @pl.when(first)
    def _():
        tok_copy(r).start()

    @pl.when(r == rows - 1)
    def _():
        small_o[...] = jnp.sum(small_s[...], 0, keepdims=True)

        @pl.when(stage >= count - 2)
        def _():
            turn_left()

        for name in save_order:
            save_copy(name).wait()

        @pl.when(jnp.logical_not(first))
        def _():
            for i in range(row_count):
                hop(i).wait_send()

        @pl.when(first)
        def _():
            for i in range(row_count):
                tok_copy(i).wait()


def whole(a):
    return pl.BlockSpec(a.shape, lambda r, n=a.ndim: (0,) * n, pipeline_mode=pl.Buffered(1))


ANYWHERE = pl.BlockSpec(memory_space=pl.ANY)
SCALAR = pl.BlockSpec(memory_space=pltpu.SMEM)
VMEM_LIMIT = 60 * 1024 * 1024


def run_forward(count, tokens, lengths, scales, weights):
    w_qkv, b_qkv, w_out, b_out, w_up, b_up, w_down, b_down, gain, shift = weights
    rows, seq, width = tokens.shape
    ff = w_up.shape[1]
    big = lambda n, t: jax.ShapeDtypeStruct((rows, seq, n), t)
    saves = [
        (width, BF16), (3 * width, BF16), (width, F32), (width, F32), (width, BF16), (128, F32),
        (ff, BF16), (width, BF16), (128, F32),
    ]
    heads = width // HEAD_DIM
    lefts = [(ff, BF16), (width, BF16), (width, BF16), (width, BF16)]
    heavy = (w_qkv, w_out, w_up, w_down)
    dense = (b_qkv, b_out, b_up, b_down, gain, shift)
    tok = rows * seq
    return pl.pallas_call(
        lambda *refs: fwd_kernel(count, *refs),
        grid=(rows,),
        in_specs=[SCALAR, SCALAR, ANYWHERE] + [ANYWHERE] * 4 + [whole(a) for a in dense],
        out_specs=[ANYWHERE] * 12 + [pl.BlockSpec((4, 8, 128), lambda r: (0, 0, 0))],
        out_shape=[big(n, t) for n, t in saves]
        + [
            big(ff + 3 * width, BF16),
            jax.ShapeDtypeStruct((rows, heads, seq, seq), BF16),
            jax.ShapeDtypeStruct((rows, seq // count, width), BF16),
            jax.ShapeDtypeStruct((4, 8, 128), F32),
        ],
        scratch_shapes=[pltpu.VMEM(a.shape, a.dtype) for a in heavy]
        + [pltpu.SemaphoreType.DMA((4,))]
        + [pltpu.VMEM((rows, seq, width), BF16), pltpu.VMEM((rows, seq, width), BF16)]
        + [pltpu.VMEM((seq, n), t) for n, t in saves[1:] + lefts]
        + [
            pltpu.VMEM((seq, width), F32),
            pltpu.VMEM((seq, width), F32),
            pltpu.VMEM((2, seq, CHUNK), F32),
            pltpu.VMEM((2, 6, seq, PAIR), BF16),
            pltpu.VMEM((2, seq, seq), F32),
            pltpu.VMEM((heads, seq, seq), BF16),
            pltpu.VMEM((2, seq, PAIR), F32),
            pltpu.VMEM((seq, 128), F32),
            pltpu.SemaphoreType.DMA((14,)),
            pltpu.SemaphoreType.DMA((rows,)),
            pltpu.SemaphoreType.DMA((rows,)),
            pltpu.SemaphoreType.DMA((rows,)),
            pltpu.SemaphoreType.DMA((rows, count)),
            pltpu.SemaphoreType.DMA((rows,)),
        ],
        compiler_params=pltpu.CompilerParams(
            collective_id=0, has_side_effects=True, vmem_limit_bytes=VMEM_LIMIT,
            dimension_semantics=("arbitrary",),
        ),
        cost_estimate=pl.CostEstimate(
            flops=2 * tok * (4 * width * width + 2 * width * ff + 2 * seq * width),
            bytes_accessed=tok * 28000, transcendentals=tok * 3 * ff,
        ),
    )(lengths, scales, tokens, *heavy, *dense)


def run_backward(count, seeds, lengths, scales, weights, kept):
    w_qkv, b_qkv, w_out, b_out, w_up, b_up, w_down, b_down, gain, shift = weights
    *loads, left, exps = kept
    loads.append(exps)
    rows, seq, width = seeds.shape
    ff = w_up.shape[1]
    big = lambda n, t: jax.ShapeDtypeStruct((rows, seq, n), t)
    saves = [(3 * width, BF16), (width, BF16), (ff, BF16), (width, BF16)]
    heavy = (w_qkv, w_out, w_up, w_down)
    dense = (gain, shift)
    tok = rows * seq
    small = 6 * width + ff + 3 * width
    return pl.pallas_call(
        lambda *refs: bwd_kernel(count, *refs),
        grid=(rows,),
        in_specs=[SCALAR, SCALAR, ANYWHERE] + [ANYWHERE] * 4 + [whole(a) for a in dense] + [ANYWHERE] * 11,
        out_specs=[ANYWHERE] * 6 + [pl.BlockSpec((1, small), lambda r: (0, 0))],
        out_shape=[big(n, t) for n, t in saves]
        + [
            big(width, BF16), jax.ShapeDtypeStruct((left.shape[2], rows * seq), BF16),
            jax.ShapeDtypeStruct((1, small), F32),
        ],
        scratch_shapes=[pltpu.VMEM(a.shape, a.dtype) for a in heavy]
        + [
            pltpu.SemaphoreType.DMA((4,)),
            pltpu.VMEM((2, seq, width), BF16),
            pltpu.VMEM((2, width, seq), BF16),
            pltpu.SemaphoreType.DMA((2,)),
            pltpu.SemaphoreType.DMA((2,)),
        ]
        + [pltpu.VMEM((rows, seq, width), BF16)]
        + [pltpu.VMEM(a.shape[1:], a.dtype) for a in loads]
        + [pltpu.VMEM((seq, n), t) for n, t in saves]
        + [
            pltpu.VMEM((2, seq, PAIR), BF16),
            pltpu.VMEM((seq, width), F32),
            pltpu.VMEM((seq, width), F32),
            pltpu.VMEM((2, seq, CHUNK), F32),
            pltpu.VMEM((2, 2, seq, PAIR), BF16),
            pltpu.VMEM((2, seq, seq), F32),
            pltpu.VMEM((2, seq, seq), BF16),
            pltpu.VMEM((PAIR, seq), F32),
            pltpu.VMEM((PAIR, seq), F32),
            pltpu.VMEM((2, seq, PAIR), F32),
            pltpu.VMEM((2, PAIR, seq), BF16),
            pltpu.VMEM((2, PAIR, seq), BF16),
            pltpu.VMEM((2, 2, seq, PAIR), F32),
            pltpu.VMEM((8, small), F32),
            pltpu.SemaphoreType.DMA((10,)),
            pltpu.SemaphoreType.DMA((4,)),
            pltpu.SemaphoreType.DMA((rows,)),
            pltpu.SemaphoreType.DMA((rows,)),
            pltpu.SemaphoreType.DMA((rows,)),
            pltpu.SemaphoreType.DMA((rows,)),
        ],
        compiler_params=pltpu.CompilerParams(
            collective_id=1, has_side_effects=True, vmem_limit_bytes=VMEM_LIMIT,
            dimension_semantics=("arbitrary",),
        ),
        cost_estimate=pl.CostEstimate(
            flops=2 * tok * (4 * width * width + 2 * width * ff + 5 * seq * width),
            bytes_accessed=tok * 28000, transcendentals=tok * ff,
        ),
    )(lengths, scales, seeds, *heavy, *dense, left, *loads)


def ring_to_dp(pos, n):
    return jnp.where(pos < n // 2, 2 * pos, 2 * (n - pos) - 1)


def dp_to_ring(j, n):
    return jnp.where(j % 2 == 0, j // 2, n - 1 - j // 2)


def grad_kernel(count, n, *refs):
    (
        left, ddn, dup, dproj, dbr, small, g0,
        gq_o, go_o, gu_o, gd_o, small_o, gtok_o,
        slots_d, slots_u, slots_q, slots_s, wide_v, thin_v, ddn_v, dup_v, dpo_v,
        wide_sem, thin_sem, right_sem,
        send_d, recv_d, send_u, recv_u, send_q, recv_q, send_s, recv_s, tok_send, tok_recv,
    ) = refs
    width = ddn.shape[1]
    ff = dup.shape[1]
    shard, shard_ff = width // n, ff // n
    row_count, seq = g0.shape[0], g0.shape[1]
    piece = seq // count
    stage = lax.axis_index("pipe")
    me = lax.axis_index("dp")
    pos = dp_to_ring(me, n)
    first = stage == 0
    ahead = ring_to_dp(lax.rem(pos + 1, n), n)
    behind = ring_to_dp(lax.rem(pos + n - 1, n), n)
    target = (ahead, behind)

    def chunk(d, step):
        at = pos + 2 * n - 1 - step if d == 0 else pos + 1 + step
        return ring_to_dp(lax.rem(at, n), n)

    def wide_copy(d, step):
        rows = pl.ds(pl.multiple_of(chunk(d, step) * shard_ff, 16), shard_ff)
        return pltpu.make_async_copy(left.at[rows, :], wide_v.at[d], wide_sem.at[d])

    def thin_copy(k, d, step):
        rows = pl.ds(pl.multiple_of(ff + k * width + chunk(d, step) * shard, 16), shard)
        return pltpu.make_async_copy(left.at[rows, :], thin_v.at[k, d], thin_sem.at[k, d])

    rights = [
        (ddn, ddn_v), (dup, dup_v), (dproj, dpo_v.at[:, pl.ds(0, 3 * width)]),
        (dbr, dpo_v.at[:, pl.ds(3 * width, width)]),
    ]

    def right_copy(k):
        return pltpu.make_async_copy(rights[k][0], rights[k][1], right_sem.at[k])

    for d in range(2):
        wide_copy(d, 0).start()
    right_copy(0).start()
    right_copy(1).start()
    for d in range(2):
        thin_copy(0, d, 0).start()
    right_copy(2).start()
    right_copy(3).start()
    for d in range(2):
        thin_copy(1, d, 0).start()
        if d == 1:
            thin_copy(2, d, 0).start()

    barrier = pltpu.get_barrier_semaphore()
    for peer in target:
        pl.semaphore_signal(barrier, inc=1, device_id={"dp": peer}, device_id_type=LOGICAL)

    @pl.when(first)
    def _():
        pl.semaphore_wait(barrier, 1 + count)

    @pl.when(jnp.logical_not(first))
    def _():
        pl.semaphore_signal(barrier, inc=1, device_id={"pipe": jnp.int32(0)}, device_id_type=LOGICAL)
        pl.semaphore_wait(barrier, 2)

    def tok_part(i, p):
        return pltpu.make_async_remote_copy(
            src_ref=g0.at[i, pl.ds(p * piece, piece)], dst_ref=gtok_o.at[i],
            send_sem=tok_send.at[i, p], recv_sem=tok_recv.at[i],
            device_id={"pipe": jnp.int32(p)}, device_id_type=LOGICAL,
        )

    def tok_own(i):
        return pltpu.make_async_copy(g0.at[i, pl.ds(0, piece)], gtok_o.at[i], tok_send.at[i, 0])

    @pl.when(first)
    def _():
        for i in range(row_count):
            for p in range(1, count):
                tok_part(i, p).start()
            tok_own(i).start()

    def message(slots, send, recv, d, at):
        return pltpu.make_async_remote_copy(
            src_ref=slots.at[d, at], dst_ref=slots.at[d, jnp.minimum(at + 1, n - 1)],
            send_sem=send.at[d, at], recv_sem=recv.at[d, jnp.minimum(at + 1, n - 1)],
            device_id={"dp": target[d]}, device_id_type=LOGICAL,
        )

    def arrived(slots, send, recv, d, at):
        return pltpu.make_async_remote_copy(
            src_ref=slots.at[d, at], dst_ref=slots.at[d, at],
            send_sem=send.at[d, at], recv_sem=recv.at[d, at],
            device_id={"dp": target[d]}, device_id_type=LOGICAL,
        )

    def lane(slots, send, recv, d, step, mine, finish):
        @pl.when(step == 0)
        def _():
            slots[d, 0] = mine.astype(BF16)

        @pl.when(step > 0)
        def _():
            arrived(slots, send, recv, d, step).wait_recv()

            @pl.when(step < n - 1)
            def _():
                slots[d, step] = (slots[d, step].astype(F32) + mine).astype(BF16)

            @pl.when(step == n - 1)
            def _():
                finish(slots[d, step].astype(F32) + mine)

        @pl.when(step < n - 1)
        def _():
            message(slots, send, recv, d, step).start()

    def small_message(at):
        return pltpu.make_async_remote_copy(
            src_ref=slots_s.at[at], dst_ref=slots_s.at[jnp.minimum(at + 1, n - 1)],
            send_sem=send_s.at[at], recv_sem=recv_s.at[jnp.minimum(at + 1, n - 1)],
            device_id={"dp": target[0]}, device_id_type=LOGICAL,
        )

    def small_arrived(at):
        return pltpu.make_async_remote_copy(
            src_ref=slots_s.at[at], dst_ref=slots_s.at[at], send_sem=send_s.at[at],
            recv_sem=recv_s.at[at], device_id={"dp": target[0]}, device_id_type=LOGICAL,
        )

    sum_rows = lax.broadcasted_iota(jnp.int32, (16, 128), 0) < 9

    def small_step(step):
        mine = small[chunk(0, step)]

        @pl.when(step == 0)
        def _():
            slots_s[0] = mine

        @pl.when(step > 0)
        def _():
            small_arrived(step).wait_recv()
            got = slots_s[step]
            slots_s[step] = jnp.where(sum_rows, got + mine, jnp.maximum(got, mine))

        @pl.when(step < n - 1)
        def _():
            small_message(step).start()

        @pl.when(step == n - 1)
        def _():
            small_o[...] = slots_s[step]

    half, half_ff = width // 2, ff // 2

    def fetched(copy, step, *args):
        copy(*args, step).wait()

    def refill(copy, step, *args):
        @pl.when(step < n - 1)
        def _():
            copy(*args, step + 1).start()

    def right_ready(k, step):
        @pl.when(step == 0)
        def _():
            right_copy(k).wait()

    def turn(step, _):
        right_ready(0, step)
        for d in range(2):
            cols = slice(d * half, (d + 1) * half)
            fetched(wide_copy, step, d)
            mine = dot_nn(wide_v[d], ddn_v[:, cols])
            refill(wide_copy, step, d)

            def finish_down(total):
                gd_o[:, cols] = total

            lane(slots_d, send_d, recv_d, d, step, mine, finish_down)
        small_step(step)
        right_ready(1, step)
        for d in range(2):
            cols = slice(d * half_ff, (d + 1) * half_ff)
            fetched(thin_copy, step, 0, d)
            mine = dot_nn(thin_v[0, d], dup_v[:, cols])
            refill(thin_copy, step, 0, d)

            def finish_up(total):
                gu_o[:, cols] = total

            lane(slots_u, send_u, recv_u, d, step, mine, finish_up)
        right_ready(2, step)
        right_ready(3, step)
        fetched(thin_copy, step, 1, 0)
        mine = dot_nn(thin_v[1, 0], dpo_v[:, 0 : 2 * width])
        refill(thin_copy, step, 1, 0)

        def finish_ahead(total):
            gq_o[:, 0 : 2 * width] = total

        lane(slots_q, send_q, recv_q, 0, step, mine, finish_ahead)
        fetched(thin_copy, step, 1, 1)
        fetched(thin_copy, step, 2, 1)
        mine = jnp.concatenate(
            [
                dot_nn(thin_v[1, 1], dpo_v[:, 2 * width : 3 * width]),
                dot_nn(thin_v[2, 1], dpo_v[:, 3 * width : 4 * width]),
            ],
            1,
        )
        refill(thin_copy, step, 1, 1)
        refill(thin_copy, step, 2, 1)

        def finish_behind(total):
            gq_o[:, 2 * width : 3 * width] = total[:, 0:width]
            go_o[...] = total[:, width : 2 * width]

        lane(slots_q, send_q, recv_q, 1, step, mine, finish_behind)
        return 0

    lax.fori_loop(0, n, turn, 0)

    def drain(at, _):
        for d in range(2):
            message(slots_d, send_d, recv_d, d, at).wait_send()
            message(slots_u, send_u, recv_u, d, at).wait_send()
            message(slots_q, send_q, recv_q, d, at).wait_send()
        small_message(at).wait_send()
        return 0

    lax.fori_loop(0, n - 1, drain, 0)

    @pl.when(first)
    def _():
        for i in range(row_count):
            for p in range(1, count):
                tok_part(i, p).wait_send()
            tok_own(i).wait()

    @pl.when(jnp.logical_not(first))
    def _():
        for i in range(row_count):
            tok_part(i, 1).wait_recv()


def run_grads(count, n, left, dproj, dbr, dup, ddn, g0, small):
    rows, seq, width = g0.shape
    ff = dup.shape[2]
    flat = lambda a: a.reshape(rows * seq, a.shape[2])
    tok = rows * seq
    shard, shard_ff = width // n, ff // n
    ops = [left] + [flat(a) for a in (ddn, dup, dproj, dbr)]
    vmem = pl.BlockSpec(memory_space=pltpu.VMEM)
    sem = pltpu.SemaphoreType.DMA
    return pl.pallas_call(
        lambda *refs: grad_kernel(count, n, *refs),
        in_specs=[ANYWHERE] * 5 + [vmem, ANYWHERE],
        out_specs=[vmem] * 5 + [ANYWHERE],
        out_shape=[
            jax.ShapeDtypeStruct((shard, 3 * width), F32),
            jax.ShapeDtypeStruct((shard, width), F32),
            jax.ShapeDtypeStruct((shard, ff), F32),
            jax.ShapeDtypeStruct((shard_ff, width), F32),
            jax.ShapeDtypeStruct((16, 128), F32),
            jax.ShapeDtypeStruct((rows, seq // count, width), BF16),
        ],
        scratch_shapes=[
            pltpu.VMEM((2, n, shard_ff, width // 2), BF16),
            pltpu.VMEM((2, n, shard, ff // 2), BF16),
            pltpu.VMEM((2, n, shard, 2 * width), BF16),
            pltpu.VMEM((n, 16, 128), F32),
            pltpu.VMEM((2, shard_ff, tok), BF16),
            pltpu.VMEM((3, 2, shard, tok), BF16),
            pltpu.VMEM((tok, width), BF16),
            pltpu.VMEM((tok, ff), BF16),
            pltpu.VMEM((tok, 4 * width), BF16),
            sem((2,)), sem((3, 2)), sem((4,)),
            sem((2, n)), sem((2, n)), sem((2, n)), sem((2, n)), sem((2, n)), sem((2, n)),
            sem((n,)), sem((n,)), sem((rows, count)), sem((rows,)),
        ],
        compiler_params=pltpu.CompilerParams(
            collective_id=2, has_side_effects=True, vmem_limit_bytes=VMEM_LIMIT,
        ),
        cost_estimate=pl.CostEstimate(
            flops=2 * tok * (4 * width * width + 2 * width * ff), bytes_accessed=tok * 25000, transcendentals=0,
        ),
    )(*ops, small, g0)


def place_kernel(n, *refs):
    small, outs = refs[6], refs[7:]
    larges, smalls, sem = outs[:6], outs[6:13], outs[13]
    copies = [pltpu.make_async_copy(refs[i], larges[i], sem.at[i]) for i in range(6)]
    for copy in copies:
        copy.start()
    flat = jnp.concatenate([small[i : i + 1, :] for i in range(9)], 1)
    gain, shift, s_out, s_down, s_up, s_qv, top = smalls
    thin = gain.shape[2]
    at = 0
    for ref, index in ((gain, 0), (gain, 1), (shift, 0), (shift, 1)):
        ref[0, index : index + 1, :] = flat[:, at : at + thin]
        at += thin
    for ref in (s_out, s_down, s_up, s_qv):
        ref[...] = flat[:, at : at + ref.shape[1]]
        at += ref.shape[1]
    top[...] = small[9:10, 0:4]
    for copy in copies:
        copy.wait()


def place(n, mixed, grad_tokens, grads, small, width, ff):
    larges = [mixed, grad_tokens, *[g[None] for g in grads]]
    shapes = [jax.ShapeDtypeStruct(a.shape, a.dtype) for a in larges]
    thin = width // n
    smalls = [(1, 2, thin), (1, 2, thin), (1, thin), (1, thin), (1, ff // n), (1, 2 * thin), (1, 4)]
    vmem = pl.BlockSpec(memory_space=pltpu.VMEM)
    return pl.pallas_call(
        lambda *refs: place_kernel(n, *refs),
        in_specs=[ANYWHERE] * 6 + [vmem],
        out_specs=[ANYWHERE] * 6 + [vmem] * 7,
        out_shape=shapes + [jax.ShapeDtypeStruct(s, F32) for s in smalls],
        scratch_shapes=[pltpu.SemaphoreType.DMA((6,))],
    )(*larges, small)


def weight_grad(left, right):
    g = jnp.einsum("rsd,rse->de", left, right, preferred_element_type=F32).astype(BF16)
    return lax.psum_scatter(g, "dp", scatter_dimension=0, tiled=True).astype(F32)


def share_pieces(whole_rows, count, stage):
    piece = whole_rows.shape[1] // count
    mine = whole_rows[:, :piece]
    for p in range(1, count):
        got = lax.ppermute(whole_rows[:, p * piece : (p + 1) * piece], "pipe", [(0, p)])
        mine = jnp.where(stage == p, got, mine)
    return mine


def shards(
    tokens, lengths, ema_scales, w_qkv, bias_qv, w_out, bias_out, w_up, bias_up, w_down, bias_down,
    ln_gain, ln_bias, cotangent,
):
    count = lax.axis_size("pipe")
    n = lax.axis_size("dp")
    width = tokens.shape[2]
    ff = w_up.shape[2]
    b_qkv = jnp.concatenate([bias_qv[:, :width], jnp.zeros_like(bias_qv[:, :width]), bias_qv[:, width:]], 1)
    weights = (
        w_qkv[0], b_qkv, w_out[0], bias_out, w_up[0], bias_up, w_down[0], bias_down, ln_gain[0], ln_bias[0],
    )
    *kept, mixed, peaks = run_forward(count, tokens, lengths, ema_scales, weights)
    left = kept[-2]
    dproj, dbr, dup, ddn, g0, turned, small = run_backward(
        count, cotangent, lengths, ema_scales, weights, kept
    )
    sums = small[0]
    parts, at = [], 0
    for size in (width, width, width, width, width, width, ff, width, width, width):
        parts.append(sums[at : at + size])
        at += size
    parts[7:] = [jnp.concatenate([parts[7], parts[9]])]
    packed = jnp.concatenate([v.reshape(n, -1) for v in parts], 1)
    peak = jnp.max(peaks, (1, 2))
    sums_width = packed.shape[1]
    if n >= 4 and n % 2 == 0 and width // n % 16 == 0 and ff // n % 128 == 0 and sums_width == 9 * 128:
        top = jnp.broadcast_to(jnp.pad(peak, (0, 124))[None, None], (n, 7, 128))
        with_peak = jnp.concatenate([packed.reshape(n, 9, 128), top], 1)
        g_qkv, g_out, g_up, g_down, small_sum, grad_tokens = run_grads(
            count, n, turned, dproj, dbr, dup, ddn, g0, with_peak
        )
        placed = place(n, mixed, grad_tokens, (g_qkv, g_out, g_up, g_down), small_sum, width, ff)
        mixed, grad_tokens, g_qkv, g_out, g_up, g_down, g_gain, g_shift, s_out, s_down, s_up, s_qv, top = placed
        return (
            mixed, grad_tokens, g_qkv, s_qv, g_out, s_out, g_up, s_up, g_down, s_down, g_gain, g_shift, top,
        )
    else:
        g_down = weight_grad(left[:, :, :ff], ddn)
        g_up = weight_grad(left[:, :, ff : ff + width], dup)
        g_qkv = weight_grad(left[:, :, ff + width : ff + 2 * width], dproj)
        g_out = weight_grad(left[:, :, ff + 2 * width :], dbr)
        mine = lax.psum_scatter(packed, "dp", scatter_dimension=0, tiled=True)
        batch_max = lax.pmax(peak, "dp")[None]
        grad_tokens = share_pieces(g0, count, lax.axis_index("pipe"))
    outs, at = [], 0
    for size in (width, width, width, width, width, width, ff, 2 * width):
        outs.append(mine[:, at : at + size // n])
        at += size // n
    gain0, gain1, shift0, shift1, s_out, s_down, s_up, s_qv = outs
    g_gain = jnp.stack([gain0, gain1], 1)
    g_shift = jnp.stack([shift0, shift1], 1)
    return (
        mixed, grad_tokens, g_qkv[None], s_qv, g_out[None], s_out, g_up[None], s_up, g_down[None], s_down,
        g_gain, g_shift, batch_max,
    )


def solution(mesh):
    return jax.shard_map(
        shards,
        mesh=mesh,
        in_specs=(
            P("dp", None, None), P("dp"), P("pipe", None), P("pipe", None, None), P("pipe", None),
            P("pipe", None, None), P("pipe", None), P("pipe", None, None), P("pipe", None),
            P("pipe", None, None), P("pipe", None), P("pipe", None, None), P("pipe", None, None),
            P("dp", None, None),
        ),
        out_specs=(
            P("dp", "pipe", None), P("dp", "pipe", None), P("pipe", "dp", None), P("pipe", "dp"),
            P("pipe", "dp", None), P("pipe", "dp"), P("pipe", "dp", None), P("pipe", "dp"),
            P("pipe", "dp", None), P("pipe", "dp"), P("pipe", None, "dp"), P("pipe", None, "dp"),
            P("pipe", None),
        ),
        check_vma=False,
    )
```

```python
import jax
import jax.numpy as jnp
from jax import lax
from jax.experimental import pallas as pl
from jax.experimental.pallas import tpu as pltpu
from jax.sharding import PartitionSpec as P

HEAD_DIM = 64
PAIR = 2 * HEAD_DIM
EPS = 1e-06
MASKED = -1000000000.0
CHUNK = 512
PIECE = 256
BLOCK = 16
OPS = 64
LOGICAL = pl.DeviceIdType.MESH
F32 = jnp.float32
BF16 = jnp.bfloat16

ERF_POLY = (
    0.7978823511659165,
    0.03634481045269742,
    -4.5110171354091134e-05,
    -5.02654469142584e-05,
    3.0867937984305273e-06,
    -6.60140005994544e-08,
)
ERF_CLAMP = 5.2 * 5.2
HALF_LOG2E = -0.7213475204444817
LOG2_TWICE_DENSITY = -0.3257480647361593


def dot_nn(a, b):
    return jnp.dot(a, b, preferred_element_type=F32)


def dot_nt(a, b):
    return lax.dot_general(a, b, (((1,), (1,)), ((), ())), preferred_element_type=F32)


def dot_tn(a, b):
    return lax.dot_general(a, b, (((0,), (0,)), ((), ())), preferred_element_type=F32)


def fold_rows(v):
    return jnp.sum(v.reshape(v.shape[0] // 8, 8, v.shape[1]), 0)


def peak_rows(v):
    tiles = [v[:, i : i + 128] for i in range(0, v.shape[1], 128)]
    top = tiles[0]
    for tile in tiles[1:]:
        top = jnp.maximum(top, tile)
    return jnp.max(top.reshape(v.shape[0] // 8, 8, 128), 0)


def greet(stage, count):
    barrier = pltpu.get_barrier_semaphore()
    for step in range(1, count):
        peer = lax.rem(stage + step, count)
        pl.semaphore_signal(barrier, inc=1, device_id={"pipe": peer}, device_id_type=LOGICAL)
    pl.semaphore_wait(barrier, count - 1)


def activation(u, ceiling, inv_ceiling):
    square = u * u
    w = jnp.minimum(square, ERF_CLAMP)
    poly = w * ERF_POLY[-1] + ERF_POLY[-2]
    for coef in ERF_POLY[-3::-1]:
        poly = poly * w + coef
    twice_cdf = 1.0 + jnp.tanh(u * poly)
    act = (0.5 * u) * twice_cdf
    ratio = jnp.tanh(act * inv_ceiling)
    twice_density = jnp.exp2(square * HALF_LOG2E + LOG2_TWICE_DENSITY)
    twice_slope = (1.0 - ratio * ratio) * (twice_cdf + u * twice_density)
    return act, ceiling * ratio, twice_slope


def fwd_kernel(count, *refs):
    (
        lens, scales, tokens, h_qkv, h_out, h_up, h_down, b_qkv, b_out, b_up, b_down, gain, shift,
        x_o, qkv_o, inv_o, ctx_o, n1_o, rs1_o, sl_o, n2_o, rs2_o, left_o, exp_o,
        mixed_o, peaks_o,
        w_qkv, w_out, w_up, w_down, w_sem,
        xin, xout, qkv_s, inv_s, ctx_s, n1_s, rs1_s, sl_s, n2_s, rs2_s, aq_s, hq_s, xq_s, cq_s,
        acc, hid, up_s, ops_s, s_s, e_s, o_s, amax_s,
        save_sem, in_sem, send_sem, recv_sem, mix_send, mix_recv,
    ) = refs
    r = pl.program_id(0)
    rows = pl.num_programs(0)
    row_count = tokens.shape[0]
    seq, width = tokens.shape[1], tokens.shape[2]
    ff = w_up.shape[1]
    piece = seq // count
    stage = lax.axis_index("pipe")
    first = stage == 0
    last = stage == count - 1

    left = {"aq": (0, ff), "hq": (ff, width), "xq": (ff + width, width), "cq": (ff + 2 * width, width)}
    staged = {
        "x": (xin.at[r], x_o), "qkv": (qkv_s, qkv_o), "inv": (inv_s, inv_o), "ctx": (ctx_s, ctx_o),
        "n1": (n1_s, n1_o), "rs1": (rs1_s, rs1_o), "sl": (sl_s, sl_o), "n2": (n2_s, n2_o),
        "rs2": (rs2_s, rs2_o), "aq": (aq_s, left_o), "hq": (hq_s, left_o), "xq": (xq_s, left_o),
        "cq": (cq_s, left_o), "exp": (e_s, exp_o),
    }
    order = list(staged)
    early = ("x", "xq", "qkv", "inv", "ctx", "cq", "exp")
    late = ("n1", "rs1", "hq", "aq", "sl", "n2", "rs2")
    fetches = [(h_qkv, w_qkv), (h_out, w_out), (h_up, w_up), (h_down, w_down)]

    def weight_copy(k):
        return pltpu.make_async_copy(fetches[k][0], fetches[k][1], w_sem.at[k])

    def save_copy(name):
        src, dst = staged[name]
        dst = dst.at[r]
        if name in left:
            dst = dst.at[:, pl.ds(*left[name])]
        return pltpu.make_async_copy(src, dst, save_sem.at[order.index(name)])

    def token_copy(i):
        return pltpu.make_async_copy(tokens.at[i], xin.at[i], in_sem.at[i])

    def hop(i):
        return pltpu.make_async_remote_copy(
            src_ref=xout.at[i], dst_ref=xin.at[i], send_sem=send_sem.at[i], recv_sem=recv_sem.at[i],
            device_id={"pipe": lax.rem(stage + 1, count)}, device_id_type=LOGICAL,
        )

    def mix_part(i, p):
        return pltpu.make_async_remote_copy(
            src_ref=xout.at[i, pl.ds(p * piece, piece)], dst_ref=mixed_o.at[i],
            send_sem=mix_send.at[i, p], recv_sem=mix_recv.at[i],
            device_id={"pipe": jnp.int32(p)}, device_id_type=LOGICAL,
        )

    def mix_own(i):
        return pltpu.make_async_copy(
            xout.at[i, pl.ds((count - 1) * piece, piece)], mixed_o.at[i], mix_send.at[i, count - 1]
        )

    @pl.when(r == 0)
    def _():
        greet(stage, count)
        peaks_o[...] = jnp.zeros_like(peaks_o)
        for k in range(4):
            weight_copy(k).start()

        @pl.when(first)
        def _():
            for i in range(row_count):
                token_copy(i).start()

    @pl.when(first)
    def _():
        token_copy(r).wait()

    @pl.when(jnp.logical_not(first))
    def _():
        hop(r).wait_recv()

    length = lens[r]
    m0, m1, m2, m3 = scales[0, 0], scales[0, 1], scales[0, 2], scales[0, 3]
    i0, i1, i2, i3 = 1.0 / m0, 1.0 / m1, 1.0 / m2, 1.0 / m3

    def row_mask(start, size):
        return (start + lax.broadcasted_iota(jnp.int32, (size, 1), 0)) < length

    def blocks(size, body, init=0, begin=0, end=seq):
        step = lambda i, c: body(i * size, pl.ds(i * size, size), c)
        return lax.fori_loop(begin // size, end // size, step, init, unroll=True)

    def weave(dots, size, body, init=0):
        total, cut = seq // size, 0
        for k, dot in enumerate(dots):
            dot()
            begin, cut = cut, total * (k + 1) // len(dots)
            init = blocks(size, body, init, begin * size, cut * size)
        return init

    no_peak = jnp.zeros((8, 128), F32)

    @pl.when(r > 0)
    def _():
        for name in early:
            save_copy(name).wait()

    @pl.when(r == 0)
    def _():
        weight_copy(0).wait()

    def quant_in(start, at, top):
        x = xin[r, at, :].astype(F32)
        xq_s[at, :] = (m0 * jnp.tanh(x * i0)).astype(BF16)
        return jnp.maximum(top, masked_peak(x, start))

    def masked_peak(v, start):
        return peak_rows(jnp.where(row_mask(start, v.shape[0]), jnp.abs(v), 0.0))

    peaks_o[0] = jnp.maximum(peaks_o[0], blocks(BLOCK, quant_in, no_peak))
    for j in range(3):
        cols = pl.ds(j * width, width)
        proj = dot_nn(xq_s[...], w_qkv[:, cols]) + b_qkv[:, cols]
        qkv_s[:, cols] = proj.astype(BF16)

    one = jnp.ones((), BF16)
    zero = jnp.zeros((), BF16)
    head_scale = jnp.asarray(HEAD_DIM ** -0.5, BF16)

    def prepare(p):
        slot = p % 2

        def body(start, at, c):
            lane = lax.broadcasted_iota(jnp.int32, (OPS, PAIR), 1)
            lo = lane < HEAD_DIM
            spot = jnp.where(lo, lane, lane - HEAD_DIM)
            bias = jnp.where(row_mask(start, OPS), 0.0, MASKED)
            extra = jnp.where(spot == 0, jnp.broadcast_to(bias, (OPS, PAIR)), 0.0).astype(BF16)
            q2 = qkv_s[at, p * PAIR : (p + 1) * PAIR] * head_scale
            k2 = qkv_s[at, width + p * PAIR : width + (p + 1) * PAIR]
            v2 = qkv_s[at, 2 * width + p * PAIR : 2 * width + (p + 1) * PAIR]
            ops_s[slot, 0, at, :] = jnp.where(lo, q2, one)
            ops_s[slot, 1, at, :] = jnp.where(lo, one, q2)
            ops_s[slot, 2, at, :] = jnp.where(lo, k2, extra)
            ops_s[slot, 3, at, :] = jnp.where(lo, extra, k2)
            ops_s[slot, 4, at, :] = jnp.where(lo, v2, one)
            ops_s[slot, 5, at, :] = jnp.where(lo, one, v2)
            return c

        blocks(OPS, body)

    def scores(h):
        p, side = h // 2, h % 2

        def piece_of(k):
            def run():
                keys = pl.ds(k * PIECE, PIECE)
                s_s[side, :, keys] = dot_nt(ops_s[p % 2, side], ops_s[p % 2, 2 + side, keys, :])

            return run

        return [piece_of(k) for k in range(seq // PIECE)]

    def soften(h):
        def body(start, at, c):
            s = s_s[h % 2, at, :]
            e_s[h, at, :] = jnp.exp(s - jnp.max(s, -1, keepdims=True)).astype(BF16)
            return c

        return body

    def collect(h):
        p, side = h // 2, h % 2

        def piece_of(k):
            def run():
                queries = pl.ds(k * PIECE, PIECE)
                o_s[side, queries, :] = dot_nn(e_s[h, queries, :], ops_s[p % 2, 4 + side])

            return run

        return [piece_of(k) for k in range(seq // PIECE)]

    def settle(p, peak):
        cols = slice(p * PAIR, (p + 1) * PAIR)

        def body(start, at, top):
            lo = lax.broadcasted_iota(jnp.int32, (OPS, PAIR), 1) < HEAD_DIM
            o_a, o_b = o_s[0, at, :], o_s[1, at, :]
            total = pltpu.roll(jnp.where(lo, o_b, o_a), HEAD_DIM, 1)
            inverse = 1.0 / total
            c = jnp.where(lo, o_a, o_b) * inverse
            inv_s[at, cols] = inverse
            ctx_s[at, cols] = c
            cq_s[at, cols] = (m1 * jnp.tanh(c * i1)).astype(BF16)
            return jnp.maximum(top, masked_peak(c, start))

        return blocks(OPS, body, peak)

    heads = 2 * (width // PAIR)
    peak = no_peak
    prepare(0)
    for dot in scores(0):
        dot()
    for h in range(heads):
        dots = []
        if h + 1 < heads:
            if (h + 1) % 2 == 0:
                prepare((h + 1) // 2)
            dots += scores(h + 1)
        if h > 0:
            dots += collect(h - 1)
        weave(dots, BLOCK, soften(h))
        if h > 0 and h % 2 == 0:
            peak = settle(h // 2 - 1, peak)
    for dot in collect(heads - 1):
        dot()
    peak = settle(heads // 2 - 1, peak)
    peaks_o[1] = jnp.maximum(peaks_o[1], peak)

    for name in early:
        save_copy(name).start()

    @pl.when(r > 0)
    def _():
        for name in late:
            save_copy(name).wait()

    @pl.when(r == 0)
    def _():
        for k in (1, 2, 3):
            weight_copy(k).wait()

    def out_piece(k):
        def run():
            at = pl.ds(k * PIECE, PIECE)
            acc[at, :] = dot_nn(cq_s[at, :], w_out[...])

        return run

    def norm_one(start, at, top):
        s = xin[r, at, :].astype(F32) + (acc[at, :] + b_out[...])
        center = s - jnp.mean(s, -1, keepdims=True)
        rs = lax.rsqrt(jnp.mean(center * center, -1, keepdims=True) + EPS)
        n = center * rs
        h = n * gain[0:1, :] + shift[0:1, :]
        n1_s[at, :] = n.astype(BF16)
        rs1_s[at, :] = jnp.broadcast_to(rs, (BLOCK, 128))
        hid[at, :] = h
        hq_s[at, :] = (m2 * jnp.tanh(h * i2)).astype(BF16)
        return jnp.maximum(top, masked_peak(h, start))

    out_piece(0)()
    top = weave([out_piece(k) for k in range(1, seq // PIECE)] + [lambda: None], BLOCK, norm_one, no_peak)
    peaks_o[2] = jnp.maximum(peaks_o[2], top)

    chunks = ff // CHUNK

    def up_chunk(c):
        def piece_of(k):
            def run():
                part = dot_nn(hq_s[...], w_up[:, pl.ds(c * CHUNK + k * PIECE, PIECE)])
                up_s[c % 2, :, pl.ds(k * PIECE, PIECE)] = part

            return run

        return [piece_of(k) for k in range(CHUNK // PIECE)]

    def act_chunk(c):
        cols = pl.ds(c * CHUNK, CHUNK)

        def body(start, at, carry):
            act, low, slope = activation(up_s[c % 2, at, :] + b_up[:, cols], m3, i3)
            aq_s[at, cols] = low.astype(BF16)
            sl_s[at, cols] = slope.astype(BF16)
            size = jnp.abs(act)
            top = size[:, 0:128]
            for i in range(128, CHUNK, 128):
                top = jnp.maximum(top, size[:, i : i + 128])
            amax_s[at, :] = top if c == 0 else jnp.maximum(amax_s[at, :], top)
            return carry

        return body

    def down_chunk(c):
        def piece_of(k):
            def run():
                cols = pl.ds(k * PIECE, PIECE)
                part = dot_nn(aq_s[:, pl.ds(c * CHUNK, CHUNK)], w_down[pl.ds(c * CHUNK, CHUNK), cols])
                acc[:, cols] = part if c == 0 else acc[:, cols] + part

            return run

        return [piece_of(k) for k in range(width // PIECE)]

    for dot in up_chunk(0):
        dot()
    for c in range(chunks):
        dots = []
        if c + 1 < chunks:
            dots += up_chunk(c + 1)
        if c > 0:
            dots += down_chunk(c - 1)
        weave(dots, BLOCK, act_chunk(c))
    peaks_o[3] = jnp.maximum(peaks_o[3], masked_peak(amax_s[...], 0))

    def norm_two(start, at, c):
        s = hid[at, :] + (acc[at, :] + b_down[...])
        center = s - jnp.mean(s, -1, keepdims=True)
        rs = lax.rsqrt(jnp.mean(center * center, -1, keepdims=True) + EPS)
        n = center * rs
        n2_s[at, :] = n.astype(BF16)
        rs2_s[at, :] = jnp.broadcast_to(rs, (BLOCK, 128))
        xout[r, at, :] = (n * gain[1:2, :] + shift[1:2, :]).astype(BF16)
        return c

    def down_last(k):
        def run():
            at, cols = pl.ds(k * PIECE, PIECE), pl.ds((chunks - 1) * CHUNK, CHUNK)
            acc[at, :] += dot_nn(aq_s[at, cols], w_down[cols, :])

        return run

    down_last(0)()
    weave([down_last(k) for k in range(1, seq // PIECE)] + [lambda: None], BLOCK, norm_two)
    for name in late:
        save_copy(name).start()

    @pl.when(jnp.logical_not(last))
    def _():
        hop(r).start()

    @pl.when(last)
    def _():
        for p in range(count - 1):
            mix_part(r, p).start()
        mix_own(r).start()

    @pl.when(r == rows - 1)
    def _():
        for name in order:
            save_copy(name).wait()

        @pl.when(jnp.logical_not(last))
        def _():
            for i in range(row_count):
                hop(i).wait_send()
            for i in range(row_count):
                mix_part(i, 0).wait_recv()

        @pl.when(last)
        def _():
            for i in range(row_count):
                for p in range(count - 1):
                    mix_part(i, p).wait_send()
                mix_own(i).wait()


def bwd_kernel(count, *refs):
    (
        lens, scales, seeds, h_qkv, h_out, h_up, h_down, gain, shift, left_i,
        x_i, qkv_i, inv_i, ctx_i, n1_i, rs1_i, sl_i, n2_i, rs2_i, exp_i,
        dproj_o, dbr_o, dup_o, ddn_o, gtok_o, left_o, small_o,
        w_qkv, w_out, w_up, w_down, w_sem, turn_in, turn_out, turn_in_sem, turn_out_sem,
        gin, x_s, qkv_s, inv_s, ctx_s, n1_s, rs1_s, sl_s, n2_s, rs2_s, e_s,
        dproj_s, dbr_s, dup_s, ddn_s, dctx_s, acc, dr,
        up_s, ops_s, g_s, ds_s, gv_s, gk_s, gq_s, q_t, do_t, inner_s,
        load_sem, save_sem, in_sem, send_sem, recv_sem, tok_send,
    ) = refs
    r = pl.program_id(0)
    rows = pl.num_programs(0)
    row_count = seeds.shape[0]
    seq, width = seeds.shape[1], seeds.shape[2]
    ff = w_up.shape[1]
    piece = seq // count
    stage = lax.axis_index("pipe")
    first = stage == 0
    last = stage == count - 1

    loaded = {
        "n2": (n2_i, n2_s), "rs2": (rs2_i, rs2_s), "sl": (sl_i, sl_s), "n1": (n1_i, n1_s),
        "rs1": (rs1_i, rs1_s), "ctx": (ctx_i, ctx_s), "qkv": (qkv_i, qkv_s), "inv": (inv_i, inv_s),
        "x": (x_i, x_s), "exp": (exp_i, e_s),
    }
    load_order = list(loaded)
    early = ("n2", "rs2", "sl", "n1", "rs1")
    late = ("ctx", "qkv", "inv", "exp", "x")
    staged = {
        "ddn": (ddn_s, ddn_o), "dup": (dup_s, dup_o), "dbr": (dbr_s, dbr_o), "dproj": (dproj_s, dproj_o),
    }
    save_order = list(staged)

    def load_copy(name, i):
        src, dst = loaded[name]
        return pltpu.make_async_copy(src.at[i], dst, load_sem.at[load_order.index(name)])

    def save_copy(name):
        src, dst = staged[name]
        return pltpu.make_async_copy(src, dst.at[r], save_sem.at[save_order.index(name)])

    def seed_copy(i):
        return pltpu.make_async_copy(seeds.at[i], gin.at[i], in_sem.at[i])

    def hop(i):
        return pltpu.make_async_remote_copy(
            src_ref=gin.at[i], dst_ref=gin.at[i], send_sem=send_sem.at[i], recv_sem=recv_sem.at[i],
            device_id={"pipe": lax.rem(stage + count - 1, count)}, device_id_type=LOGICAL,
        )

    def tok_copy(i):
        return pltpu.make_async_copy(gin.at[i], gtok_o.at[i], tok_send.at[i])

    fetches = [(h_down, w_down), (h_up, w_up), (h_out, w_out), (h_qkv, w_qkv)]

    def weight_copy(k):
        return pltpu.make_async_copy(fetches[k][0], fetches[k][1], w_sem.at[k])

    parts = left_i.shape[2] // width
    turns = row_count * parts

    def turn_load(i):
        cols = pl.ds(pl.multiple_of(i % parts * width, 128), width)
        return pltpu.make_async_copy(left_i.at[i // parts, :, cols], turn_in.at[i % 2], turn_in_sem.at[i % 2])

    def turn_store(i):
        rows_at = pl.ds(pl.multiple_of(i % parts * width, 128), width)
        cols = pl.ds(pl.multiple_of(i // parts * seq, 128), seq)
        return pltpu.make_async_copy(turn_out.at[i % 2], left_o.at[rows_at, cols], turn_out_sem.at[i % 2])

    def turn_left():
        turn_load(0).start()

        def body(i, c):
            @pl.when(i + 1 < turns)
            def _():
                turn_load(i + 1).start()

            turn_load(i).wait()

            @pl.when(i >= 2)
            def _():
                turn_store(i - 2).wait()

            turn_out[i % 2] = turn_in[i % 2].T
            turn_store(i).start()
            return c

        lax.fori_loop(0, turns, body, 0)
        turn_store(turns - 2).wait()
        turn_store(turns - 1).wait()

    @pl.when(r == 0)
    def _():
        greet(stage, count)
        small_o[...] = jnp.zeros_like(small_o)

        @pl.when(last)
        def _():
            for i in range(row_count):
                seed_copy(i).start()

        for name in ("n2", "rs2"):
            load_copy(name, 0).start()
        weight_copy(0).start()
        for name in early[2:]:
            load_copy(name, 0).start()
        for k in (1, 2, 3):
            weight_copy(k).start()
        for name in late:
            load_copy(name, 0).start()

        @pl.when(stage < count - 2)
        def _():
            turn_left()

    @pl.when(last)
    def _():
        seed_copy(r).wait()

    @pl.when(jnp.logical_not(last))
    def _():
        hop(r).wait_recv()

    length = lens[r]
    m0, m1, m2 = scales[0, 0], scales[0, 1], scales[0, 2]
    i0, i1, i2 = 1.0 / m0, 1.0 / m1, 1.0 / m2

    offsets = {}
    at_col = 0
    for name, size in (
        ("gain0", width), ("gain1", width), ("shift0", width), ("shift1", width),
        ("out", width), ("down", width), ("up", ff), ("qkv", 3 * width),
    ):
        offsets[name] = at_col
        at_col += size

    def blocks(size, body, init=0, begin=0, end=seq):
        step = lambda i, c: body(i * size, pl.ds(i * size, size), c)
        return lax.fori_loop(begin // size, end // size, step, init, unroll=True)

    def weave(dots, size, body, init=0):
        total, cut = seq // size, 0
        for k, dot in enumerate(dots):
            dot()
            begin, cut = cut, total * (k + 1) // len(dots)
            init = blocks(size, body, init, begin * size, cut * size)
        return init

    def row_mask(start, size):
        return (start + lax.broadcasted_iota(jnp.int32, (size, 1), 0)) < length

    def put_small(name, v, col=0):
        small_o[:, pl.ds(offsets[name] + col, v.shape[1])] += v

    no_sum = jnp.zeros((8, width), F32)

    for name in early:
        load_copy(name, r).wait()

    @pl.when(r > 0)
    def _():
        for name in ("ddn", "dup", "dbr"):
            save_copy(name).wait()

    @pl.when(r == 0)
    def _():
        for k in (0, 1):
            weight_copy(k).wait()

    def norm_two(start, at, sums):
        dy = jnp.where(row_mask(start, BLOCK), gin[r, at, :].astype(F32), 0.0)
        n = n2_s[at, :].astype(F32)
        e = dy * gain[1:2, :]
        mean_e = jnp.mean(e, -1, keepdims=True)
        mean_en = jnp.mean(e * n, -1, keepdims=True)
        d = (e - mean_e - n * mean_en) * rs2_s[at, 0:1]
        dr[at, :] = d
        ddn_s[at, :] = d.astype(BF16)
        return sums[0] + fold_rows(dy * n), sums[1] + fold_rows(dy), sums[2] + fold_rows(d)

    for name, v in zip(("gain1", "shift1", "down"), blocks(BLOCK, norm_two, (no_sum,) * 3)):
        put_small(name, v)

    chunks = ff // CHUNK

    def dact_chunk(c):
        def piece_of(k):
            def run():
                at = pl.ds(c * CHUNK + k * PIECE, PIECE)
                up_s[c % 2, :, pl.ds(k * PIECE, PIECE)] = dot_nt(ddn_s[...], w_down[at, :])

            return run

        return [piece_of(k) for k in range(CHUNK // PIECE)]

    def slope_chunk(c):
        cols = pl.ds(c * CHUNK, CHUNK)

        def body(start, at, total):
            d = (0.5 * up_s[c % 2, at, :]) * sl_s[at, cols].astype(F32)
            dup_s[at, cols] = d.astype(BF16)
            return total + fold_rows(d)

        return body

    def dhid_chunk(c):
        cols = pl.ds(c * CHUNK, CHUNK)

        def piece_of(k):
            def run():
                at = pl.ds(k * PIECE, PIECE)
                part = dot_nt(dup_s[:, cols], w_up[at, cols])
                acc[:, at] = part if c == 0 else acc[:, at] + part

            return run

        return [piece_of(k) for k in range(width // PIECE)]

    for dot in dact_chunk(0):
        dot()
    for c in range(chunks):
        dots = []
        if c + 1 < chunks:
            dots += dact_chunk(c + 1)
        if c > 0:
            dots += dhid_chunk(c - 1)
        put_small("up", weave(dots, BLOCK, slope_chunk(c), jnp.zeros((8, CHUNK), F32)), c * CHUNK)

    def norm_one(start, at, sums):
        n = n1_s[at, :].astype(F32)
        t = jnp.tanh((n * gain[0:1, :] + shift[0:1, :]) * i2)
        dy = dr[at, :] + acc[at, :] * (1.0 - t * t)
        e = dy * gain[0:1, :]
        mean_e = jnp.mean(e, -1, keepdims=True)
        mean_en = jnp.mean(e * n, -1, keepdims=True)
        d = (e - mean_e - n * mean_en) * rs1_s[at, 0:1]
        dr[at, :] = d
        dbr_s[at, :] = d.astype(BF16)
        return sums[0] + fold_rows(dy * n), sums[1] + fold_rows(dy), sums[2] + fold_rows(d)

    def dhid_last(k):
        def run():
            at, cols = pl.ds(k * PIECE, PIECE), pl.ds((chunks - 1) * CHUNK, CHUNK)
            acc[at, :] += dot_nt(dup_s[at, cols], w_up[:, cols])

        return run

    dhid_last(0)()
    dots = [dhid_last(k) for k in range(1, seq // PIECE)] + [lambda: None]
    for name, v in zip(("gain0", "shift0", "out"), weave(dots, BLOCK, norm_one, (no_sum,) * 3)):
        put_small(name, v)

    for name in ("ddn", "dup", "dbr"):
        save_copy(name).start()

    @pl.when(r + 1 < rows)
    def _():
        for name in early:
            load_copy(name, r + 1).start()

    for name in late:
        load_copy(name, r).wait()

    @pl.when(r > 0)
    def _():
        save_copy("dproj").wait()

    @pl.when(r == 0)
    def _():
        for k in (2, 3):
            weight_copy(k).wait()

    for k in range(width // PIECE):
        acc[:, pl.ds(k * PIECE, PIECE)] = dot_nt(dbr_s[...], w_out[pl.ds(k * PIECE, PIECE), :])

    zero = jnp.zeros((), BF16)
    head_scale = jnp.asarray(HEAD_DIM ** -0.5, BF16)

    def prepare(p):
        slot = p % 2
        cols = slice(p * PAIR, (p + 1) * PAIR)

        def body(start, at, c):
            lo = lax.broadcasted_iota(jnp.int32, (OPS, PAIR), 1) < HEAD_DIM
            ctx = ctx_s[at, cols]
            t = jnp.tanh(ctx * i1)
            low = (acc[at, cols] * (1.0 - t * t) * inv_s[at, cols]).astype(BF16)
            dctx_s[slot, at, :] = low
            inner = low.astype(F32) * ctx
            whole_sum = jnp.sum(inner, -1, keepdims=True)
            lower = jnp.sum(jnp.where(lo, inner, 0.0), -1, keepdims=True)
            inner_s[slot, 0, at, :] = jnp.broadcast_to(lower, (OPS, PAIR))
            inner_s[slot, 1, at, :] = jnp.broadcast_to(whole_sum - lower, (OPS, PAIR))
            v2 = qkv_s[at, 2 * width + p * PAIR : 2 * width + (p + 1) * PAIR]
            ops_s[slot, 0, at, :] = jnp.where(lo, v2, zero)
            ops_s[slot, 1, at, :] = jnp.where(lo, zero, v2)
            return c

        blocks(OPS, body)
        q_t[slot] = (qkv_s[:, cols] * head_scale).T
        do_t[slot] = dctx_s[slot].T

    def scores(h):
        slot, side = h // 2 % 2, h % 2

        def piece_of(k):
            def run():
                keys = pl.ds(k * PIECE, PIECE)
                g_s[side, :, keys] = dot_nt(dctx_s[slot], ops_s[slot, side, keys, :])

            return run

        return [piece_of(k) for k in range(seq // PIECE)]

    def soften(h):
        slot, side = h // 2 % 2, h % 2

        def body(start, at, c):
            inner = jnp.concatenate([inner_s[slot, side, at, :]] * (seq // PAIR), 1)
            ds_s[side, at, :] = (e_s[h, at, :].astype(F32) * (g_s[side, at, :] - inner)).astype(BF16)
            return c

        return body

    def collect(h):
        slot, side = h // 2 % 2, h % 2
        rows_at = slice(side * HEAD_DIM, (side + 1) * HEAD_DIM)

        def grad_v(k):
            def run():
                keys = pl.ds(k * PIECE, PIECE)
                gv_s[rows_at, keys] = dot_nn(do_t[slot, rows_at, :], e_s[h, :, keys])

            return run

        def grad_k(k):
            def run():
                keys = pl.ds(k * PIECE, PIECE)
                gk_s[rows_at, keys] = dot_nn(q_t[slot, rows_at, :], ds_s[side, :, keys])

            return run

        def grad_q(k):
            def run():
                queries = pl.ds(k * PIECE, PIECE)
                keys_low = qkv_s[:, width + h // 2 * PAIR : width + (h // 2 + 1) * PAIR]
                gq_s[side, queries, :] = dot_nn(ds_s[side, queries, :], keys_low)

            return run

        return [make(k) for make in (grad_v, grad_k, grad_q) for k in range(seq // PIECE)]

    def settle(p):
        def body(start, at, c):
            lo = lax.broadcasted_iota(jnp.int32, (OPS, PAIR), 1) < HEAD_DIM
            q = jnp.where(lo, gq_s[0, at, :], gq_s[1, at, :]) * (HEAD_DIM ** -0.5)
            dproj_s[at, p * PAIR : (p + 1) * PAIR] = q.astype(BF16)
            return c

        blocks(OPS, body)
        dproj_s[:, width + p * PAIR : width + (p + 1) * PAIR] = gk_s[...].astype(BF16).T
        dproj_s[:, 2 * width + p * PAIR : 2 * width + (p + 1) * PAIR] = gv_s[...].astype(BF16).T

    heads = 2 * (width // PAIR)
    prepare(0)
    for dot in scores(0):
        dot()
    for h in range(heads):
        dots = []
        if h + 1 < heads:
            if (h + 1) % 2 == 0:
                prepare((h + 1) // 2)
            dots += scores(h + 1)
        if h > 0:
            dots += collect(h - 1)
        weave(dots, BLOCK, soften(h))
        if h > 0 and h % 2 == 0:
            settle(h // 2 - 1)
    for dot in collect(heads - 1):
        dot()
    settle(heads // 2 - 1)
    def dx_piece(k):
        def run():
            at = pl.ds(k * PIECE, PIECE)
            acc[:, at] = dot_nt(dproj_s[...], w_qkv[at, :])

        return run

    def quant_in(k):
        cols = pl.ds(k * PIECE, PIECE)
        values = pl.ds(2 * width + k * PIECE, PIECE)

        def body(start, at, sums):
            t = jnp.tanh(x_s[at, cols].astype(F32) * i0)
            gin[r, at, cols] = (dr[at, cols] + acc[at, cols] * (1.0 - t * t)).astype(BF16)
            return (
                sums[0] + fold_rows(dproj_s[at, cols].astype(F32)),
                sums[1] + fold_rows(dproj_s[at, values].astype(F32)),
            )

        return body

    dx_piece(0)()
    pieces = width // PIECE
    for k in range(pieces):
        dots = [dx_piece(k + 1)] if k + 1 < pieces else [lambda: None]
        sums = weave(dots, BLOCK, quant_in(k), (jnp.zeros((8, PIECE), F32),) * 2)
        put_small("qkv", sums[0], k * PIECE)
        put_small("qkv", sums[1], 2 * width + k * PIECE)
    save_copy("dproj").start()

    @pl.when(r + 1 < rows)
    def _():
        for name in late:
            load_copy(name, r + 1).start()

    @pl.when(jnp.logical_not(first))
    def _():
        hop(r).start()

    @pl.when(first)
    def _():
        tok_copy(r).start()

    @pl.when(r == rows - 1)
    def _():
        @pl.when(stage >= count - 2)
        def _():
            turn_left()

        for name in save_order:
            save_copy(name).wait()

        @pl.when(jnp.logical_not(first))
        def _():
            for i in range(row_count):
                hop(i).wait_send()

        @pl.when(first)
        def _():
            for i in range(row_count):
                tok_copy(i).wait()


def whole(a):
    return pl.BlockSpec(a.shape, lambda r, n=a.ndim: (0,) * n, pipeline_mode=pl.Buffered(1))


ANYWHERE = pl.BlockSpec(memory_space=pl.ANY)
SCALAR = pl.BlockSpec(memory_space=pltpu.SMEM)
VMEM_LIMIT = 60 * 1024 * 1024


def run_forward(count, tokens, lengths, scales, weights):
    w_qkv, b_qkv, w_out, b_out, w_up, b_up, w_down, b_down, gain, shift = weights
    rows, seq, width = tokens.shape
    ff = w_up.shape[1]
    big = lambda n, t: jax.ShapeDtypeStruct((rows, seq, n), t)
    saves = [
        (width, BF16), (3 * width, BF16), (width, F32), (width, F32), (width, BF16), (128, F32),
        (ff, BF16), (width, BF16), (128, F32),
    ]
    heads = width // HEAD_DIM
    lefts = [(ff, BF16), (width, BF16), (width, BF16), (width, BF16)]
    heavy = (w_qkv, w_out, w_up, w_down)
    dense = (b_qkv, b_out, b_up, b_down, gain, shift)
    tok = rows * seq
    return pl.pallas_call(
        lambda *refs: fwd_kernel(count, *refs),
        grid=(rows,),
        in_specs=[SCALAR, SCALAR, ANYWHERE] + [ANYWHERE] * 4 + [whole(a) for a in dense],
        out_specs=[ANYWHERE] * 12 + [pl.BlockSpec((4, 8, 128), lambda r: (0, 0, 0))],
        out_shape=[big(n, t) for n, t in saves]
        + [
            big(ff + 3 * width, BF16),
            jax.ShapeDtypeStruct((rows, heads, seq, seq), BF16),
            jax.ShapeDtypeStruct((rows, seq // count, width), BF16),
            jax.ShapeDtypeStruct((4, 8, 128), F32),
        ],
        scratch_shapes=[pltpu.VMEM(a.shape, a.dtype) for a in heavy]
        + [pltpu.SemaphoreType.DMA((4,))]
        + [pltpu.VMEM((rows, seq, width), BF16), pltpu.VMEM((rows, seq, width), BF16)]
        + [pltpu.VMEM((seq, n), t) for n, t in saves[1:] + lefts]
        + [
            pltpu.VMEM((seq, width), F32),
            pltpu.VMEM((seq, width), F32),
            pltpu.VMEM((2, seq, CHUNK), F32),
            pltpu.VMEM((2, 6, seq, PAIR), BF16),
            pltpu.VMEM((2, seq, seq), F32),
            pltpu.VMEM((heads, seq, seq), BF16),
            pltpu.VMEM((2, seq, PAIR), F32),
            pltpu.VMEM((seq, 128), F32),
            pltpu.SemaphoreType.DMA((14,)),
            pltpu.SemaphoreType.DMA((rows,)),
            pltpu.SemaphoreType.DMA((rows,)),
            pltpu.SemaphoreType.DMA((rows,)),
            pltpu.SemaphoreType.DMA((rows, count)),
            pltpu.SemaphoreType.DMA((rows,)),
        ],
        compiler_params=pltpu.CompilerParams(
            collective_id=0, has_side_effects=True, vmem_limit_bytes=VMEM_LIMIT,
            dimension_semantics=("arbitrary",),
        ),
        cost_estimate=pl.CostEstimate(
            flops=2 * tok * (4 * width * width + 2 * width * ff + 2 * seq * width),
            bytes_accessed=tok * 28000, transcendentals=tok * 3 * ff,
        ),
    )(lengths, scales, tokens, *heavy, *dense)


def run_backward(count, seeds, lengths, scales, weights, kept):
    w_qkv, b_qkv, w_out, b_out, w_up, b_up, w_down, b_down, gain, shift = weights
    *loads, left, exps = kept
    loads.append(exps)
    rows, seq, width = seeds.shape
    ff = w_up.shape[1]
    big = lambda n, t: jax.ShapeDtypeStruct((rows, seq, n), t)
    saves = [(3 * width, BF16), (width, BF16), (ff, BF16), (width, BF16)]
    heavy = (w_qkv, w_out, w_up, w_down)
    dense = (gain, shift)
    tok = rows * seq
    small = 6 * width + ff + 3 * width
    return pl.pallas_call(
        lambda *refs: bwd_kernel(count, *refs),
        grid=(rows,),
        in_specs=[SCALAR, SCALAR, ANYWHERE] + [ANYWHERE] * 4 + [whole(a) for a in dense] + [ANYWHERE] * 11,
        out_specs=[ANYWHERE] * 6 + [pl.BlockSpec((8, small), lambda r: (0, 0))],
        out_shape=[big(n, t) for n, t in saves]
        + [
            big(width, BF16), jax.ShapeDtypeStruct((left.shape[2], rows * seq), BF16),
            jax.ShapeDtypeStruct((8, small), F32),
        ],
        scratch_shapes=[pltpu.VMEM(a.shape, a.dtype) for a in heavy]
        + [
            pltpu.SemaphoreType.DMA((4,)),
            pltpu.VMEM((2, seq, width), BF16),
            pltpu.VMEM((2, width, seq), BF16),
            pltpu.SemaphoreType.DMA((2,)),
            pltpu.SemaphoreType.DMA((2,)),
        ]
        + [pltpu.VMEM((rows, seq, width), BF16)]
        + [pltpu.VMEM(a.shape[1:], a.dtype) for a in loads]
        + [pltpu.VMEM((seq, n), t) for n, t in saves]
        + [
            pltpu.VMEM((2, seq, PAIR), BF16),
            pltpu.VMEM((seq, width), F32),
            pltpu.VMEM((seq, width), F32),
            pltpu.VMEM((2, seq, CHUNK), F32),
            pltpu.VMEM((2, 2, seq, PAIR), BF16),
            pltpu.VMEM((2, seq, seq), F32),
            pltpu.VMEM((2, seq, seq), BF16),
            pltpu.VMEM((PAIR, seq), F32),
            pltpu.VMEM((PAIR, seq), F32),
            pltpu.VMEM((2, seq, PAIR), F32),
            pltpu.VMEM((2, PAIR, seq), BF16),
            pltpu.VMEM((2, PAIR, seq), BF16),
            pltpu.VMEM((2, 2, seq, PAIR), F32),
            pltpu.SemaphoreType.DMA((10,)),
            pltpu.SemaphoreType.DMA((4,)),
            pltpu.SemaphoreType.DMA((rows,)),
            pltpu.SemaphoreType.DMA((rows,)),
            pltpu.SemaphoreType.DMA((rows,)),
            pltpu.SemaphoreType.DMA((rows,)),
        ],
        compiler_params=pltpu.CompilerParams(
            collective_id=1, has_side_effects=True, vmem_limit_bytes=VMEM_LIMIT,
            dimension_semantics=("arbitrary",),
        ),
        cost_estimate=pl.CostEstimate(
            flops=2 * tok * (4 * width * width + 2 * width * ff + 5 * seq * width),
            bytes_accessed=tok * 28000, transcendentals=tok * ff,
        ),
    )(lengths, scales, seeds, *heavy, *dense, left, *loads)


def ring_to_dp(pos, n):
    return jnp.where(pos < n // 2, 2 * pos, 2 * (n - pos) - 1)


def dp_to_ring(j, n):
    return jnp.where(j % 2 == 0, j // 2, n - 1 - j // 2)


def grad_kernel(count, n, *refs):
    (
        left, ddn, dup, dproj, dbr, small, g0,
        gq_o, go_o, gu_o, gd_o, small_o, gtok_o,
        slots_d, slots_u, slots_q, slots_s, wide_v, thin_v, ddn_v, dup_v, dpo_v, mine_u, mine_q,
        wide_sem, thin_sem, right_sem,
        send_d, recv_d, send_u, recv_u, send_q, recv_q, send_s, recv_s, tok_send, tok_recv,
    ) = refs
    width = ddn.shape[1]
    ff = dup.shape[1]
    shard, shard_ff = width // n, ff // n
    row_count, seq = g0.shape[0], g0.shape[1]
    piece = seq // count
    stage = lax.axis_index("pipe")
    me = lax.axis_index("dp")
    pos = dp_to_ring(me, n)
    first = stage == 0
    ahead = ring_to_dp(lax.rem(pos + 1, n), n)
    behind = ring_to_dp(lax.rem(pos + n - 1, n), n)
    target = (ahead, behind)

    def chunk(d, step):
        at = pos + 2 * n - 1 - step if d == 0 else pos + 1 + step
        return ring_to_dp(lax.rem(at, n), n)

    def wide_copy(d, step):
        rows = pl.ds(pl.multiple_of(chunk(d, step) * shard_ff, 16), shard_ff)
        return pltpu.make_async_copy(left.at[rows, :], wide_v.at[d], wide_sem.at[d])

    def thin_copy(k, d, step):
        at = lax.rem(step, 2)
        rows = pl.ds(pl.multiple_of(ff + k * width + chunk(d, step) * shard, 16), shard)
        place_at = pl.ds(pl.multiple_of(at * shard, 16), shard)
        return pltpu.make_async_copy(left.at[rows, :], thin_v.at[min(2 * k + d, 4), place_at, :], thin_sem.at[k, d, at])

    rights = [
        (ddn, ddn_v), (dup, dup_v), (dproj, dpo_v.at[:, pl.ds(0, 3 * width)]),
        (dbr, dpo_v.at[:, pl.ds(3 * width, width)]),
    ]

    def right_copy(k):
        return pltpu.make_async_copy(rights[k][0], rights[k][1], right_sem.at[k])

    for d in range(2):
        wide_copy(d, 0).start()
    right_copy(0).start()
    right_copy(1).start()
    for d in range(2):
        for at in range(2):
            thin_copy(0, d, at).start()
    right_copy(2).start()
    right_copy(3).start()
    for k, d in ((1, 0), (1, 1), (2, 1)):
        for at in range(2):
            thin_copy(k, d, at).start()

    barrier = pltpu.get_barrier_semaphore()
    for peer in target:
        pl.semaphore_signal(barrier, inc=1, device_id={"dp": peer}, device_id_type=LOGICAL)

    @pl.when(first)
    def _():
        pl.semaphore_wait(barrier, 1 + count)

    @pl.when(jnp.logical_not(first))
    def _():
        pl.semaphore_signal(barrier, inc=1, device_id={"pipe": jnp.int32(0)}, device_id_type=LOGICAL)
        pl.semaphore_wait(barrier, 2)

    def tok_part(i, p):
        return pltpu.make_async_remote_copy(
            src_ref=g0.at[i, pl.ds(p * piece, piece)], dst_ref=gtok_o.at[i],
            send_sem=tok_send.at[i, p], recv_sem=tok_recv.at[i],
            device_id={"pipe": jnp.int32(p)}, device_id_type=LOGICAL,
        )

    def tok_own(i):
        return pltpu.make_async_copy(g0.at[i, pl.ds(0, piece)], gtok_o.at[i], tok_send.at[i, 0])

    @pl.when(first)
    def _():
        for i in range(row_count):
            for p in range(1, count):
                tok_part(i, p).start()
            tok_own(i).start()

    def message(slots, send, recv, d, at):
        return pltpu.make_async_remote_copy(
            src_ref=slots.at[d, at], dst_ref=slots.at[d, jnp.minimum(at + 1, n - 1)],
            send_sem=send.at[d, at], recv_sem=recv.at[d, jnp.minimum(at + 1, n - 1)],
            device_id={"dp": target[d]}, device_id_type=LOGICAL,
        )

    def arrived(slots, send, recv, d, at):
        return pltpu.make_async_remote_copy(
            src_ref=slots.at[d, at], dst_ref=slots.at[d, at],
            send_sem=send.at[d, at], recv_sem=recv.at[d, at],
            device_id={"dp": target[d]}, device_id_type=LOGICAL,
        )

    def lane(slots, send, recv, d, step, mine, finish):
        @pl.when(step == 0)
        def _():
            slots[d, 0] = mine.astype(BF16)

        @pl.when(step > 0)
        def _():
            arrived(slots, send, recv, d, step).wait_recv()

            @pl.when(step < n - 1)
            def _():
                slots[d, step] = (slots[d, step].astype(F32) + mine).astype(BF16)

            @pl.when(step == n - 1)
            def _():
                finish(slots[d, step].astype(F32) + mine)

        @pl.when(step < n - 1)
        def _():
            message(slots, send, recv, d, step).start()

    def small_message(at):
        return pltpu.make_async_remote_copy(
            src_ref=slots_s.at[at], dst_ref=slots_s.at[jnp.minimum(at + 1, n - 1)],
            send_sem=send_s.at[at], recv_sem=recv_s.at[jnp.minimum(at + 1, n - 1)],
            device_id={"dp": target[0]}, device_id_type=LOGICAL,
        )

    def small_arrived(at):
        return pltpu.make_async_remote_copy(
            src_ref=slots_s.at[at], dst_ref=slots_s.at[at], send_sem=send_s.at[at],
            recv_sem=recv_s.at[at], device_id={"dp": target[0]}, device_id_type=LOGICAL,
        )

    sum_rows = lax.broadcasted_iota(jnp.int32, (16, 128), 0) < 9

    def small_step(step):
        mine = small[chunk(0, step)]

        @pl.when(step == 0)
        def _():
            slots_s[0] = mine

        @pl.when(step > 0)
        def _():
            small_arrived(step).wait_recv()
            got = slots_s[step]
            slots_s[step] = jnp.where(sum_rows, got + mine, jnp.maximum(got, mine))

        @pl.when(step < n - 1)
        def _():
            small_message(step).start()

        @pl.when(step == n - 1)
        def _():
            small_o[...] = slots_s[step]

    half, half_ff = width // 2, ff // 2

    def fetched(copy, step, *args):
        copy(*args, step).wait()

    def refill(copy, step, *args):
        @pl.when(step < n - 1)
        def _():
            copy(*args, step + 1).start()

    def right_ready(k, step):
        @pl.when(step == 0)
        def _():
            right_copy(k).wait()

    def turn(step, _):
        right_ready(0, step)
        for d in range(2):
            cols = slice(d * half, (d + 1) * half)
            fetched(wide_copy, step, d)
            mine = dot_nn(wide_v[d], ddn_v[:, cols])
            refill(wide_copy, step, d)

            def finish_down(total):
                gd_o[:, cols] = total

            lane(slots_d, send_d, recv_d, d, step, mine, finish_down)
        small_step(step)
        right_ready(1, step)
        paired = lax.rem(step, 2) == 0

        def together(k, d, right, store):
            for at in range(2):
                thin_copy(k, d, step + at).wait()
            both = dot_nn(thin_v[min(2 * k + d, 4)], right)
            store(0, both[:shard])
            store(1, both[shard:])

            @pl.when(step + 2 < n)
            def _():
                for at in range(2):
                    thin_copy(k, d, step + 2 + at).start()

        for d in range(2):
            cols = slice(d * half_ff, (d + 1) * half_ff)

            @pl.when(paired)
            def _():
                def store(at, v):
                    if at == 0:
                        mine_u[d] = v
                    else:
                        gu_o[:, cols] = v

                together(0, d, dup_v[:, cols], store)

            @pl.when(jnp.logical_not(paired))
            def _():
                mine_u[d] = gu_o[:, cols]

            def finish_up(total):
                gu_o[:, cols] = total

            lane(slots_u, send_u, recv_u, d, step, mine_u[d], finish_up)
        right_ready(2, step)
        right_ready(3, step)

        @pl.when(paired)
        def _():
            def store(at, v):
                if at == 0:
                    mine_q[0] = v
                else:
                    gq_o[:, 0 : 2 * width] = v

            together(1, 0, dpo_v[:, 0 : 2 * width], store)

        @pl.when(jnp.logical_not(paired))
        def _():
            mine_q[0] = gq_o[:, 0 : 2 * width]

        def finish_ahead(total):
            gq_o[:, 0 : 2 * width] = total

        lane(slots_q, send_q, recv_q, 0, step, mine_q[0], finish_ahead)

        @pl.when(paired)
        def _():
            for k, out, cols in ((1, gq_o, slice(2 * width, 3 * width)), (2, go_o, slice(0, width))):
                def store(at, v):
                    if at == 0:
                        mine_q[1, :, (k - 1) * width : k * width] = v
                    else:
                        out[:, cols] = v

                together(k, 1, dpo_v[:, (k + 1) * width : (k + 2) * width], store)

        @pl.when(jnp.logical_not(paired))
        def _():
            mine_q[1, :, 0:width] = gq_o[:, 2 * width : 3 * width]
            mine_q[1, :, width : 2 * width] = go_o[...]

        def finish_behind(total):
            gq_o[:, 2 * width : 3 * width] = total[:, 0:width]
            go_o[...] = total[:, width : 2 * width]

        lane(slots_q, send_q, recv_q, 1, step, mine_q[1], finish_behind)
        return 0

    lax.fori_loop(0, n, turn, 0)

    def drain(at, _):
        for d in range(2):
            message(slots_d, send_d, recv_d, d, at).wait_send()
            message(slots_u, send_u, recv_u, d, at).wait_send()
            message(slots_q, send_q, recv_q, d, at).wait_send()
        small_message(at).wait_send()
        return 0

    lax.fori_loop(0, n - 1, drain, 0)

    @pl.when(first)
    def _():
        for i in range(row_count):
            for p in range(1, count):
                tok_part(i, p).wait_send()
            tok_own(i).wait()

    @pl.when(jnp.logical_not(first))
    def _():
        for i in range(row_count):
            tok_part(i, 1).wait_recv()


def run_grads(count, n, left, dproj, dbr, dup, ddn, g0, small):
    rows, seq, width = g0.shape
    ff = dup.shape[2]
    flat = lambda a: a.reshape(rows * seq, a.shape[2])
    tok = rows * seq
    shard, shard_ff = width // n, ff // n
    ops = [left] + [flat(a) for a in (ddn, dup, dproj, dbr)]
    vmem = pl.BlockSpec(memory_space=pltpu.VMEM)
    sem = pltpu.SemaphoreType.DMA
    return pl.pallas_call(
        lambda *refs: grad_kernel(count, n, *refs),
        in_specs=[ANYWHERE] * 5 + [vmem, ANYWHERE],
        out_specs=[vmem] * 5 + [ANYWHERE],
        out_shape=[
            jax.ShapeDtypeStruct((shard, 3 * width), F32),
            jax.ShapeDtypeStruct((shard, width), F32),
            jax.ShapeDtypeStruct((shard, ff), F32),
            jax.ShapeDtypeStruct((shard_ff, width), F32),
            jax.ShapeDtypeStruct((16, 128), F32),
            jax.ShapeDtypeStruct((rows, seq // count, width), BF16),
        ],
        scratch_shapes=[
            pltpu.VMEM((2, n, shard_ff, width // 2), BF16),
            pltpu.VMEM((2, n, shard, ff // 2), BF16),
            pltpu.VMEM((2, n, shard, 2 * width), BF16),
            pltpu.VMEM((n, 16, 128), F32),
            pltpu.VMEM((2, shard_ff, tok), BF16),
            pltpu.VMEM((5, 2 * shard, tok), BF16),
            pltpu.VMEM((tok, width), BF16),
            pltpu.VMEM((tok, ff), BF16),
            pltpu.VMEM((tok, 4 * width), BF16),
            pltpu.VMEM((2, shard, ff // 2), F32),
            pltpu.VMEM((2, shard, 2 * width), F32),
            sem((2,)), sem((3, 2, 2)), sem((4,)),
            sem((2, n)), sem((2, n)), sem((2, n)), sem((2, n)), sem((2, n)), sem((2, n)),
            sem((n,)), sem((n,)), sem((rows, count)), sem((rows,)),
        ],
        compiler_params=pltpu.CompilerParams(
            collective_id=2, has_side_effects=True, vmem_limit_bytes=VMEM_LIMIT,
        ),
        cost_estimate=pl.CostEstimate(
            flops=2 * tok * (4 * width * width + 2 * width * ff), bytes_accessed=tok * 25000, transcendentals=0,
        ),
    )(*ops, small, g0)


def place_kernel(*refs):
    larges, small, outs, smalls = refs[:6], refs[6], refs[7:13], refs[13:]
    for source, out in zip(larges, outs):
        out[...] = source[...].reshape(out.shape)
    flat = jnp.concatenate([small[i : i + 1, :] for i in range(9)], 1)
    gain, shift, s_out, s_down, s_up, s_qv, top = smalls
    thin = gain.shape[2]
    at = 0
    for ref, index in ((gain, 0), (gain, 1), (shift, 0), (shift, 1)):
        ref[0, index : index + 1, :] = flat[:, at : at + thin]
        at += thin
    for ref in (s_out, s_down, s_up, s_qv):
        ref[...] = flat[:, at : at + ref.shape[1]]
        at += ref.shape[1]
    top[...] = small[9:10, 0:4]


def place(n, larges, small, width, ff):
    thin = width // n
    shapes = [jax.ShapeDtypeStruct(v.shape, v.dtype) for v in larges[:2]]
    shapes += [jax.ShapeDtypeStruct((1, *v.shape), v.dtype) for v in larges[2:]]
    smalls = [(1, 2, thin), (1, 2, thin), (1, thin), (1, thin), (1, ff // n), (1, 2 * thin), (1, 4)]
    vmem = pl.BlockSpec(memory_space=pltpu.VMEM)
    return pl.pallas_call(
        place_kernel,
        in_specs=[vmem] * 7,
        out_specs=[vmem] * 13,
        out_shape=shapes + [jax.ShapeDtypeStruct(s, F32) for s in smalls],
        compiler_params=pltpu.CompilerParams(vmem_limit_bytes=VMEM_LIMIT),
    )(*larges, small)


def weight_grad(left, right):
    g = jnp.einsum("rsd,rse->de", left, right, preferred_element_type=F32).astype(BF16)
    return lax.psum_scatter(g, "dp", scatter_dimension=0, tiled=True).astype(F32)


def share_pieces(whole_rows, count, stage):
    piece = whole_rows.shape[1] // count
    mine = whole_rows[:, :piece]
    for p in range(1, count):
        got = lax.ppermute(whole_rows[:, p * piece : (p + 1) * piece], "pipe", [(0, p)])
        mine = jnp.where(stage == p, got, mine)
    return mine


def shards(
    tokens, lengths, ema_scales, w_qkv, bias_qv, w_out, bias_out, w_up, bias_up, w_down, bias_down,
    ln_gain, ln_bias, cotangent,
):
    count = lax.axis_size("pipe")
    n = lax.axis_size("dp")
    width = tokens.shape[2]
    ff = w_up.shape[2]
    b_qkv = jnp.concatenate([bias_qv[:, :width], jnp.zeros_like(bias_qv[:, :width]), bias_qv[:, width:]], 1)
    weights = (
        w_qkv[0], b_qkv, w_out[0], bias_out, w_up[0], bias_up, w_down[0], bias_down, ln_gain[0], ln_bias[0],
    )
    *kept, mixed, peaks = run_forward(count, tokens, lengths, ema_scales, weights)
    left = kept[-2]
    dproj, dbr, dup, ddn, g0, turned, small = run_backward(
        count, cotangent, lengths, ema_scales, weights, kept
    )
    sums = jnp.sum(small, 0)
    parts, at = [], 0
    for size in (width, width, width, width, width, width, ff, width, width, width):
        parts.append(sums[at : at + size])
        at += size
    parts[7:] = [jnp.concatenate([parts[7], parts[9]])]
    packed = jnp.concatenate([v.reshape(n, -1) for v in parts], 1)
    peak = jnp.max(peaks, (1, 2))
    sums_width = packed.shape[1]
    if n >= 4 and n % 2 == 0 and width // n % 16 == 0 and ff // n % 128 == 0 and sums_width == 9 * 128:
        top = jnp.broadcast_to(jnp.pad(peak, (0, 124))[None, None], (n, 7, 128))
        with_peak = jnp.concatenate([packed.reshape(n, 9, 128), top], 1)
        g_qkv, g_out, g_up, g_down, small_sum, grad_tokens = run_grads(
            count, n, turned, dproj, dbr, dup, ddn, g0, with_peak
        )
        larges = (mixed, grad_tokens, g_qkv, g_out, g_up, g_down)
        placed = place(n, larges, small_sum, width, ff)
        mixed, grad_tokens, g_qkv, g_out, g_up, g_down, g_gain, g_shift, s_out, s_down, s_up, s_qv, top = placed
        return (
            mixed, grad_tokens, g_qkv, s_qv, g_out, s_out, g_up, s_up, g_down, s_down, g_gain, g_shift, top,
        )
    else:
        g_down = weight_grad(left[:, :, :ff], ddn)
        g_up = weight_grad(left[:, :, ff : ff + width], dup)
        g_qkv = weight_grad(left[:, :, ff + width : ff + 2 * width], dproj)
        g_out = weight_grad(left[:, :, ff + 2 * width :], dbr)
        mine = lax.psum_scatter(packed, "dp", scatter_dimension=0, tiled=True)
        batch_max = lax.pmax(peak, "dp")[None]
        grad_tokens = share_pieces(g0, count, lax.axis_index("pipe"))
    outs, at = [], 0
    for size in (width, width, width, width, width, width, ff, 2 * width):
        outs.append(mine[:, at : at + size // n])
        at += size // n
    gain0, gain1, shift0, shift1, s_out, s_down, s_up, s_qv = outs
    g_gain = jnp.stack([gain0, gain1], 1)
    g_shift = jnp.stack([shift0, shift1], 1)
    return (
        mixed, grad_tokens, g_qkv[None], s_qv, g_out[None], s_out, g_up[None], s_up, g_down[None], s_down,
        g_gain, g_shift, batch_max,
    )


def solution(mesh):
    return jax.shard_map(
        shards,
        mesh=mesh,
        in_specs=(
            P("dp", None, None), P("dp"), P("pipe", None), P("pipe", None, None), P("pipe", None),
            P("pipe", None, None), P("pipe", None), P("pipe", None, None), P("pipe", None),
            P("pipe", None, None), P("pipe", None), P("pipe", None, None), P("pipe", None, None),
            P("dp", None, None),
        ),
        out_specs=(
            P("dp", "pipe", None), P("dp", "pipe", None), P("pipe", "dp", None), P("pipe", "dp"),
            P("pipe", "dp", None), P("pipe", "dp"), P("pipe", "dp", None), P("pipe", "dp"),
            P("pipe", "dp", None), P("pipe", "dp"), P("pipe", None, "dp"), P("pipe", None, "dp"),
            P("pipe", None),
        ),
        check_vma=False,
    )
```

```python
import jax
import jax.numpy as jnp
from jax import lax
from jax.experimental import pallas as pl
from jax.experimental.pallas import tpu as pltpu
from jax.sharding import PartitionSpec as P

HEAD_DIM = 64
PAIR = 2 * HEAD_DIM
EPS = 1e-06
MASKED = -1000000000.0
CHUNK = 512
PIECE = 256
BLOCK = 16
OPS = 64
LOGICAL = pl.DeviceIdType.MESH
F32 = jnp.float32
BF16 = jnp.bfloat16

ERF_POLY = (
    0.7978823511659165,
    0.03634481045269742,
    -4.5110171354091134e-05,
    -5.02654469142584e-05,
    3.0867937984305273e-06,
    -6.60140005994544e-08,
)
ERF_CLAMP = 5.2 * 5.2
HALF_LOG2E = -0.7213475204444817
LOG2_TWICE_DENSITY = -0.3257480647361593


def dot_nn(a, b):
    return jnp.dot(a, b, preferred_element_type=F32)


def dot_nt(a, b):
    return lax.dot_general(a, b, (((1,), (1,)), ((), ())), preferred_element_type=F32)


def dot_tn(a, b):
    return lax.dot_general(a, b, (((0,), (0,)), ((), ())), preferred_element_type=F32)


def fold_rows(v):
    return jnp.sum(v.reshape(v.shape[0] // 8, 8, v.shape[1]), 0)


def peak_rows(v):
    tiles = [v[:, i : i + 128] for i in range(0, v.shape[1], 128)]
    top = tiles[0]
    for tile in tiles[1:]:
        top = jnp.maximum(top, tile)
    return jnp.max(top.reshape(v.shape[0] // 8, 8, 128), 0)


def greet(stage, count):
    barrier = pltpu.get_barrier_semaphore()
    for step in range(1, count):
        peer = lax.rem(stage + step, count)
        pl.semaphore_signal(barrier, inc=1, device_id={"pipe": peer}, device_id_type=LOGICAL)
    pl.semaphore_wait(barrier, count - 1)


def activation(u, ceiling, inv_ceiling):
    square = u * u
    w = jnp.minimum(square, ERF_CLAMP)
    poly = w * ERF_POLY[-1] + ERF_POLY[-2]
    for coef in ERF_POLY[-3::-1]:
        poly = poly * w + coef
    twice_cdf = 1.0 + jnp.tanh(u * poly)
    act = (0.5 * u) * twice_cdf
    ratio = jnp.tanh(act * inv_ceiling)
    twice_density = jnp.exp2(square * HALF_LOG2E + LOG2_TWICE_DENSITY)
    twice_slope = (1.0 - ratio * ratio) * (twice_cdf + u * twice_density)
    return act, ceiling * ratio, twice_slope


def fwd_kernel(count, *refs):
    (
        lens, scales, tokens, h_qkv, h_out, h_up, h_down, b_qkv, b_out, b_up, b_down, gain, shift,
        x_o, qkv_o, inv_o, ctx_o, n1_o, rs1_o, sl_o, n2_o, rs2_o, left_o, exp_o,
        mixed_o, peaks_o,
        w_qkv, w_out, w_up, w_down, w_sem,
        xin, xout, qkv_s, inv_s, ctx_s, n1_s, rs1_s, sl_s, n2_s, rs2_s, aq_s, hq_s, xq_s, cq_s,
        acc, hid, up_s, ops_s, s_s, e_s, o_s, amax_s,
        save_sem, in_sem, send_sem, recv_sem, mix_send, mix_recv,
    ) = refs
    r = pl.program_id(0)
    rows = pl.num_programs(0)
    row_count = tokens.shape[0]
    seq, width = tokens.shape[1], tokens.shape[2]
    ff = w_up.shape[1]
    piece = seq // count
    stage = lax.axis_index("pipe")
    first = stage == 0
    last = stage == count - 1

    left = {"aq": (0, ff), "hq": (ff, width), "xq": (ff + width, width), "cq": (ff + 2 * width, width)}
    staged = {
        "x": (xin.at[r], x_o), "qkv": (qkv_s, qkv_o), "inv": (inv_s, inv_o), "ctx": (ctx_s, ctx_o),
        "n1": (n1_s, n1_o), "rs1": (rs1_s, rs1_o), "sl": (sl_s, sl_o), "n2": (n2_s, n2_o),
        "rs2": (rs2_s, rs2_o), "aq": (aq_s, left_o), "hq": (hq_s, left_o), "xq": (xq_s, left_o),
        "cq": (cq_s, left_o), "exp": (e_s, exp_o),
    }
    order = list(staged)
    early = ("x", "xq", "qkv", "inv", "ctx", "cq", "exp")
    late = ("n1", "rs1", "hq", "aq", "sl", "n2", "rs2")
    fetches = [(h_qkv, w_qkv), (h_out, w_out), (h_up, w_up), (h_down, w_down)]

    def weight_copy(k):
        return pltpu.make_async_copy(fetches[k][0], fetches[k][1], w_sem.at[k])

    def save_copy(name):
        src, dst = staged[name]
        dst = dst.at[r]
        if name in left:
            dst = dst.at[:, pl.ds(*left[name])]
        return pltpu.make_async_copy(src, dst, save_sem.at[order.index(name)])

    def token_copy(i):
        return pltpu.make_async_copy(tokens.at[i], xin.at[i], in_sem.at[i])

    def hop(i):
        return pltpu.make_async_remote_copy(
            src_ref=xout.at[i], dst_ref=xin.at[i], send_sem=send_sem.at[i], recv_sem=recv_sem.at[i],
            device_id={"pipe": lax.rem(stage + 1, count)}, device_id_type=LOGICAL,
        )

    def mix_part(i, p):
        return pltpu.make_async_remote_copy(
            src_ref=xout.at[i, pl.ds(p * piece, piece)], dst_ref=mixed_o.at[i],
            send_sem=mix_send.at[i, p], recv_sem=mix_recv.at[i],
            device_id={"pipe": jnp.int32(p)}, device_id_type=LOGICAL,
        )

    def mix_own(i):
        return pltpu.make_async_copy(
            xout.at[i, pl.ds((count - 1) * piece, piece)], mixed_o.at[i], mix_send.at[i, count - 1]
        )

    @pl.when(r == 0)
    def _():
        greet(stage, count)
        peaks_o[...] = jnp.zeros_like(peaks_o)
        for k in range(4):
            weight_copy(k).start()

        @pl.when(first)
        def _():
            for i in range(row_count):
                token_copy(i).start()

    @pl.when(first)
    def _():
        token_copy(r).wait()

    @pl.when(jnp.logical_not(first))
    def _():
        hop(r).wait_recv()

    length = lens[r]
    m0, m1, m2, m3 = scales[0, 0], scales[0, 1], scales[0, 2], scales[0, 3]
    i0, i1, i2, i3 = 1.0 / m0, 1.0 / m1, 1.0 / m2, 1.0 / m3

    def row_mask(start, size):
        return (start + lax.broadcasted_iota(jnp.int32, (size, 1), 0)) < length

    def blocks(size, body, init=0, begin=0, end=seq):
        step = lambda i, c: body(i * size, pl.ds(i * size, size), c)
        return lax.fori_loop(begin // size, end // size, step, init, unroll=True)

    def weave(dots, size, body, init=0):
        total, cut = seq // size, 0
        for k, dot in enumerate(dots):
            dot()
            begin, cut = cut, total * (k + 1) // len(dots)
            init = blocks(size, body, init, begin * size, cut * size)
        return init

    no_peak = jnp.zeros((8, 128), F32)

    @pl.when(r > 0)
    def _():
        for name in early:
            save_copy(name).wait()

    @pl.when(r == 0)
    def _():
        weight_copy(0).wait()

    def quant_in(start, at, top):
        x = xin[r, at, :].astype(F32)
        xq_s[at, :] = (m0 * jnp.tanh(x * i0)).astype(BF16)
        return jnp.maximum(top, masked_peak(x, start))

    def masked_peak(v, start):
        return peak_rows(jnp.where(row_mask(start, v.shape[0]), jnp.abs(v), 0.0))

    peaks_o[0] = jnp.maximum(peaks_o[0], blocks(BLOCK, quant_in, no_peak))
    def project(g):
        def piece_of(part):
            def run():
                cols = slice(part * width + g * PIECE, part * width + (g + 1) * PIECE)
                proj = dot_nn(xq_s[...], w_qkv[:, cols]) + b_qkv[:, cols]
                qkv_s[:, cols] = proj.astype(BF16)

            return run

        return [piece_of(part) for part in range(3)]

    one = jnp.ones((), BF16)
    zero = jnp.zeros((), BF16)
    head_scale = jnp.asarray(HEAD_DIM ** -0.5, BF16)

    def prepare(p):
        slot = p % 2

        def body(start, at, c):
            lane = lax.broadcasted_iota(jnp.int32, (OPS, PAIR), 1)
            lo = lane < HEAD_DIM
            spot = jnp.where(lo, lane, lane - HEAD_DIM)
            bias = jnp.where(row_mask(start, OPS), 0.0, MASKED)
            extra = jnp.where(spot == 0, jnp.broadcast_to(bias, (OPS, PAIR)), 0.0).astype(BF16)
            q2 = qkv_s[at, p * PAIR : (p + 1) * PAIR] * head_scale
            k2 = qkv_s[at, width + p * PAIR : width + (p + 1) * PAIR]
            v2 = qkv_s[at, 2 * width + p * PAIR : 2 * width + (p + 1) * PAIR]
            ops_s[slot, 0, at, :] = jnp.where(lo, q2, one)
            ops_s[slot, 1, at, :] = jnp.where(lo, one, q2)
            ops_s[slot, 2, at, :] = jnp.where(lo, k2, extra)
            ops_s[slot, 3, at, :] = jnp.where(lo, extra, k2)
            ops_s[slot, 4, at, :] = jnp.where(lo, v2, one)
            ops_s[slot, 5, at, :] = jnp.where(lo, one, v2)
            return c

        blocks(OPS, body)

    def scores(h):
        p, side = h // 2, h % 2

        def piece_of(k):
            def run():
                keys = pl.ds(k * PIECE, PIECE)
                s_s[side, :, keys] = dot_nt(ops_s[p % 2, side], ops_s[p % 2, 2 + side, keys, :])

            return run

        return [piece_of(k) for k in range(seq // PIECE)]

    def soften(h):
        def body(start, at, c):
            s = s_s[h % 2, at, :]
            e_s[h, at, :] = jnp.exp(s - jnp.max(s, -1, keepdims=True)).astype(BF16)
            return c

        return body

    def collect(h):
        p, side = h // 2, h % 2

        def piece_of(k):
            def run():
                queries = pl.ds(k * PIECE, PIECE)
                o_s[side, queries, :] = dot_nn(e_s[h, queries, :], ops_s[p % 2, 4 + side])

            return run

        return [piece_of(k) for k in range(seq // PIECE)]

    def settle(p, peak):
        cols = slice(p * PAIR, (p + 1) * PAIR)

        def body(start, at, top):
            lo = lax.broadcasted_iota(jnp.int32, (OPS, PAIR), 1) < HEAD_DIM
            o_a, o_b = o_s[0, at, :], o_s[1, at, :]
            total = pltpu.roll(jnp.where(lo, o_b, o_a), HEAD_DIM, 1)
            inverse = 1.0 / total
            c = jnp.where(lo, o_a, o_b) * inverse
            inv_s[at, cols] = inverse
            ctx_s[at, cols] = c
            cq_s[at, cols] = (m1 * jnp.tanh(c * i1)).astype(BF16)
            return jnp.maximum(top, masked_peak(c, start))

        return blocks(OPS, body, peak)

    heads = 2 * (width // PAIR)
    groups = width // PIECE
    span = heads // groups
    peak = no_peak
    for dot in project(0):
        dot()
    prepare(0)
    for dot in scores(0):
        dot()
    for h in range(heads):
        g, turn = h // span, h % span
        dots = []
        if h + 1 < heads:
            if (h + 1) % 2 == 0:
                prepare((h + 1) // 2)
            dots += scores(h + 1)
        if h > 0:
            dots += collect(h - 1)
        if g + 1 < groups and turn < 3:
            dots.append(project(g + 1)[turn])
        weave(dots, BLOCK, soften(h))
        if h > 0 and h % 2 == 0:
            peak = settle(h // 2 - 1, peak)
    for dot in collect(heads - 1):
        dot()
    peak = settle(heads // 2 - 1, peak)
    peaks_o[1] = jnp.maximum(peaks_o[1], peak)

    for name in early:
        save_copy(name).start()

    @pl.when(r > 0)
    def _():
        for name in late:
            save_copy(name).wait()

    @pl.when(r == 0)
    def _():
        for k in (1, 2, 3):
            weight_copy(k).wait()

    def out_piece(k):
        def run():
            at = pl.ds(k * PIECE, PIECE)
            acc[at, :] = dot_nn(cq_s[at, :], w_out[...])

        return run

    def norm_one(start, at, top):
        s = xin[r, at, :].astype(F32) + (acc[at, :] + b_out[...])
        center = s - jnp.mean(s, -1, keepdims=True)
        rs = lax.rsqrt(jnp.mean(center * center, -1, keepdims=True) + EPS)
        n = center * rs
        h = n * gain[0:1, :] + shift[0:1, :]
        n1_s[at, :] = n.astype(BF16)
        rs1_s[at, :] = jnp.broadcast_to(rs, (BLOCK, 128))
        hid[at, :] = h
        hq_s[at, :] = (m2 * jnp.tanh(h * i2)).astype(BF16)
        return jnp.maximum(top, masked_peak(h, start))

    out_piece(0)()
    top = weave([out_piece(k) for k in range(1, seq // PIECE)] + [lambda: None], BLOCK, norm_one, no_peak)
    peaks_o[2] = jnp.maximum(peaks_o[2], top)

    chunks = ff // CHUNK

    def up_chunk(c):
        def piece_of(k):
            def run():
                part = dot_nn(hq_s[...], w_up[:, pl.ds(c * CHUNK + k * PIECE, PIECE)])
                up_s[c % 2, :, pl.ds(k * PIECE, PIECE)] = part

            return run

        return [piece_of(k) for k in range(CHUNK // PIECE)]

    def act_chunk(c):
        cols = pl.ds(c * CHUNK, CHUNK)

        def body(start, at, carry):
            act, low, slope = activation(up_s[c % 2, at, :] + b_up[:, cols], m3, i3)
            aq_s[at, cols] = low.astype(BF16)
            sl_s[at, cols] = slope.astype(BF16)
            size = jnp.abs(act)
            top = size[:, 0:128]
            for i in range(128, CHUNK, 128):
                top = jnp.maximum(top, size[:, i : i + 128])
            amax_s[at, :] = top if c == 0 else jnp.maximum(amax_s[at, :], top)
            return carry

        return body

    def down_chunk(c):
        def piece_of(k):
            def run():
                cols = pl.ds(k * PIECE, PIECE)
                part = dot_nn(aq_s[:, pl.ds(c * CHUNK, CHUNK)], w_down[pl.ds(c * CHUNK, CHUNK), cols])
                acc[:, cols] = part if c == 0 else acc[:, cols] + part

            return run

        return [piece_of(k) for k in range(width // PIECE)]

    for dot in up_chunk(0):
        dot()
    for c in range(chunks):
        dots = []
        if c + 1 < chunks:
            dots += up_chunk(c + 1)
        if c > 0:
            dots += down_chunk(c - 1)
        weave(dots, BLOCK, act_chunk(c))
    peaks_o[3] = jnp.maximum(peaks_o[3], masked_peak(amax_s[...], 0))

    def norm_two(start, at, c):
        s = hid[at, :] + (acc[at, :] + b_down[...])
        center = s - jnp.mean(s, -1, keepdims=True)
        rs = lax.rsqrt(jnp.mean(center * center, -1, keepdims=True) + EPS)
        n = center * rs
        n2_s[at, :] = n.astype(BF16)
        rs2_s[at, :] = jnp.broadcast_to(rs, (BLOCK, 128))
        xout[r, at, :] = (n * gain[1:2, :] + shift[1:2, :]).astype(BF16)
        return c

    def down_last(k):
        def run():
            at, cols = pl.ds(k * PIECE, PIECE), pl.ds((chunks - 1) * CHUNK, CHUNK)
            acc[at, :] += dot_nn(aq_s[at, cols], w_down[cols, :])

        return run

    down_last(0)()
    weave([down_last(k) for k in range(1, seq // PIECE)] + [lambda: None], BLOCK, norm_two)
    for name in late:
        save_copy(name).start()

    @pl.when(jnp.logical_not(last))
    def _():
        hop(r).start()

    @pl.when(last)
    def _():
        for p in range(count - 1):
            mix_part(r, p).start()
        mix_own(r).start()

    @pl.when(r == rows - 1)
    def _():
        for name in order:
            save_copy(name).wait()

        @pl.when(jnp.logical_not(last))
        def _():
            for i in range(row_count):
                hop(i).wait_send()
            for i in range(row_count):
                mix_part(i, 0).wait_recv()

        @pl.when(last)
        def _():
            for i in range(row_count):
                for p in range(count - 1):
                    mix_part(i, p).wait_send()
                mix_own(i).wait()


def bwd_kernel(count, *refs):
    (
        lens, scales, seeds, h_qkv, h_out, h_up, h_down, gain, shift, left_i,
        x_i, qkv_i, inv_i, ctx_i, n1_i, rs1_i, sl_i, n2_i, rs2_i, exp_i,
        dproj_o, dbr_o, dup_o, ddn_o, gtok_o, left_o, small_o,
        w_qkv, w_out, w_up, w_down, w_sem, turn_in, turn_out, turn_in_sem, turn_out_sem,
        gin, x_s, qkv_s, inv_s, ctx_s, n1_s, rs1_s, sl_s, n2_s, rs2_s, e_s,
        dproj_s, dbr_s, dup_s, ddn_s, dctx_s, acc, dr,
        up_s, ops_s, g_s, ds_s, gv_s, gk_s, gq_s, q_t, do_t, inner_s,
        load_sem, save_sem, in_sem, send_sem, recv_sem, tok_send,
    ) = refs
    r = pl.program_id(0)
    rows = pl.num_programs(0)
    row_count = seeds.shape[0]
    seq, width = seeds.shape[1], seeds.shape[2]
    ff = w_up.shape[1]
    piece = seq // count
    stage = lax.axis_index("pipe")
    first = stage == 0
    last = stage == count - 1

    loaded = {
        "n2": (n2_i, n2_s), "rs2": (rs2_i, rs2_s), "sl": (sl_i, sl_s), "n1": (n1_i, n1_s),
        "rs1": (rs1_i, rs1_s), "ctx": (ctx_i, ctx_s), "qkv": (qkv_i, qkv_s), "inv": (inv_i, inv_s),
        "x": (x_i, x_s), "exp": (exp_i, e_s),
    }
    load_order = list(loaded)
    early = ("n2", "rs2", "sl", "n1", "rs1")
    late = ("ctx", "qkv", "inv", "exp", "x")
    staged = {
        "ddn": (ddn_s, ddn_o), "dup": (dup_s, dup_o), "dbr": (dbr_s, dbr_o), "dproj": (dproj_s, dproj_o),
    }
    save_order = list(staged)

    def load_copy(name, i):
        src, dst = loaded[name]
        return pltpu.make_async_copy(src.at[i], dst, load_sem.at[load_order.index(name)])

    def save_copy(name):
        src, dst = staged[name]
        return pltpu.make_async_copy(src, dst.at[r], save_sem.at[save_order.index(name)])

    def seed_copy(i):
        return pltpu.make_async_copy(seeds.at[i], gin.at[i], in_sem.at[i])

    def hop(i):
        return pltpu.make_async_remote_copy(
            src_ref=gin.at[i], dst_ref=gin.at[i], send_sem=send_sem.at[i], recv_sem=recv_sem.at[i],
            device_id={"pipe": lax.rem(stage + count - 1, count)}, device_id_type=LOGICAL,
        )

    def tok_copy(i):
        return pltpu.make_async_copy(gin.at[i], gtok_o.at[i], tok_send.at[i])

    fetches = [(h_down, w_down), (h_up, w_up), (h_out, w_out), (h_qkv, w_qkv)]

    def weight_copy(k):
        return pltpu.make_async_copy(fetches[k][0], fetches[k][1], w_sem.at[k])

    parts = left_i.shape[2] // width
    turns = row_count * parts

    def turn_load(i):
        cols = pl.ds(pl.multiple_of(i % parts * width, 128), width)
        return pltpu.make_async_copy(left_i.at[i // parts, :, cols], turn_in.at[i % 2], turn_in_sem.at[i % 2])

    def turn_store(i):
        rows_at = pl.ds(pl.multiple_of(i % parts * width, 128), width)
        cols = pl.ds(pl.multiple_of(i // parts * seq, 128), seq)
        return pltpu.make_async_copy(turn_out.at[i % 2], left_o.at[rows_at, cols], turn_out_sem.at[i % 2])

    def turn_left():
        turn_load(0).start()

        def body(i, c):
            @pl.when(i + 1 < turns)
            def _():
                turn_load(i + 1).start()

            turn_load(i).wait()

            @pl.when(i >= 2)
            def _():
                turn_store(i - 2).wait()

            turn_out[i % 2] = turn_in[i % 2].T
            turn_store(i).start()
            return c

        lax.fori_loop(0, turns, body, 0)
        turn_store(turns - 2).wait()
        turn_store(turns - 1).wait()

    @pl.when(r == 0)
    def _():
        greet(stage, count)
        small_o[...] = jnp.zeros_like(small_o)

        @pl.when(last)
        def _():
            for i in range(row_count):
                seed_copy(i).start()

        for name in ("n2", "rs2"):
            load_copy(name, 0).start()
        weight_copy(0).start()
        for name in early[2:]:
            load_copy(name, 0).start()
        for k in (1, 2, 3):
            weight_copy(k).start()
        for name in late:
            load_copy(name, 0).start()

        @pl.when(stage < count - 2)
        def _():
            turn_left()

    @pl.when(last)
    def _():
        seed_copy(r).wait()

    @pl.when(jnp.logical_not(last))
    def _():
        hop(r).wait_recv()

    length = lens[r]
    m0, m1, m2 = scales[0, 0], scales[0, 1], scales[0, 2]
    i0, i1, i2 = 1.0 / m0, 1.0 / m1, 1.0 / m2

    offsets = {}
    at_col = 0
    for name, size in (
        ("gain0", width), ("gain1", width), ("shift0", width), ("shift1", width),
        ("out", width), ("down", width), ("up", ff), ("qkv", 3 * width),
    ):
        offsets[name] = at_col
        at_col += size

    def blocks(size, body, init=0, begin=0, end=seq):
        step = lambda i, c: body(i * size, pl.ds(i * size, size), c)
        return lax.fori_loop(begin // size, end // size, step, init, unroll=True)

    def weave(dots, size, body, init=0):
        total, cut = seq // size, 0
        for k, dot in enumerate(dots):
            dot()
            begin, cut = cut, total * (k + 1) // len(dots)
            init = blocks(size, body, init, begin * size, cut * size)
        return init

    def row_mask(start, size):
        return (start + lax.broadcasted_iota(jnp.int32, (size, 1), 0)) < length

    def put_small(name, v, col=0):
        small_o[:, pl.ds(offsets[name] + col, v.shape[1])] += v

    no_sum = jnp.zeros((8, width), F32)

    for name in early:
        load_copy(name, r).wait()

    @pl.when(r > 0)
    def _():
        for name in ("ddn", "dup", "dbr"):
            save_copy(name).wait()

    @pl.when(r == 0)
    def _():
        for k in (0, 1):
            weight_copy(k).wait()

    def norm_two(start, at, sums):
        dy = jnp.where(row_mask(start, BLOCK), gin[r, at, :].astype(F32), 0.0)
        n = n2_s[at, :].astype(F32)
        e = dy * gain[1:2, :]
        mean_e = jnp.mean(e, -1, keepdims=True)
        mean_en = jnp.mean(e * n, -1, keepdims=True)
        d = (e - mean_e - n * mean_en) * rs2_s[at, 0:1]
        dr[at, :] = d
        ddn_s[at, :] = d.astype(BF16)
        return sums[0] + fold_rows(dy * n), sums[1] + fold_rows(dy), sums[2] + fold_rows(d)

    for name, v in zip(("gain1", "shift1", "down"), blocks(BLOCK, norm_two, (no_sum,) * 3)):
        put_small(name, v)

    chunks = ff // CHUNK

    def dact_chunk(c):
        def piece_of(k):
            def run():
                at = pl.ds(c * CHUNK + k * PIECE, PIECE)
                up_s[c % 2, :, pl.ds(k * PIECE, PIECE)] = dot_nt(ddn_s[...], w_down[at, :])

            return run

        return [piece_of(k) for k in range(CHUNK // PIECE)]

    def slope_chunk(c):
        cols = pl.ds(c * CHUNK, CHUNK)

        def body(start, at, total):
            d = (0.5 * up_s[c % 2, at, :]) * sl_s[at, cols].astype(F32)
            dup_s[at, cols] = d.astype(BF16)
            return total + fold_rows(d)

        return body

    def dhid_chunk(c):
        cols = pl.ds(c * CHUNK, CHUNK)

        def piece_of(k):
            def run():
                at = pl.ds(k * PIECE, PIECE)
                part = dot_nt(dup_s[:, cols], w_up[at, cols])
                acc[:, at] = part if c == 0 else acc[:, at] + part

            return run

        return [piece_of(k) for k in range(width // PIECE)]

    for dot in dact_chunk(0):
        dot()
    for c in range(chunks):
        dots = []
        if c + 1 < chunks:
            dots += dact_chunk(c + 1)
        if c > 0:
            dots += dhid_chunk(c - 1)
        put_small("up", weave(dots, BLOCK, slope_chunk(c), jnp.zeros((8, CHUNK), F32)), c * CHUNK)

    def norm_one(start, at, sums):
        n = n1_s[at, :].astype(F32)
        t = jnp.tanh((n * gain[0:1, :] + shift[0:1, :]) * i2)
        dy = dr[at, :] + acc[at, :] * (1.0 - t * t)
        e = dy * gain[0:1, :]
        mean_e = jnp.mean(e, -1, keepdims=True)
        mean_en = jnp.mean(e * n, -1, keepdims=True)
        d = (e - mean_e - n * mean_en) * rs1_s[at, 0:1]
        dr[at, :] = d
        dbr_s[at, :] = d.astype(BF16)
        return sums[0] + fold_rows(dy * n), sums[1] + fold_rows(dy), sums[2] + fold_rows(d)

    def dhid_last(k):
        def run():
            at, cols = pl.ds(k * PIECE, PIECE), pl.ds((chunks - 1) * CHUNK, CHUNK)
            acc[at, :] += dot_nt(dup_s[at, cols], w_up[:, cols])

        return run

    dhid_last(0)()
    dots = [dhid_last(k) for k in range(1, seq // PIECE)] + [lambda: None]
    for name, v in zip(("gain0", "shift0", "out"), weave(dots, BLOCK, norm_one, (no_sum,) * 3)):
        put_small(name, v)

    for name in ("ddn", "dup", "dbr"):
        save_copy(name).start()

    @pl.when(r + 1 < rows)
    def _():
        for name in early:
            load_copy(name, r + 1).start()

    for name in late:
        load_copy(name, r).wait()

    @pl.when(r > 0)
    def _():
        save_copy("dproj").wait()

    @pl.when(r == 0)
    def _():
        for k in (2, 3):
            weight_copy(k).wait()

    def dctx_piece(g):
        def run():
            at = pl.ds(g * PIECE, PIECE)
            acc[:, at] = dot_nt(dbr_s[...], w_out[at, :])

        return run

    zero = jnp.zeros((), BF16)
    head_scale = jnp.asarray(HEAD_DIM ** -0.5, BF16)

    def prepare(p):
        slot = p % 2
        cols = slice(p * PAIR, (p + 1) * PAIR)

        def body(start, at, c):
            lo = lax.broadcasted_iota(jnp.int32, (OPS, PAIR), 1) < HEAD_DIM
            ctx = ctx_s[at, cols]
            t = jnp.tanh(ctx * i1)
            low = (acc[at, cols] * (1.0 - t * t) * inv_s[at, cols]).astype(BF16)
            dctx_s[slot, at, :] = low
            inner = low.astype(F32) * ctx
            whole_sum = jnp.sum(inner, -1, keepdims=True)
            lower = jnp.sum(jnp.where(lo, inner, 0.0), -1, keepdims=True)
            inner_s[slot, 0, at, :] = jnp.broadcast_to(lower, (OPS, PAIR))
            inner_s[slot, 1, at, :] = jnp.broadcast_to(whole_sum - lower, (OPS, PAIR))
            v2 = qkv_s[at, 2 * width + p * PAIR : 2 * width + (p + 1) * PAIR]
            ops_s[slot, 0, at, :] = jnp.where(lo, v2, zero)
            ops_s[slot, 1, at, :] = jnp.where(lo, zero, v2)
            return c

        blocks(OPS, body)
        q_t[slot] = (qkv_s[:, cols] * head_scale).T
        do_t[slot] = dctx_s[slot].T

    def scores(h):
        slot, side = h // 2 % 2, h % 2

        def piece_of(k):
            def run():
                keys = pl.ds(k * PIECE, PIECE)
                g_s[side, :, keys] = dot_nt(dctx_s[slot], ops_s[slot, side, keys, :])

            return run

        return [piece_of(k) for k in range(seq // PIECE)]

    def soften(h):
        slot, side = h // 2 % 2, h % 2

        def body(start, at, c):
            inner = jnp.concatenate([inner_s[slot, side, at, :]] * (seq // PAIR), 1)
            ds_s[side, at, :] = (e_s[h, at, :].astype(F32) * (g_s[side, at, :] - inner)).astype(BF16)
            return c

        return body

    def collect(h):
        slot, side = h // 2 % 2, h % 2
        rows_at = slice(side * HEAD_DIM, (side + 1) * HEAD_DIM)

        def grad_v(k):
            def run():
                keys = pl.ds(k * PIECE, PIECE)
                gv_s[rows_at, keys] = dot_nn(do_t[slot, rows_at, :], e_s[h, :, keys])

            return run

        def grad_k(k):
            def run():
                keys = pl.ds(k * PIECE, PIECE)
                gk_s[rows_at, keys] = dot_nn(q_t[slot, rows_at, :], ds_s[side, :, keys])

            return run

        def grad_q(k):
            def run():
                queries = pl.ds(k * PIECE, PIECE)
                keys_low = qkv_s[:, width + h // 2 * PAIR : width + (h // 2 + 1) * PAIR]
                gq_s[side, queries, :] = dot_nn(ds_s[side, queries, :], keys_low)

            return run

        return [make(k) for make in (grad_v, grad_k, grad_q) for k in range(seq // PIECE)]

    def settle(p):
        def body(start, at, c):
            lo = lax.broadcasted_iota(jnp.int32, (OPS, PAIR), 1) < HEAD_DIM
            q = jnp.where(lo, gq_s[0, at, :], gq_s[1, at, :]) * (HEAD_DIM ** -0.5)
            dproj_s[at, p * PAIR : (p + 1) * PAIR] = q.astype(BF16)
            return c

        blocks(OPS, body)
        dproj_s[:, width + p * PAIR : width + (p + 1) * PAIR] = gk_s[...].astype(BF16).T
        dproj_s[:, 2 * width + p * PAIR : 2 * width + (p + 1) * PAIR] = gv_s[...].astype(BF16).T

    heads = 2 * (width // PAIR)
    groups = width // PIECE
    span = heads // groups
    dctx_piece(0)()
    prepare(0)
    for dot in scores(0):
        dot()
    for h in range(heads):
        g, turn = h // span, h % span
        dots = []
        if h + 1 < heads:
            if (h + 1) % 2 == 0:
                prepare((h + 1) // 2)
            dots += scores(h + 1)
        if h > 0:
            dots += collect(h - 1)
        if g + 1 < groups and turn == 0:
            dots.append(dctx_piece(g + 1))
        weave(dots, BLOCK, soften(h))
        if h > 0 and h % 2 == 0:
            settle(h // 2 - 1)
    for dot in collect(heads - 1):
        dot()
    settle(heads // 2 - 1)

    def dx_piece(k):
        def run():
            at = pl.ds(k * PIECE, PIECE)
            acc[:, at] = dot_nt(dproj_s[...], w_qkv[at, :])

        return run

    def quant_in(k):
        cols = pl.ds(k * PIECE, PIECE)
        values = pl.ds(2 * width + k * PIECE, PIECE)

        def body(start, at, sums):
            t = jnp.tanh(x_s[at, cols].astype(F32) * i0)
            gin[r, at, cols] = (dr[at, cols] + acc[at, cols] * (1.0 - t * t)).astype(BF16)
            return (
                sums[0] + fold_rows(dproj_s[at, cols].astype(F32)),
                sums[1] + fold_rows(dproj_s[at, values].astype(F32)),
            )

        return body

    dx_piece(0)()
    pieces = width // PIECE
    for k in range(pieces):
        dots = [dx_piece(k + 1)] if k + 1 < pieces else [lambda: None]
        sums = weave(dots, BLOCK, quant_in(k), (jnp.zeros((8, PIECE), F32),) * 2)
        put_small("qkv", sums[0], k * PIECE)
        put_small("qkv", sums[1], 2 * width + k * PIECE)
    save_copy("dproj").start()

    @pl.when(r + 1 < rows)
    def _():
        for name in late:
            load_copy(name, r + 1).start()

    @pl.when(jnp.logical_not(first))
    def _():
        hop(r).start()

    @pl.when(first)
    def _():
        tok_copy(r).start()

    @pl.when(r == rows - 1)
    def _():
        @pl.when(stage >= count - 2)
        def _():
            turn_left()

        for name in save_order:
            save_copy(name).wait()

        @pl.when(jnp.logical_not(first))
        def _():
            for i in range(row_count):
                hop(i).wait_send()

        @pl.when(first)
        def _():
            for i in range(row_count):
                tok_copy(i).wait()


def whole(a):
    return pl.BlockSpec(a.shape, lambda r, n=a.ndim: (0,) * n, pipeline_mode=pl.Buffered(1))


ANYWHERE = pl.BlockSpec(memory_space=pl.ANY)
SCALAR = pl.BlockSpec(memory_space=pltpu.SMEM)
VMEM_LIMIT = 60 * 1024 * 1024


def run_forward(count, tokens, lengths, scales, weights):
    w_qkv, b_qkv, w_out, b_out, w_up, b_up, w_down, b_down, gain, shift = weights
    rows, seq, width = tokens.shape
    ff = w_up.shape[1]
    big = lambda n, t: jax.ShapeDtypeStruct((rows, seq, n), t)
    saves = [
        (width, BF16), (3 * width, BF16), (width, F32), (width, F32), (width, BF16), (128, F32),
        (ff, BF16), (width, BF16), (128, F32),
    ]
    heads = width // HEAD_DIM
    lefts = [(ff, BF16), (width, BF16), (width, BF16), (width, BF16)]
    heavy = (w_qkv, w_out, w_up, w_down)
    dense = (b_qkv, b_out, b_up, b_down, gain, shift)
    tok = rows * seq
    return pl.pallas_call(
        lambda *refs: fwd_kernel(count, *refs),
        grid=(rows,),
        in_specs=[SCALAR, SCALAR, ANYWHERE] + [ANYWHERE] * 4 + [whole(a) for a in dense],
        out_specs=[ANYWHERE] * 12 + [pl.BlockSpec((4, 8, 128), lambda r: (0, 0, 0))],
        out_shape=[big(n, t) for n, t in saves]
        + [
            big(ff + 3 * width, BF16),
            jax.ShapeDtypeStruct((rows, heads, seq, seq), BF16),
            jax.ShapeDtypeStruct((rows, seq // count, width), BF16),
            jax.ShapeDtypeStruct((4, 8, 128), F32),
        ],
        scratch_shapes=[pltpu.VMEM(a.shape, a.dtype) for a in heavy]
        + [pltpu.SemaphoreType.DMA((4,))]
        + [pltpu.VMEM((rows, seq, width), BF16), pltpu.VMEM((rows, seq, width), BF16)]
        + [pltpu.VMEM((seq, n), t) for n, t in saves[1:] + lefts]
        + [
            pltpu.VMEM((seq, width), F32),
            pltpu.VMEM((seq, width), F32),
            pltpu.VMEM((2, seq, CHUNK), F32),
            pltpu.VMEM((2, 6, seq, PAIR), BF16),
            pltpu.VMEM((2, seq, seq), F32),
            pltpu.VMEM((heads, seq, seq), BF16),
            pltpu.VMEM((2, seq, PAIR), F32),
            pltpu.VMEM((seq, 128), F32),
            pltpu.SemaphoreType.DMA((14,)),
            pltpu.SemaphoreType.DMA((rows,)),
            pltpu.SemaphoreType.DMA((rows,)),
            pltpu.SemaphoreType.DMA((rows,)),
            pltpu.SemaphoreType.DMA((rows, count)),
            pltpu.SemaphoreType.DMA((rows,)),
        ],
        compiler_params=pltpu.CompilerParams(
            collective_id=0, has_side_effects=True, vmem_limit_bytes=VMEM_LIMIT,
            dimension_semantics=("arbitrary",),
        ),
        cost_estimate=pl.CostEstimate(
            flops=2 * tok * (4 * width * width + 2 * width * ff + 2 * seq * width),
            bytes_accessed=tok * 28000, transcendentals=tok * 3 * ff,
        ),
    )(lengths, scales, tokens, *heavy, *dense)


def run_backward(count, seeds, lengths, scales, weights, kept):
    w_qkv, b_qkv, w_out, b_out, w_up, b_up, w_down, b_down, gain, shift = weights
    *loads, left, exps = kept
    loads.append(exps)
    rows, seq, width = seeds.shape
    ff = w_up.shape[1]
    big = lambda n, t: jax.ShapeDtypeStruct((rows, seq, n), t)
    saves = [(3 * width, BF16), (width, BF16), (ff, BF16), (width, BF16)]
    heavy = (w_qkv, w_out, w_up, w_down)
    dense = (gain, shift)
    tok = rows * seq
    small = 6 * width + ff + 3 * width
    return pl.pallas_call(
        lambda *refs: bwd_kernel(count, *refs),
        grid=(rows,),
        in_specs=[SCALAR, SCALAR, ANYWHERE] + [ANYWHERE] * 4 + [whole(a) for a in dense] + [ANYWHERE] * 11,
        out_specs=[ANYWHERE] * 6 + [pl.BlockSpec((8, small), lambda r: (0, 0))],
        out_shape=[big(n, t) for n, t in saves]
        + [
            big(width, BF16), jax.ShapeDtypeStruct((left.shape[2], rows * seq), BF16),
            jax.ShapeDtypeStruct((8, small), F32),
        ],
        scratch_shapes=[pltpu.VMEM(a.shape, a.dtype) for a in heavy]
        + [
            pltpu.SemaphoreType.DMA((4,)),
            pltpu.VMEM((2, seq, width), BF16),
            pltpu.VMEM((2, width, seq), BF16),
            pltpu.SemaphoreType.DMA((2,)),
            pltpu.SemaphoreType.DMA((2,)),
        ]
        + [pltpu.VMEM((rows, seq, width), BF16)]
        + [pltpu.VMEM(a.shape[1:], a.dtype) for a in loads]
        + [pltpu.VMEM((seq, n), t) for n, t in saves]
        + [
            pltpu.VMEM((2, seq, PAIR), BF16),
            pltpu.VMEM((seq, width), F32),
            pltpu.VMEM((seq, width), F32),
            pltpu.VMEM((2, seq, CHUNK), F32),
            pltpu.VMEM((2, 2, seq, PAIR), BF16),
            pltpu.VMEM((2, seq, seq), F32),
            pltpu.VMEM((2, seq, seq), BF16),
            pltpu.VMEM((PAIR, seq), F32),
            pltpu.VMEM((PAIR, seq), F32),
            pltpu.VMEM((2, seq, PAIR), F32),
            pltpu.VMEM((2, PAIR, seq), BF16),
            pltpu.VMEM((2, PAIR, seq), BF16),
            pltpu.VMEM((2, 2, seq, PAIR), F32),
            pltpu.SemaphoreType.DMA((10,)),
            pltpu.SemaphoreType.DMA((4,)),
            pltpu.SemaphoreType.DMA((rows,)),
            pltpu.SemaphoreType.DMA((rows,)),
            pltpu.SemaphoreType.DMA((rows,)),
            pltpu.SemaphoreType.DMA((rows,)),
        ],
        compiler_params=pltpu.CompilerParams(
            collective_id=1, has_side_effects=True, vmem_limit_bytes=VMEM_LIMIT,
            dimension_semantics=("arbitrary",),
        ),
        cost_estimate=pl.CostEstimate(
            flops=2 * tok * (4 * width * width + 2 * width * ff + 5 * seq * width),
            bytes_accessed=tok * 28000, transcendentals=tok * ff,
        ),
    )(lengths, scales, seeds, *heavy, *dense, left, *loads)


def ring_to_dp(pos, n):
    return jnp.where(pos < n // 2, 2 * pos, 2 * (n - pos) - 1)


def dp_to_ring(j, n):
    return jnp.where(j % 2 == 0, j // 2, n - 1 - j // 2)


def grad_kernel(count, n, *refs):
    (
        left, ddn, dup, dproj, dbr, small, g0,
        gq_o, go_o, gu_o, gd_o, small_o, gtok_o,
        slots_d, slots_u, slots_q, slots_s, wide_v, thin_v, ddn_v, dup_v, dpo_v, mine_u, mine_q,
        wide_sem, thin_sem, right_sem,
        send_d, recv_d, send_u, recv_u, send_q, recv_q, send_s, recv_s, tok_send, tok_recv,
    ) = refs
    width = ddn.shape[1]
    ff = dup.shape[1]
    shard, shard_ff = width // n, ff // n
    row_count, seq = g0.shape[0], g0.shape[1]
    piece = seq // count
    stage = lax.axis_index("pipe")
    me = lax.axis_index("dp")
    pos = dp_to_ring(me, n)
    first = stage == 0
    ahead = ring_to_dp(lax.rem(pos + 1, n), n)
    behind = ring_to_dp(lax.rem(pos + n - 1, n), n)
    target = (ahead, behind)

    def chunk(d, step):
        at = pos + 2 * n - 1 - step if d == 0 else pos + 1 + step
        return ring_to_dp(lax.rem(at, n), n)

    def wide_copy(d, step):
        rows = pl.ds(pl.multiple_of(chunk(d, step) * shard_ff, 16), shard_ff)
        return pltpu.make_async_copy(left.at[rows, :], wide_v.at[d], wide_sem.at[d])

    def thin_copy(k, d, step):
        at = lax.rem(step, 2)
        rows = pl.ds(pl.multiple_of(ff + k * width + chunk(d, step) * shard, 16), shard)
        place_at = pl.ds(pl.multiple_of(at * shard, 16), shard)
        return pltpu.make_async_copy(left.at[rows, :], thin_v.at[min(2 * k + d, 4), place_at, :], thin_sem.at[k, d, at])

    rights = [
        (ddn, ddn_v), (dup, dup_v), (dproj, dpo_v.at[:, pl.ds(0, 3 * width)]),
        (dbr, dpo_v.at[:, pl.ds(3 * width, width)]),
    ]

    def right_copy(k):
        return pltpu.make_async_copy(rights[k][0], rights[k][1], right_sem.at[k])

    for d in range(2):
        wide_copy(d, 0).start()
    right_copy(0).start()
    right_copy(1).start()
    for d in range(2):
        for at in range(2):
            thin_copy(0, d, at).start()
    right_copy(2).start()
    right_copy(3).start()
    for k, d in ((1, 0), (1, 1), (2, 1)):
        for at in range(2):
            thin_copy(k, d, at).start()

    barrier = pltpu.get_barrier_semaphore()
    for peer in target:
        pl.semaphore_signal(barrier, inc=1, device_id={"dp": peer}, device_id_type=LOGICAL)

    @pl.when(first)
    def _():
        pl.semaphore_wait(barrier, 1 + count)

    @pl.when(jnp.logical_not(first))
    def _():
        pl.semaphore_signal(barrier, inc=1, device_id={"pipe": jnp.int32(0)}, device_id_type=LOGICAL)
        pl.semaphore_wait(barrier, 2)

    def tok_part(i, p):
        return pltpu.make_async_remote_copy(
            src_ref=g0.at[i, pl.ds(p * piece, piece)], dst_ref=gtok_o.at[i],
            send_sem=tok_send.at[i, p], recv_sem=tok_recv.at[i],
            device_id={"pipe": jnp.int32(p)}, device_id_type=LOGICAL,
        )

    def tok_own(i):
        return pltpu.make_async_copy(g0.at[i, pl.ds(0, piece)], gtok_o.at[i], tok_send.at[i, 0])

    @pl.when(first)
    def _():
        for i in range(row_count):
            for p in range(1, count):
                tok_part(i, p).start()
            tok_own(i).start()

    def message(slots, send, recv, d, at):
        return pltpu.make_async_remote_copy(
            src_ref=slots.at[d, at], dst_ref=slots.at[d, jnp.minimum(at + 1, n - 1)],
            send_sem=send.at[d, at], recv_sem=recv.at[d, jnp.minimum(at + 1, n - 1)],
            device_id={"dp": target[d]}, device_id_type=LOGICAL,
        )

    def arrived(slots, send, recv, d, at):
        return pltpu.make_async_remote_copy(
            src_ref=slots.at[d, at], dst_ref=slots.at[d, at],
            send_sem=send.at[d, at], recv_sem=recv.at[d, at],
            device_id={"dp": target[d]}, device_id_type=LOGICAL,
        )

    def lane(slots, send, recv, d, step, mine, finish):
        @pl.when(step == 0)
        def _():
            slots[d, 0] = mine.astype(BF16)

        @pl.when(step > 0)
        def _():
            arrived(slots, send, recv, d, step).wait_recv()

            @pl.when(step < n - 1)
            def _():
                slots[d, step] = (slots[d, step].astype(F32) + mine).astype(BF16)

            @pl.when(step == n - 1)
            def _():
                finish(slots[d, step].astype(F32) + mine)

        @pl.when(step < n - 1)
        def _():
            message(slots, send, recv, d, step).start()

    def small_message(at):
        return pltpu.make_async_remote_copy(
            src_ref=slots_s.at[at], dst_ref=slots_s.at[jnp.minimum(at + 1, n - 1)],
            send_sem=send_s.at[at], recv_sem=recv_s.at[jnp.minimum(at + 1, n - 1)],
            device_id={"dp": target[0]}, device_id_type=LOGICAL,
        )

    def small_arrived(at):
        return pltpu.make_async_remote_copy(
            src_ref=slots_s.at[at], dst_ref=slots_s.at[at], send_sem=send_s.at[at],
            recv_sem=recv_s.at[at], device_id={"dp": target[0]}, device_id_type=LOGICAL,
        )

    sum_rows = lax.broadcasted_iota(jnp.int32, (16, 128), 0) < 9

    def small_step(step):
        mine = small[chunk(0, step)]

        @pl.when(step == 0)
        def _():
            slots_s[0] = mine

        @pl.when(step > 0)
        def _():
            small_arrived(step).wait_recv()
            got = slots_s[step]
            slots_s[step] = jnp.where(sum_rows, got + mine, jnp.maximum(got, mine))

        @pl.when(step < n - 1)
        def _():
            small_message(step).start()

        @pl.when(step == n - 1)
        def _():
            small_o[...] = slots_s[step]

    half, half_ff = width // 2, ff // 2

    def fetched(copy, step, *args):
        copy(*args, step).wait()

    def refill(copy, step, *args):
        @pl.when(step < n - 1)
        def _():
            copy(*args, step + 1).start()

    def right_ready(k, step):
        @pl.when(step == 0)
        def _():
            right_copy(k).wait()

    def turn(step, _):
        right_ready(0, step)
        for d in range(2):
            cols = slice(d * half, (d + 1) * half)
            fetched(wide_copy, step, d)
            mine = dot_nn(wide_v[d], ddn_v[:, cols])
            refill(wide_copy, step, d)

            def finish_down(total):
                gd_o[:, cols] = total

            lane(slots_d, send_d, recv_d, d, step, mine, finish_down)
        small_step(step)
        right_ready(1, step)
        paired = lax.rem(step, 2) == 0

        def together(k, d, right, store):
            for at in range(2):
                thin_copy(k, d, step + at).wait()
            both = dot_nn(thin_v[min(2 * k + d, 4)], right)
            store(0, both[:shard])
            store(1, both[shard:])

            @pl.when(step + 2 < n)
            def _():
                for at in range(2):
                    thin_copy(k, d, step + 2 + at).start()

        for d in range(2):
            cols = slice(d * half_ff, (d + 1) * half_ff)

            @pl.when(paired)
            def _():
                def store(at, v):
                    if at == 0:
                        mine_u[d] = v
                    else:
                        gu_o[:, cols] = v

                together(0, d, dup_v[:, cols], store)

            @pl.when(jnp.logical_not(paired))
            def _():
                mine_u[d] = gu_o[:, cols]

            def finish_up(total):
                gu_o[:, cols] = total

            lane(slots_u, send_u, recv_u, d, step, mine_u[d], finish_up)
        right_ready(2, step)
        right_ready(3, step)

        @pl.when(paired)
        def _():
            def store(at, v):
                if at == 0:
                    mine_q[0] = v
                else:
                    gq_o[:, 0 : 2 * width] = v

            together(1, 0, dpo_v[:, 0 : 2 * width], store)

        @pl.when(jnp.logical_not(paired))
        def _():
            mine_q[0] = gq_o[:, 0 : 2 * width]

        def finish_ahead(total):
            gq_o[:, 0 : 2 * width] = total

        lane(slots_q, send_q, recv_q, 0, step, mine_q[0], finish_ahead)

        @pl.when(paired)
        def _():
            for k, out, cols in ((1, gq_o, slice(2 * width, 3 * width)), (2, go_o, slice(0, width))):
                def store(at, v):
                    if at == 0:
                        mine_q[1, :, (k - 1) * width : k * width] = v
                    else:
                        out[:, cols] = v

                together(k, 1, dpo_v[:, (k + 1) * width : (k + 2) * width], store)

        @pl.when(jnp.logical_not(paired))
        def _():
            mine_q[1, :, 0:width] = gq_o[:, 2 * width : 3 * width]
            mine_q[1, :, width : 2 * width] = go_o[...]

        def finish_behind(total):
            gq_o[:, 2 * width : 3 * width] = total[:, 0:width]
            go_o[...] = total[:, width : 2 * width]

        lane(slots_q, send_q, recv_q, 1, step, mine_q[1], finish_behind)
        return 0

    lax.fori_loop(0, n, turn, 0)

    def drain(at, _):
        for d in range(2):
            message(slots_d, send_d, recv_d, d, at).wait_send()
            message(slots_u, send_u, recv_u, d, at).wait_send()
            message(slots_q, send_q, recv_q, d, at).wait_send()
        small_message(at).wait_send()
        return 0

    lax.fori_loop(0, n - 1, drain, 0)

    @pl.when(first)
    def _():
        for i in range(row_count):
            for p in range(1, count):
                tok_part(i, p).wait_send()
            tok_own(i).wait()

    @pl.when(jnp.logical_not(first))
    def _():
        for i in range(row_count):
            tok_part(i, 1).wait_recv()


def run_grads(count, n, left, dproj, dbr, dup, ddn, g0, small):
    rows, seq, width = g0.shape
    ff = dup.shape[2]
    flat = lambda a: a.reshape(rows * seq, a.shape[2])
    tok = rows * seq
    shard, shard_ff = width // n, ff // n
    ops = [left] + [flat(a) for a in (ddn, dup, dproj, dbr)]
    vmem = pl.BlockSpec(memory_space=pltpu.VMEM)
    sem = pltpu.SemaphoreType.DMA
    return pl.pallas_call(
        lambda *refs: grad_kernel(count, n, *refs),
        in_specs=[ANYWHERE] * 5 + [vmem, ANYWHERE],
        out_specs=[vmem] * 5 + [ANYWHERE],
        out_shape=[
            jax.ShapeDtypeStruct((shard, 3 * width), F32),
            jax.ShapeDtypeStruct((shard, width), F32),
            jax.ShapeDtypeStruct((shard, ff), F32),
            jax.ShapeDtypeStruct((shard_ff, width), F32),
            jax.ShapeDtypeStruct((16, 128), F32),
            jax.ShapeDtypeStruct((rows, seq // count, width), BF16),
        ],
        scratch_shapes=[
            pltpu.VMEM((2, n, shard_ff, width // 2), BF16),
            pltpu.VMEM((2, n, shard, ff // 2), BF16),
            pltpu.VMEM((2, n, shard, 2 * width), BF16),
            pltpu.VMEM((n, 16, 128), F32),
            pltpu.VMEM((2, shard_ff, tok), BF16),
            pltpu.VMEM((5, 2 * shard, tok), BF16),
            pltpu.VMEM((tok, width), BF16),
            pltpu.VMEM((tok, ff), BF16),
            pltpu.VMEM((tok, 4 * width), BF16),
            pltpu.VMEM((2, shard, ff // 2), F32),
            pltpu.VMEM((2, shard, 2 * width), F32),
            sem((2,)), sem((3, 2, 2)), sem((4,)),
            sem((2, n)), sem((2, n)), sem((2, n)), sem((2, n)), sem((2, n)), sem((2, n)),
            sem((n,)), sem((n,)), sem((rows, count)), sem((rows,)),
        ],
        compiler_params=pltpu.CompilerParams(
            collective_id=2, has_side_effects=True, vmem_limit_bytes=VMEM_LIMIT,
        ),
        cost_estimate=pl.CostEstimate(
            flops=2 * tok * (4 * width * width + 2 * width * ff), bytes_accessed=tok * 25000, transcendentals=0,
        ),
    )(*ops, small, g0)


def place_kernel(*refs):
    larges, small, outs, smalls = refs[:6], refs[6], refs[7:13], refs[13:]
    for source, out in zip(larges, outs):
        out[...] = source[...].reshape(out.shape)
    flat = jnp.concatenate([small[i : i + 1, :] for i in range(9)], 1)
    gain, shift, s_out, s_down, s_up, s_qv, top = smalls
    thin = gain.shape[2]
    at = 0
    for ref, index in ((gain, 0), (gain, 1), (shift, 0), (shift, 1)):
        ref[0, index : index + 1, :] = flat[:, at : at + thin]
        at += thin
    for ref in (s_out, s_down, s_up, s_qv):
        ref[...] = flat[:, at : at + ref.shape[1]]
        at += ref.shape[1]
    top[...] = small[9:10, 0:4]


def place(n, larges, small, width, ff):
    thin = width // n
    shapes = [jax.ShapeDtypeStruct(v.shape, v.dtype) for v in larges[:2]]
    shapes += [jax.ShapeDtypeStruct((1, *v.shape), v.dtype) for v in larges[2:]]
    smalls = [(1, 2, thin), (1, 2, thin), (1, thin), (1, thin), (1, ff // n), (1, 2 * thin), (1, 4)]
    vmem = pl.BlockSpec(memory_space=pltpu.VMEM)
    return pl.pallas_call(
        place_kernel,
        in_specs=[vmem] * 7,
        out_specs=[vmem] * 13,
        out_shape=shapes + [jax.ShapeDtypeStruct(s, F32) for s in smalls],
        compiler_params=pltpu.CompilerParams(vmem_limit_bytes=VMEM_LIMIT),
    )(*larges, small)


def weight_grad(left, right):
    g = jnp.einsum("rsd,rse->de", left, right, preferred_element_type=F32).astype(BF16)
    return lax.psum_scatter(g, "dp", scatter_dimension=0, tiled=True).astype(F32)


def share_pieces(whole_rows, count, stage):
    piece = whole_rows.shape[1] // count
    mine = whole_rows[:, :piece]
    for p in range(1, count):
        got = lax.ppermute(whole_rows[:, p * piece : (p + 1) * piece], "pipe", [(0, p)])
        mine = jnp.where(stage == p, got, mine)
    return mine


def shards(
    tokens, lengths, ema_scales, w_qkv, bias_qv, w_out, bias_out, w_up, bias_up, w_down, bias_down,
    ln_gain, ln_bias, cotangent,
):
    count = lax.axis_size("pipe")
    n = lax.axis_size("dp")
    width = tokens.shape[2]
    ff = w_up.shape[2]
    b_qkv = jnp.concatenate([bias_qv[:, :width], jnp.zeros_like(bias_qv[:, :width]), bias_qv[:, width:]], 1)
    weights = (
        w_qkv[0], b_qkv, w_out[0], bias_out, w_up[0], bias_up, w_down[0], bias_down, ln_gain[0], ln_bias[0],
    )
    *kept, mixed, peaks = run_forward(count, tokens, lengths, ema_scales, weights)
    left = kept[-2]
    dproj, dbr, dup, ddn, g0, turned, small = run_backward(
        count, cotangent, lengths, ema_scales, weights, kept
    )
    sums = jnp.sum(small, 0)
    parts, at = [], 0
    for size in (width, width, width, width, width, width, ff, width, width, width):
        parts.append(sums[at : at + size])
        at += size
    parts[7:] = [jnp.concatenate([parts[7], parts[9]])]
    packed = jnp.concatenate([v.reshape(n, -1) for v in parts], 1)
    peak = jnp.max(peaks, (1, 2))
    sums_width = packed.shape[1]
    if n >= 4 and n % 2 == 0 and width // n % 16 == 0 and ff // n % 128 == 0 and sums_width == 9 * 128:
        top = jnp.broadcast_to(jnp.pad(peak, (0, 124))[None, None], (n, 7, 128))
        with_peak = jnp.concatenate([packed.reshape(n, 9, 128), top], 1)
        g_qkv, g_out, g_up, g_down, small_sum, grad_tokens = run_grads(
            count, n, turned, dproj, dbr, dup, ddn, g0, with_peak
        )
        larges = (mixed, grad_tokens, g_qkv, g_out, g_up, g_down)
        placed = place(n, larges, small_sum, width, ff)
        mixed, grad_tokens, g_qkv, g_out, g_up, g_down, g_gain, g_shift, s_out, s_down, s_up, s_qv, top = placed
        return (
            mixed, grad_tokens, g_qkv, s_qv, g_out, s_out, g_up, s_up, g_down, s_down, g_gain, g_shift, top,
        )
    else:
        g_down = weight_grad(left[:, :, :ff], ddn)
        g_up = weight_grad(left[:, :, ff : ff + width], dup)
        g_qkv = weight_grad(left[:, :, ff + width : ff + 2 * width], dproj)
        g_out = weight_grad(left[:, :, ff + 2 * width :], dbr)
        mine = lax.psum_scatter(packed, "dp", scatter_dimension=0, tiled=True)
        batch_max = lax.pmax(peak, "dp")[None]
        grad_tokens = share_pieces(g0, count, lax.axis_index("pipe"))
    outs, at = [], 0
    for size in (width, width, width, width, width, width, ff, 2 * width):
        outs.append(mine[:, at : at + size // n])
        at += size // n
    gain0, gain1, shift0, shift1, s_out, s_down, s_up, s_qv = outs
    g_gain = jnp.stack([gain0, gain1], 1)
    g_shift = jnp.stack([shift0, shift1], 1)
    return (
        mixed, grad_tokens, g_qkv[None], s_qv, g_out[None], s_out, g_up[None], s_up, g_down[None], s_down,
        g_gain, g_shift, batch_max,
    )


def solution(mesh):
    return jax.shard_map(
        shards,
        mesh=mesh,
        in_specs=(
            P("dp", None, None), P("dp"), P("pipe", None), P("pipe", None, None), P("pipe", None),
            P("pipe", None, None), P("pipe", None), P("pipe", None, None), P("pipe", None),
            P("pipe", None, None), P("pipe", None), P("pipe", None, None), P("pipe", None, None),
            P("dp", None, None),
        ),
        out_specs=(
            P("dp", "pipe", None), P("dp", "pipe", None), P("pipe", "dp", None), P("pipe", "dp"),
            P("pipe", "dp", None), P("pipe", "dp"), P("pipe", "dp", None), P("pipe", "dp"),
            P("pipe", "dp", None), P("pipe", "dp"), P("pipe", None, "dp"), P("pipe", None, "dp"),
            P("pipe", None),
        ),
        check_vma=False,
    )
```

```python
import jax
import jax.numpy as jnp
from jax import lax
from jax.experimental import pallas as pl
from jax.experimental.pallas import tpu as pltpu
from jax.sharding import PartitionSpec as P

HEAD_DIM = 64
PAIR = 2 * HEAD_DIM
EPS = 1e-06
MASKED = -1000000000.0
CHUNK = 512
PIECE = 256
BLOCK = 32
OPS = 64
LOGICAL = pl.DeviceIdType.MESH
F32 = jnp.float32
BF16 = jnp.bfloat16

ERF_POLY = (
    0.7978823511659165,
    0.03634481045269742,
    -4.5110171354091134e-05,
    -5.02654469142584e-05,
    3.0867937984305273e-06,
    -6.60140005994544e-08,
)
ERF_CLAMP = 5.2 * 5.2
HALF_LOG2E = -0.7213475204444817
LOG2_TWICE_DENSITY = -0.3257480647361593


def dot_nn(a, b):
    return jnp.dot(a, b, preferred_element_type=F32)


def dot_nt(a, b):
    return lax.dot_general(a, b, (((1,), (1,)), ((), ())), preferred_element_type=F32)


def dot_tn(a, b):
    return lax.dot_general(a, b, (((0,), (0,)), ((), ())), preferred_element_type=F32)


def fold_rows(v):
    return jnp.sum(v.reshape(v.shape[0] // 8, 8, v.shape[1]), 0)


def peak_rows(v):
    tiles = [v[:, i : i + 128] for i in range(0, v.shape[1], 128)]
    top = tiles[0]
    for tile in tiles[1:]:
        top = jnp.maximum(top, tile)
    return jnp.max(top.reshape(v.shape[0] // 8, 8, 128), 0)


def greet(stage, count):
    barrier = pltpu.get_barrier_semaphore()
    for step in range(1, count):
        peer = lax.rem(stage + step, count)
        pl.semaphore_signal(barrier, inc=1, device_id={"pipe": peer}, device_id_type=LOGICAL)
    pl.semaphore_wait(barrier, count - 1)


def activation(u, ceiling, inv_ceiling):
    square = u * u
    w = jnp.minimum(square, ERF_CLAMP)
    poly = w * ERF_POLY[-1] + ERF_POLY[-2]
    for coef in ERF_POLY[-3::-1]:
        poly = poly * w + coef
    twice_cdf = 1.0 + jnp.tanh(u * poly)
    act = (0.5 * u) * twice_cdf
    ratio = jnp.tanh(act * inv_ceiling)
    twice_density = jnp.exp2(square * HALF_LOG2E + LOG2_TWICE_DENSITY)
    twice_slope = (1.0 - ratio * ratio) * (twice_cdf + u * twice_density)
    return act, ceiling * ratio, twice_slope


def fwd_kernel(count, *refs):
    (
        lens, scales, tokens, h_qkv, h_out, h_up, h_down, b_qkv, b_out, b_up, b_down, gain, shift,
        x_o, qkv_o, inv_o, ctx_o, n1_o, rs1_o, sl_o, n2_o, rs2_o, left_o, exp_o,
        mixed_o, peaks_o,
        w_qkv, w_out, w_up, w_down, w_sem,
        xin, xout, qkv_s, inv_s, ctx_s, n1_s, rs1_s, sl_s, n2_s, rs2_s, aq_s, hq_s, xq_s, cq_s,
        acc, hid, up_s, ops_s, s_s, e_s, o_s, amax_s,
        save_sem, in_sem, send_sem, recv_sem, mix_send, mix_recv,
    ) = refs
    r = pl.program_id(0)
    rows = pl.num_programs(0)
    row_count = tokens.shape[0]
    seq, width = tokens.shape[1], tokens.shape[2]
    ff = w_up.shape[1]
    piece = seq // count
    stage = lax.axis_index("pipe")
    first = stage == 0
    last = stage == count - 1

    left = {"aq": (0, ff), "hq": (ff, width), "xq": (ff + width, width), "cq": (ff + 2 * width, width)}
    staged = {
        "x": (xin.at[r], x_o), "qkv": (qkv_s, qkv_o), "inv": (inv_s, inv_o), "ctx": (ctx_s, ctx_o),
        "n1": (n1_s, n1_o), "rs1": (rs1_s, rs1_o), "sl": (sl_s, sl_o), "n2": (n2_s, n2_o),
        "rs2": (rs2_s, rs2_o), "aq": (aq_s, left_o), "hq": (hq_s, left_o), "xq": (xq_s, left_o),
        "cq": (cq_s, left_o), "exp": (e_s, exp_o),
    }
    order = list(staged)
    early = ("x", "xq", "qkv", "inv", "ctx", "cq", "exp")
    late = ("n1", "rs1", "hq", "aq", "sl", "n2", "rs2")
    fetches = [(h_qkv, w_qkv), (h_out, w_out), (h_up, w_up), (h_down, w_down)]

    def weight_copy(k):
        return pltpu.make_async_copy(fetches[k][0], fetches[k][1], w_sem.at[k])

    def save_copy(name):
        src, dst = staged[name]
        dst = dst.at[r]
        if name in left:
            dst = dst.at[:, pl.ds(*left[name])]
        return pltpu.make_async_copy(src, dst, save_sem.at[order.index(name)])

    def token_copy(i):
        return pltpu.make_async_copy(tokens.at[i], xin.at[i], in_sem.at[i])

    def hop(i):
        return pltpu.make_async_remote_copy(
            src_ref=xout.at[i], dst_ref=xin.at[i], send_sem=send_sem.at[i], recv_sem=recv_sem.at[i],
            device_id={"pipe": lax.rem(stage + 1, count)}, device_id_type=LOGICAL,
        )

    def mix_part(i, p):
        return pltpu.make_async_remote_copy(
            src_ref=xout.at[i, pl.ds(p * piece, piece)], dst_ref=mixed_o.at[i],
            send_sem=mix_send.at[i, p], recv_sem=mix_recv.at[i],
            device_id={"pipe": jnp.int32(p)}, device_id_type=LOGICAL,
        )

    def mix_own(i):
        return pltpu.make_async_copy(
            xout.at[i, pl.ds((count - 1) * piece, piece)], mixed_o.at[i], mix_send.at[i, count - 1]
        )

    @pl.when(r == 0)
    def _():
        greet(stage, count)
        peaks_o[...] = jnp.zeros_like(peaks_o)
        for k in range(4):
            weight_copy(k).start()

        @pl.when(first)
        def _():
            for i in range(row_count):
                token_copy(i).start()

    @pl.when(first)
    def _():
        token_copy(r).wait()

    @pl.when(jnp.logical_not(first))
    def _():
        hop(r).wait_recv()

    length = lens[r]
    m0, m1, m2, m3 = scales[0, 0], scales[0, 1], scales[0, 2], scales[0, 3]
    i0, i1, i2, i3 = 1.0 / m0, 1.0 / m1, 1.0 / m2, 1.0 / m3

    def row_mask(start, size):
        return (start + lax.broadcasted_iota(jnp.int32, (size, 1), 0)) < length

    def blocks(size, body, init=0, begin=0, end=seq):
        step = lambda i, c: body(i * size, pl.ds(i * size, size), c)
        return lax.fori_loop(begin // size, end // size, step, init, unroll=True)

    def weave(dots, size, body, init=0):
        total, cut = seq // size, 0
        for k, dot in enumerate(dots):
            dot()
            begin, cut = cut, total * (k + 1) // len(dots)
            init = blocks(size, body, init, begin * size, cut * size)
        return init

    no_peak = jnp.zeros((8, 128), F32)

    @pl.when(r > 0)
    def _():
        for name in early:
            save_copy(name).wait()

    @pl.when(r == 0)
    def _():
        weight_copy(0).wait()

    def quant_in(start, at, top):
        x = xin[r, at, :].astype(F32)
        xq_s[at, :] = (m0 * jnp.tanh(x * i0)).astype(BF16)
        return jnp.maximum(top, masked_peak(x, start))

    def masked_peak(v, start):
        return peak_rows(jnp.where(row_mask(start, v.shape[0]), jnp.abs(v), 0.0))

    peaks_o[0] = jnp.maximum(peaks_o[0], blocks(BLOCK, quant_in, no_peak))
    for j in range(3):
        cols = pl.ds(j * width, width)
        proj = dot_nn(xq_s[...], w_qkv[:, cols]) + b_qkv[:, cols]
        qkv_s[:, cols] = proj.astype(BF16)

    one = jnp.ones((), BF16)
    zero = jnp.zeros((), BF16)
    head_scale = jnp.asarray(HEAD_DIM ** -0.5, BF16)

    def prepare(p):
        slot = p % 2

        def body(start, at, c):
            lane = lax.broadcasted_iota(jnp.int32, (OPS, PAIR), 1)
            lo = lane < HEAD_DIM
            spot = jnp.where(lo, lane, lane - HEAD_DIM)
            bias = jnp.where(row_mask(start, OPS), 0.0, MASKED)
            extra = jnp.where(spot == 0, jnp.broadcast_to(bias, (OPS, PAIR)), 0.0).astype(BF16)
            q2 = qkv_s[at, p * PAIR : (p + 1) * PAIR] * head_scale
            k2 = qkv_s[at, width + p * PAIR : width + (p + 1) * PAIR]
            v2 = qkv_s[at, 2 * width + p * PAIR : 2 * width + (p + 1) * PAIR]
            ops_s[slot, 0, at, :] = jnp.where(lo, q2, one)
            ops_s[slot, 1, at, :] = jnp.where(lo, one, q2)
            ops_s[slot, 2, at, :] = jnp.where(lo, k2, extra)
            ops_s[slot, 3, at, :] = jnp.where(lo, extra, k2)
            ops_s[slot, 4, at, :] = jnp.where(lo, v2, one)
            ops_s[slot, 5, at, :] = jnp.where(lo, one, v2)
            return c

        blocks(OPS, body)

    def scores(h):
        p, side = h // 2, h % 2

        def piece_of(k):
            def run():
                keys = pl.ds(k * PIECE, PIECE)
                s_s[side, :, keys] = dot_nt(ops_s[p % 2, side], ops_s[p % 2, 2 + side, keys, :])

            return run

        return [piece_of(k) for k in range(seq // PIECE)]

    def soften(h):
        def body(start, at, c):
            s = s_s[h % 2, at, :]
            e_s[h, at, :] = jnp.exp(s - jnp.max(s, -1, keepdims=True)).astype(BF16)
            return c

        return body

    def collect(h):
        p, side = h // 2, h % 2

        def piece_of(k):
            def run():
                queries = pl.ds(k * PIECE, PIECE)
                o_s[side, queries, :] = dot_nn(e_s[h, queries, :], ops_s[p % 2, 4 + side])

            return run

        return [piece_of(k) for k in range(seq // PIECE)]

    def settle(p, peak):
        cols = slice(p * PAIR, (p + 1) * PAIR)

        def body(start, at, top):
            lo = lax.broadcasted_iota(jnp.int32, (OPS, PAIR), 1) < HEAD_DIM
            o_a, o_b = o_s[0, at, :], o_s[1, at, :]
            total = pltpu.roll(jnp.where(lo, o_b, o_a), HEAD_DIM, 1)
            inverse = 1.0 / total
            c = jnp.where(lo, o_a, o_b) * inverse
            inv_s[at, cols] = inverse
            ctx_s[at, cols] = c
            cq_s[at, cols] = (m1 * jnp.tanh(c * i1)).astype(BF16)
            return jnp.maximum(top, masked_peak(c, start))

        return blocks(OPS, body, peak)

    heads = 2 * (width // PAIR)
    peak = no_peak
    prepare(0)
    for dot in scores(0):
        dot()
    for h in range(heads):
        dots = []
        if h + 1 < heads:
            if (h + 1) % 2 == 0:
                prepare((h + 1) // 2)
            dots += scores(h + 1)
        if h > 0:
            dots += collect(h - 1)
        weave(dots, BLOCK, soften(h))
        if h > 0 and h % 2 == 0:
            peak = settle(h // 2 - 1, peak)
    for dot in collect(heads - 1):
        dot()
    peak = settle(heads // 2 - 1, peak)
    peaks_o[1] = jnp.maximum(peaks_o[1], peak)

    for name in early:
        save_copy(name).start()

    @pl.when(r > 0)
    def _():
        for name in late:
            save_copy(name).wait()

    @pl.when(r == 0)
    def _():
        for k in (1, 2, 3):
            weight_copy(k).wait()

    def out_piece(k):
        def run():
            at = pl.ds(k * PIECE, PIECE)
            acc[at, :] = dot_nn(cq_s[at, :], w_out[...])

        return run

    def norm_one(start, at, top):
        s = xin[r, at, :].astype(F32) + (acc[at, :] + b_out[...])
        center = s - jnp.mean(s, -1, keepdims=True)
        rs = lax.rsqrt(jnp.mean(center * center, -1, keepdims=True) + EPS)
        n = center * rs
        h = n * gain[0:1, :] + shift[0:1, :]
        n1_s[at, :] = n.astype(BF16)
        rs1_s[at, :] = jnp.broadcast_to(rs, (BLOCK, 128))
        hid[at, :] = h
        hq_s[at, :] = (m2 * jnp.tanh(h * i2)).astype(BF16)
        return jnp.maximum(top, masked_peak(h, start))

    out_piece(0)()
    top = weave([out_piece(k) for k in range(1, seq // PIECE)] + [lambda: None], BLOCK, norm_one, no_peak)
    peaks_o[2] = jnp.maximum(peaks_o[2], top)

    chunks = ff // CHUNK

    def up_chunk(c):
        def piece_of(k):
            def run():
                part = dot_nn(hq_s[...], w_up[:, pl.ds(c * CHUNK + k * PIECE, PIECE)])
                up_s[c % 2, :, pl.ds(k * PIECE, PIECE)] = part

            return run

        return [piece_of(k) for k in range(CHUNK // PIECE)]

    def act_chunk(c):
        cols = pl.ds(c * CHUNK, CHUNK)

        def body(start, at, carry):
            act, low, slope = activation(up_s[c % 2, at, :] + b_up[:, cols], m3, i3)
            aq_s[at, cols] = low.astype(BF16)
            sl_s[at, cols] = slope.astype(BF16)
            size = jnp.abs(act)
            top = size[:, 0:128]
            for i in range(128, CHUNK, 128):
                top = jnp.maximum(top, size[:, i : i + 128])
            amax_s[at, :] = top if c == 0 else jnp.maximum(amax_s[at, :], top)
            return carry

        return body

    def down_chunk(c):
        def piece_of(k):
            def run():
                cols = pl.ds(k * PIECE, PIECE)
                part = dot_nn(aq_s[:, pl.ds(c * CHUNK, CHUNK)], w_down[pl.ds(c * CHUNK, CHUNK), cols])
                acc[:, cols] = part if c == 0 else acc[:, cols] + part

            return run

        return [piece_of(k) for k in range(width // PIECE)]

    for dot in up_chunk(0):
        dot()
    for c in range(chunks):
        dots = []
        if c + 1 < chunks:
            dots += up_chunk(c + 1)
        if c > 0:
            dots += down_chunk(c - 1)
        weave(dots, BLOCK, act_chunk(c))
    peaks_o[3] = jnp.maximum(peaks_o[3], masked_peak(amax_s[...], 0))

    def norm_two(start, at, c):
        s = hid[at, :] + (acc[at, :] + b_down[...])
        center = s - jnp.mean(s, -1, keepdims=True)
        rs = lax.rsqrt(jnp.mean(center * center, -1, keepdims=True) + EPS)
        n = center * rs
        n2_s[at, :] = n.astype(BF16)
        rs2_s[at, :] = jnp.broadcast_to(rs, (BLOCK, 128))
        xout[r, at, :] = (n * gain[1:2, :] + shift[1:2, :]).astype(BF16)
        return c

    def down_last(k):
        def run():
            at, cols = pl.ds(k * PIECE, PIECE), pl.ds((chunks - 1) * CHUNK, CHUNK)
            acc[at, :] += dot_nn(aq_s[at, cols], w_down[cols, :])

        return run

    down_last(0)()
    weave([down_last(k) for k in range(1, seq // PIECE)] + [lambda: None], BLOCK, norm_two)
    for name in late:
        save_copy(name).start()

    @pl.when(jnp.logical_not(last))
    def _():
        hop(r).start()

    @pl.when(last)
    def _():
        for p in range(count - 1):
            mix_part(r, p).start()
        mix_own(r).start()

    @pl.when(r == rows - 1)
    def _():
        for name in order:
            save_copy(name).wait()

        @pl.when(jnp.logical_not(last))
        def _():
            for i in range(row_count):
                hop(i).wait_send()
            for i in range(row_count):
                mix_part(i, 0).wait_recv()

        @pl.when(last)
        def _():
            for i in range(row_count):
                for p in range(count - 1):
                    mix_part(i, p).wait_send()
                mix_own(i).wait()


def bwd_kernel(count, *refs):
    (
        lens, scales, seeds, h_qkv, h_out, h_up, h_down, gain, shift, left_i,
        x_i, qkv_i, inv_i, ctx_i, n1_i, rs1_i, sl_i, n2_i, rs2_i, exp_i,
        dproj_o, dbr_o, dup_o, ddn_o, gtok_o, left_o, small_o,
        w_qkv, w_out, w_up, w_down, w_sem, turn_in, turn_out, turn_in_sem, turn_out_sem,
        gin, x_s, qkv_s, inv_s, ctx_s, n1_s, rs1_s, sl_s, n2_s, rs2_s, e_s,
        dproj_s, dbr_s, dup_s, ddn_s, dctx_s, acc, dr,
        up_s, ops_s, g_s, ds_s, gv_s, gk_s, gq_s, q_t, do_t, inner_s,
        load_sem, save_sem, in_sem, send_sem, recv_sem, tok_send,
    ) = refs
    r = pl.program_id(0)
    rows = pl.num_programs(0)
    row_count = seeds.shape[0]
    seq, width = seeds.shape[1], seeds.shape[2]
    ff = w_up.shape[1]
    piece = seq // count
    stage = lax.axis_index("pipe")
    first = stage == 0
    last = stage == count - 1

    loaded = {
        "n2": (n2_i, n2_s), "rs2": (rs2_i, rs2_s), "sl": (sl_i, sl_s), "n1": (n1_i, n1_s),
        "rs1": (rs1_i, rs1_s), "ctx": (ctx_i, ctx_s), "qkv": (qkv_i, qkv_s), "inv": (inv_i, inv_s),
        "x": (x_i, x_s), "exp": (exp_i, e_s),
    }
    load_order = list(loaded)
    early = ("n2", "rs2", "sl", "n1", "rs1")
    late = ("ctx", "qkv", "inv", "exp", "x")
    staged = {
        "ddn": (ddn_s, ddn_o), "dup": (dup_s, dup_o), "dbr": (dbr_s, dbr_o), "dproj": (dproj_s, dproj_o),
    }
    save_order = list(staged)

    def load_copy(name, i):
        src, dst = loaded[name]
        return pltpu.make_async_copy(src.at[i], dst, load_sem.at[load_order.index(name)])

    def save_copy(name):
        src, dst = staged[name]
        return pltpu.make_async_copy(src, dst.at[r], save_sem.at[save_order.index(name)])

    def seed_copy(i):
        return pltpu.make_async_copy(seeds.at[i], gin.at[i], in_sem.at[i])

    def hop(i):
        return pltpu.make_async_remote_copy(
            src_ref=gin.at[i], dst_ref=gin.at[i], send_sem=send_sem.at[i], recv_sem=recv_sem.at[i],
            device_id={"pipe": lax.rem(stage + count - 1, count)}, device_id_type=LOGICAL,
        )

    def tok_copy(i):
        return pltpu.make_async_copy(gin.at[i], gtok_o.at[i], tok_send.at[i])

    fetches = [(h_down, w_down), (h_up, w_up), (h_out, w_out), (h_qkv, w_qkv)]

    def weight_copy(k):
        return pltpu.make_async_copy(fetches[k][0], fetches[k][1], w_sem.at[k])

    parts = left_i.shape[2] // width
    turns = row_count * parts

    def turn_load(i):
        cols = pl.ds(pl.multiple_of(i % parts * width, 128), width)
        return pltpu.make_async_copy(left_i.at[i // parts, :, cols], turn_in.at[i % 2], turn_in_sem.at[i % 2])

    def turn_store(i):
        rows_at = pl.ds(pl.multiple_of(i % parts * width, 128), width)
        cols = pl.ds(pl.multiple_of(i // parts * seq, 128), seq)
        return pltpu.make_async_copy(turn_out.at[i % 2], left_o.at[rows_at, cols], turn_out_sem.at[i % 2])

    def turn_left():
        turn_load(0).start()

        def body(i, c):
            @pl.when(i + 1 < turns)
            def _():
                turn_load(i + 1).start()

            turn_load(i).wait()

            @pl.when(i >= 2)
            def _():
                turn_store(i - 2).wait()

            turn_out[i % 2] = turn_in[i % 2].T
            turn_store(i).start()
            return c

        lax.fori_loop(0, turns, body, 0)
        turn_store(turns - 2).wait()
        turn_store(turns - 1).wait()

    @pl.when(r == 0)
    def _():
        greet(stage, count)
        small_o[...] = jnp.zeros_like(small_o)

        @pl.when(last)
        def _():
            for i in range(row_count):
                seed_copy(i).start()

        for name in ("n2", "rs2"):
            load_copy(name, 0).start()
        weight_copy(0).start()
        for name in early[2:]:
            load_copy(name, 0).start()
        for k in (1, 2, 3):
            weight_copy(k).start()
        for name in late:
            load_copy(name, 0).start()

        @pl.when(stage < count - 2)
        def _():
            turn_left()

    @pl.when(last)
    def _():
        seed_copy(r).wait()

    @pl.when(jnp.logical_not(last))
    def _():
        hop(r).wait_recv()

    length = lens[r]
    m0, m1, m2 = scales[0, 0], scales[0, 1], scales[0, 2]
    i0, i1, i2 = 1.0 / m0, 1.0 / m1, 1.0 / m2

    offsets = {}
    at_col = 0
    for name, size in (
        ("gain0", width), ("gain1", width), ("shift0", width), ("shift1", width),
        ("out", width), ("down", width), ("up", ff), ("qkv", 3 * width),
    ):
        offsets[name] = at_col
        at_col += size

    def blocks(size, body, init=0, begin=0, end=seq):
        step = lambda i, c: body(i * size, pl.ds(i * size, size), c)
        return lax.fori_loop(begin // size, end // size, step, init, unroll=True)

    def weave(dots, size, body, init=0):
        total, cut = seq // size, 0
        for k, dot in enumerate(dots):
            dot()
            begin, cut = cut, total * (k + 1) // len(dots)
            init = blocks(size, body, init, begin * size, cut * size)
        return init

    def row_mask(start, size):
        return (start + lax.broadcasted_iota(jnp.int32, (size, 1), 0)) < length

    def put_small(name, v, col=0):
        small_o[:, pl.ds(offsets[name] + col, v.shape[1])] += v

    no_sum = jnp.zeros((8, width), F32)

    for name in early:
        load_copy(name, r).wait()

    @pl.when(r > 0)
    def _():
        for name in ("ddn", "dup", "dbr"):
            save_copy(name).wait()

    @pl.when(r == 0)
    def _():
        for k in (0, 1):
            weight_copy(k).wait()

    def norm_two(start, at, sums):
        dy = jnp.where(row_mask(start, BLOCK), gin[r, at, :].astype(F32), 0.0)
        n = n2_s[at, :].astype(F32)
        e = dy * gain[1:2, :]
        mean_e = jnp.mean(e, -1, keepdims=True)
        mean_en = jnp.mean(e * n, -1, keepdims=True)
        d = (e - mean_e - n * mean_en) * rs2_s[at, 0:1]
        dr[at, :] = d
        ddn_s[at, :] = d.astype(BF16)
        return sums[0] + fold_rows(dy * n), sums[1] + fold_rows(dy), sums[2] + fold_rows(d)

    for name, v in zip(("gain1", "shift1", "down"), blocks(BLOCK, norm_two, (no_sum,) * 3)):
        put_small(name, v)

    chunks = ff // CHUNK

    def dact_chunk(c):
        def piece_of(k):
            def run():
                at = pl.ds(c * CHUNK + k * PIECE, PIECE)
                up_s[c % 2, :, pl.ds(k * PIECE, PIECE)] = dot_nt(ddn_s[...], w_down[at, :])

            return run

        return [piece_of(k) for k in range(CHUNK // PIECE)]

    def slope_chunk(c):
        cols = pl.ds(c * CHUNK, CHUNK)

        def body(start, at, total):
            d = (0.5 * up_s[c % 2, at, :]) * sl_s[at, cols].astype(F32)
            dup_s[at, cols] = d.astype(BF16)
            return total + fold_rows(d)

        return body

    def dhid_chunk(c):
        cols = pl.ds(c * CHUNK, CHUNK)

        def piece_of(k):
            def run():
                at = pl.ds(k * PIECE, PIECE)
                part = dot_nt(dup_s[:, cols], w_up[at, cols])
                acc[:, at] = part if c == 0 else acc[:, at] + part

            return run

        return [piece_of(k) for k in range(width // PIECE)]

    for dot in dact_chunk(0):
        dot()
    for c in range(chunks):
        dots = []
        if c + 1 < chunks:
            dots += dact_chunk(c + 1)
        if c > 0:
            dots += dhid_chunk(c - 1)
        put_small("up", weave(dots, BLOCK, slope_chunk(c), jnp.zeros((8, CHUNK), F32)), c * CHUNK)

    def norm_one(start, at, sums):
        n = n1_s[at, :].astype(F32)
        t = jnp.tanh((n * gain[0:1, :] + shift[0:1, :]) * i2)
        dy = dr[at, :] + acc[at, :] * (1.0 - t * t)
        e = dy * gain[0:1, :]
        mean_e = jnp.mean(e, -1, keepdims=True)
        mean_en = jnp.mean(e * n, -1, keepdims=True)
        d = (e - mean_e - n * mean_en) * rs1_s[at, 0:1]
        dr[at, :] = d
        dbr_s[at, :] = d.astype(BF16)
        return sums[0] + fold_rows(dy * n), sums[1] + fold_rows(dy), sums[2] + fold_rows(d)

    def dhid_last(k):
        def run():
            at, cols = pl.ds(k * PIECE, PIECE), pl.ds((chunks - 1) * CHUNK, CHUNK)
            acc[at, :] += dot_nt(dup_s[at, cols], w_up[:, cols])

        return run

    dhid_last(0)()
    dots = [dhid_last(k) for k in range(1, seq // PIECE)] + [lambda: None]
    for name, v in zip(("gain0", "shift0", "out"), weave(dots, BLOCK, norm_one, (no_sum,) * 3)):
        put_small(name, v)

    for name in ("ddn", "dup", "dbr"):
        save_copy(name).start()

    @pl.when(r + 1 < rows)
    def _():
        for name in early:
            load_copy(name, r + 1).start()

    for name in late:
        load_copy(name, r).wait()

    @pl.when(r > 0)
    def _():
        save_copy("dproj").wait()

    @pl.when(r == 0)
    def _():
        for k in (2, 3):
            weight_copy(k).wait()

    for k in range(width // PIECE):
        acc[:, pl.ds(k * PIECE, PIECE)] = dot_nt(dbr_s[...], w_out[pl.ds(k * PIECE, PIECE), :])

    zero = jnp.zeros((), BF16)
    head_scale = jnp.asarray(HEAD_DIM ** -0.5, BF16)

    def prepare(p):
        slot = p % 2
        cols = slice(p * PAIR, (p + 1) * PAIR)

        def body(start, at, c):
            lo = lax.broadcasted_iota(jnp.int32, (OPS, PAIR), 1) < HEAD_DIM
            ctx = ctx_s[at, cols]
            t = jnp.tanh(ctx * i1)
            low = (acc[at, cols] * (1.0 - t * t) * inv_s[at, cols]).astype(BF16)
            dctx_s[slot, at, :] = low
            inner = low.astype(F32) * ctx
            whole_sum = jnp.sum(inner, -1, keepdims=True)
            lower = jnp.sum(jnp.where(lo, inner, 0.0), -1, keepdims=True)
            inner_s[slot, 0, at, :] = jnp.broadcast_to(lower, (OPS, PAIR))
            inner_s[slot, 1, at, :] = jnp.broadcast_to(whole_sum - lower, (OPS, PAIR))
            v2 = qkv_s[at, 2 * width + p * PAIR : 2 * width + (p + 1) * PAIR]
            ops_s[slot, 0, at, :] = jnp.where(lo, v2, zero)
            ops_s[slot, 1, at, :] = jnp.where(lo, zero, v2)
            return c

        blocks(OPS, body)
        q_t[slot] = (qkv_s[:, cols] * head_scale).T
        do_t[slot] = dctx_s[slot].T

    def scores(h):
        slot, side = h // 2 % 2, h % 2

        def piece_of(k):
            def run():
                keys = pl.ds(k * PIECE, PIECE)
                g_s[side, :, keys] = dot_nt(dctx_s[slot], ops_s[slot, side, keys, :])

            return run

        return [piece_of(k) for k in range(seq // PIECE)]

    def soften(h):
        slot, side = h // 2 % 2, h % 2

        def body(start, at, c):
            inner = jnp.concatenate([inner_s[slot, side, at, :]] * (seq // PAIR), 1)
            ds_s[side, at, :] = (e_s[h, at, :].astype(F32) * (g_s[side, at, :] - inner)).astype(BF16)
            return c

        return body

    def collect(h):
        slot, side = h // 2 % 2, h % 2
        rows_at = slice(side * HEAD_DIM, (side + 1) * HEAD_DIM)

        def grad_v(k):
            def run():
                keys = pl.ds(k * PIECE, PIECE)
                gv_s[rows_at, keys] = dot_nn(do_t[slot, rows_at, :], e_s[h, :, keys])

            return run

        def grad_k(k):
            def run():
                keys = pl.ds(k * PIECE, PIECE)
                gk_s[rows_at, keys] = dot_nn(q_t[slot, rows_at, :], ds_s[side, :, keys])

            return run

        def grad_q(k):
            def run():
                queries = pl.ds(k * PIECE, PIECE)
                keys_low = qkv_s[:, width + h // 2 * PAIR : width + (h // 2 + 1) * PAIR]
                gq_s[side, queries, :] = dot_nn(ds_s[side, queries, :], keys_low)

            return run

        return [make(k) for make in (grad_v, grad_k, grad_q) for k in range(seq // PIECE)]

    def settle(p):
        def body(start, at, c):
            lo = lax.broadcasted_iota(jnp.int32, (OPS, PAIR), 1) < HEAD_DIM
            q = jnp.where(lo, gq_s[0, at, :], gq_s[1, at, :]) * (HEAD_DIM ** -0.5)
            dproj_s[at, p * PAIR : (p + 1) * PAIR] = q.astype(BF16)
            return c

        blocks(OPS, body)
        dproj_s[:, width + p * PAIR : width + (p + 1) * PAIR] = gk_s[...].astype(BF16).T
        dproj_s[:, 2 * width + p * PAIR : 2 * width + (p + 1) * PAIR] = gv_s[...].astype(BF16).T

    heads = 2 * (width // PAIR)
    prepare(0)
    for dot in scores(0):
        dot()
    for h in range(heads):
        dots = []
        if h + 1 < heads:
            if (h + 1) % 2 == 0:
                prepare((h + 1) // 2)
            dots += scores(h + 1)
        if h > 0:
            dots += collect(h - 1)
        weave(dots, BLOCK, soften(h))
        if h > 0 and h % 2 == 0:
            settle(h // 2 - 1)
    for dot in collect(heads - 1):
        dot()
    settle(heads // 2 - 1)
    def dx_piece(k):
        def run():
            at = pl.ds(k * PIECE, PIECE)
            acc[:, at] = dot_nt(dproj_s[...], w_qkv[at, :])

        return run

    def quant_in(k):
        cols = pl.ds(k * PIECE, PIECE)
        values = pl.ds(2 * width + k * PIECE, PIECE)

        def body(start, at, sums):
            t = jnp.tanh(x_s[at, cols].astype(F32) * i0)
            gin[r, at, cols] = (dr[at, cols] + acc[at, cols] * (1.0 - t * t)).astype(BF16)
            return (
                sums[0] + fold_rows(dproj_s[at, cols].astype(F32)),
                sums[1] + fold_rows(dproj_s[at, values].astype(F32)),
            )

        return body

    dx_piece(0)()
    pieces = width // PIECE
    for k in range(pieces):
        dots = [dx_piece(k + 1)] if k + 1 < pieces else [lambda: None]
        sums = weave(dots, BLOCK, quant_in(k), (jnp.zeros((8, PIECE), F32),) * 2)
        put_small("qkv", sums[0], k * PIECE)
        put_small("qkv", sums[1], 2 * width + k * PIECE)
    save_copy("dproj").start()

    @pl.when(r + 1 < rows)
    def _():
        for name in late:
            load_copy(name, r + 1).start()

    @pl.when(jnp.logical_not(first))
    def _():
        hop(r).start()

    @pl.when(first)
    def _():
        tok_copy(r).start()

    @pl.when(r == rows - 1)
    def _():
        @pl.when(stage >= count - 2)
        def _():
            turn_left()

        for name in save_order:
            save_copy(name).wait()

        @pl.when(jnp.logical_not(first))
        def _():
            for i in range(row_count):
                hop(i).wait_send()

        @pl.when(first)
        def _():
            for i in range(row_count):
                tok_copy(i).wait()


def whole(a):
    return pl.BlockSpec(a.shape, lambda r, n=a.ndim: (0,) * n, pipeline_mode=pl.Buffered(1))


ANYWHERE = pl.BlockSpec(memory_space=pl.ANY)
SCALAR = pl.BlockSpec(memory_space=pltpu.SMEM)
VMEM_LIMIT = 60 * 1024 * 1024


def run_forward(count, tokens, lengths, scales, weights):
    w_qkv, b_qkv, w_out, b_out, w_up, b_up, w_down, b_down, gain, shift = weights
    rows, seq, width = tokens.shape
    ff = w_up.shape[1]
    big = lambda n, t: jax.ShapeDtypeStruct((rows, seq, n), t)
    saves = [
        (width, BF16), (3 * width, BF16), (width, F32), (width, F32), (width, BF16), (128, F32),
        (ff, BF16), (width, BF16), (128, F32),
    ]
    heads = width // HEAD_DIM
    lefts = [(ff, BF16), (width, BF16), (width, BF16), (width, BF16)]
    heavy = (w_qkv, w_out, w_up, w_down)
    dense = (b_qkv, b_out, b_up, b_down, gain, shift)
    tok = rows * seq
    return pl.pallas_call(
        lambda *refs: fwd_kernel(count, *refs),
        grid=(rows,),
        in_specs=[SCALAR, SCALAR, ANYWHERE] + [ANYWHERE] * 4 + [whole(a) for a in dense],
        out_specs=[ANYWHERE] * 12 + [pl.BlockSpec((4, 8, 128), lambda r: (0, 0, 0))],
        out_shape=[big(n, t) for n, t in saves]
        + [
            big(ff + 3 * width, BF16),
            jax.ShapeDtypeStruct((rows, heads, seq, seq), BF16),
            jax.ShapeDtypeStruct((rows, seq // count, width), BF16),
            jax.ShapeDtypeStruct((4, 8, 128), F32),
        ],
        scratch_shapes=[pltpu.VMEM(a.shape, a.dtype) for a in heavy]
        + [pltpu.SemaphoreType.DMA((4,))]
        + [pltpu.VMEM((rows, seq, width), BF16), pltpu.VMEM((rows, seq, width), BF16)]
        + [pltpu.VMEM((seq, n), t) for n, t in saves[1:] + lefts]
        + [
            pltpu.VMEM((seq, width), F32),
            pltpu.VMEM((seq, width), F32),
            pltpu.VMEM((2, seq, CHUNK), F32),
            pltpu.VMEM((2, 6, seq, PAIR), BF16),
            pltpu.VMEM((2, seq, seq), F32),
            pltpu.VMEM((heads, seq, seq), BF16),
            pltpu.VMEM((2, seq, PAIR), F32),
            pltpu.VMEM((seq, 128), F32),
            pltpu.SemaphoreType.DMA((14,)),
            pltpu.SemaphoreType.DMA((rows,)),
            pltpu.SemaphoreType.DMA((rows,)),
            pltpu.SemaphoreType.DMA((rows,)),
            pltpu.SemaphoreType.DMA((rows, count)),
            pltpu.SemaphoreType.DMA((rows,)),
        ],
        compiler_params=pltpu.CompilerParams(
            collective_id=0, has_side_effects=True, vmem_limit_bytes=VMEM_LIMIT,
            dimension_semantics=("arbitrary",),
        ),
        cost_estimate=pl.CostEstimate(
            flops=2 * tok * (4 * width * width + 2 * width * ff + 2 * seq * width),
            bytes_accessed=tok * 28000, transcendentals=tok * 3 * ff,
        ),
    )(lengths, scales, tokens, *heavy, *dense)


def run_backward(count, seeds, lengths, scales, weights, kept):
    w_qkv, b_qkv, w_out, b_out, w_up, b_up, w_down, b_down, gain, shift = weights
    *loads, left, exps = kept
    loads.append(exps)
    rows, seq, width = seeds.shape
    ff = w_up.shape[1]
    big = lambda n, t: jax.ShapeDtypeStruct((rows, seq, n), t)
    saves = [(3 * width, BF16), (width, BF16), (ff, BF16), (width, BF16)]
    heavy = (w_qkv, w_out, w_up, w_down)
    dense = (gain, shift)
    tok = rows * seq
    small = 6 * width + ff + 3 * width
    return pl.pallas_call(
        lambda *refs: bwd_kernel(count, *refs),
        grid=(rows,),
        in_specs=[SCALAR, SCALAR, ANYWHERE] + [ANYWHERE] * 4 + [whole(a) for a in dense] + [ANYWHERE] * 11,
        out_specs=[ANYWHERE] * 6 + [pl.BlockSpec((8, small), lambda r: (0, 0))],
        out_shape=[big(n, t) for n, t in saves]
        + [
            big(width, BF16), jax.ShapeDtypeStruct((left.shape[2], rows * seq), BF16),
            jax.ShapeDtypeStruct((8, small), F32),
        ],
        scratch_shapes=[pltpu.VMEM(a.shape, a.dtype) for a in heavy]
        + [
            pltpu.SemaphoreType.DMA((4,)),
            pltpu.VMEM((2, seq, width), BF16),
            pltpu.VMEM((2, width, seq), BF16),
            pltpu.SemaphoreType.DMA((2,)),
            pltpu.SemaphoreType.DMA((2,)),
        ]
        + [pltpu.VMEM((rows, seq, width), BF16)]
        + [pltpu.VMEM(a.shape[1:], a.dtype) for a in loads]
        + [pltpu.VMEM((seq, n), t) for n, t in saves]
        + [
            pltpu.VMEM((2, seq, PAIR), BF16),
            pltpu.VMEM((seq, width), F32),
            pltpu.VMEM((seq, width), F32),
            pltpu.VMEM((2, seq, CHUNK), F32),
            pltpu.VMEM((2, 2, seq, PAIR), BF16),
            pltpu.VMEM((2, seq, seq), F32),
            pltpu.VMEM((2, seq, seq), BF16),
            pltpu.VMEM((PAIR, seq), F32),
            pltpu.VMEM((PAIR, seq), F32),
            pltpu.VMEM((2, seq, PAIR), F32),
            pltpu.VMEM((2, PAIR, seq), BF16),
            pltpu.VMEM((2, PAIR, seq), BF16),
            pltpu.VMEM((2, 2, seq, PAIR), F32),
            pltpu.SemaphoreType.DMA((10,)),
            pltpu.SemaphoreType.DMA((4,)),
            pltpu.SemaphoreType.DMA((rows,)),
            pltpu.SemaphoreType.DMA((rows,)),
            pltpu.SemaphoreType.DMA((rows,)),
            pltpu.SemaphoreType.DMA((rows,)),
        ],
        compiler_params=pltpu.CompilerParams(
            collective_id=1, has_side_effects=True, vmem_limit_bytes=VMEM_LIMIT,
            dimension_semantics=("arbitrary",),
        ),
        cost_estimate=pl.CostEstimate(
            flops=2 * tok * (4 * width * width + 2 * width * ff + 5 * seq * width),
            bytes_accessed=tok * 28000, transcendentals=tok * ff,
        ),
    )(lengths, scales, seeds, *heavy, *dense, left, *loads)


def ring_to_dp(pos, n):
    return jnp.where(pos < n // 2, 2 * pos, 2 * (n - pos) - 1)


def dp_to_ring(j, n):
    return jnp.where(j % 2 == 0, j // 2, n - 1 - j // 2)


def grad_kernel(count, n, *refs):
    (
        left, ddn, dup, dproj, dbr, small, g0,
        gq_o, go_o, gu_o, gd_o, small_o, gtok_o,
        slots_d, slots_u, slots_q, slots_s, wide_v, thin_v, ddn_v, dup_v, dpo_v, mine_u, mine_q,
        wide_sem, thin_sem, right_sem,
        send_d, recv_d, send_u, recv_u, send_q, recv_q, send_s, recv_s, tok_send, tok_recv,
    ) = refs
    width = ddn.shape[1]
    ff = dup.shape[1]
    shard, shard_ff = width // n, ff // n
    row_count, seq = g0.shape[0], g0.shape[1]
    piece = seq // count
    stage = lax.axis_index("pipe")
    me = lax.axis_index("dp")
    pos = dp_to_ring(me, n)
    first = stage == 0
    ahead = ring_to_dp(lax.rem(pos + 1, n), n)
    behind = ring_to_dp(lax.rem(pos + n - 1, n), n)
    target = (ahead, behind)

    def chunk(d, step):
        at = pos + 2 * n - 1 - step if d == 0 else pos + 1 + step
        return ring_to_dp(lax.rem(at, n), n)

    def wide_copy(d, step):
        rows = pl.ds(pl.multiple_of(chunk(d, step) * shard_ff, 16), shard_ff)
        return pltpu.make_async_copy(left.at[rows, :], wide_v.at[d], wide_sem.at[d])

    def thin_copy(k, d, step):
        at = lax.rem(step, 2)
        rows = pl.ds(pl.multiple_of(ff + k * width + chunk(d, step) * shard, 16), shard)
        place_at = pl.ds(pl.multiple_of(at * shard, 16), shard)
        return pltpu.make_async_copy(left.at[rows, :], thin_v.at[min(2 * k + d, 4), place_at, :], thin_sem.at[k, d, at])

    rights = [
        (ddn, ddn_v), (dup, dup_v), (dproj, dpo_v.at[:, pl.ds(0, 3 * width)]),
        (dbr, dpo_v.at[:, pl.ds(3 * width, width)]),
    ]

    def right_copy(k):
        return pltpu.make_async_copy(rights[k][0], rights[k][1], right_sem.at[k])

    for d in range(2):
        wide_copy(d, 0).start()
    right_copy(0).start()
    right_copy(1).start()
    for d in range(2):
        for at in range(2):
            thin_copy(0, d, at).start()
    right_copy(2).start()
    right_copy(3).start()
    for k, d in ((1, 0), (1, 1), (2, 1)):
        for at in range(2):
            thin_copy(k, d, at).start()

    barrier = pltpu.get_barrier_semaphore()
    for peer in target:
        pl.semaphore_signal(barrier, inc=1, device_id={"dp": peer}, device_id_type=LOGICAL)

    @pl.when(first)
    def _():
        pl.semaphore_wait(barrier, 1 + count)

    @pl.when(jnp.logical_not(first))
    def _():
        pl.semaphore_signal(barrier, inc=1, device_id={"pipe": jnp.int32(0)}, device_id_type=LOGICAL)
        pl.semaphore_wait(barrier, 2)

    def tok_part(i, p):
        return pltpu.make_async_remote_copy(
            src_ref=g0.at[i, pl.ds(p * piece, piece)], dst_ref=gtok_o.at[i],
            send_sem=tok_send.at[i, p], recv_sem=tok_recv.at[i],
            device_id={"pipe": jnp.int32(p)}, device_id_type=LOGICAL,
        )

    def tok_own(i):
        return pltpu.make_async_copy(g0.at[i, pl.ds(0, piece)], gtok_o.at[i], tok_send.at[i, 0])

    @pl.when(first)
    def _():
        for i in range(row_count):
            for p in range(1, count):
                tok_part(i, p).start()
            tok_own(i).start()

    def message(slots, send, recv, d, at):
        return pltpu.make_async_remote_copy(
            src_ref=slots.at[d, at], dst_ref=slots.at[d, jnp.minimum(at + 1, n - 1)],
            send_sem=send.at[d, at], recv_sem=recv.at[d, jnp.minimum(at + 1, n - 1)],
            device_id={"dp": target[d]}, device_id_type=LOGICAL,
        )

    def arrived(slots, send, recv, d, at):
        return pltpu.make_async_remote_copy(
            src_ref=slots.at[d, at], dst_ref=slots.at[d, at],
            send_sem=send.at[d, at], recv_sem=recv.at[d, at],
            device_id={"dp": target[d]}, device_id_type=LOGICAL,
        )

    def lane(slots, send, recv, d, step, mine, finish):
        @pl.when(step == 0)
        def _():
            slots[d, 0] = mine.astype(BF16)

        @pl.when(step > 0)
        def _():
            arrived(slots, send, recv, d, step).wait_recv()

            @pl.when(step < n - 1)
            def _():
                slots[d, step] = (slots[d, step].astype(F32) + mine).astype(BF16)

            @pl.when(step == n - 1)
            def _():
                finish(slots[d, step].astype(F32) + mine)

        @pl.when(step < n - 1)
        def _():
            message(slots, send, recv, d, step).start()

    def small_message(at):
        return pltpu.make_async_remote_copy(
            src_ref=slots_s.at[at], dst_ref=slots_s.at[jnp.minimum(at + 1, n - 1)],
            send_sem=send_s.at[at], recv_sem=recv_s.at[jnp.minimum(at + 1, n - 1)],
            device_id={"dp": target[0]}, device_id_type=LOGICAL,
        )

    def small_arrived(at):
        return pltpu.make_async_remote_copy(
            src_ref=slots_s.at[at], dst_ref=slots_s.at[at], send_sem=send_s.at[at],
            recv_sem=recv_s.at[at], device_id={"dp": target[0]}, device_id_type=LOGICAL,
        )

    sum_rows = lax.broadcasted_iota(jnp.int32, (16, 128), 0) < 9

    def small_step(step):
        mine = small[chunk(0, step)]

        @pl.when(step == 0)
        def _():
            slots_s[0] = mine

        @pl.when(step > 0)
        def _():
            small_arrived(step).wait_recv()
            got = slots_s[step]
            slots_s[step] = jnp.where(sum_rows, got + mine, jnp.maximum(got, mine))

        @pl.when(step < n - 1)
        def _():
            small_message(step).start()

        @pl.when(step == n - 1)
        def _():
            small_o[...] = slots_s[step]

    half, half_ff = width // 2, ff // 2

    def fetched(copy, step, *args):
        copy(*args, step).wait()

    def refill(copy, step, *args):
        @pl.when(step < n - 1)
        def _():
            copy(*args, step + 1).start()

    def right_ready(k, step):
        @pl.when(step == 0)
        def _():
            right_copy(k).wait()

    def turn(step, _):
        right_ready(0, step)
        for d in range(2):
            cols = slice(d * half, (d + 1) * half)
            fetched(wide_copy, step, d)
            mine = dot_nn(wide_v[d], ddn_v[:, cols])
            refill(wide_copy, step, d)

            def finish_down(total):
                gd_o[:, cols] = total

            lane(slots_d, send_d, recv_d, d, step, mine, finish_down)
        small_step(step)
        right_ready(1, step)
        paired = lax.rem(step, 2) == 0

        def together(k, d, right, store):
            for at in range(2):
                thin_copy(k, d, step + at).wait()
            both = dot_nn(thin_v[min(2 * k + d, 4)], right)
            store(0, both[:shard])
            store(1, both[shard:])

            @pl.when(step + 2 < n)
            def _():
                for at in range(2):
                    thin_copy(k, d, step + 2 + at).start()

        for d in range(2):
            cols = slice(d * half_ff, (d + 1) * half_ff)

            @pl.when(paired)
            def _():
                def store(at, v):
                    if at == 0:
                        mine_u[d] = v
                    else:
                        gu_o[:, cols] = v

                together(0, d, dup_v[:, cols], store)

            @pl.when(jnp.logical_not(paired))
            def _():
                mine_u[d] = gu_o[:, cols]

            def finish_up(total):
                gu_o[:, cols] = total

            lane(slots_u, send_u, recv_u, d, step, mine_u[d], finish_up)
        right_ready(2, step)
        right_ready(3, step)

        @pl.when(paired)
        def _():
            def store(at, v):
                if at == 0:
                    mine_q[0] = v
                else:
                    gq_o[:, 0 : 2 * width] = v

            together(1, 0, dpo_v[:, 0 : 2 * width], store)

        @pl.when(jnp.logical_not(paired))
        def _():
            mine_q[0] = gq_o[:, 0 : 2 * width]

        def finish_ahead(total):
            gq_o[:, 0 : 2 * width] = total

        lane(slots_q, send_q, recv_q, 0, step, mine_q[0], finish_ahead)

        @pl.when(paired)
        def _():
            for k, out, cols in ((1, gq_o, slice(2 * width, 3 * width)), (2, go_o, slice(0, width))):
                def store(at, v):
                    if at == 0:
                        mine_q[1, :, (k - 1) * width : k * width] = v
                    else:
                        out[:, cols] = v

                together(k, 1, dpo_v[:, (k + 1) * width : (k + 2) * width], store)

        @pl.when(jnp.logical_not(paired))
        def _():
            mine_q[1, :, 0:width] = gq_o[:, 2 * width : 3 * width]
            mine_q[1, :, width : 2 * width] = go_o[...]

        def finish_behind(total):
            gq_o[:, 2 * width : 3 * width] = total[:, 0:width]
            go_o[...] = total[:, width : 2 * width]

        lane(slots_q, send_q, recv_q, 1, step, mine_q[1], finish_behind)
        return 0

    lax.fori_loop(0, n, turn, 0)

    def drain(at, _):
        for d in range(2):
            message(slots_d, send_d, recv_d, d, at).wait_send()
            message(slots_u, send_u, recv_u, d, at).wait_send()
            message(slots_q, send_q, recv_q, d, at).wait_send()
        small_message(at).wait_send()
        return 0

    lax.fori_loop(0, n - 1, drain, 0)

    @pl.when(first)
    def _():
        for i in range(row_count):
            for p in range(1, count):
                tok_part(i, p).wait_send()
            tok_own(i).wait()

    @pl.when(jnp.logical_not(first))
    def _():
        for i in range(row_count):
            tok_part(i, 1).wait_recv()


def run_grads(count, n, left, dproj, dbr, dup, ddn, g0, small):
    rows, seq, width = g0.shape
    ff = dup.shape[2]
    flat = lambda a: a.reshape(rows * seq, a.shape[2])
    tok = rows * seq
    shard, shard_ff = width // n, ff // n
    ops = [left] + [flat(a) for a in (ddn, dup, dproj, dbr)]
    vmem = pl.BlockSpec(memory_space=pltpu.VMEM)
    sem = pltpu.SemaphoreType.DMA
    return pl.pallas_call(
        lambda *refs: grad_kernel(count, n, *refs),
        in_specs=[ANYWHERE] * 5 + [vmem, ANYWHERE],
        out_specs=[vmem] * 5 + [ANYWHERE],
        out_shape=[
            jax.ShapeDtypeStruct((shard, 3 * width), F32),
            jax.ShapeDtypeStruct((shard, width), F32),
            jax.ShapeDtypeStruct((shard, ff), F32),
            jax.ShapeDtypeStruct((shard_ff, width), F32),
            jax.ShapeDtypeStruct((16, 128), F32),
            jax.ShapeDtypeStruct((rows, seq // count, width), BF16),
        ],
        scratch_shapes=[
            pltpu.VMEM((2, n, shard_ff, width // 2), BF16),
            pltpu.VMEM((2, n, shard, ff // 2), BF16),
            pltpu.VMEM((2, n, shard, 2 * width), BF16),
            pltpu.VMEM((n, 16, 128), F32),
            pltpu.VMEM((2, shard_ff, tok), BF16),
            pltpu.VMEM((5, 2 * shard, tok), BF16),
            pltpu.VMEM((tok, width), BF16),
            pltpu.VMEM((tok, ff), BF16),
            pltpu.VMEM((tok, 4 * width), BF16),
            pltpu.VMEM((2, shard, ff // 2), F32),
            pltpu.VMEM((2, shard, 2 * width), F32),
            sem((2,)), sem((3, 2, 2)), sem((4,)),
            sem((2, n)), sem((2, n)), sem((2, n)), sem((2, n)), sem((2, n)), sem((2, n)),
            sem((n,)), sem((n,)), sem((rows, count)), sem((rows,)),
        ],
        compiler_params=pltpu.CompilerParams(
            collective_id=2, has_side_effects=True, vmem_limit_bytes=VMEM_LIMIT,
        ),
        cost_estimate=pl.CostEstimate(
            flops=2 * tok * (4 * width * width + 2 * width * ff), bytes_accessed=tok * 25000, transcendentals=0,
        ),
    )(*ops, small, g0)


def place_kernel(*refs):
    larges, small, outs, smalls = refs[:6], refs[6], refs[7:13], refs[13:]
    for source, out in zip(larges, outs):
        out[...] = source[...].reshape(out.shape)
    flat = jnp.concatenate([small[i : i + 1, :] for i in range(9)], 1)
    gain, shift, s_out, s_down, s_up, s_qv, top = smalls
    thin = gain.shape[2]
    at = 0
    for ref, index in ((gain, 0), (gain, 1), (shift, 0), (shift, 1)):
        ref[0, index : index + 1, :] = flat[:, at : at + thin]
        at += thin
    for ref in (s_out, s_down, s_up, s_qv):
        ref[...] = flat[:, at : at + ref.shape[1]]
        at += ref.shape[1]
    top[...] = small[9:10, 0:4]


def place(n, larges, small, width, ff):
    thin = width // n
    shapes = [jax.ShapeDtypeStruct(v.shape, v.dtype) for v in larges[:2]]
    shapes += [jax.ShapeDtypeStruct((1, *v.shape), v.dtype) for v in larges[2:]]
    smalls = [(1, 2, thin), (1, 2, thin), (1, thin), (1, thin), (1, ff // n), (1, 2 * thin), (1, 4)]
    vmem = pl.BlockSpec(memory_space=pltpu.VMEM)
    return pl.pallas_call(
        place_kernel,
        in_specs=[vmem] * 7,
        out_specs=[vmem] * 13,
        out_shape=shapes + [jax.ShapeDtypeStruct(s, F32) for s in smalls],
        compiler_params=pltpu.CompilerParams(vmem_limit_bytes=VMEM_LIMIT),
    )(*larges, small)


def weight_grad(left, right):
    g = jnp.einsum("rsd,rse->de", left, right, preferred_element_type=F32).astype(BF16)
    return lax.psum_scatter(g, "dp", scatter_dimension=0, tiled=True).astype(F32)


def share_pieces(whole_rows, count, stage):
    piece = whole_rows.shape[1] // count
    mine = whole_rows[:, :piece]
    for p in range(1, count):
        got = lax.ppermute(whole_rows[:, p * piece : (p + 1) * piece], "pipe", [(0, p)])
        mine = jnp.where(stage == p, got, mine)
    return mine


def shards(
    tokens, lengths, ema_scales, w_qkv, bias_qv, w_out, bias_out, w_up, bias_up, w_down, bias_down,
    ln_gain, ln_bias, cotangent,
):
    count = lax.axis_size("pipe")
    n = lax.axis_size("dp")
    width = tokens.shape[2]
    ff = w_up.shape[2]
    b_qkv = jnp.concatenate([bias_qv[:, :width], jnp.zeros_like(bias_qv[:, :width]), bias_qv[:, width:]], 1)
    weights = (
        w_qkv[0], b_qkv, w_out[0], bias_out, w_up[0], bias_up, w_down[0], bias_down, ln_gain[0], ln_bias[0],
    )
    *kept, mixed, peaks = run_forward(count, tokens, lengths, ema_scales, weights)
    left = kept[-2]
    dproj, dbr, dup, ddn, g0, turned, small = run_backward(
        count, cotangent, lengths, ema_scales, weights, kept
    )
    sums = jnp.sum(small, 0)
    parts, at = [], 0
    for size in (width, width, width, width, width, width, ff, width, width, width):
        parts.append(sums[at : at + size])
        at += size
    parts[7:] = [jnp.concatenate([parts[7], parts[9]])]
    packed = jnp.concatenate([v.reshape(n, -1) for v in parts], 1)
    peak = jnp.max(peaks, (1, 2))
    sums_width = packed.shape[1]
    if n >= 4 and n % 2 == 0 and width // n % 16 == 0 and ff // n % 128 == 0 and sums_width == 9 * 128:
        top = jnp.broadcast_to(jnp.pad(peak, (0, 124))[None, None], (n, 7, 128))
        with_peak = jnp.concatenate([packed.reshape(n, 9, 128), top], 1)
        g_qkv, g_out, g_up, g_down, small_sum, grad_tokens = run_grads(
            count, n, turned, dproj, dbr, dup, ddn, g0, with_peak
        )
        larges = (mixed, grad_tokens, g_qkv, g_out, g_up, g_down)
        placed = place(n, larges, small_sum, width, ff)
        mixed, grad_tokens, g_qkv, g_out, g_up, g_down, g_gain, g_shift, s_out, s_down, s_up, s_qv, top = placed
        return (
            mixed, grad_tokens, g_qkv, s_qv, g_out, s_out, g_up, s_up, g_down, s_down, g_gain, g_shift, top,
        )
    else:
        g_down = weight_grad(left[:, :, :ff], ddn)
        g_up = weight_grad(left[:, :, ff : ff + width], dup)
        g_qkv = weight_grad(left[:, :, ff + width : ff + 2 * width], dproj)
        g_out = weight_grad(left[:, :, ff + 2 * width :], dbr)
        mine = lax.psum_scatter(packed, "dp", scatter_dimension=0, tiled=True)
        batch_max = lax.pmax(peak, "dp")[None]
        grad_tokens = share_pieces(g0, count, lax.axis_index("pipe"))
    outs, at = [], 0
    for size in (width, width, width, width, width, width, ff, 2 * width):
        outs.append(mine[:, at : at + size // n])
        at += size // n
    gain0, gain1, shift0, shift1, s_out, s_down, s_up, s_qv = outs
    g_gain = jnp.stack([gain0, gain1], 1)
    g_shift = jnp.stack([shift0, shift1], 1)
    return (
        mixed, grad_tokens, g_qkv[None], s_qv, g_out[None], s_out, g_up[None], s_up, g_down[None], s_down,
        g_gain, g_shift, batch_max,
    )


def solution(mesh):
    return jax.shard_map(
        shards,
        mesh=mesh,
        in_specs=(
            P("dp", None, None), P("dp"), P("pipe", None), P("pipe", None, None), P("pipe", None),
            P("pipe", None, None), P("pipe", None), P("pipe", None, None), P("pipe", None),
            P("pipe", None, None), P("pipe", None), P("pipe", None, None), P("pipe", None, None),
            P("dp", None, None),
        ),
        out_specs=(
            P("dp", "pipe", None), P("dp", "pipe", None), P("pipe", "dp", None), P("pipe", "dp"),
            P("pipe", "dp", None), P("pipe", "dp"), P("pipe", "dp", None), P("pipe", "dp"),
            P("pipe", "dp", None), P("pipe", "dp"), P("pipe", None, "dp"), P("pipe", None, "dp"),
            P("pipe", None),
        ),
        check_vma=False,
    )
```
